32 devices in a mesh: dom: 8 (over z, x), feat: 4 (over y, core).
Axes of the slice: x: 2, y: 2, z: 4, core: 2. Of those that a mesh axis runs over, the one named last changes fastest.
Arguments:
- features: float32 [12288, 1024], P('dom', 'feat'), may hold values from -6 to 6
- degree: int32 [12288], P('dom'), may hold values from 1 to 9
- diag_adj: float32 [12288, 128], P('dom'), may hold values from -0.5 to 0.5
- remote_adj: float32 [8, 6, 128, 128], P('dom'), may hold values from -0.5 to 0.5
- read_block: int32 [8, 8], P('dom'), may hold values from 0 to 12, as said below
- tile_src: int32 [8, 6], P('dom'), may hold values from 0 to 7, as said below
- tile_row: int32 [8, 6], P('dom'), may hold values from 0 to 11, as said below
- w_first: float32 [1024, 1024], P('feat'), may hold values from -0.25 to 0.25
- b_first: float32 [1024], replicated, may hold values from -2 to 2
- w_second: float32 [1024, 1024], P('feat'), may hold values from -0.25 to 0.25
- b_second: float32 [1024], replicated, may hold values from -2 to 2
Outputs:
- embed: float32 [12288, 1024], P(('dom', 'feat'))
The draws below stay inside these ranges and needn't reach their ends.
Inputs may be any that keep to these rules, and one draw needn't show every extreme that they name: `read_block`: entry [s, d] is the block of partition s that partition d reads, or 12 if d does not read s. Every partition reads exactly 3 other partitions, one block of each, and never itself. `tile_src`: tiles come in groups of 2 consecutive tiles with the same source partition; the sources of a partition's tiles are exactly the 3 partitions that it reads according to read_block. `tile_row`: within a group of 2 tiles with the same source, the block rows are distinct.
All inputs are finite; a program needn't handle non-finite values.
Results may differ from the reference program's by a relative error of at most 0.0003.
Values sent between devices are 32-bit elements; how exact they have to be, the bound alone decides.
No kernel may reach another device: no remote copies, remote signals or barrier semaphores. Data moves between devices by JAX's collectives and lax.ppermute only.
A program may use at most 128 MiB of HBM per device.

```python
import jax
import jax.numpy as jnp
from jax import lax

HIDDEN_SIZE = 1024
TILE = 128
BLK_DEV = 12
TOUCH = 2
NPARTS = 8
READS = 3
REMOTE = 6
PART = 1536
VERTS = 12288


def graph_tables(key):
    base = jax.random.fold_in(key, 7)
    key_pop, key_noise, key_block, key_rows = jax.random.split(base, 4)
    popular = jax.random.randint(key_pop, (NPARTS,), 0, 4) * 256
    noise = jax.random.randint(key_noise, (NPARTS, NPARTS), 0, 1024)
    indices = jnp.arange(NPARTS, dtype=jnp.int32)
    score = (noise + popular[None, :]) * 4096 + indices[None, :]
    score = jnp.where(indices[:, None] == indices[None, :], -1, score)
    _, sources = lax.top_k(score, READS)
    sources = sources.astype(jnp.int32)
    chosen = jax.random.randint(key_block, (NPARTS, READS), 0, BLK_DEV)
    readers = jnp.broadcast_to(indices[:, None], sources.shape)
    table = jnp.full((NPARTS, NPARTS), BLK_DEV, jnp.int32).at[sources, readers].set(chosen.astype(jnp.int32))
    row_scores = jax.random.randint(key_rows, (NPARTS, READS, BLK_DEV), 0, 1 << 20) * BLK_DEV + jnp.arange(BLK_DEV, dtype=jnp.int32)
    _, rows = lax.top_k(row_scores, TOUCH)
    tile_rows = rows.astype(jnp.int32).reshape(NPARTS, REMOTE)
    tile_sources = jnp.broadcast_to(sources[:, :, None], (NPARTS, READS, TOUCH)).reshape(NPARTS, REMOTE)
    return (table, tile_sources, tile_rows)


def draw_read_block(key, part):
    return graph_tables(key)[0]


def draw_tile_src(key, part):
    return graph_tables(key)[1]


def draw_tile_row(key, part):
    return graph_tables(key)[2]


def with_ends(drawn, stream_key, smallest, top_value):
    spot = [jax.random.randint(jax.random.fold_in(stream_key, axis), (), 0, length) for axis, length in enumerate(drawn.shape)]
    longest = drawn.shape.index(max(drawn.shape))
    next_to = spot[:longest] + [(spot[longest] + 1) % drawn.shape[longest]] + spot[longest + 1:]
    return drawn.at[tuple(spot)].set(smallest).at[tuple(next_to)].set(top_value)


def level_of(key, shape, cuts, low, high):
    def one(dim, parts):
        steps = jax.random.uniform(jax.random.fold_in(jax.random.fold_in(key, 6), dim), (parts,), jnp.float32, low / len(cuts), high / len(cuts))
        return jnp.repeat(jnp.exp(steps), shape[dim] // parts).reshape((-1,) + (1,) * (len(shape) - dim - 1))

    level = one(*cuts[0])
    for cut in cuts[1:]:
        level = level * one(*cut)
    return level


def gaussian(rng, dims, scale, reach, cuts=(), kind=jnp.bfloat16):
    entries = jax.random.normal(rng, dims, jnp.float32) * scale
    if len(cuts) > 0:
        entries = level_of(rng, dims, cuts, -0.22, 0.18) * entries
    return jnp.clip(entries, min=-reach, max=reach).astype(kind)


def setup_inputs(seed: int = 0) -> dict:
    key_of = jax.random.split(jax.random.key(seed), 12)
    features = gaussian(key_of[0], (VERTS, HIDDEN_SIZE), 1.0, 6.0, ((0, 8), (1, 4)), jnp.float32)
    degree = with_ends(jax.random.randint(key_of[1], (VERTS,), 1, 10), jax.random.fold_in(key_of[1], 1), 1, 9).astype(jnp.int32)
    diag_adj = gaussian(key_of[2], (VERTS, TILE), (TILE * (1 + REMOTE // BLK_DEV)) ** -0.5, 0.5, ((0, 8),), jnp.float32)
    remote_adj = gaussian(key_of[3], (NPARTS, REMOTE, TILE, TILE), (TILE * (1 + REMOTE // BLK_DEV)) ** -0.5, 0.5, ((0, 8),), jnp.float32)
    read_block = draw_read_block(jax.random.fold_in(key_of[11], 71), 0)
    tile_src = draw_tile_src(jax.random.fold_in(key_of[11], 71), 0)
    tile_row = draw_tile_row(jax.random.fold_in(key_of[11], 71), 0)
    w_first = gaussian(key_of[7], (HIDDEN_SIZE, HIDDEN_SIZE), (HIDDEN_SIZE // 2) ** -0.5, 0.25, ((0, 4),), jnp.float32)
    b_first = gaussian(key_of[8], (HIDDEN_SIZE,), 0.3, 2.0, (), jnp.float32)
    w_second = gaussian(key_of[9], (HIDDEN_SIZE, HIDDEN_SIZE), (HIDDEN_SIZE // 2) ** -0.5, 0.25, ((0, 4),), jnp.float32)
    b_second = gaussian(key_of[10], (HIDDEN_SIZE,), 0.3, 2.0, (), jnp.float32)
    return dict(features=features, degree=degree, diag_adj=diag_adj, remote_adj=remote_adj, read_block=read_block, tile_src=tile_src, tile_row=tile_row, w_first=w_first, b_first=b_first, w_second=w_second, b_second=b_second)


def layer(hidden_in, scaling, diag_adj, remote_adj, read_block, tile_src, tile_row, weight, bias, rectify):
    width = hidden_in.shape[1]
    scaled = hidden_in * scaling[:, None]
    blocks = scaled.reshape(NPARTS, BLK_DEV, TILE, width)
    diag_tiles = diag_adj.reshape(NPARTS, BLK_DEV, TILE, TILE)
    part_scaling = scaling.reshape(NPARTS, PART)
    levels = jnp.arange(BLK_DEV, dtype=jnp.int32)

    def one_part(items):
        own_tiles, adjacency, sources, rows, part_index, row_scaling = items
        own_blocks = blocks[part_index]
        own = jnp.einsum('bij,bjf->bif', own_tiles, own_blocks, precision=lax.Precision.HIGHEST)
        chosen = read_block[sources, part_index]
        picked = blocks[sources, chosen]
        products = jnp.einsum('kij,kjf->kif', adjacency, picked, precision=lax.Precision.HIGHEST)
        row_onehot = (rows[None, :] == levels[:, None]).astype(scaled.dtype)
        remote = jnp.einsum('bk,kif->bif', row_onehot, products, precision=lax.Precision.HIGHEST)
        aggregated = (own + remote).reshape(PART, width) * row_scaling[:, None]
        mixed = jnp.dot(aggregated, weight, precision=lax.Precision.HIGHEST) + bias[None, :]
        if rectify:
            mixed = jnp.maximum(mixed, 0.0)
        return mixed
    result = lax.map(one_part, (diag_tiles, remote_adj, tile_src, tile_row, jnp.arange(NPARTS, dtype=jnp.int32), part_scaling))
    return result.reshape(VERTS, width)

def reference(features, degree, diag_adj, remote_adj, read_block, tile_src, tile_row, w_first, b_first, w_second, b_second):
    scaling = lax.rsqrt(degree.astype(jnp.float32))
    hidden = layer(features, scaling, diag_adj, remote_adj, read_block, tile_src, tile_row, w_first, b_first, True)
    return layer(hidden, scaling, diag_adj, remote_adj, read_block, tile_src, tile_row, w_second, b_second, False)
```

```python
import functools

import jax
import jax.numpy as jnp
from jax import lax
from jax.experimental import pallas as pl
from jax.experimental.pallas import tpu as pltpu
from jax.sharding import PartitionSpec as P

LANES = 128
VMEM_LIMIT = 48 * 1024 * 1024
VMEM = pl.BlockSpec(memory_space=pltpu.VMEM)
SMEM = pl.BlockSpec(memory_space=pltpu.SMEM)


def dot3(a, b):
    return jnp.dot(a, b, precision=lax.Precision.HIGH, preferred_element_type=jnp.float32)


def call(body, in_specs, outs, scratch=(), flops=0):
    moved = sum(o.size * 4 for o in outs)
    return pl.pallas_call(
        body,
        out_shape=list(outs),
        in_specs=list(in_specs),
        out_specs=[VMEM] * len(outs),
        scratch_shapes=list(scratch),
        compiler_params=pltpu.CompilerParams(vmem_limit_bytes=VMEM_LIMIT),
        cost_estimate=pl.CostEstimate(flops=flops, bytes_accessed=2 * moved, transcendentals=0),
    )


def f32(*dims):
    return jax.ShapeDtypeStruct(dims, jnp.float32)


def copy_wanted(want_ref, source, blocks_out):
    tile = blocks_out[0].shape[0]
    for j, block in enumerate(blocks_out):
        start = pl.multiple_of(want_ref[j] * tile, tile)
        block[...] = source[pl.ds(start, tile), :]


def scale_body(parts, want_ref, *refs):
    sums, spread, scaled, blocks_out = refs[:parts], refs[parts], refs[parts + 1], refs[parts + 2 :]
    total = sums[0][...]
    for extra in sums[1:]:
        total = total + extra[...]
    scaled[...] = total * spread[...]
    copy_wanted(want_ref, scaled, blocks_out)


def own_body(diag, scaled, base):
    tile = diag.shape[1]
    for i in range(diag.shape[0] // tile):
        rows = pl.ds(i * tile, tile)
        base[rows, :] = dot3(diag[rows, :], scaled[rows, :])


def add_remote(slot_ref, row_ref, remote, incoming, total):
    tile = remote.shape[1]
    tiles = remote.shape[0]
    for j, block in enumerate(incoming):

        def step(k, carry, j=j, block=block):
            @pl.when(slot_ref[k] == j)
            def _():
                rows = pl.ds(pl.multiple_of(row_ref[k] * tile, tile), tile)
                total[rows, :] += dot3(remote[k], block[...])

            return carry

        lax.fori_loop(0, tiles, step, 0)


def hidden_body(peers, slot_ref, row_ref, want_ref, *refs):
    incoming = refs[:peers]
    base, remote, spread, bias, scaled = refs[peers : peers + 5]
    blocks_out, total = refs[peers + 5 : -1], refs[-1]
    total[...] = base[...]
    add_remote(slot_ref, row_ref, remote, incoming, total)
    hidden = jnp.maximum(total[...] * spread[...] + bias[...], 0.0)
    scaled[...] = hidden * spread[...]
    copy_wanted(want_ref, scaled, blocks_out)


def pieces_body(peers, slot_ref, row_ref, place_ref, *refs):
    incoming = refs[:peers]
    base, remote, spread = refs[peers : peers + 3]
    pieces, total = refs[peers + 3 : -1], refs[-1]
    total[...] = base[...]
    add_remote(slot_ref, row_ref, remote, incoming, total)
    total[...] = total[...] * spread[...]
    height = pieces[0].shape[0]
    for j, piece in enumerate(pieces):
        start = pl.multiple_of(place_ref[j] * height, height)
        piece[...] = total[pl.ds(start, height), :]


def solution(mesh):
    parts = mesh.shape["dom"]
    feats = mesh.shape["feat"]
    sides = 2 if feats % 2 == 0 else 1
    halves = feats // sides
    paired = parts & (parts - 1) == 0

    def peer(s, k):
        return s ^ k if paired else (s + k) % parts

    def origin_slot(me, src):
        return me ^ src if paired else (me - src) % parts

    def dom_send(x, k):
        return lax.ppermute(x, "dom", [(s, peer(s, k)) for s in range(parts)])

    def feat_target(f, dh, dl):
        return (f // sides + dh) % halves * sides + (f % sides + dl) % sides

    def feat_source(f, dh, dl):
        return (f // sides - dh) % halves * sides + (f % sides - dl) % sides

    def feat_send(x, dh, dl):
        return lax.ppermute(x, "feat", [(f, feat_target(f, dh, dl)) for f in range(feats)])

    def per_device(
        features,
        degree,
        diag_adj,
        remote_adj,
        read_block,
        tile_src,
        tile_row,
        w_first,
        b_first,
        w_second,
        b_second,
    ):
        part, own_cols = features.shape
        width = w_first.shape[1]
        tile = diag_adj.shape[1]
        blocks = part // tile
        remote = remote_adj[0]
        tiles = remote.shape[0]
        cols = width // feats
        chunk = LANES if cols % LANES == 0 else cols
        chunks = cols // chunk
        me = lax.axis_index("dom")
        f = lax.axis_index("feat")
        half, side = f // sides, f % sides
        peers = parts - 1

        scaling = lax.rsqrt(degree.astype(jnp.float32))
        spread = jnp.broadcast_to(scaling[:, None], (part, chunk))
        targets = jnp.stack([jnp.asarray(peer(me, k), jnp.int32) for k in range(1, parts)])
        want = jnp.minimum(read_block[0][targets], blocks - 1)
        slot = origin_slot(me, tile_src[0]) - 1
        row = tile_row[0]
        shifts = [(dh, dl) for dh in range(halves) for dl in range(sides)]
        place = jnp.stack([jnp.asarray(feat_target(f, dh, dl), jnp.int32) for dh, dl in shifts])

        w_grid = w_first.reshape(own_cols, halves, sides, cols)

        def w_cols(dl):
            return lax.dynamic_index_in_dim(w_grid, (side + dl) % sides, 2, keepdims=False)

        x_all = [features] + [feat_send(features, 0, dl) for dl in range(1, sides)]
        w_all = [w_cols(0)] + [feat_send(w_cols(dl), 0, dl) for dl in range(1, sides)]

        def partial_sum(dh, c):
            total = 0.0
            for x, w in zip(x_all, w_all):
                block = lax.dynamic_index_in_dim(w, (half + dh) % halves, 1, keepdims=False)
                total = total + dot3(x, block[:, c * chunk : (c + 1) * chunk])
            return total

        w2_half = [w_second] + [feat_send(w_second, dh, 0) for dh in range(1, halves)]

        sums = []
        for c in range(chunks):
            received = [feat_send(partial_sum(dh, c), dh, 0) for dh in range(1, halves)]
            sums.append([partial_sum(0, c)] + received)

        flops = 6 * blocks * tile * tile * chunk
        remote_flops = 6 * tiles * tile * tile * chunk
        block_shapes = [f32(tile, chunk)] * peers
        bias_all = b_first.reshape(feats, chunks, 1, chunk)
        bias_own = lax.dynamic_index_in_dim(bias_all, f, 0, keepdims=False)

        def own(scaled):
            return call(own_body, [VMEM] * 2, [f32(part, chunk)], flops=flops)(diag_adj, scaled)[0]

        collected = []
        for c in range(chunks):
            scaled, *outgoing = call(
                functools.partial(scale_body, halves),
                [SMEM] + [VMEM] * (halves + 1),
                [f32(part, chunk)] + block_shapes,
            )(want, *sums[c], spread)
            incoming = [dom_send(b, k + 1) for k, b in enumerate(outgoing)]
            base = own(scaled)
            scaled, *outgoing = call(
                functools.partial(hidden_body, peers),
                [SMEM] * 3 + [VMEM] * (peers + 4),
                [f32(part, chunk)] + block_shapes,
                [pltpu.VMEM((part, chunk), jnp.float32)],
                remote_flops,
            )(slot, row, want, *incoming, base, remote, spread, bias_own[c])
            incoming = [dom_send(b, k + 1) for k, b in enumerate(outgoing)]
            base = own(scaled)
            pieces = call(
                functools.partial(pieces_body, peers),
                [SMEM] * 3 + [VMEM] * (peers + 3),
                [f32(part // feats, chunk)] * feats,
                [pltpu.VMEM((part, chunk), jnp.float32)],
                remote_flops,
            )(slot, row, place, *incoming, base, remote, spread)
            collected.append(
                [p if dh == 0 and dl == 0 else feat_send(p, dh, dl) for (dh, dl), p in zip(shifts, pieces)]
            )

        w2_all = [[w] + [feat_send(w, 0, dl) for dl in range(1, sides)] for w in w2_half]
        out = b_second[None, :]
        for c in range(chunks):
            for (dh, dl), piece in zip(shifts, collected[c]):
                out = out + dot3(piece, w2_all[dh][dl][c * chunk : (c + 1) * chunk])
        return out

    return jax.shard_map(
        per_device,
        mesh=mesh,
        in_specs=(
            P("dom", "feat"),
            P("dom"),
            P("dom", None),
            P("dom", None, None, None),
            P("dom", None),
            P("dom", None),
            P("dom", None),
            P("feat", None),
            P(),
            P("feat", None),
            P(),
        ),
        out_specs=P(("dom", "feat"), None),
        check_vma=False,
    )
```

```python
import functools

import jax
import jax.numpy as jnp
from jax import lax
from jax.experimental import pallas as pl
from jax.experimental.pallas import tpu as pltpu
from jax.sharding import PartitionSpec as P

LANES = 128
TOUCH = 2
VMEM_LIMIT = 48 * 1024 * 1024
VMEM = pl.BlockSpec(memory_space=pltpu.VMEM)
SMEM = pl.BlockSpec(memory_space=pltpu.SMEM)


def dot3(a, b):
    return jnp.dot(a, b, precision=lax.Precision.HIGH, preferred_element_type=jnp.float32)


def f32(*dims):
    return jax.ShapeDtypeStruct(dims, jnp.float32)


def call(body, scalars, arrays, outs, scratch=(), flops=0):
    moved = sum(4 * a.size for a in list(arrays) + list(outs))
    return pl.pallas_call(
        body,
        out_shape=list(outs),
        in_specs=[SMEM] * len(scalars) + [VMEM] * len(arrays),
        out_specs=[VMEM] * len(outs),
        scratch_shapes=list(scratch),
        compiler_params=pltpu.CompilerParams(vmem_limit_bytes=VMEM_LIMIT),
        cost_estimate=pl.CostEstimate(flops=flops, bytes_accessed=moved, transcendentals=0),
    )(*scalars, *arrays)


def rows_at(index, height):
    return pl.ds(pl.multiple_of(index * height, height), height)


def outgoing_body(want_ref, features, spread, blocks):
    tile, cols = blocks.shape[1:]
    chunk = spread.shape[1]
    for d in range(blocks.shape[0]):
        rows = rows_at(want_ref[d], tile)
        for c in range(cols // chunk):
            lanes = pl.ds(c * chunk, chunk)
            blocks[d, :, lanes] = features[rows, lanes] * spread[rows, :]


def arrange_body(place_ref, weight, *arranged):
    halves = arranged[0].shape[1] // (weight.shape[1] // place_ref.shape[0])
    cols = arranged[0].shape[1] // halves
    for dl, out in enumerate(arranged):
        for dh in range(halves):
            index = place_ref[dh * len(arranged) + dl]
            lanes = pl.ds(pl.multiple_of(index * cols, cols), cols)
            out[:, pl.ds(dh * cols, cols)] = weight[:, lanes]


def chosen_body(source_ref, incoming, chosen):
    tile = incoming.shape[1]
    for g in range(chosen.shape[0] // tile):
        chosen[pl.ds(g * tile, tile), :] = incoming[source_ref[TOUCH * g]]


def own_sum_body(diag, spread, *refs):
    sums, base, scaled = refs[:-2], refs[-2], refs[-1]
    total = sums[0][...]
    for extra in sums[1:]:
        total = total + extra[...]
    scaled[...] = total * spread[...]
    own_body(diag, scaled, base)


def own_body(diag, scaled, base):
    tile = diag.shape[1]
    for i in range(diag.shape[0] // tile):
        rows = pl.ds(i * tile, tile)
        base[rows, :] = dot3(diag[rows, :], scaled[rows, :])


def hidden_body(row_ref, want_ref, base, remote, spread, bias, *refs):
    sums, scaled, blocks, total = refs[:-3], refs[-3], refs[-2], refs[-1]
    tiles, tile = remote.shape[:2]
    total[...] = base[...]
    for g in range(tiles // TOUCH):
        rows = pl.ds(g * tile, tile)
        block = sums[0][rows, :]
        for extra in sums[1:]:
            block = block + extra[rows, :]
        for k in range(TOUCH * g, TOUCH * g + TOUCH):
            total[rows_at(row_ref[k], tile), :] += dot3(remote[k], block)
    hidden = jnp.maximum(total[...] * spread[...] + bias[...], 0.0)
    scaled[...] = hidden * spread[...]
    for d in range(blocks.shape[0]):
        blocks[d] = scaled[rows_at(want_ref[d], tile), :]


def pieces_body(source_ref, row_ref, place_ref, base, remote, spread, incoming, *refs):
    pieces, total = refs[:-1], refs[-1]
    tiles, tile = remote.shape[:2]
    total[...] = base[...]
    for k in range(tiles):
        total[rows_at(row_ref[k], tile), :] += dot3(remote[k], incoming[source_ref[k]])
    total[...] = total[...] * spread[...]
    height = pieces[0].shape[0]
    for j, piece in enumerate(pieces):
        piece[...] = total[rows_at(place_ref[j], height), :]


def product_body(count, start, *refs):
    pieces, weights, out = refs[:count], refs[count : 2 * count], refs[-1]
    total = start[...]
    for piece, weight in zip(pieces, weights):
        total = total + dot3(piece[...], weight[...])
    out[...] = total


def add_product(start, pieces, weights, c):
    rows, chunk = pieces[0].shape
    width = weights[0].shape[1]
    step = min(2 * LANES, width)
    count = len(pieces)
    return pl.pallas_call(
        functools.partial(product_body, count),
        out_shape=f32(rows, width),
        grid=(width // step,),
        in_specs=[pl.BlockSpec((start.shape[0], step), lambda j: (0, j))]
        + [pl.BlockSpec((rows, chunk), lambda j: (0, 0))] * count
        + [pl.BlockSpec((chunk, step), lambda j: (c, j))] * count,
        out_specs=pl.BlockSpec((rows, step), lambda j: (0, j)),
        compiler_params=pltpu.CompilerParams(vmem_limit_bytes=VMEM_LIMIT),
        cost_estimate=pl.CostEstimate(
            flops=6 * count * rows * chunk * width,
            bytes_accessed=4 * count * chunk * (rows + width) + 8 * rows * width,
            transcendentals=0,
        ),
    )(start, *pieces, *weights)


def solution(mesh):
    parts = mesh.shape["dom"]
    feats = mesh.shape["feat"]
    sides = 2 if feats % 2 == 0 else 1
    halves = feats // sides

    def feat_target(f, dh, dl):
        return (f // sides + dh) % halves * sides + (f % sides + dl) % sides

    def feat_send(x, dh, dl):
        return lax.ppermute(x, "feat", [(f, feat_target(f, dh, dl)) for f in range(feats)])

    def dom_exchange(x):
        return lax.all_to_all(x, "dom", split_axis=0, concat_axis=0, tiled=True)

    def per_device(
        features,
        degree,
        diag_adj,
        remote_adj,
        read_block,
        tile_src,
        tile_row,
        w_first,
        b_first,
        w_second,
        b_second,
    ):
        part, cols = features.shape
        tile = diag_adj.shape[1]
        blocks = part // tile
        remote = remote_adj[0]
        tiles = remote.shape[0]
        chunk = LANES if cols % LANES == 0 else cols
        chunks = cols // chunk
        f = lax.axis_index("feat")
        source, row = tile_src[0], tile_row[0]
        want = jnp.minimum(read_block[0], blocks - 1)
        shifts = [(dh, dl) for dh in range(halves) for dl in range(sides)]
        place = jnp.stack([jnp.asarray(feat_target(f, dh, dl), jnp.int32) for dh, dl in shifts])
        own_flops = 6 * blocks * tile * tile * chunk
        remote_flops = 6 * tiles * tile * tile * chunk
        total_scratch = [pltpu.VMEM((part, chunk), jnp.float32)]

        x_all = [features] + [feat_send(features, 0, dl) for dl in range(1, sides)]
        w_mine, *w_others = call(
            arrange_body, [place], [w_first], [f32(w_first.shape[0], halves * cols)] * sides
        )
        w_all = [w_mine] + [feat_send(w, 0, dl) for dl, w in enumerate(w_others, 1)]

        scaling = lax.rsqrt(degree.astype(jnp.float32))
        spread = jnp.broadcast_to(scaling[:, None], (part, chunk))
        (outgoing,) = call(outgoing_body, [want], [features, spread], [f32(parts, tile, cols)])
        incoming = dom_exchange(outgoing)

        def summed(lefts, c):
            def partial(dh):
                lanes = slice(dh * cols + c * chunk, dh * cols + (c + 1) * chunk)
                return sum(dot3(x, w[:, lanes]) for x, w in zip(lefts, w_all))

            received = [feat_send(partial(dh), dh, 0) for dh in range(1, halves)]
            return [partial(0)] + received

        own_sums = [summed(x_all, c) for c in range(chunks)]

        (chosen,) = call(chosen_body, [source], [incoming], [f32(tiles // TOUCH * tile, cols)])
        chosen_all = [chosen] + [feat_send(chosen, 0, dl) for dl in range(1, sides)]
        remote_sums = [summed(chosen_all, c) for c in range(chunks)]

        w_second, _ = lax.optimization_barrier((w_second, remote_sums[-1][-1]))
        w2_half = [w_second] + [feat_send(w_second, dh, 0) for dh in range(1, halves)]

        bias_all = b_first.reshape(feats, chunks, 1, chunk)
        bias_own = lax.dynamic_index_in_dim(bias_all, f, 0, keepdims=False)

        collected = []
        for c in range(chunks):
            base, _ = call(
                own_sum_body, [], [diag_adj, spread, *own_sums[c]], [f32(part, chunk)] * 2, flops=own_flops
            )
            scaled, outgoing = call(
                hidden_body,
                [row, want],
                [base, remote, spread, bias_own[c], *remote_sums[c]],
                [f32(part, chunk), f32(parts, tile, chunk)],
                total_scratch,
                remote_flops,
            )
            incoming = dom_exchange(outgoing)
            (base,) = call(own_body, [], [diag_adj, scaled], [f32(part, chunk)], flops=own_flops)
            pieces = call(
                pieces_body,
                [source, row, place],
                [base, remote, spread, incoming],
                [f32(part // feats, chunk)] * feats,
                total_scratch,
                remote_flops,
            )
            collected.append(
                [p if dh == 0 and dl == 0 else feat_send(p, dh, dl) for (dh, dl), p in zip(shifts, pieces)]
            )

        w2_all = [w if dl == 0 else feat_send(w, 0, dl) for w in w2_half for dl in range(sides)]
        out = b_second[None, :]
        for c in range(chunks):
            out = add_product(out, collected[c], w2_all, c)
        return out

    return jax.shard_map(
        per_device,
        mesh=mesh,
        in_specs=(
            P("dom", "feat"),
            P("dom"),
            P("dom", None),
            P("dom", None, None, None),
            P("dom", None),
            P("dom", None),
            P("dom", None),
            P("feat", None),
            P(),
            P("feat", None),
            P(),
        ),
        out_specs=P(("dom", "feat"), None),
        check_vma=False,
    )
```

```python
import functools
import math

import jax
import jax.numpy as jnp
from jax import lax
from jax.experimental import pallas as pl
from jax.experimental.pallas import tpu as pltpu
from jax.sharding import PartitionSpec as P

LANES = 128
TOUCH = 2
VMEM_LIMIT = 16 * 1024 * 1024
VMEM = pl.BlockSpec(memory_space=pltpu.VMEM)
SMEM = pl.BlockSpec(memory_space=pltpu.SMEM)
HBM = pl.BlockSpec(memory_space=pl.ANY)


def dot3(a, b):
    return jnp.dot(a, b, precision=lax.Precision.HIGH, preferred_element_type=jnp.float32)


def f32(*dims):
    return jax.ShapeDtypeStruct(dims, jnp.float32)


def call(body, scalars, arrays, outs, scratch=(), flops=0, hbm=()):
    moved = sum(4 * a.size for a in list(arrays) + list(outs))
    return pl.pallas_call(
        body,
        out_shape=list(outs),
        in_specs=[SMEM] * len(scalars) + [VMEM] * len(arrays),
        out_specs=[HBM if i in hbm else VMEM for i in range(len(outs))],
        scratch_shapes=list(scratch),
        compiler_params=pltpu.CompilerParams(vmem_limit_bytes=VMEM_LIMIT),
        cost_estimate=pl.CostEstimate(flops=flops, bytes_accessed=moved, transcendentals=0),
    )(*scalars, *arrays)


def rows_at(index, height):
    return pl.ds(pl.multiple_of(index * height, height), height)


def outgoing_body(want_ref, features, spread, blocks, held, sems):
    count, tile, cols = held.shape
    chunk = spread.shape[1]
    copies = [pltpu.make_async_copy(held.at[d], blocks.at[d], sems.at[d]) for d in range(count)]
    for d in range(count):
        rows = rows_at(want_ref[d], tile)
        for c in range(cols // chunk):
            lanes = pl.ds(c * chunk, chunk)
            held[d, :, lanes] = features[rows, lanes] * spread[rows, :]
        copies[d].start()
    for copy in copies:
        copy.wait()


def partial_body(count, layout, step, place_ref, *refs):
    lefts, rights, outs = refs[:count], refs[count : 2 * count], refs[2 * count :]
    cols = lefts[0].shape[1]
    for dh, pieces in layout:
        index = place_ref[dh * count]
        lanes = pl.ds(pl.multiple_of(index * cols, cols), cols)
        right = jnp.concatenate([w[:, lanes] for w in rights], axis=0)
        for start, stop, targets in pieces:

            def one(i, carry, start=start, targets=targets, right=right):
                rows = pl.ds(pl.multiple_of(start + i * step, step), step)
                left = jnp.concatenate([x[rows, :] for x in lefts], axis=1)
                result = dot3(left, right)
                for c, at, offset in targets:
                    out = outs[at]
                    chunk = out.shape[1]
                    place = pl.ds(pl.multiple_of(start - offset + i * step, step), step)
                    out[place, :] = result[:, c * chunk : (c + 1) * chunk]
                return carry

            lax.fori_loop(0, (stop - start) // step, one, 0)


def chosen_body(source_ref, incoming, chosen):
    tile = incoming.shape[1]
    for g in range(chosen.shape[0] // tile):
        chosen[pl.ds(g * tile, tile), :] = incoming[source_ref[TOUCH * g]]


def own_sum_body(split, diag, spread, own, *refs):
    received, base, scaled = refs[:-2], refs[-2], refs[-1]
    height = own.shape[0] // split
    for s in range(split):
        rows = pl.ds(s * height, height)
        total = own[rows, :]
        for extra in received[s::split]:
            total = total + extra[...]
        scaled[rows, :] = total * spread[rows, :]
    own_body(diag, scaled, base)


def own_body(diag, scaled, base):
    tile = diag.shape[1]
    for i in range(diag.shape[0] // tile):
        rows = pl.ds(i * tile, tile)
        base[rows, :] = dot3(diag[rows, :], scaled[rows, :])


def hidden_body(row_ref, want_ref, base, remote, spread, bias, *refs):
    sums, (scaled, blocks, total, sems) = refs[:-4], refs[-4:]
    tiles, tile = remote.shape[:2]
    total[...] = base[...]
    for g in range(tiles // TOUCH):
        rows = pl.ds(g * tile, tile)
        block = sums[0][rows, :]
        for extra in sums[1:]:
            block = block + extra[rows, :]
        for k in range(TOUCH * g, TOUCH * g + TOUCH):
            total[rows_at(row_ref[k], tile), :] += dot3(remote[k], block)
    hidden = jnp.maximum(total[...] * spread[...] + bias[...], 0.0)
    scaled[...] = hidden * spread[...]
    copies = [
        pltpu.make_async_copy(scaled.at[rows_at(want_ref[d], tile)], blocks.at[d], sems.at[d])
        for d in range(blocks.shape[0])
    ]
    for copy in copies:
        copy.start()
    for copy in copies:
        copy.wait()


def pieces_body(source_ref, row_ref, place_ref, base, remote, spread, incoming, *refs):
    pieces, total = refs[:-1], refs[-1]
    tiles, tile = remote.shape[:2]
    total[...] = base[...]
    for k in range(tiles):
        total[rows_at(row_ref[k], tile), :] += dot3(remote[k], incoming[source_ref[k]])
    total[...] = total[...] * spread[...]
    height = pieces[0].shape[0]
    for j, piece in enumerate(pieces):
        piece[...] = total[rows_at(place_ref[j], height), :]


def product_body(count, start, *refs):
    pieces, weights, out = refs[:count], refs[count : 2 * count], refs[-1]
    left = jnp.concatenate([p[...] for p in pieces], axis=1)
    right = jnp.concatenate([w[...] for w in weights], axis=0)
    out[...] = start[...] + dot3(left, right)


def add_product(start, pieces, weights):
    rows, chunk = pieces[0].shape
    width = weights[0][0].shape[1]
    step = min(2 * LANES, width)
    count = len(pieces)
    return pl.pallas_call(
        functools.partial(product_body, count),
        out_shape=f32(rows, width),
        grid=(width // step,),
        in_specs=[pl.BlockSpec((start.shape[0], step), lambda j: (0, j))]
        + [pl.BlockSpec((rows, chunk), lambda j: (0, 0))] * count
        + [pl.BlockSpec((chunk, step), lambda j, c=c: (c, j)) for _, c in weights],
        out_specs=pl.BlockSpec((rows, step), lambda j: (0, j)),
        compiler_params=pltpu.CompilerParams(vmem_limit_bytes=VMEM_LIMIT),
        cost_estimate=pl.CostEstimate(
            flops=6 * count * rows * chunk * width,
            bytes_accessed=4 * count * chunk * (rows + width) + 8 * rows * width,
            transcendentals=0,
        ),
    )(start, *pieces, *[w for w, _ in weights])


def solution(mesh):
    parts = mesh.shape["dom"]
    feats = mesh.shape["feat"]
    sides = 2 if feats % 2 == 0 else 1
    halves = feats // sides

    def feat_target(f, dh, dl):
        return (f // sides + dh) % halves * sides + (f % sides + dl) % sides

    def feat_send(x, dh, dl):
        return lax.ppermute(x, "feat", [(f, feat_target(f, dh, dl)) for f in range(feats)])

    def dom_exchange(x):
        return lax.all_to_all(x, "dom", split_axis=0, concat_axis=0, tiled=True)

    def per_device(
        features,
        degree,
        diag_adj,
        remote_adj,
        read_block,
        tile_src,
        tile_row,
        w_first,
        b_first,
        w_second,
        b_second,
    ):
        part, cols = features.shape
        tile = diag_adj.shape[1]
        blocks = part // tile
        remote = remote_adj[0]
        tiles = remote.shape[0]
        chunk = LANES if cols % LANES == 0 else cols
        chunks = cols // chunk
        f = lax.axis_index("feat")
        source, row = tile_src[0], tile_row[0]
        want = jnp.minimum(read_block[0], blocks - 1)
        shifts = [(dh, dl) for dh in range(halves) for dl in range(sides)]
        place = jnp.stack([jnp.asarray(feat_target(f, dh, dl), jnp.int32) for dh, dl in shifts])
        own_flops = 6 * blocks * tile * tile * chunk
        remote_flops = 6 * tiles * tile * tile * chunk
        total_scratch = [pltpu.VMEM((part, chunk), jnp.float32)]

        shares = chunks if parts % chunks == 0 else 1
        share = lax.axis_index("dom") % shares
        share_rows = w_second.shape[0] // shares

        def share_send(x, k):
            pairs = [(s, s // shares * shares + (s % shares + k) % shares) for s in range(parts)]
            return lax.ppermute(x, "dom", pairs)

        w2_sent = lax.dynamic_slice_in_dim(w_second, share * share_rows, share_rows, 0)
        w2_got = [feat_send(w2_sent, dh, 0) for dh in range(1, halves)]

        x_all = [features] + [feat_send(features, 0, dl) for dl in range(1, sides)]
        w_all = [w_first] + [feat_send(w_first, 0, dl) for dl in range(1, sides)]

        scaling = lax.rsqrt(degree.astype(jnp.float32))
        spread = jnp.broadcast_to(scaling[:, None], (part, chunk))
        (outgoing,) = call(
            outgoing_body,
            [want],
            [features, spread],
            [f32(parts, tile, cols)],
            [pltpu.VMEM((parts, tile, cols), jnp.float32), pltpu.SemaphoreType.DMA((parts,))],
            hbm=(0,),
        )
        incoming = dom_exchange(outgoing)

        def partials(lefts, shifts_made, split):
            rows = lefts[0].shape[0]
            layout, outs = [], []
            for dh in shifts_made:
                at = len(outs)
                late = rows // split
                outs += [f32(rows, chunk)] + [f32(late, chunk)] * (split * (chunks - 1))
                pieces = []
                for s in range(split):
                    targets = [(0, at, 0)]
                    targets += [(c, at + (c - 1) * split + s + 1, s * late) for c in range(1, chunks)]
                    pieces.append((s * late, (s + 1) * late, targets))
                layout.append((dh, pieces))
            made = call(
                functools.partial(partial_body, sides, layout, math.gcd(2 * LANES, rows // split)),
                [place],
                [*lefts, *w_all],
                outs,
                flops=6 * rows * cols * cols * sides * len(layout),
            )
            each = len(made) // len(layout)
            return [
                [made[i * each : i * each + 1]]
                + [made[i * each + 1 + (c - 1) * split :][:split] for c in range(1, chunks)]
                for i in range(len(layout))
            ]

        others = list(range(1, halves))
        split = 2
        sends = partials(x_all, others, split)
        own_parts = partials(x_all, [0], 1)[0]
        sends, w2_got = lax.optimization_barrier((sends, w2_got))
        received = [[feat_send(parts_of[0][0], dh, 0)] for dh, parts_of in zip(others, sends)]

        (chosen,) = call(chosen_body, [source], [incoming], [f32(tiles // TOUCH * tile, cols)])
        chosen_all = [chosen] + [feat_send(chosen, 0, dl) for dl in range(1, sides)]
        remote_sends = partials(chosen_all, others, 1)
        remote_own = partials(chosen_all, [0], 1)[0]

        late = [[parts_of[c][1:] for c in range(1, chunks)] for parts_of in sends]
        late, remote_sends = lax.optimization_barrier((late, remote_sends))

        own_sums = [[own_parts[0][0]] + [r[0] for r in received]]
        for c in range(1, chunks):
            own_sums.append([own_parts[c][0]])
            for dh, parts_of, rest in zip(others, sends, late):
                own_sums[c] += [feat_send(parts_of[c][0], dh, 0)]
                own_sums[c] += [feat_send(p, dh, 0) for p in rest[c - 1]]
        remote_sums = [
            [remote_own[c][0]] + [feat_send(parts_of[c][0], dh, 0) for dh, parts_of in zip(others, remote_sends)]
            for c in range(chunks)
        ]

        bias_all = b_first.reshape(feats, chunks, 1, chunk)
        bias_own = lax.dynamic_index_in_dim(bias_all, f, 0, keepdims=False)

        collected = []
        outgoing = None
        for c in range(chunks):
            if c > 0:
                own_sums[c], outgoing = lax.optimization_barrier((own_sums[c], outgoing))
            base, _ = call(
                functools.partial(own_sum_body, 1 if c == 0 else split),
                [],
                [diag_adj, spread, *own_sums[c]],
                [f32(part, chunk)] * 2,
                flops=own_flops,
            )
            scaled, outgoing = call(
                hidden_body,
                [row, want],
                [base, remote, spread, bias_own[c], *remote_sums[c]],
                [f32(part, chunk), f32(parts, tile, chunk)],
                total_scratch + [pltpu.SemaphoreType.DMA((parts,))],
                remote_flops,
                hbm=(1,),
            )
            incoming = dom_exchange(outgoing)
            (base,) = call(own_body, [], [diag_adj, scaled], [f32(part, chunk)], flops=own_flops)
            pieces = call(
                pieces_body,
                [source, row, place],
                [base, remote, spread, incoming],
                [f32(part // feats, chunk)] * feats,
                total_scratch,
                remote_flops,
            )
            collected.append(
                [p if dh == 0 and dl == 0 else feat_send(p, dh, dl) for (dh, dl), p in zip(shifts, pieces)]
            )

        w2_groups = [[got] + [share_send(got, k) for k in range(1, shares)] for got in w2_got]
        w2_core = [w_second] + [feat_send(w_second, 0, dl) for dl in range(1, sides)]
        out = b_second[None, :]
        for c in range(chunks):
            weights = [(w, c) for w in w2_core]
            for group in w2_groups:
                if shares == 1:
                    block = group[0][c * chunk : (c + 1) * chunk]
                else:
                    block = lax.select_n((share - c) % shares, *group)
                weights += [(block, 0)] + [(feat_send(block, 0, dl), 0) for dl in range(1, sides)]
            out = add_product(out, collected[c], weights)
        return out

    return jax.shard_map(
        per_device,
        mesh=mesh,
        in_specs=(
            P("dom", "feat"),
            P("dom"),
            P("dom", None),
            P("dom", None, None, None),
            P("dom", None),
            P("dom", None),
            P("dom", None),
            P("feat", None),
            P(),
            P("feat", None),
            P(),
        ),
        out_specs=P(("dom", "feat"), None),
        check_vma=False,
    )
```

```python
import functools

import jax
import jax.numpy as jnp
from jax import lax
from jax.experimental import pallas as pl
from jax.experimental.pallas import tpu as pltpu
from jax.sharding import PartitionSpec as P

LANES = 128
TOUCH = 2
VMEM_LIMIT = 20 * 1024 * 1024
VMEM = pl.BlockSpec(memory_space=pltpu.VMEM)
SMEM = pl.BlockSpec(memory_space=pltpu.SMEM)
ANY = pl.BlockSpec(memory_space=pl.ANY)
PARAMS = pltpu.CompilerParams(vmem_limit_bytes=VMEM_LIMIT)


def dot(a, b):
    return jnp.dot(a, b, preferred_element_type=jnp.float32)


def dot3(a, b):
    return jnp.dot(a, b, precision=lax.Precision.HIGH, preferred_element_type=jnp.float32)


def halved(x):
    high = x.astype(jnp.bfloat16)
    return high, (x - high.astype(jnp.float32)).astype(jnp.bfloat16)


def f32(*dims):
    return jax.ShapeDtypeStruct(dims, jnp.float32)


def rows_at(index, height):
    return pl.ds(pl.multiple_of(index * height, height), height)


def scratch(*dims):
    return pltpu.VMEM(dims, jnp.float32)


def start_all(pairs, sems, first):
    copies = [pltpu.make_async_copy(a, b, sems.at[first + i]) for i, (a, b) in enumerate(pairs)]
    for copy in copies:
        copy.start()
    return copies


def wait_all(copies):
    for copy in copies:
        copy.wait()


def outgoing_body(want_ref, features, spread, blocks):
    chunk = spread.shape[1]
    for c in range(features.shape[1] // chunk):
        lanes = pl.ds(c * chunk, chunk)
        blocks[0, :, lanes] = features[:, lanes] * spread[...]


def outgoing_blocks(want, features, spread, tile):
    cols, chunk = features.shape[1], spread.shape[1]
    count = want.shape[0]
    return pl.pallas_call(
        outgoing_body,
        out_shape=f32(count, tile, cols),
        grid_spec=pltpu.PrefetchScalarGridSpec(
            num_scalar_prefetch=1,
            grid=(count,),
            in_specs=[
                pl.BlockSpec((tile, cols), lambda d, want: (want[d], 0)),
                pl.BlockSpec((tile, chunk), lambda d, want: (want[d], 0)),
            ],
            out_specs=pl.BlockSpec((1, tile, cols), lambda d, want: (d, 0, 0)),
        ),
        compiler_params=PARAMS,
    )(want, features, spread)


def partial_body(count, place_ref, *refs):
    lefts, rights, outs = refs[:count], refs[count : 2 * count], refs[2 * count :]
    left = jnp.concatenate([x[...] for x in lefts], axis=1)
    right = jnp.concatenate([w[...] for w in rights], axis=0)
    result = dot3(left, right)
    width = outs[0].shape[1]
    for c, out in enumerate(outs):
        out[...] = result[:, c * width : (c + 1) * width]


def partial_sums(place, at, lefts, weights, step, pieces):
    rows, cols = lefts[0].shape
    depth = weights[0].shape[0]
    count = len(lefts)
    width = cols // pieces
    return pl.pallas_call(
        functools.partial(partial_body, count),
        out_shape=[f32(rows, width)] * pieces,
        grid_spec=pltpu.PrefetchScalarGridSpec(
            num_scalar_prefetch=1,
            grid=(rows // step,),
            in_specs=[pl.BlockSpec((step, cols), lambda i, place: (i, 0))] * count
            + [pl.BlockSpec((depth, cols), lambda i, place: (0, place[at]))] * count,
            out_specs=[pl.BlockSpec((step, width), lambda i, place: (i, 0))] * pieces,
        ),
        compiler_params=PARAMS,
        cost_estimate=pl.CostEstimate(
            flops=6 * rows * depth * cols * count,
            bytes_accessed=4 * (count + 1) * rows * cols,
            transcendentals=0,
        ),
    )(place, *lefts, *weights)


def chosen_body(source_ref, incoming, chosen, sems):
    tile = incoming.shape[1]
    groups = chosen.shape[0] // tile
    wait_all(
        start_all(
            [(incoming.at[source_ref[TOUCH * g]], chosen.at[pl.ds(g * tile, tile)]) for g in range(groups)],
            sems,
            0,
        )
    )


def chosen_blocks(source, incoming):
    tile, cols = incoming.shape[1:]
    groups = source.shape[0] // TOUCH
    return pl.pallas_call(
        chosen_body,
        out_shape=f32(groups * tile, cols),
        in_specs=[SMEM, ANY],
        out_specs=ANY,
        scratch_shapes=[pltpu.SemaphoreType.DMA((groups,))],
        compiler_params=PARAMS,
    )(source, incoming)


def own_body(diag, spread, *refs):
    sums, base = refs[:-1], refs[-1]
    tile = diag.shape[1]
    for i in range(diag.shape[0] // tile):
        rows = pl.ds(i * tile, tile)
        total = sums[0][rows, :]
        for extra in sums[1:]:
            total = total + extra[rows, :]
        base[rows, :] = dot3(diag[rows, :], total * spread[rows, :])


def own_part(diag, spread, sums, c, step):
    rows, tile = diag.shape
    chunk = spread.shape[1]
    return pl.pallas_call(
        own_body,
        out_shape=f32(rows, chunk),
        grid=(rows // step,),
        in_specs=[pl.BlockSpec((step, tile), lambda i: (i, 0)), pl.BlockSpec((step, chunk), lambda i: (i, 0))]
        + [pl.BlockSpec((step, chunk), lambda i: (i, c))] * len(sums),
        out_specs=pl.BlockSpec((step, chunk), lambda i: (i, 0)),
        compiler_params=PARAMS,
    )(diag, spread, *sums)


def hidden_body(count, offset, row_ref, want_ref, first_ref, bias, base, remote, spread, diag, *refs):
    sums, (blocks, base_out), refs = refs[:count], refs[count : count + 2], refs[count + 2 :]
    sums_in, (total, remote_in, spread_in, diag_in, scaled, sems) = refs[:count], refs[count:]
    tiles, tile = remote.shape[:2]
    parts = blocks.shape[0]
    chunk = total.shape[1]
    early = start_all(
        list(zip(sums, sums_in)) + [(remote, remote_in), (base, total), (spread, spread_in), (diag, diag_in)],
        sems,
        0,
    )
    wait_all(early[: count + 2])
    for g in range(tiles // TOUCH):
        rows = pl.ds(g * tile, tile)
        block = sums_in[0][rows, :]
        for extra in sums_in[1:]:
            block = block + extra[rows, :]
        for k in range(TOUCH * g, TOUCH * g + TOUCH):
            total[rows_at(row_ref[k], tile), :] += dot3(remote_in[k], block)
    lanes = pl.ds(pl.multiple_of(first_ref[0] + offset, chunk), chunk)
    shift = bias[:, lanes]
    wait_all(early[count + 2 :])
    scaled[...] = jnp.maximum(total[...] * spread_in[...] + shift, 0.0) * spread_in[...]
    copies = start_all(
        [(scaled.at[rows_at(want_ref[d], tile)], blocks.at[d]) for d in range(parts)], sems, count + 4
    )
    for i in range(diag.shape[0] // tile):
        rows = pl.ds(i * tile, tile)
        total[rows, :] = dot3(diag_in[rows, :], scaled[rows, :])
    copies += start_all([(total, base_out)], sems, count + 4 + parts)
    wait_all(copies)


def hidden_blocks(row, want, first, offset, bias, base, remote, spread, diag, sums):
    rows, chunk = base.shape
    tile = diag.shape[1]
    parts = want.shape[0]
    count = len(sums)
    return pl.pallas_call(
        functools.partial(hidden_body, count, offset),
        out_shape=[f32(parts, tile, chunk), f32(rows, chunk)],
        in_specs=[SMEM] * 3 + [VMEM] + [ANY] * (4 + count),
        out_specs=[ANY, ANY],
        scratch_shapes=[scratch(*s.shape) for s in sums]
        + [scratch(*a.shape) for a in (base, remote, spread, diag, base)]
        + [pltpu.SemaphoreType.DMA((count + 5 + parts,))],
        compiler_params=PARAMS,
    )(row, want, first, bias, base, remote, spread, diag, *sums)


def pieces_body(source_ref, row_ref, place_ref, base, remote, spread, incoming, *refs):
    pieces, (total, remote_in, spread_in, incoming_in, sems) = refs[:-5], refs[-5:]
    tiles, tile = remote.shape[:2]
    early = start_all(
        [(incoming, incoming_in), (remote, remote_in), (base, total), (spread, spread_in)], sems, 0
    )
    wait_all(early[:3])
    for k in range(tiles):
        total[rows_at(row_ref[k], tile), :] += dot3(remote_in[k], incoming_in[source_ref[k]])
    wait_all(early[3:])
    total[...] = total[...] * spread_in[...]
    height = pieces[0].shape[0]
    wait_all(
        start_all([(total.at[rows_at(place_ref[j], height)], p) for j, p in enumerate(pieces)], sems, 4)
    )


def feature_pieces(source, row, place, base, remote, spread, incoming):
    rows, chunk = base.shape
    feats = place.shape[0]
    return pl.pallas_call(
        pieces_body,
        out_shape=[f32(rows // feats, chunk)] * feats,
        in_specs=[SMEM] * 3 + [ANY] * 4,
        out_specs=[ANY] * feats,
        scratch_shapes=[scratch(*a.shape) for a in (base, remote, spread, incoming)]
        + [pltpu.SemaphoreType.DMA((4 + feats,))],
        compiler_params=PARAMS,
    )(source, row, place, base, remote, spread, incoming)


def product_body(count, start, *refs):
    pieces, weights, (out, high, low) = refs[:count], refs[count : 2 * count], refs[2 * count :]
    chunk = pieces[0].shape[1]

    @pl.when(pl.program_id(0) == 0)
    def _():
        for j, piece in enumerate(pieces):
            lanes = pl.ds(j * chunk, chunk)
            high[:, lanes], low[:, lanes] = halved(piece[...])

    w_high, w_low = halved(jnp.concatenate([w[...] for w in weights], axis=0))
    product = dot(high[...], w_high) + (dot(high[...], w_low) + dot(low[...], w_high))
    out[...] = start[...] + product


def add_product(start, pieces, weights):
    rows, chunk = pieces[0].shape
    width = weights[0][0].shape[1]
    step = min(2 * LANES, width)
    count = len(pieces)
    return pl.pallas_call(
        functools.partial(product_body, count),
        out_shape=f32(rows, width),
        grid=(width // step,),
        in_specs=[pl.BlockSpec((start.shape[0], step), lambda j: (0, j))]
        + [pl.BlockSpec((rows, chunk), lambda j: (0, 0))] * count
        + [pl.BlockSpec((chunk, step), lambda j, c=c: (c, j)) for _, c in weights],
        out_specs=pl.BlockSpec((rows, step), lambda j: (0, j)),
        scratch_shapes=[pltpu.VMEM((rows, count * chunk), jnp.bfloat16)] * 2,
        compiler_params=PARAMS,
        cost_estimate=pl.CostEstimate(
            flops=6 * count * rows * chunk * width,
            bytes_accessed=4 * count * chunk * (rows + width) + 8 * rows * width,
            transcendentals=0,
        ),
    )(start, *pieces, *[w for w, _ in weights])


def solution(mesh):
    parts = mesh.shape["dom"]
    feats = mesh.shape["feat"]
    sides = 2 if feats % 2 == 0 else 1
    halves = feats // sides

    def feat_target(f, dh, dl):
        return (f // sides + dh) % halves * sides + (f % sides + dl) % sides

    def feat_send(x, dh, dl):
        return lax.ppermute(x, "feat", [(f, feat_target(f, dh, dl)) for f in range(feats)])

    def dom_exchange(x):
        return lax.all_to_all(x, "dom", split_axis=0, concat_axis=0, tiled=True)

    def per_device(
        features,
        degree,
        diag_adj,
        remote_adj,
        read_block,
        tile_src,
        tile_row,
        w_first,
        b_first,
        w_second,
        b_second,
    ):
        part, cols = features.shape
        tile = diag_adj.shape[1]
        blocks = part // tile
        remote = remote_adj[0]
        chunk = LANES if cols % LANES == 0 else cols
        chunks = cols // chunk
        f = lax.axis_index("feat")
        source, row = tile_src[0], tile_row[0]
        want = jnp.minimum(read_block[0], blocks - 1)
        shifts = [(dh, dl) for dh in range(halves) for dl in range(sides)]
        place = jnp.stack([jnp.asarray(feat_target(f, dh, dl), jnp.int32) for dh, dl in shifts])
        first = jnp.reshape(jnp.asarray(f * cols, jnp.int32), (1,))
        others = list(range(1, halves))
        piece = part // feats

        x_all = [features] + [feat_send(features, 0, dl) for dl in range(1, sides)]
        w_all = [w_first] + [feat_send(w_first, 0, dl) for dl in range(1, sides)]
        scaling = lax.rsqrt(degree.astype(jnp.float32))
        spread = jnp.broadcast_to(scaling[:, None], (part, chunk))
        outgoing = outgoing_blocks(want, features, spread, tile)

        sends = [partial_sums(place, dh * sides, x_all, w_all, 2 * tile, 1)[0] for dh in others]
        outgoing, sends = lax.optimization_barrier((outgoing, sends))
        incoming = dom_exchange(outgoing)
        sums = [partial_sums(place, 0, x_all, w_all, 2 * tile, 1)[0]]
        sums += [feat_send(x, dh, 0) for dh, x in zip(others, sends)]

        chosen = chosen_blocks(source, incoming)
        chosen_all = [chosen] + [feat_send(chosen, 0, dl) for dl in range(1, sides)]
        height = chosen.shape[0]
        remote_sends = [partial_sums(place, dh * sides, chosen_all, w_all, height, chunks) for dh in others]
        remote_own = partial_sums(place, 0, chosen_all, w_all, height, chunks)
        remote_sums = [
            [remote_own[c]] + [feat_send(x[c], dh, 0) for dh, x in zip(others, remote_sends)]
            for c in range(chunks)
        ]

        shares = chunks if parts % chunks == 0 else 1
        share = lax.axis_index("dom") % shares
        share_rows = w_second.shape[0] // shares

        def share_send(x, k):
            pairs = [(s, s // shares * shares + (s % shares + k) % shares) for s in range(parts)]
            return lax.ppermute(x, "dom", pairs)

        w2_sent = lax.dynamic_slice_in_dim(w_second, share * share_rows, share_rows, 0)
        w2_sent, _ = lax.optimization_barrier((w2_sent, [s[1:] for s in remote_sums]))
        w2_got = [feat_send(w2_sent, dh, 0) for dh in others]

        base = [own_part(diag_adj, spread, sums, c, piece) for c in range(chunks)]
        bias = b_first[None, :]
        collected = []
        outgoing = None
        for c in range(chunks):
            if c > 0:
                base[c], outgoing = lax.optimization_barrier((base[c], outgoing))
            outgoing, base_next = hidden_blocks(
                row, want, first, c * chunk, bias, base[c], remote, spread, diag_adj, remote_sums[c]
            )
            incoming = dom_exchange(outgoing)
            pieces = feature_pieces(source, row, place, base_next, remote, spread, incoming)
            collected.append(
                [p if dh == 0 and dl == 0 else feat_send(p, dh, dl) for (dh, dl), p in zip(shifts, pieces)]
            )

        w2_groups = [[got] + [share_send(got, k) for k in range(1, shares)] for got in w2_got]
        w2_core = [w_second] + [feat_send(w_second, 0, dl) for dl in range(1, sides)]
        out = b_second[None, :]
        for c in range(chunks):
            weights = [(w, c) for w in w2_core]
            for group in w2_groups:
                if shares == 1:
                    block = group[0][c * chunk : (c + 1) * chunk]
                else:
                    block = lax.select_n((share - c) % shares, *group)
                weights += [(block, 0)] + [(feat_send(block, 0, dl), 0) for dl in range(1, sides)]
            out = add_product(out, collected[c], weights)
        return out

    return jax.shard_map(
        per_device,
        mesh=mesh,
        in_specs=(
            P("dom", "feat"),
            P("dom"),
            P("dom", None),
            P("dom", None, None, None),
            P("dom", None),
            P("dom", None),
            P("dom", None),
            P("feat", None),
            P(),
            P("feat", None),
            P(),
        ),
        out_specs=P(("dom", "feat"), None),
        check_vma=False,
    )
```

```python
import functools

import jax
import jax.numpy as jnp
from jax import lax
from jax.experimental import pallas as pl
from jax.experimental.pallas import tpu as pltpu
from jax.sharding import PartitionSpec as P

LANES = 128
TOUCH = 2
VMEM_LIMIT = 24 * 1024 * 1024
VMEM = pl.BlockSpec(memory_space=pltpu.VMEM)
SMEM = pl.BlockSpec(memory_space=pltpu.SMEM)
HBM = pl.BlockSpec(memory_space=pltpu.HBM)
PARAMS = pltpu.CompilerParams(vmem_limit_bytes=VMEM_LIMIT)


def dot3(a, b):
    return jnp.dot(a, b, precision=lax.Precision.HIGH, preferred_element_type=jnp.float32)


def two_parts(x):
    high = x.astype(jnp.bfloat16)
    return high, (x - high.astype(jnp.float32)).astype(jnp.bfloat16)


def left_parts(x):
    high, low = two_parts(x)
    return jnp.concatenate([high, low, high], axis=1)


def right_parts(w):
    high, low = two_parts(w)
    return jnp.concatenate([high, high, low], axis=0)


def f32(*dims):
    return jax.ShapeDtypeStruct(dims, jnp.float32)


def rows_at(index, height):
    return pl.ds(pl.multiple_of(index * height, height), height)


def scratch(*dims):
    return pltpu.VMEM(dims, jnp.float32)


def start_all(pairs, sems, first):
    copies = [pltpu.make_async_copy(a, b, sems.at[first + i]) for i, (a, b) in enumerate(pairs)]
    for copy in copies:
        copy.start()
    return copies


def wait_all(copies):
    for copy in copies:
        copy.wait()


def cost(flops):
    return pl.CostEstimate(flops=flops, bytes_accessed=0, transcendentals=0)


def slice_body(index_ref, source, out, sem):
    wait_all(start_all([(source.at[rows_at(index_ref[0], out.shape[0])], out)], sem, 0))


def row_block(index, source, height):
    return pl.pallas_call(
        slice_body,
        out_shape=f32(height, source.shape[1]),
        in_specs=[SMEM, HBM],
        out_specs=HBM,
        scratch_shapes=[pltpu.SemaphoreType.DMA((1,))],
        compiler_params=PARAMS,
    )(index, source)


def outgoing_body(want_ref, features, spread, blocks, held, spread_in, sems):
    count, tile, cols = held.shape
    chunk = spread_in.shape[2]
    last = features.shape[0] // tile - 1
    rows = [rows_at(jnp.minimum(want_ref[d], last), tile) for d in range(count)]
    loads = start_all([(features.at[r], held.at[d]) for d, r in enumerate(rows)], sems, 0)
    loads += start_all([(spread.at[r], spread_in.at[d]) for d, r in enumerate(rows)], sems, count)
    stores = []
    for d in range(count):
        loads[d].wait()
        loads[count + d].wait()
        for c in range(cols // chunk):
            lanes = pl.ds(c * chunk, chunk)
            held[d, :, lanes] = held[d, :, lanes] * spread_in[d]
        stores += start_all([(held.at[d], blocks.at[d])], sems, 2 * count + d)
    wait_all(stores)


def outgoing_blocks(want, features, spread, tile):
    cols, chunk = features.shape[1], spread.shape[1]
    count = want.shape[0]
    return pl.pallas_call(
        outgoing_body,
        out_shape=f32(count, tile, cols),
        in_specs=[SMEM, HBM, HBM],
        out_specs=HBM,
        scratch_shapes=[
            scratch(count, tile, cols),
            scratch(count, tile, chunk),
            pltpu.SemaphoreType.DMA((3 * count,)),
        ],
        compiler_params=PARAMS,
    )(want, features, spread)


def partial_body(count, at, steps, carried, place_ref, *refs):
    lefts, rights, refs = refs[:count], refs[count : 2 * count], refs[2 * count :]
    passing, refs = refs[: len(carried)], refs[len(carried) :]
    outs, (left, right, result, sems) = refs[:-4], refs[-4:]
    cols = lefts[0].shape[1]
    chunk = outs[0].shape[1]
    lanes = pl.ds(pl.multiple_of(place_ref[at] * cols, cols), cols)
    used = 0
    weights_in = start_all([(w.at[:, lanes], right.at[j]) for j, w in enumerate(rights)], sems, used)
    used += count
    stores = start_all(
        [(p, outs[o].at[pl.ds(offset, p.shape[0])]) for p, (o, offset) in zip(passing, carried)], sems, used
    )
    used += len(carried)
    loads = []
    for start, stop, _ in steps:
        rows = pl.ds(start, stop - start)
        pairs = [(x.at[rows], left.at[rows, pl.ds(j * cols, cols)]) for j, x in enumerate(lefts)]
        loads.append(start_all(pairs, sems, used))
        used += count
    wait_all(weights_in)
    weight = right_parts(jnp.concatenate([right[j] for j in range(count)], axis=0))
    for (start, stop, targets), ready in zip(steps, loads):
        wait_all(ready)
        rows = pl.ds(start, stop - start)
        result[rows, :] = jnp.dot(left_parts(left[rows, :]), weight, preferred_element_type=jnp.float32)
        pairs = [
            (result.at[rows, pl.ds(c * chunk, chunk)], outs[o].at[pl.ds(offset, stop - start)])
            for c, o, offset in targets
        ]
        stores += start_all(pairs, sems, used)
        used += len(pairs)
    wait_all(stores)


def partial_sums(place, at, lefts, weights, steps, shapes, passing=(), carried=()):
    rows, cols = lefts[0].shape
    depth = weights[0].shape[0]
    count = len(lefts)
    copies = count + len(carried) + sum(count + len(targets) for _, _, targets in steps)
    return pl.pallas_call(
        functools.partial(partial_body, count, at, steps, carried),
        out_shape=[f32(*s) for s in shapes],
        in_specs=[SMEM] + [HBM] * (2 * count + len(passing)),
        out_specs=[HBM] * len(shapes),
        scratch_shapes=[
            scratch(rows, count * cols),
            scratch(count, depth, cols),
            scratch(rows, cols),
            pltpu.SemaphoreType.DMA((copies,)),
        ],
        compiler_params=PARAMS,
        cost_estimate=cost(6 * rows * depth * cols * count),
    )(place, *lefts, *weights, *passing)


def chosen_body(source_ref, incoming, chosen, sems):
    tile = incoming.shape[1]
    groups = chosen.shape[0] // tile
    pairs = [(incoming.at[source_ref[TOUCH * g]], chosen.at[pl.ds(g * tile, tile)]) for g in range(groups)]
    wait_all(start_all(pairs, sems, 0))


def chosen_blocks(source, incoming):
    tile, cols = incoming.shape[1:]
    groups = source.shape[0] // TOUCH
    return pl.pallas_call(
        chosen_body,
        out_shape=f32(groups * tile, cols),
        in_specs=[SMEM, HBM],
        out_specs=HBM,
        scratch_shapes=[pltpu.SemaphoreType.DMA((groups,))],
        compiler_params=PARAMS,
    )(source, incoming)


def received_pairs(layout, received, recv_in):
    return [
        (received[r].at[pl.ds(start, stop - start)], recv_in.at[h, pl.ds(offset, stop - start)])
        for h, r, start, stop, offset in layout
    ]


def own_total(diag_in, spread_in, own_in, recv_in, total):
    tile = diag_in.shape[1]
    for i in range(diag_in.shape[0] // tile):
        rows = pl.ds(i * tile, tile)
        mixed = own_in[rows, :]
        for h in range(recv_in.shape[0]):
            mixed = mixed + recv_in[h, rows, :]
        total[rows, :] = dot3(diag_in[rows, :], mixed * spread_in[rows, :])


def own_body(layout, diag, spread, own, *refs):
    received, (base, diag_in, spread_in, own_in, recv_in, total, sems) = refs[:-7], refs[-7:]
    pairs = [(diag, diag_in), (spread, spread_in), (own, own_in)]
    wait_all(start_all(pairs + received_pairs(layout, received, recv_in), sems, 0))
    own_total(diag_in, spread_in, own_in, recv_in, total)
    wait_all(start_all([(total, base)], sems, 3 + len(layout)))


def own_part(diag, spread, own, received, layout, others):
    return pl.pallas_call(
        functools.partial(own_body, layout),
        out_shape=f32(*own.shape),
        in_specs=[HBM] * (3 + len(received)),
        out_specs=HBM,
        scratch_shapes=[scratch(*a.shape) for a in (diag, spread, own)]
        + [scratch(others, *own.shape), scratch(*own.shape), pltpu.SemaphoreType.DMA((4 + len(layout),))],
        compiler_params=PARAMS,
        cost_estimate=cost(0),
    )(diag, spread, own, *received)


def hidden_body(
    count, reach, layout, lane_offset, row_ref, want_ref, first_ref, bias, base, remote, spread, diag, *refs
):
    remote_sums, refs = refs[:count], refs[count:]
    received, refs = refs[:reach], refs[reach:]
    blocks, base_out, total, remote_in, spread_in, diag_in, scaled, sums_in, recv_in, sems = refs
    tiles, tile = remote.shape[:2]
    parts = blocks.shape[0]
    chunk = total.shape[1]
    height = sums_in.shape[1]
    begin = total if reach == 0 else scaled
    pairs = [(base, begin), (spread, spread_in), (diag, diag_in)]
    pairs += received_pairs(layout, received, recv_in)
    late = [(remote, remote_in)]
    late += [(s.at[pl.ds(s.shape[0] - height, height)], sums_in.at[j]) for j, s in enumerate(remote_sums)]
    if reach == 0:
        tail = start_all(late, sems, 0)
        first = start_all(pairs, sems, len(late))
        wait_all(first[:1])
    else:
        first = start_all(pairs, sems, 0)
        tail = start_all(late, sems, len(pairs))
        wait_all(first)
        own_total(diag_in, spread_in, scaled, recv_in, total)
    wait_all(tail)
    for g in range(tiles // TOUCH):
        rows = pl.ds(g * tile, tile)
        block = sums_in[0, rows, :]
        for j in range(1, count):
            block = block + sums_in[j, rows, :]
        for k in range(TOUCH * g, TOUCH * g + TOUCH):
            total[rows_at(row_ref[k], tile), :] += dot3(remote_in[k], block)
    lanes = pl.ds(pl.multiple_of(first_ref[0] + lane_offset, chunk), chunk)
    shift = bias[:, lanes]
    if reach == 0:
        wait_all(first[1:])
    scaled[...] = jnp.maximum(total[...] * spread_in[...] + shift, 0.0) * spread_in[...]
    used = len(pairs) + len(late)
    last = scaled.shape[0] // tile - 1
    copies = start_all(
        [(scaled.at[rows_at(jnp.minimum(want_ref[d], last), tile)], blocks.at[d]) for d in range(parts)],
        sems,
        used,
    )
    for i in range(last + 1):
        rows = pl.ds(i * tile, tile)
        total[rows, :] = dot3(diag_in[rows, :], scaled[rows, :])
    copies += start_all([(total, base_out)], sems, used + parts)
    wait_all(copies)


def hidden_blocks(
    row, want, first, lane_offset, bias, base, remote, spread, diag, remote_sums, received, layout, others, flops
):
    rows, chunk = base.shape
    tile = diag.shape[1]
    parts = want.shape[0]
    count = len(remote_sums)
    height = remote.shape[0] // TOUCH * tile
    return pl.pallas_call(
        functools.partial(hidden_body, count, len(received), layout, lane_offset),
        out_shape=[f32(parts, tile, chunk), f32(rows, chunk)],
        in_specs=[SMEM] * 3 + [VMEM] + [HBM] * (4 + count + len(received)),
        out_specs=[HBM, HBM],
        scratch_shapes=[scratch(*a.shape) for a in (base, remote, spread, diag, base)]
        + [scratch(count, height, chunk), scratch(others, *base.shape)]
        + [pltpu.SemaphoreType.DMA((5 + len(layout) + count + parts,))],
        compiler_params=PARAMS,
        cost_estimate=cost(flops),
    )(row, want, first, bias, base, remote, spread, diag, *remote_sums, *received)


def pieces_body(source_ref, row_ref, place_ref, base, remote, spread, incoming, *refs):
    pieces, (total, remote_in, spread_in, incoming_in, sems) = refs[:-5], refs[-5:]
    tiles, tile = remote.shape[:2]
    early = start_all(
        [(incoming, incoming_in), (remote, remote_in), (base, total), (spread, spread_in)], sems, 0
    )
    wait_all(early[:3])
    for k in range(tiles):
        total[rows_at(row_ref[k], tile), :] += dot3(remote_in[k], incoming_in[source_ref[k]])
    wait_all(early[3:])
    total[...] = total[...] * spread_in[...]
    height = pieces[0].shape[0]
    pairs = [(total.at[rows_at(place_ref[j], height)], p) for j, p in enumerate(pieces)]
    wait_all(start_all(pairs, sems, 4))


def feature_pieces(source, row, place, base, remote, spread, incoming):
    rows, chunk = base.shape
    feats = place.shape[0]
    return pl.pallas_call(
        pieces_body,
        out_shape=[f32(rows // feats, chunk)] * feats,
        in_specs=[SMEM] * 3 + [HBM] * 4,
        out_specs=[HBM] * feats,
        scratch_shapes=[scratch(*a.shape) for a in (base, remote, spread, incoming)]
        + [pltpu.SemaphoreType.DMA((4 + feats,))],
        compiler_params=PARAMS,
        cost_estimate=cost(0),
    )(source, row, place, base, remote, spread, incoming)


def product_body(count, choices, turn_ref, start, *refs):
    pieces, weights, (out, left) = refs[:count], refs[count:-2], refs[-2:]
    chunk = pieces[0].shape[1]

    @pl.when(pl.program_id(0) == 0)
    def _():
        left[...] = left_parts(jnp.concatenate([p[...] for p in pieces], axis=1))

    blocks, at = [], 0
    for number in choices:
        block = weights[at][...]
        for k in range(1, number):
            block = jnp.where(turn_ref[0] == k, weights[at + k][...], block)
        blocks.append(block)
        at += number
    right = right_parts(jnp.concatenate(blocks, axis=0))
    out[...] = start[...] + jnp.dot(left[...], right, preferred_element_type=jnp.float32)


def add_product(turn, start, pieces, weights):
    rows, chunk = pieces[0].shape
    width = start.shape[1]
    step = min(2 * LANES, width)
    count = len(pieces)
    flat = [w for group in weights for w in group]
    return pl.pallas_call(
        functools.partial(product_body, count, [len(group) for group in weights]),
        out_shape=f32(rows, width),
        grid_spec=pltpu.PrefetchScalarGridSpec(
            num_scalar_prefetch=1,
            grid=(width // step,),
            in_specs=[pl.BlockSpec((start.shape[0], step), lambda j, turn: (0, j))]
            + [pl.BlockSpec((rows, chunk), lambda j, turn: (0, 0))] * count
            + [pl.BlockSpec((chunk, step), lambda j, turn, c=c: (c, j)) for _, c in flat],
            out_specs=pl.BlockSpec((rows, step), lambda j, turn: (0, j)),
            scratch_shapes=[pltpu.VMEM((rows, 3 * count * chunk), jnp.bfloat16)],
        ),
        compiler_params=PARAMS,
        cost_estimate=cost(6 * count * rows * chunk * width),
    )(turn, start, *pieces, *[w for w, _ in flat])


def solution(mesh):
    parts = mesh.shape["dom"]
    feats = mesh.shape["feat"]
    sides = 2 if feats % 2 == 0 else 1
    halves = feats // sides
    others = list(range(1, halves))

    def feat_target(f, dh, dl):
        return (f // sides + dh) % halves * sides + (f % sides + dl) % sides

    def feat_send(x, dh, dl):
        return lax.ppermute(x, "feat", [(f, feat_target(f, dh, dl)) for f in range(feats)])

    def dom_exchange(x):
        return lax.all_to_all(x, "dom", split_axis=0, concat_axis=0, tiled=True)

    def per_device(
        features,
        degree,
        diag_adj,
        remote_adj,
        read_block,
        tile_src,
        tile_row,
        w_first,
        b_first,
        w_second,
        b_second,
    ):
        part, cols = features.shape
        tile = diag_adj.shape[1]
        blocks = part // tile
        remote = remote_adj[0]
        chunk = LANES if cols % LANES == 0 else cols
        chunks = cols // chunk
        f = lax.axis_index("feat")
        want, source, row = read_block[0], tile_src[0], tile_row[0]
        shifts = [(dh, dl) for dh in range(halves) for dl in range(sides)]
        place = jnp.stack([jnp.asarray(feat_target(f, dh, dl), jnp.int32) for dh, dl in shifts])
        first = jnp.reshape(jnp.asarray(f * cols, jnp.int32), (1,))
        bias = b_first[None, :]

        x_all = [features] + [feat_send(features, 0, dl) for dl in range(1, sides)]
        w_all = [w_first] + [feat_send(w_first, 0, dl) for dl in range(1, sides)]

        shares = chunks if parts % chunks == 0 else 1
        share = jnp.reshape(jnp.asarray(lax.axis_index("dom") % shares, jnp.int32), (1,))
        share_rows = w_second.shape[0] // shares

        def share_send(x, k):
            pairs = [(s, s // shares * shares + (s % shares + k) % shares) for s in range(parts)]
            return lax.ppermute(x, "dom", pairs)

        w2_sent = row_block(share, w_second, share_rows)
        w2_got = [feat_send(w2_sent, dh, 0) for dh in others]

        scaling = lax.rsqrt(degree.astype(jnp.float32))
        spread = jnp.broadcast_to(scaling[:, None], (part, chunk))
        outgoing = outgoing_blocks(want, features, spread, tile)
        incoming = dom_exchange(outgoing)

        early = blocks * 5 // 12 * tile if chunks > 1 else part
        late = part - early
        marks = sorted({0, early // 2 // tile * tile, early, early + late // 2 // tile * tile, part})
        spans = list(zip(marks[:-1], marks[1:]))
        x_all[0], _ = lax.optimization_barrier((features, outgoing))
        send_steps = []
        for start, stop in spans:
            targets = [(0, 0, start)]
            for c in range(1, chunks):
                if stop <= early:
                    targets.append((c, 0, part + (c - 1) * early + start))
                else:
                    targets.append((c, 1, (c - 1) * late + start - early))
            send_steps.append((start, stop, targets))
        send_shapes = [(part + (chunks - 1) * early, chunk)]
        if late > 0:
            send_shapes.append(((chunks - 1) * late, chunk))
        sends = [partial_sums(place, dh * sides, x_all, w_all, send_steps, send_shapes) for dh in others]
        front = [feat_send(x[0], dh, 0) for dh, x in zip(others, sends)]

        own_steps = [(a, b, [(c, c, a) for c in range(chunks)]) for a, b in spans]
        own = partial_sums(place, 0, x_all, w_all, own_steps, [(part, chunk)] * chunks)

        w2_got, _ = lax.optimization_barrier((w2_got, [x[0] for x in sends]))
        w2_groups = [[got] + [share_send(got, k) for k in range(1, shares)] for got in w2_got]
        w2_core = [w_second] + [feat_send(w_second, 0, dl) for dl in range(1, sides)]
        w2_far = [[feat_send(w, 0, dl) if dl > 0 else w for w in g] for g in w2_groups for dl in range(sides)]

        incoming, own, w2_core, w2_far = lax.optimization_barrier((incoming, own, w2_core, w2_far))
        chosen = chosen_blocks(source, incoming)
        chosen_all = [chosen] + [feat_send(chosen, 0, dl) for dl in range(1, sides)]
        height = chosen.shape[0]
        tail_rows = (chunks - 1) * late
        remote_steps = [
            (0, height, [(0, 0, 0)] + [(c, 1, tail_rows + (c - 1) * height) for c in range(1, chunks)])
        ]
        remote_shapes = [(height, chunk)]
        if chunks > 1:
            remote_shapes.append((tail_rows + (chunks - 1) * height, chunk))
        remote_sends = [
            partial_sums(place, dh * sides, chosen_all, w_all, remote_steps, remote_shapes, x[1:], [(1, 0)] * len(x[1:]))
            for dh, x in zip(others, sends)
        ]
        remote_front = [feat_send(x[0], dh, 0) for dh, x in zip(others, remote_sends)]
        rest = [feat_send(x[1], dh, 0) for dh, x in zip(others, remote_sends)] if chunks > 1 else []
        own_remote_steps = [(0, height, [(c, c, 0) for c in range(chunks)])]
        remote_own = partial_sums(
            place, 0, chosen_all, w_all, own_remote_steps, [(height, chunk)] * chunks
        )

        reach = len(others)
        first_layout = [(h, h, 0, part, 0) for h in range(reach)]
        base = own_part(diag_adj, spread, own[0], front, first_layout, reach)
        collected = []
        outgoing = None
        for c in range(chunks):
            if c == 0:
                begin, received, layout = base, [], []
                remote_sums = [remote_own[0]] + remote_front
            else:
                begin, _ = lax.optimization_barrier((own[c], outgoing))
                received = front + rest
                layout = []
                for h in range(reach):
                    layout.append((h, h, part + (c - 1) * early, part + c * early, 0))
                    if late > 0:
                        layout.append((h, reach + h, (c - 1) * late, c * late, early))
                ends = tail_rows + c * height
                remote_sums = [remote_own[c]] + [r if ends == r.shape[0] else r[:ends] for r in rest]
            outgoing, base_next = hidden_blocks(
                row,
                want,
                first,
                c * chunk,
                bias,
                begin,
                remote,
                spread,
                diag_adj,
                remote_sums,
                received,
                layout,
                reach,
                0 if c == 0 else 10**11 // 2,
            )
            incoming = dom_exchange(outgoing)
            pieces = feature_pieces(source, row, place, base_next, remote, spread, incoming)
            collected.append(
                [p if dh == 0 and dl == 0 else feat_send(p, dh, dl) for (dh, dl), p in zip(shifts, pieces)]
            )

        out = b_second[None, :]
        for c in range(chunks):
            weights = [[(w, c)] for w in w2_core]
            if shares == 1:
                weights += [[(group[0], c)] for group in w2_far]
            else:
                weights += [[(w, 0) for w in group] for group in w2_far]
            out = add_product((share - c) % shares, out, collected[c], weights)
        return out

    return jax.shard_map(
        per_device,
        mesh=mesh,
        in_specs=(
            P("dom", "feat"),
            P("dom"),
            P("dom", None),
            P("dom", None, None, None),
            P("dom", None),
            P("dom", None),
            P("dom", None),
            P("feat", None),
            P(),
            P("feat", None),
            P(),
        ),
        out_specs=P(("dom", "feat"), None),
        check_vma=False,
    )
```

```python
import functools

import jax
import jax.numpy as jnp
from jax import lax
from jax.experimental import pallas as pl
from jax.experimental.pallas import tpu as pltpu
from jax.sharding import PartitionSpec as P

LANES = 128
TOUCH = 2
HINT = 5 * 10**10
VMEM_LIMIT = 24 * 1024 * 1024
VMEM = pl.BlockSpec(memory_space=pltpu.VMEM)
SMEM = pl.BlockSpec(memory_space=pltpu.SMEM)
HBM = pl.BlockSpec(memory_space=pltpu.HBM)
PARAMS = pltpu.CompilerParams(vmem_limit_bytes=VMEM_LIMIT)


def dot3(a, b):
    return jnp.dot(a, b, precision=lax.Precision.HIGH, preferred_element_type=jnp.float32)


def two_parts(x):
    high = x.astype(jnp.bfloat16)
    return high, (x - high.astype(jnp.float32)).astype(jnp.bfloat16)


def left_parts(x):
    high, low = two_parts(x)
    return jnp.concatenate([high, low, high], axis=1)


def right_parts(w):
    high, low = two_parts(w)
    return jnp.concatenate([high, high, low], axis=0)


def f32(*dims):
    return jax.ShapeDtypeStruct(dims, jnp.float32)


def hbm(*dims):
    return pltpu.HBM(dims, jnp.float32)


def pinned(*arrays):
    return [pltpu.with_memory_space_constraint(a, pltpu.HBM) for a in arrays]


def rows_at(index, height):
    return pl.ds(pl.multiple_of(index * height, height), height)


def scratch(*dims):
    return pltpu.VMEM(dims, jnp.float32)


def start_all(pairs, sems, first):
    copies = [pltpu.make_async_copy(a, b, sems.at[first + i]) for i, (a, b) in enumerate(pairs)]
    for copy in copies:
        copy.start()
    return copies


def wait_all(copies):
    for copy in copies:
        copy.wait()


def cost(flops):
    return pl.CostEstimate(flops=flops, bytes_accessed=0, transcendentals=0)


def copy_body(index_ref, source, out):
    out[...] = source[...]


def row_block(index, source, height):
    width = source.shape[1]
    return pl.pallas_call(
        copy_body,
        out_shape=hbm(height, width),
        grid_spec=pltpu.PrefetchScalarGridSpec(
            num_scalar_prefetch=1,
            grid=(1,),
            in_specs=[pl.BlockSpec((height, width), lambda i, index: (index[0], 0))],
            out_specs=pl.BlockSpec((height, width), lambda i, index: (0, 0)),
        ),
        compiler_params=PARAMS,
        cost_estimate=cost(0),
    )(index, source)


def outgoing_body(want_ref, features, spread, blocks):
    chunk = spread.shape[1]
    for c in range(features.shape[1] // chunk):
        lanes = pl.ds(c * chunk, chunk)
        blocks[0, :, lanes] = features[:, lanes] * spread[...]


def outgoing_blocks(want, features, spread, tile):
    cols, chunk = features.shape[1], spread.shape[1]
    count = want.shape[0]
    last = features.shape[0] // tile - 1
    return pl.pallas_call(
        outgoing_body,
        out_shape=hbm(count, tile, cols),
        grid_spec=pltpu.PrefetchScalarGridSpec(
            num_scalar_prefetch=1,
            grid=(count,),
            in_specs=[
                pl.BlockSpec((tile, cols), lambda d, want: (jnp.minimum(want[d], last), 0)),
                pl.BlockSpec((tile, chunk), lambda d, want: (jnp.minimum(want[d], last), 0)),
            ],
            out_specs=pl.BlockSpec((1, tile, cols), lambda d, want: (d, 0, 0)),
        ),
        compiler_params=PARAMS,
        cost_estimate=cost(HINT),
    )(want, features, spread)


def partial_body(count, at, steps, place_ref, *refs):
    lefts, rights, refs = refs[:count], refs[count : 2 * count], refs[2 * count :]
    outs, (left, right, result, sems) = refs[:-4], refs[-4:]
    cols = lefts[0].shape[1]
    chunk = outs[0].shape[1]
    lanes = pl.ds(pl.multiple_of(place_ref[at] * cols, cols), cols)
    used = 0
    weights_in = start_all([(w.at[:, lanes], right.at[j]) for j, w in enumerate(rights)], sems, used)
    used += count
    loads, stores = [], []
    for start, stop, _ in steps:
        rows = pl.ds(start, stop - start)
        pairs = [(x.at[rows], left.at[rows, pl.ds(j * cols, cols)]) for j, x in enumerate(lefts)]
        loads.append(start_all(pairs, sems, used))
        used += count
    wait_all(weights_in)
    weight = right_parts(jnp.concatenate([right[j] for j in range(count)], axis=0))
    for (start, stop, targets), ready in zip(steps, loads):
        wait_all(ready)
        rows = pl.ds(start, stop - start)
        result[rows, :] = jnp.dot(left_parts(left[rows, :]), weight, preferred_element_type=jnp.float32)
        pairs = [
            (result.at[rows, pl.ds(c * chunk, chunk)], outs[o].at[pl.ds(offset, stop - start)])
            for c, o, offset in targets
        ]
        stores += start_all(pairs, sems, used)
        used += len(pairs)
    wait_all(stores)


def partial_sums(place, at, lefts, weights, steps, shapes, flops):
    rows, cols = lefts[0].shape
    depth = weights[0].shape[0]
    count = len(lefts)
    copies = count + sum(count + len(targets) for _, _, targets in steps)
    return pl.pallas_call(
        functools.partial(partial_body, count, at, steps),
        out_shape=[hbm(*s) for s in shapes],
        in_specs=[SMEM] + [HBM] * (2 * count),
        out_specs=[HBM] * len(shapes),
        scratch_shapes=[
            scratch(rows, count * cols),
            scratch(count, depth, cols),
            scratch(rows, cols),
            pltpu.SemaphoreType.DMA((copies,)),
        ],
        compiler_params=PARAMS,
        cost_estimate=cost(flops),
    )(place, *pinned(lefts[0]), *lefts[1:], *pinned(weights[0]), *weights[1:])


def chosen_body(source_ref, incoming, chosen):
    chosen[...] = incoming[0]


def chosen_blocks(source, incoming):
    tile, cols = incoming.shape[1:]
    groups = source.shape[0] // TOUCH
    return pl.pallas_call(
        chosen_body,
        out_shape=hbm(groups * tile, cols),
        grid_spec=pltpu.PrefetchScalarGridSpec(
            num_scalar_prefetch=1,
            grid=(groups,),
            in_specs=[pl.BlockSpec((1, tile, cols), lambda g, source: (source[TOUCH * g], 0, 0))],
            out_specs=pl.BlockSpec((tile, cols), lambda g, source: (g, 0)),
        ),
        compiler_params=PARAMS,
        cost_estimate=cost(0),
    )(source, incoming)


def joined_body(count, *refs):
    sources, (out, held, sems) = refs[:count], refs[count:]
    offsets, at = [], 0
    for x in sources:
        offsets.append(pl.ds(at, x.shape[0]))
        at += x.shape[0]
    loads = start_all([(x, held.at[rows]) for x, rows in zip(sources, offsets)], sems, 0)
    stores = []
    for j, rows in enumerate(offsets):
        loads[j].wait()
        stores += start_all([(held.at[rows], out.at[rows])], sems, count + j)
    wait_all(stores)


def joined(sources):
    rows, cols = sum(x.shape[0] for x in sources), sources[0].shape[1]
    count = len(sources)
    return pl.pallas_call(
        functools.partial(joined_body, count),
        out_shape=hbm(rows, cols),
        in_specs=[HBM] * count,
        out_specs=HBM,
        scratch_shapes=[scratch(rows, cols), pltpu.SemaphoreType.DMA((2 * count,))],
        compiler_params=PARAMS,
        cost_estimate=cost(HINT),
    )(*pinned(*sources))


def received_pairs(layout, received, recv_in):
    return [
        (received[r].at[pl.ds(start, stop - start)], recv_in.at[h, pl.ds(offset, stop - start)])
        for h, r, start, stop, offset in layout
    ]


def own_total(diag_in, spread_in, own_in, recv_in, total):
    tile = diag_in.shape[1]
    for i in range(diag_in.shape[0] // tile):
        rows = pl.ds(i * tile, tile)
        mixed = own_in[rows, :]
        for h in range(recv_in.shape[0]):
            mixed = mixed + recv_in[h, rows, :]
        total[rows, :] = dot3(diag_in[rows, :], mixed * spread_in[rows, :])


def own_body(layout, diag, spread, own, *refs):
    received, (base, diag_in, spread_in, own_in, recv_in, total, sems) = refs[:-7], refs[-7:]
    pairs = [(diag, diag_in), (spread, spread_in), (own, own_in)]
    wait_all(start_all(pairs + received_pairs(layout, received, recv_in), sems, 0))
    own_total(diag_in, spread_in, own_in, recv_in, total)
    wait_all(start_all([(total, base)], sems, 3 + len(layout)))


def own_part(diag, spread, own, received, layout, others):
    return pl.pallas_call(
        functools.partial(own_body, layout),
        out_shape=hbm(*own.shape),
        in_specs=[HBM] * (3 + len(received)),
        out_specs=HBM,
        scratch_shapes=[scratch(*a.shape) for a in (diag, spread, own)]
        + [scratch(others, *own.shape), scratch(*own.shape), pltpu.SemaphoreType.DMA((4 + len(layout),))],
        compiler_params=PARAMS,
        cost_estimate=cost(0),
    )(*pinned(diag, spread, own), *received)


def hidden_body(
    count, reach, layout, lane_offset, row_ref, want_ref, first_ref, bias, base, remote, spread, diag, *refs
):
    remote_sums, refs = refs[:count], refs[count:]
    received, refs = refs[:reach], refs[reach:]
    blocks, base_out, total, remote_in, spread_in, diag_in, scaled, sums_in, recv_in, sems = refs
    tiles, tile = remote.shape[:2]
    parts = blocks.shape[0]
    chunk = total.shape[1]
    height = sums_in.shape[1]
    begin = total if reach == 0 else scaled
    pairs = [(base, begin), (spread, spread_in), (diag, diag_in)]
    pairs += received_pairs(layout, received, recv_in)
    late = [(remote, remote_in)]
    late += [(s.at[pl.ds(s.shape[0] - height, height)], sums_in.at[j]) for j, s in enumerate(remote_sums)]
    if reach == 0:
        tail = start_all(late, sems, 0)
        first = start_all(pairs, sems, len(late))
        wait_all(first[:1])
    else:
        first = start_all(pairs, sems, 0)
        tail = start_all(late, sems, len(pairs))
        wait_all(first)
        own_total(diag_in, spread_in, scaled, recv_in, total)
    wait_all(tail)
    for g in range(tiles // TOUCH):
        rows = pl.ds(g * tile, tile)
        block = sums_in[0, rows, :]
        for j in range(1, count):
            block = block + sums_in[j, rows, :]
        for k in range(TOUCH * g, TOUCH * g + TOUCH):
            total[rows_at(row_ref[k], tile), :] += dot3(remote_in[k], block)
    lanes = pl.ds(pl.multiple_of(first_ref[0] + lane_offset, chunk), chunk)
    shift = bias[:, lanes]
    if reach == 0:
        wait_all(first[1:])
    scaled[...] = jnp.maximum(total[...] * spread_in[...] + shift, 0.0) * spread_in[...]
    used = len(pairs) + len(late)
    last = scaled.shape[0] // tile - 1
    copies = start_all(
        [(scaled.at[rows_at(jnp.minimum(want_ref[d], last), tile)], blocks.at[d]) for d in range(parts)],
        sems,
        used,
    )
    for i in range(last + 1):
        rows = pl.ds(i * tile, tile)
        total[rows, :] = dot3(diag_in[rows, :], scaled[rows, :])
    copies += start_all([(total, base_out)], sems, used + parts)
    wait_all(copies)


def hidden_blocks(
    row, want, first, lane_offset, bias, base, remote, spread, diag, remote_sums, received, layout, others, flops
):
    rows, chunk = base.shape
    tile = diag.shape[1]
    parts = want.shape[0]
    count = len(remote_sums)
    height = remote.shape[0] // TOUCH * tile
    return pl.pallas_call(
        functools.partial(hidden_body, count, len(received), layout, lane_offset),
        out_shape=[hbm(parts, tile, chunk), hbm(rows, chunk)],
        in_specs=[SMEM] * 3 + [VMEM] + [HBM] * (4 + count + len(received)),
        out_specs=[HBM, HBM],
        scratch_shapes=[scratch(*a.shape) for a in (base, remote, spread, diag, base)]
        + [scratch(count, height, chunk), scratch(others, *base.shape)]
        + [pltpu.SemaphoreType.DMA((5 + len(layout) + count + parts,))],
        compiler_params=PARAMS,
        cost_estimate=cost(flops),
    )(row, want, first, bias, *pinned(base, remote, spread, diag, remote_sums[0]), *remote_sums[1:], *received)


def pieces_body(source_ref, row_ref, place_ref, base, remote, spread, incoming, *refs):
    pieces, (total, remote_in, spread_in, incoming_in, sems) = refs[:-5], refs[-5:]
    tiles, tile = remote.shape[:2]
    early = start_all(
        [(incoming, incoming_in), (remote, remote_in), (base, total), (spread, spread_in)], sems, 0
    )
    wait_all(early[:3])
    for k in range(tiles):
        total[rows_at(row_ref[k], tile), :] += dot3(remote_in[k], incoming_in[source_ref[k]])
    wait_all(early[3:])
    total[...] = total[...] * spread_in[...]
    height = pieces[0].shape[0]
    pairs = [(total.at[rows_at(place_ref[j], height)], p) for j, p in enumerate(pieces)]
    wait_all(start_all(pairs, sems, 4))


def feature_pieces(source, row, place, base, remote, spread, incoming):
    rows, chunk = base.shape
    feats = place.shape[0]
    return pl.pallas_call(
        pieces_body,
        out_shape=[hbm(rows // feats, chunk)] * feats,
        in_specs=[SMEM] * 3 + [HBM] * 4,
        out_specs=[HBM] * feats,
        scratch_shapes=[scratch(*a.shape) for a in (base, remote, spread, incoming)]
        + [pltpu.SemaphoreType.DMA((4 + feats,))],
        compiler_params=PARAMS,
        cost_estimate=cost(0),
    )(source, row, place, *pinned(base, remote, spread), incoming)


def product_body(count, choices, turn_ref, start, *refs):
    pieces, weights, (out, left) = refs[:count], refs[count:-2], refs[-2:]
    chunk = pieces[0].shape[1]

    @pl.when(pl.program_id(0) == 0)
    def _():
        left[...] = left_parts(jnp.concatenate([p[...] for p in pieces], axis=1))

    blocks, at = [], 0
    for number in choices:
        block = weights[at][...]
        for k in range(1, number):
            block = jnp.where(turn_ref[0] == k, weights[at + k][...], block)
        blocks.append(block)
        at += number
    right = right_parts(jnp.concatenate(blocks, axis=0))
    out[...] = start[...] + jnp.dot(left[...], right, preferred_element_type=jnp.float32)


def add_product(turn, start, pieces, weights):
    rows, chunk = pieces[0].shape
    width = start.shape[1]
    step = min(2 * LANES, width)
    count = len(pieces)
    flat = [w for group in weights for w in group]
    return pl.pallas_call(
        functools.partial(product_body, count, [len(group) for group in weights]),
        out_shape=f32(rows, width),
        grid_spec=pltpu.PrefetchScalarGridSpec(
            num_scalar_prefetch=1,
            grid=(width // step,),
            in_specs=[pl.BlockSpec((start.shape[0], step), lambda j, turn: (0, j))]
            + [pl.BlockSpec((rows, chunk), lambda j, turn: (0, 0))] * count
            + [pl.BlockSpec((chunk, step), lambda j, turn, c=c: (c, j)) for _, c in flat],
            out_specs=pl.BlockSpec((rows, step), lambda j, turn: (0, j)),
            scratch_shapes=[pltpu.VMEM((rows, 3 * count * chunk), jnp.bfloat16)],
        ),
        compiler_params=PARAMS,
        cost_estimate=cost(6 * count * rows * chunk * width),
    )(turn, start, *pieces, *[w for w, _ in flat])


def solution(mesh):
    parts = mesh.shape["dom"]
    feats = mesh.shape["feat"]
    sides = 2 if feats % 2 == 0 else 1
    halves = feats // sides
    others = list(range(1, halves))

    def feat_target(f, dh, dl):
        return (f // sides + dh) % halves * sides + (f % sides + dl) % sides

    def feat_send(x, dh, dl):
        return lax.ppermute(x, "feat", [(f, feat_target(f, dh, dl)) for f in range(feats)])

    def dom_exchange(x):
        return lax.all_to_all(x, "dom", split_axis=0, concat_axis=0, tiled=True)

    def per_device(
        features,
        degree,
        diag_adj,
        remote_adj,
        read_block,
        tile_src,
        tile_row,
        w_first,
        b_first,
        w_second,
        b_second,
    ):
        part, cols = features.shape
        tile = diag_adj.shape[1]
        blocks = part // tile
        remote = remote_adj[0]
        chunk = LANES if cols % LANES == 0 else cols
        chunks = cols // chunk
        f = lax.axis_index("feat")
        want, source, row = read_block[0], tile_src[0], tile_row[0]
        shifts = [(dh, dl) for dh in range(halves) for dl in range(sides)]
        place = jnp.stack([jnp.asarray(feat_target(f, dh, dl), jnp.int32) for dh, dl in shifts])
        first = jnp.reshape(jnp.asarray(f * cols, jnp.int32), (1,))
        bias = b_first[None, :]

        x_all = [features] + [feat_send(features, 0, dl) for dl in range(1, sides)]
        w_all = [w_first] + [feat_send(w_first, 0, dl) for dl in range(1, sides)]

        shares = chunks if parts % chunks == 0 else 1
        share = jnp.reshape(jnp.asarray(lax.axis_index("dom") % shares, jnp.int32), (1,))
        share_rows = w_second.shape[0] // shares

        def share_send(x, k):
            pairs = [(s, s // shares * shares + (s % shares + k) % shares) for s in range(parts)]
            return lax.ppermute(x, "dom", pairs)

        w2_sent = row_block(share, w_second, share_rows)
        w2_got = [feat_send(w2_sent, dh, 0) for dh in others]

        scaling = lax.rsqrt(degree.astype(jnp.float32))
        spread = jnp.broadcast_to(scaling[:, None], (part, chunk))
        outgoing = outgoing_blocks(want, features, spread, tile)
        incoming = dom_exchange(outgoing)

        early = blocks * 5 // 12 * tile if chunks > 1 else part
        late = part - early
        marks = sorted({0, early // 2 // tile * tile, early, early + late // 2 // tile * tile, part})
        spans = list(zip(marks[:-1], marks[1:]))
        x_all[0], _ = lax.optimization_barrier((features, outgoing))
        send_steps = []
        for start, stop in spans:
            targets = [(0, 0, start)]
            for c in range(1, chunks):
                if stop <= early:
                    targets.append((c, 0, part + (c - 1) * early + start))
                else:
                    targets.append((c, 1, (c - 1) * late + start - early))
            send_steps.append((start, stop, targets))
        send_shapes = [(part + (chunks - 1) * early, chunk)]
        if late > 0:
            send_shapes.append(((chunks - 1) * late, chunk))
        sends = [partial_sums(place, dh * sides, x_all, w_all, send_steps, send_shapes, 0) for dh in others]
        sends, w2_got = lax.optimization_barrier((sends, w2_got))
        front = [feat_send(x[0], dh, 0) for dh, x in zip(others, sends)]

        own_steps = [(a, b, [(c, c, a) for c in range(chunks)]) for a, b in spans]
        own = partial_sums(place, 0, x_all, w_all, own_steps, [(part, chunk)] * chunks, HINT)

        w2_got, _ = lax.optimization_barrier((w2_got, own))
        w2_groups = [[got] + [share_send(got, k) for k in range(1, shares)] for got in w2_got]
        incoming, own, w2_groups = lax.optimization_barrier((incoming, own, w2_groups))
        w2_core = [w_second] + [feat_send(w_second, 0, dl) for dl in range(1, sides)]
        w2_far = [[feat_send(w, 0, dl) if dl > 0 else w for w in g] for g in w2_groups for dl in range(sides)]
        chosen = chosen_blocks(source, incoming)
        chosen_all = [chosen] + [feat_send(chosen, 0, dl) for dl in range(1, sides)]
        height = chosen.shape[0]
        tail_rows = (chunks - 1) * late
        remote_steps = [(0, height, [(c, c, 0) for c in range(chunks)])]
        remote_shapes = [(height, chunk)] * chunks
        remote_sends = [
            partial_sums(place, dh * sides, chosen_all, w_all, remote_steps, remote_shapes, 0) for dh in others
        ]
        remote_front = [feat_send(x[0], dh, 0) for dh, x in zip(others, remote_sends)]
        rest = []
        if chunks > 1:
            rest = [
                feat_send(joined([*x[1:], *r[1:]]), dh, 0) for dh, x, r in zip(others, sends, remote_sends)
            ]
        own_remote_steps = [(0, height, [(c, c, 0) for c in range(chunks)])]
        remote_own = partial_sums(place, 0, chosen_all, w_all, own_remote_steps, remote_shapes, 0)

        reach = len(others)
        first_layout = [(h, h, 0, part, 0) for h in range(reach)]
        base = own_part(diag_adj, spread, own[0], front, first_layout, reach)
        collected = []
        outgoing = None
        for c in range(chunks):
            if c == 0:
                begin, received, layout = base, [], []
                remote_sums = [remote_own[0]] + remote_front
            else:
                begin, _ = lax.optimization_barrier((own[c], outgoing))
                received = front + rest
                layout = []
                for h in range(reach):
                    layout.append((h, h, part + (c - 1) * early, part + c * early, 0))
                    if late > 0:
                        layout.append((h, reach + h, (c - 1) * late, c * late, early))
                ends = tail_rows + c * height
                remote_sums = [remote_own[c]] + [r if ends == r.shape[0] else r[:ends] for r in rest]
            outgoing, base_next = hidden_blocks(
                row,
                want,
                first,
                c * chunk,
                bias,
                begin,
                remote,
                spread,
                diag_adj,
                remote_sums,
                received,
                layout,
                reach,
                0 if c == 0 else HINT,
            )
            incoming = dom_exchange(outgoing)
            pieces = feature_pieces(source, row, place, base_next, remote, spread, incoming)
            collected.append(
                [p if dh == 0 and dl == 0 else feat_send(p, dh, dl) for (dh, dl), p in zip(shifts, pieces)]
            )

        out = b_second[None, :]
        for c in range(chunks):
            weights = [[(w, c)] for w in w2_core]
            if shares == 1:
                weights += [[(group[0], c)] for group in w2_far]
            else:
                weights += [[(w, 0) for w in group] for group in w2_far]
            out = add_product((share - c) % shares, out, collected[c], weights)
        return out

    return jax.shard_map(
        per_device,
        mesh=mesh,
        in_specs=(
            P("dom", "feat"),
            P("dom"),
            P("dom", None),
            P("dom", None, None, None),
            P("dom", None),
            P("dom", None),
            P("dom", None),
            P("feat", None),
            P(),
            P("feat", None),
            P(),
        ),
        out_specs=P(("dom", "feat"), None),
        check_vma=False,
    )
```

```python
import functools

import jax
import jax.numpy as jnp
from jax import lax
from jax.experimental import pallas as pl
from jax.experimental.pallas import tpu as pltpu
from jax.sharding import PartitionSpec as P

LANES = 128
TOUCH = 2
HINT = 5 * 10**10
VMEM_LIMIT = 24 * 1024 * 1024
VMEM = pl.BlockSpec(memory_space=pltpu.VMEM)
SMEM = pl.BlockSpec(memory_space=pltpu.SMEM)
HBM = pl.BlockSpec(memory_space=pltpu.HBM)
PARAMS = pltpu.CompilerParams(vmem_limit_bytes=VMEM_LIMIT)


def dot3(a, b):
    return jnp.dot(a, b, precision=lax.Precision.HIGH, preferred_element_type=jnp.float32)


def two_parts(x):
    high = x.astype(jnp.bfloat16)
    return high, (x - high.astype(jnp.float32)).astype(jnp.bfloat16)


def left_parts(x):
    high, low = two_parts(x)
    return jnp.concatenate([high, low, high], axis=1)


def right_parts(w):
    high, low = two_parts(w)
    return jnp.concatenate([high, high, low], axis=0)


def f32(*dims):
    return jax.ShapeDtypeStruct(dims, jnp.float32)


def hbm(*dims):
    return pltpu.HBM(dims, jnp.float32)


def pinned(*arrays):
    return [pltpu.with_memory_space_constraint(a, pltpu.HBM) for a in arrays]


def rows_at(index, height):
    return pl.ds(pl.multiple_of(index * height, height), height)


def scratch(*dims):
    return pltpu.VMEM(dims, jnp.float32)


def start_all(pairs, sems, first):
    copies = [pltpu.make_async_copy(a, b, sems.at[first + i]) for i, (a, b) in enumerate(pairs)]
    for copy in copies:
        copy.start()
    return copies


def wait_all(copies):
    for copy in copies:
        copy.wait()


def cost(flops):
    return pl.CostEstimate(flops=flops, bytes_accessed=0, transcendentals=0)


def copy_body(index_ref, source, out):
    out[...] = source[...]


def row_block(index, source, height):
    width = source.shape[1]
    return pl.pallas_call(
        copy_body,
        out_shape=hbm(height, width),
        grid_spec=pltpu.PrefetchScalarGridSpec(
            num_scalar_prefetch=1,
            grid=(1,),
            in_specs=[pl.BlockSpec((height, width), lambda i, index: (index[0], 0))],
            out_specs=pl.BlockSpec((height, width), lambda i, index: (0, 0)),
        ),
        compiler_params=PARAMS,
        cost_estimate=cost(0),
    )(index, source)


def outgoing_body(want_ref, features, spread, blocks):
    chunk = spread.shape[1]
    for c in range(features.shape[1] // chunk):
        lanes = pl.ds(c * chunk, chunk)
        blocks[0, :, lanes] = features[:, lanes] * spread[...]


def outgoing_blocks(want, features, spread, tile):
    cols, chunk = features.shape[1], spread.shape[1]
    count = want.shape[0]
    last = features.shape[0] // tile - 1
    return pl.pallas_call(
        outgoing_body,
        out_shape=hbm(count, tile, cols),
        grid_spec=pltpu.PrefetchScalarGridSpec(
            num_scalar_prefetch=1,
            grid=(count,),
            in_specs=[
                pl.BlockSpec((tile, cols), lambda d, want: (jnp.minimum(want[d], last), 0)),
                pl.BlockSpec((tile, chunk), lambda d, want: (jnp.minimum(want[d], last), 0)),
            ],
            out_specs=pl.BlockSpec((1, tile, cols), lambda d, want: (d, 0, 0)),
        ),
        compiler_params=PARAMS,
        cost_estimate=cost(HINT),
    )(want, features, spread)


def partial_body(count, at, steps, place_ref, *refs):
    lefts, rights, refs = refs[:count], refs[count : 2 * count], refs[2 * count :]
    outs, (left, right, result, sems) = refs[:-4], refs[-4:]
    cols = lefts[0].shape[1]
    chunk = outs[0].shape[1]
    lanes = pl.ds(pl.multiple_of(place_ref[at] * cols, cols), cols)
    used = 0
    weights_in = start_all([(w.at[:, lanes], right.at[j]) for j, w in enumerate(rights)], sems, used)
    used += count
    loads, stores = [], []
    for start, stop, _ in steps:
        rows = pl.ds(start, stop - start)
        pairs = [(x.at[rows], left.at[rows, pl.ds(j * cols, cols)]) for j, x in enumerate(lefts)]
        loads.append(start_all(pairs, sems, used))
        used += count
    wait_all(weights_in)
    weight = right_parts(jnp.concatenate([right[j] for j in range(count)], axis=0))
    for (start, stop, targets), ready in zip(steps, loads):
        wait_all(ready)
        rows = pl.ds(start, stop - start)
        result[rows, :] = jnp.dot(left_parts(left[rows, :]), weight, preferred_element_type=jnp.float32)
        pairs = [
            (result.at[rows, pl.ds(c * chunk, chunk)], outs[o].at[pl.ds(offset, stop - start)])
            for c, o, offset in targets
        ]
        stores += start_all(pairs, sems, used)
        used += len(pairs)
    wait_all(stores)


def partial_sums(place, at, lefts, weights, steps, shapes, flops):
    rows, cols = lefts[0].shape
    depth = weights[0].shape[0]
    count = len(lefts)
    copies = count + sum(count + len(targets) for _, _, targets in steps)
    return pl.pallas_call(
        functools.partial(partial_body, count, at, steps),
        out_shape=[hbm(*s) for s in shapes],
        in_specs=[SMEM] + [HBM] * (2 * count),
        out_specs=[HBM] * len(shapes),
        scratch_shapes=[
            scratch(rows, count * cols),
            scratch(count, depth, cols),
            scratch(rows, cols),
            pltpu.SemaphoreType.DMA((copies,)),
        ],
        compiler_params=PARAMS,
        cost_estimate=cost(flops),
    )(place, *pinned(lefts[0]), *lefts[1:], *pinned(weights[0]), *weights[1:])


def chosen_body(source_ref, incoming, chosen):
    chosen[...] = incoming[0]


def chosen_blocks(source, incoming):
    tile, cols = incoming.shape[1:]
    groups = source.shape[0] // TOUCH
    return pl.pallas_call(
        chosen_body,
        out_shape=hbm(groups * tile, cols),
        grid_spec=pltpu.PrefetchScalarGridSpec(
            num_scalar_prefetch=1,
            grid=(groups,),
            in_specs=[pl.BlockSpec((1, tile, cols), lambda g, source: (source[TOUCH * g], 0, 0))],
            out_specs=pl.BlockSpec((tile, cols), lambda g, source: (g, 0)),
        ),
        compiler_params=PARAMS,
        cost_estimate=cost(0),
    )(source, incoming)


def joined_body(count, *refs):
    sources, (out, held, sems) = refs[:count], refs[count:]
    offsets, at = [], 0
    for x in sources:
        offsets.append(pl.ds(at, x.shape[0]))
        at += x.shape[0]
    loads = start_all([(x, held.at[rows]) for x, rows in zip(sources, offsets)], sems, 0)
    stores = []
    for j, rows in enumerate(offsets):
        loads[j].wait()
        stores += start_all([(held.at[rows], out.at[rows])], sems, count + j)
    wait_all(stores)


def joined(sources):
    rows, cols = sum(x.shape[0] for x in sources), sources[0].shape[1]
    count = len(sources)
    return pl.pallas_call(
        functools.partial(joined_body, count),
        out_shape=hbm(rows, cols),
        in_specs=[HBM] * count,
        out_specs=HBM,
        scratch_shapes=[scratch(rows, cols), pltpu.SemaphoreType.DMA((2 * count,))],
        compiler_params=PARAMS,
        cost_estimate=cost(0),
    )(*pinned(*sources))


def received_pairs(layout, received, recv_in):
    return [
        (received[r].at[pl.ds(start, stop - start)], recv_in.at[h, pl.ds(offset, stop - start)])
        for h, r, start, stop, offset in layout
    ]


def own_total(diag_in, spread_in, own_in, recv_in, total):
    tile = diag_in.shape[1]
    for i in range(diag_in.shape[0] // tile):
        rows = pl.ds(i * tile, tile)
        mixed = own_in[rows, :]
        for h in range(recv_in.shape[0]):
            mixed = mixed + recv_in[h, rows, :]
        total[rows, :] = dot3(diag_in[rows, :], mixed * spread_in[rows, :])


def own_body(layout, diag, spread, own, *refs):
    received, (base, recv_in, sems) = refs[:-3], refs[-3:]
    wait_all(start_all(received_pairs(layout, received, recv_in), sems, 0))
    own_total(diag, spread, own, recv_in, base)


def own_part(diag, spread, own, received, layout, others):
    return pl.pallas_call(
        functools.partial(own_body, layout),
        out_shape=f32(*own.shape),
        in_specs=[VMEM] * 3 + [HBM] * len(received),
        out_specs=VMEM,
        scratch_shapes=[scratch(others, *own.shape), pltpu.SemaphoreType.DMA((len(layout),))],
        compiler_params=PARAMS,
        cost_estimate=cost(0),
    )(diag, spread, own, *received)


def hidden_tail(
    lane_offset, row_ref, want_ref, first_ref, bias, remote, spread, diag, sums, blocks, base_out, total, scaled, sems, used
):
    tiles, tile = remote.shape[:2]
    parts = blocks.shape[0]
    chunk = total.shape[1]
    for g in range(tiles // TOUCH):
        block = sums[0][pl.ds(g * tile, tile), :]
        for x in sums[1:]:
            block = block + x[pl.ds(g * tile, tile), :]
        for k in range(TOUCH * g, TOUCH * g + TOUCH):
            total[rows_at(row_ref[k], tile), :] += dot3(remote[k], block)
    lanes = pl.ds(pl.multiple_of(first_ref[0] + lane_offset, chunk), chunk)
    scaled[...] = jnp.maximum(total[...] * spread[...] + bias[:, lanes], 0.0) * spread[...]
    last = scaled.shape[0] // tile - 1
    copies = start_all(
        [(scaled.at[rows_at(jnp.minimum(want_ref[d], last), tile)], blocks.at[d]) for d in range(parts)],
        sems,
        used,
    )
    for i in range(last + 1):
        rows = pl.ds(i * tile, tile)
        total[rows, :] = dot3(diag[rows, :], scaled[rows, :])
    copies += start_all([(total, base_out)], sems, used + parts)
    wait_all(copies)


def hidden_body(lane_offset, row_ref, want_ref, first_ref, bias, base, remote, spread, diag, *refs):
    sums, (blocks, base_out, total, scaled, sems) = refs[:-5], refs[-5:]
    total[...] = base[...]
    hidden_tail(
        lane_offset, row_ref, want_ref, first_ref, bias, remote, spread, diag, sums, blocks, base_out, total, scaled, sems, 0
    )


def hidden_blocks(row, want, first, lane_offset, bias, base, remote, spread, diag, remote_sums):
    rows, chunk = base.shape
    tile = diag.shape[1]
    parts = want.shape[0]
    return pl.pallas_call(
        functools.partial(hidden_body, lane_offset),
        out_shape=[hbm(parts, tile, chunk), hbm(rows, chunk)],
        in_specs=[SMEM] * 3 + [VMEM] * (5 + len(remote_sums)),
        out_specs=[HBM, HBM],
        scratch_shapes=[scratch(rows, chunk), scratch(rows, chunk), pltpu.SemaphoreType.DMA((parts + 1,))],
        compiler_params=PARAMS,
        cost_estimate=cost(0),
    )(row, want, first, bias, base, remote, spread, diag, *remote_sums)


def later_body(
    count, layout, lane_offset, row_ref, want_ref, first_ref, bias, own, remote, spread, diag, *refs
):
    remote_sums, refs = refs[:count], refs[count:]
    received, refs = refs[:-10], refs[-10:]
    blocks, base_out, total, remote_in, spread_in, diag_in, scaled, sums_in, recv_in, sems = refs
    height = sums_in.shape[1]
    pairs = [(own, scaled), (spread, spread_in), (diag, diag_in)]
    pairs += received_pairs(layout, received, recv_in)
    late = [(remote, remote_in)]
    late += [(s.at[pl.ds(s.shape[0] - height, height)], sums_in.at[j]) for j, s in enumerate(remote_sums)]
    first = start_all(pairs, sems, 0)
    tail = start_all(late, sems, len(pairs))
    wait_all(first)
    own_total(diag_in, spread_in, scaled, recv_in, total)
    wait_all(tail)
    sums = [sums_in.at[j] for j in range(count)]
    hidden_tail(
        lane_offset,
        row_ref,
        want_ref,
        first_ref,
        bias,
        remote_in,
        spread_in,
        diag_in,
        sums,
        blocks,
        base_out,
        total,
        scaled,
        sems,
        len(pairs) + len(late),
    )


def later_blocks(
    row, want, first, lane_offset, bias, own, remote, spread, diag, remote_sums, received, layout, others
):
    rows, chunk = own.shape
    tile = diag.shape[1]
    parts = want.shape[0]
    count = len(remote_sums)
    height = remote.shape[0] // TOUCH * tile
    return pl.pallas_call(
        functools.partial(later_body, count, layout, lane_offset),
        out_shape=[hbm(parts, tile, chunk), hbm(rows, chunk)],
        in_specs=[SMEM] * 3 + [VMEM] + [HBM] * (4 + count + len(received)),
        out_specs=[HBM, HBM],
        scratch_shapes=[scratch(*a.shape) for a in (own, remote, spread, diag, own)]
        + [scratch(count, height, chunk), scratch(others, *own.shape)]
        + [pltpu.SemaphoreType.DMA((5 + len(layout) + count + parts,))],
        compiler_params=PARAMS,
        cost_estimate=cost(0),
    )(row, want, first, bias, *pinned(own, remote, spread, diag, remote_sums[0]), *remote_sums[1:], *received)


def pieces_body(source_ref, row_ref, place_ref, base, remote, spread, incoming, *refs):
    pieces, (total, remote_in, spread_in, incoming_in, sems) = refs[:-5], refs[-5:]
    tiles, tile = remote.shape[:2]
    early = start_all(
        [(incoming, incoming_in), (remote, remote_in), (base, total), (spread, spread_in)], sems, 0
    )
    wait_all(early[:3])
    for k in range(tiles):
        total[rows_at(row_ref[k], tile), :] += dot3(remote_in[k], incoming_in[source_ref[k]])
    wait_all(early[3:])
    total[...] = total[...] * spread_in[...]
    height = pieces[0].shape[0]
    pairs = [(total.at[rows_at(place_ref[j], height)], p) for j, p in enumerate(pieces)]
    wait_all(start_all(pairs, sems, 4))


def feature_pieces(source, row, place, base, remote, spread, incoming):
    rows, chunk = base.shape
    feats = place.shape[0]
    return pl.pallas_call(
        pieces_body,
        out_shape=[hbm(rows // feats, chunk)] * feats,
        in_specs=[SMEM] * 3 + [HBM] * 4,
        out_specs=[HBM] * feats,
        scratch_shapes=[scratch(*a.shape) for a in (base, remote, spread, incoming)]
        + [pltpu.SemaphoreType.DMA((4 + feats,))],
        compiler_params=PARAMS,
        cost_estimate=cost(0),
    )(source, row, place, *pinned(base, remote, spread), incoming)


def product_body(count, choices, step, last, turn_ref, start, *refs):
    pieces, refs = refs[:count], refs[count:]
    total = sum(n for n, _, _ in choices)
    weights, (out, left, held, sems) = refs[:total], refs[total:]
    chunk = pieces[0].shape[1]
    left[...] = left_parts(jnp.concatenate([p[...] for p in pieces], axis=1))
    copies = []
    for j in range(held.shape[1] // step):
        lanes = pl.ds(j * step, step)
        blocks, at = [], 0
        for number, c, _ in choices:
            rows = pl.ds(c * chunk, chunk)
            block = weights[at][rows, lanes]
            for k in range(1, number):
                block = jnp.where(turn_ref[0] == k, weights[at + k][rows, lanes], block)
            blocks.append(block)
            at += number
        right = right_parts(jnp.concatenate(blocks, axis=0))
        made = start[:, lanes] + jnp.dot(left[...], right, preferred_element_type=jnp.float32)
        if last:
            held[:, lanes] = made
            copies += start_all([(held.at[:, lanes], out.at[:, lanes])], sems, j)
        else:
            out[:, lanes] = made
    wait_all(copies)


def add_product(turn, start, pieces, weights, last):
    rows, chunk = pieces[0].shape
    width = start.shape[1]
    step = min(2 * LANES, width)
    count = len(pieces)
    flat = [w for group in weights for w, _ in group]
    choices = [(len(group), group[0][1], 0) for group in weights]
    return pl.pallas_call(
        functools.partial(product_body, count, choices, step, last),
        out_shape=hbm(rows, width) if last else f32(rows, width),
        in_specs=[SMEM] + [VMEM] * (1 + count + len(flat)),
        out_specs=HBM if last else VMEM,
        scratch_shapes=[
            pltpu.VMEM((rows, 3 * count * chunk), jnp.bfloat16),
            scratch(rows, width),
            pltpu.SemaphoreType.DMA((width // step,)),
        ],
        compiler_params=PARAMS,
        cost_estimate=cost(6 * count * rows * chunk * width),
    )(turn, start, *pieces, *flat)


def solution(mesh):
    parts = mesh.shape["dom"]
    feats = mesh.shape["feat"]
    sides = 2 if feats % 2 == 0 else 1
    halves = feats // sides
    others = list(range(1, halves))

    def feat_target(f, dh, dl):
        return (f // sides + dh) % halves * sides + (f % sides + dl) % sides

    def feat_send(x, dh, dl):
        return lax.ppermute(x, "feat", [(f, feat_target(f, dh, dl)) for f in range(feats)])

    def dom_exchange(x):
        return lax.all_to_all(x, "dom", split_axis=0, concat_axis=0, tiled=True)

    def per_device(
        features,
        degree,
        diag_adj,
        remote_adj,
        read_block,
        tile_src,
        tile_row,
        w_first,
        b_first,
        w_second,
        b_second,
    ):
        part, cols = features.shape
        tile = diag_adj.shape[1]
        blocks = part // tile
        remote = remote_adj[0]
        chunk = LANES if cols % LANES == 0 else cols
        chunks = cols // chunk
        f = lax.axis_index("feat")
        want, source, row = read_block[0], tile_src[0], tile_row[0]
        shifts = [(dh, dl) for dh in range(halves) for dl in range(sides)]
        place = jnp.stack([jnp.asarray(feat_target(f, dh, dl), jnp.int32) for dh, dl in shifts])
        first = jnp.reshape(jnp.asarray(f * cols, jnp.int32), (1,))
        bias = b_first[None, :]

        x_all = [features] + [feat_send(features, 0, dl) for dl in range(1, sides)]
        w_all = [w_first] + [feat_send(w_first, 0, dl) for dl in range(1, sides)]

        shares = chunks if parts % chunks == 0 else 1
        share = jnp.reshape(jnp.asarray(lax.axis_index("dom") % shares, jnp.int32), (1,))
        share_rows = w_second.shape[0] // shares

        def share_send(x, k):
            pairs = [(s, s // shares * shares + (s % shares + k) % shares) for s in range(parts)]
            return lax.ppermute(x, "dom", pairs)

        w2_sent = row_block(share, w_second, share_rows)
        w2_got = [feat_send(w2_sent, dh, 0) for dh in others]

        scaling = lax.rsqrt(degree.astype(jnp.float32))
        spread = jnp.broadcast_to(scaling[:, None], (part, chunk))
        outgoing = outgoing_blocks(want, features, spread, tile)
        incoming = dom_exchange(outgoing)

        early = blocks * 5 // 12 * tile if chunks > 1 else part
        late = part - early
        marks = sorted({0, early // 2 // tile * tile, early, early + late // 2 // tile * tile, part})
        spans = list(zip(marks[:-1], marks[1:]))
        x_all[0], _ = lax.optimization_barrier((features, outgoing))
        send_steps = []
        for start, stop in spans:
            targets = [(0, 0, start)]
            for c in range(1, chunks):
                if stop <= early:
                    targets.append((c, 0, part + (c - 1) * early + start))
                else:
                    targets.append((c, 1, (c - 1) * late + start - early))
            send_steps.append((start, stop, targets))
        send_shapes = [(part + (chunks - 1) * early, chunk)]
        if late > 0:
            send_shapes.append(((chunks - 1) * late, chunk))
        sends = [partial_sums(place, dh * sides, x_all, w_all, send_steps, send_shapes, 0) for dh in others]
        sends, w2_got = lax.optimization_barrier((sends, w2_got))
        front = [feat_send(x[0], dh, 0) for dh, x in zip(others, sends)]

        own_steps = [(a, b, [(c, c, a) for c in range(chunks)]) for a, b in spans]
        own = list(partial_sums(place, 0, x_all, w_all, own_steps, [(part, chunk)] * chunks, HINT))

        w2_groups = [[got] + [share_send(got, k) for k in range(1, shares)] for got in w2_got]
        incoming, own = lax.optimization_barrier((incoming, list(own)))
        own[0], w2_groups = lax.optimization_barrier((own[0], w2_groups))
        w2_core = [w_second] + [feat_send(w_second, 0, dl) for dl in range(1, sides)]
        w2_far = [[feat_send(w, 0, dl) if dl > 0 else w for w in g] for g in w2_groups for dl in range(sides)]
        chosen = chosen_blocks(source, incoming)
        chosen_all = [chosen] + [feat_send(chosen, 0, dl) for dl in range(1, sides)]
        height = chosen.shape[0]
        tail_rows = (chunks - 1) * late
        remote_steps = [(0, height, [(c, c, 0) for c in range(chunks)])]
        remote_shapes = [(height, chunk)] * chunks
        remote_sends = [
            partial_sums(place, dh * sides, chosen_all, w_all, remote_steps, remote_shapes, 0) for dh in others
        ]
        remote_front = [feat_send(x[0], dh, 0) for dh, x in zip(others, remote_sends)]
        rest = []
        if chunks > 1:
            rest = [
                feat_send(joined([*x[1:], *r[1:]]), dh, 0) for dh, x, r in zip(others, sends, remote_sends)
            ]
        own_remote_steps = [(0, height, [(c, c, 0) for c in range(chunks)])]
        remote_own = partial_sums(place, 0, chosen_all, w_all, own_remote_steps, remote_shapes, 0)

        reach = len(others)
        first_layout = [(h, h, 0, part, 0) for h in range(reach)]
        base = own_part(diag_adj, spread, own[0], front, first_layout, reach)
        collected = []
        outgoing = None
        for c in range(chunks):
            if c == 0:
                outgoing, base_next = hidden_blocks(
                    row, want, first, 0, bias, base, remote, spread, diag_adj, [remote_own[0]] + remote_front
                )
            else:
                begin, _ = lax.optimization_barrier((own[c], outgoing))
                layout = []
                for h in range(reach):
                    layout.append((h, h, part + (c - 1) * early, part + c * early, 0))
                    if late > 0:
                        layout.append((h, reach + h, (c - 1) * late, c * late, early))
                ends = tail_rows + c * height
                remote_sums = [remote_own[c]] + [r if ends == r.shape[0] else r[:ends] for r in rest]
                outgoing, base_next = later_blocks(
                    row,
                    want,
                    first,
                    c * chunk,
                    bias,
                    begin,
                    remote,
                    spread,
                    diag_adj,
                    remote_sums,
                    front + rest,
                    layout,
                    reach,
                )
            incoming = dom_exchange(outgoing)
            pieces = feature_pieces(source, row, place, base_next, remote, spread, incoming)
            collected.append(
                [p if dh == 0 and dl == 0 else feat_send(p, dh, dl) for (dh, dl), p in zip(shifts, pieces)]
            )

        out = b_second[None, :]
        for c in range(chunks):
            weights = [[(w, c)] for w in w2_core]
            if shares == 1:
                weights += [[(group[0], c)] for group in w2_far]
            else:
                weights += [[(w, 0) for w in group] for group in w2_far]
            out = add_product((share - c) % shares, out, collected[c], weights, c == chunks - 1)
        return out

    return jax.shard_map(
        per_device,
        mesh=mesh,
        in_specs=(
            P("dom", "feat"),
            P("dom"),
            P("dom", None),
            P("dom", None, None, None),
            P("dom", None),
            P("dom", None),
            P("dom", None),
            P("feat", None),
            P(),
            P("feat", None),
            P(),
        ),
        out_specs=P(("dom", "feat"), None),
        check_vma=False,
    )
```

```python
import functools

import jax
import jax.numpy as jnp
from jax import lax
from jax.experimental import pallas as pl
from jax.experimental.pallas import tpu as pltpu
from jax.sharding import PartitionSpec as P

LANES = 128
TOUCH = 2
HINT = 5 * 10**10
VMEM_LIMIT = 24 * 1024 * 1024
VMEM = pl.BlockSpec(memory_space=pltpu.VMEM)
SMEM = pl.BlockSpec(memory_space=pltpu.SMEM)
HBM = pl.BlockSpec(memory_space=pltpu.HBM)
PARAMS = pltpu.CompilerParams(vmem_limit_bytes=VMEM_LIMIT)


def dot3(a, b):
    return jnp.dot(a, b, precision=lax.Precision.HIGH, preferred_element_type=jnp.float32)


def two_parts(x):
    high = x.astype(jnp.bfloat16)
    return high, (x - high.astype(jnp.float32)).astype(jnp.bfloat16)


def left_parts(x):
    high, low = two_parts(x)
    return jnp.concatenate([high, low, high], axis=1)


def right_parts(w):
    high, low = two_parts(w)
    return jnp.concatenate([high, high, low], axis=0)


def f32(*dims):
    return jax.ShapeDtypeStruct(dims, jnp.float32)


def hbm(*dims):
    return pltpu.HBM(dims, jnp.float32)


def pinned(*arrays):
    return [pltpu.with_memory_space_constraint(a, pltpu.HBM) for a in arrays]


def rows_at(index, height):
    return pl.ds(pl.multiple_of(index * height, height), height)


def scratch(*dims):
    return pltpu.VMEM(dims, jnp.float32)


def start_all(pairs, sems, first):
    copies = [pltpu.make_async_copy(a, b, sems.at[first + i]) for i, (a, b) in enumerate(pairs)]
    for copy in copies:
        copy.start()
    return copies


def wait_all(copies):
    for copy in copies:
        copy.wait()


def cost(flops):
    return pl.CostEstimate(flops=flops, bytes_accessed=0, transcendentals=0)


def copy_body(index_ref, source, out):
    out[...] = source[...]


def row_block(index, source, height):
    width = source.shape[1]
    return pl.pallas_call(
        copy_body,
        out_shape=hbm(height, width),
        grid_spec=pltpu.PrefetchScalarGridSpec(
            num_scalar_prefetch=1,
            grid=(1,),
            in_specs=[pl.BlockSpec((height, width), lambda i, index: (index[0], 0))],
            out_specs=pl.BlockSpec((height, width), lambda i, index: (0, 0)),
        ),
        compiler_params=PARAMS,
        cost_estimate=cost(0),
    )(index, *pinned(source))


def outgoing_body(want_ref, features, spread, blocks, held, sems):
    count, tile, cols = held.shape
    chunk = spread.shape[1]
    last = features.shape[0] // tile - 1
    copies = []
    for d in range(count):
        rows = rows_at(jnp.minimum(want_ref[d], last), tile)
        for c in range(cols // chunk):
            lanes = pl.ds(c * chunk, chunk)
            held[d, :, lanes] = features[rows, lanes] * spread[rows, :]
        copies += start_all([(held.at[d], blocks.at[d])], sems, d)
    wait_all(copies)


def outgoing_blocks(want, features, spread, tile):
    cols = features.shape[1]
    count = want.shape[0]
    return pl.pallas_call(
        outgoing_body,
        out_shape=hbm(count, tile, cols),
        in_specs=[SMEM, VMEM, VMEM],
        out_specs=HBM,
        scratch_shapes=[scratch(count, tile, cols), pltpu.SemaphoreType.DMA((count,))],
        compiler_params=PARAMS,
        cost_estimate=cost(HINT),
    )(want, features, spread)


def partial_body(count, groups, carried, place_ref, *refs):
    lefts, rights, refs = refs[:count], refs[count : 2 * count], refs[2 * count :]
    passing, refs = refs[: len(carried)], refs[len(carried) :]
    held, refs = refs[len(refs) - len(carried) :], refs[: len(refs) - len(carried)]
    outs, (left, right, result, sems) = refs[:-4], refs[-4:]
    cols = lefts[0].shape[1]
    chunk = outs[0].shape[1]
    used = 0
    weights_in, loads, stores = [], [], []
    for n, (at, _) in enumerate(groups):
        lanes = pl.ds(pl.multiple_of(place_ref[at] * cols, cols), cols)
        weights_in.append(start_all([(w.at[:, lanes], right.at[n, j]) for j, w in enumerate(rights)], sems, used))
        used += count
    for start, stop, _ in groups[0][1]:
        rows = pl.ds(start, stop - start)
        pairs = [(x.at[rows], left.at[rows, pl.ds(j * cols, cols)]) for j, x in enumerate(lefts)]
        loads.append(start_all(pairs, sems, used))
        used += count
    passed = start_all(list(zip(passing, held)), sems, used)
    used += len(carried)
    for n, (_, steps) in enumerate(groups):
        wait_all(weights_in[n])
        weight = right_parts(jnp.concatenate([right[n, j] for j in range(count)], axis=0))
        for i, (start, stop, targets) in enumerate(steps):
            if n == 0:
                wait_all(loads[i])
            rows = pl.ds(start, stop - start)
            result[n, rows, :] = jnp.dot(left_parts(left[rows, :]), weight, preferred_element_type=jnp.float32)
            pairs = [
                (result.at[n, rows, pl.ds(c * chunk, chunk)], outs[o].at[pl.ds(offset, stop - start)])
                for c, o, offset in targets
            ]
            stores += start_all(pairs, sems, used)
            used += len(pairs)
    wait_all(passed)
    pairs = [(h, outs[o].at[pl.ds(offset, h.shape[0])]) for h, (o, offset) in zip(held, carried)]
    stores += start_all(pairs, sems, used)
    wait_all(stores)


def partial_sums(place, groups, lefts, weights, shapes, flops=0, passing=(), carried=()):
    rows, cols = lefts[0].shape
    depth = weights[0].shape[0]
    count = len(lefts)
    copies = count * (len(groups) + len(groups[0][1])) + 2 * len(carried)
    copies += sum(len(targets) for _, steps in groups for _, _, targets in steps)
    return pl.pallas_call(
        functools.partial(partial_body, count, groups, carried),
        out_shape=[hbm(*s) for s in shapes],
        in_specs=[SMEM] + [HBM] * (2 * count + len(passing)),
        out_specs=[HBM] * len(shapes),
        scratch_shapes=[
            scratch(rows, count * cols),
            scratch(len(groups), count, depth, cols),
            scratch(len(groups), rows, cols),
            pltpu.SemaphoreType.DMA((copies,)),
        ]
        + [scratch(*p.shape) for p in passing],
        compiler_params=PARAMS,
        cost_estimate=cost(flops),
    )(place, *pinned(lefts[0]), *lefts[1:], *pinned(weights[0]), *weights[1:], *pinned(*passing))


def chosen_body(source_ref, incoming, chosen):
    chosen[...] = incoming[0]


def chosen_blocks(source, incoming):
    tile, cols = incoming.shape[1:]
    groups = source.shape[0] // TOUCH
    return pl.pallas_call(
        chosen_body,
        out_shape=hbm(groups * tile, cols),
        grid_spec=pltpu.PrefetchScalarGridSpec(
            num_scalar_prefetch=1,
            grid=(groups,),
            in_specs=[pl.BlockSpec((1, tile, cols), lambda g, source: (source[TOUCH * g], 0, 0))],
            out_specs=pl.BlockSpec((tile, cols), lambda g, source: (g, 0)),
        ),
        compiler_params=PARAMS,
        cost_estimate=cost(0),
    )(source, incoming)


def received_pairs(layout, received, recv_in):
    return [
        (received[r].at[pl.ds(start, stop - start)], recv_in.at[h, pl.ds(offset, stop - start)])
        for h, r, start, stop, offset in layout
    ]


def own_total(diag_in, spread_in, own_in, recv_in, total):
    tile = diag_in.shape[1]
    for i in range(diag_in.shape[0] // tile):
        rows = pl.ds(i * tile, tile)
        mixed = own_in[rows, :]
        for h in range(recv_in.shape[0]):
            mixed = mixed + recv_in[h, rows, :]
        total[rows, :] = dot3(diag_in[rows, :], mixed * spread_in[rows, :])


def own_body(layout, diag, spread, own, *refs):
    received, (base, recv_in, sems) = refs[:-3], refs[-3:]
    wait_all(start_all(received_pairs(layout, received, recv_in), sems, 0))
    own_total(diag, spread, own, recv_in, base)


def own_part(diag, spread, own, received, layout, others):
    return pl.pallas_call(
        functools.partial(own_body, layout),
        out_shape=f32(*own.shape),
        in_specs=[VMEM] * 3 + [HBM] * len(received),
        out_specs=VMEM,
        scratch_shapes=[scratch(others, *own.shape), pltpu.SemaphoreType.DMA((len(layout),))],
        compiler_params=PARAMS,
        cost_estimate=cost(0),
    )(diag, spread, own, *received)


def hidden_tail(
    lane_offset, row_ref, want_ref, first_ref, bias, remote, spread, diag, sums, blocks, base_out, total, scaled, sems, used
):
    tiles, tile = remote.shape[:2]
    parts = blocks.shape[0]
    chunk = total.shape[1]
    for g in range(tiles // TOUCH):
        block = sums[0][pl.ds(g * tile, tile), :]
        for x in sums[1:]:
            block = block + x[pl.ds(g * tile, tile), :]
        for k in range(TOUCH * g, TOUCH * g + TOUCH):
            total[rows_at(row_ref[k], tile), :] += dot3(remote[k], block)
    lanes = pl.ds(pl.multiple_of(first_ref[0] + lane_offset, chunk), chunk)
    scaled[...] = jnp.maximum(total[...] * spread[...] + bias[:, lanes], 0.0) * spread[...]
    last = scaled.shape[0] // tile - 1
    copies = start_all(
        [(scaled.at[rows_at(jnp.minimum(want_ref[d], last), tile)], blocks.at[d]) for d in range(parts)],
        sems,
        used,
    )
    for i in range(last + 1):
        rows = pl.ds(i * tile, tile)
        total[rows, :] = dot3(diag[rows, :], scaled[rows, :])
    copies += start_all([(total, base_out)], sems, used + parts)
    wait_all(copies)


def hidden_body(lane_offset, row_ref, want_ref, first_ref, bias, base, remote, spread, diag, *refs):
    sums, (blocks, base_out, total, scaled, sems) = refs[:-5], refs[-5:]
    total[...] = base[...]
    hidden_tail(
        lane_offset, row_ref, want_ref, first_ref, bias, remote, spread, diag, sums, blocks, base_out, total, scaled, sems, 0
    )


def hidden_blocks(row, want, first, lane_offset, bias, base, remote, spread, diag, remote_sums):
    rows, chunk = base.shape
    tile = diag.shape[1]
    parts = want.shape[0]
    return pl.pallas_call(
        functools.partial(hidden_body, lane_offset),
        out_shape=[hbm(parts, tile, chunk), hbm(rows, chunk)],
        in_specs=[SMEM] * 3 + [VMEM] * (5 + len(remote_sums)),
        out_specs=[HBM, HBM],
        scratch_shapes=[scratch(rows, chunk), scratch(rows, chunk), pltpu.SemaphoreType.DMA((parts + 1,))],
        compiler_params=PARAMS,
        cost_estimate=cost(HINT),
    )(row, want, first, bias, base, remote, spread, diag, *remote_sums)


def later_body(
    count, layout, lane_offset, row_ref, want_ref, first_ref, bias, own, remote, spread, diag, *refs
):
    remote_sums, refs = refs[:count], refs[count:]
    received, refs = refs[:-10], refs[-10:]
    blocks, base_out, total, remote_in, spread_in, diag_in, scaled, sums_in, recv_in, sems = refs
    height = sums_in.shape[1]
    pairs = [(own, scaled), (spread, spread_in), (diag, diag_in)]
    pairs += received_pairs(layout, received, recv_in)
    late = [(remote, remote_in)]
    late += [(s.at[pl.ds(s.shape[0] - height, height)], sums_in.at[j]) for j, s in enumerate(remote_sums)]
    first = start_all(pairs, sems, 0)
    tail = start_all(late, sems, len(pairs))
    wait_all(first)
    own_total(diag_in, spread_in, scaled, recv_in, total)
    wait_all(tail)
    sums = [sums_in.at[j] for j in range(count)]
    hidden_tail(
        lane_offset,
        row_ref,
        want_ref,
        first_ref,
        bias,
        remote_in,
        spread_in,
        diag_in,
        sums,
        blocks,
        base_out,
        total,
        scaled,
        sems,
        len(pairs) + len(late),
    )


def later_blocks(
    row, want, first, lane_offset, bias, own, remote, spread, diag, remote_sums, received, layout, others
):
    rows, chunk = own.shape
    tile = diag.shape[1]
    parts = want.shape[0]
    count = len(remote_sums)
    height = remote.shape[0] // TOUCH * tile
    return pl.pallas_call(
        functools.partial(later_body, count, layout, lane_offset),
        out_shape=[hbm(parts, tile, chunk), hbm(rows, chunk)],
        in_specs=[SMEM] * 3 + [VMEM] + [HBM] * (4 + count + len(received)),
        out_specs=[HBM, HBM],
        scratch_shapes=[scratch(*a.shape) for a in (own, remote, spread, diag, own)]
        + [scratch(count, height, chunk), scratch(others, *own.shape)]
        + [pltpu.SemaphoreType.DMA((5 + len(layout) + count + parts,))],
        compiler_params=PARAMS,
        cost_estimate=cost(HINT),
    )(row, want, first, bias, *pinned(own, remote, spread, diag, remote_sums[0]), *remote_sums[1:], *received)


def pieces_body(source_ref, row_ref, place_ref, base, remote, spread, incoming, *refs):
    pieces, (total, remote_in, spread_in, incoming_in, sems) = refs[:-5], refs[-5:]
    tiles, tile = remote.shape[:2]
    early = start_all(
        [(incoming, incoming_in), (remote, remote_in), (base, total), (spread, spread_in)], sems, 0
    )
    wait_all(early[:3])
    for k in range(tiles):
        total[rows_at(row_ref[k], tile), :] += dot3(remote_in[k], incoming_in[source_ref[k]])
    wait_all(early[3:])
    height = pieces[0].shape[0]
    copies = []
    for j in reversed(range(len(pieces))):
        rows = rows_at(place_ref[j], height)
        total[rows, :] = total[rows, :] * spread_in[rows, :]
        copies += start_all([(total.at[rows], pieces[j])], sems, 4 + j)
    wait_all(copies)


def feature_pieces(source, row, place, base, remote, spread, incoming):
    rows, chunk = base.shape
    feats = place.shape[0]
    return pl.pallas_call(
        pieces_body,
        out_shape=[hbm(rows // feats, chunk)] * feats,
        in_specs=[SMEM] * 3 + [HBM] * 4,
        out_specs=[HBM] * feats,
        scratch_shapes=[scratch(*a.shape) for a in (base, remote, spread, incoming)]
        + [pltpu.SemaphoreType.DMA((4 + feats,))],
        compiler_params=PARAMS,
        cost_estimate=cost(0),
    )(source, row, place, *pinned(base, remote, spread), incoming)


def product_body(count, choices, step, last, turn_ref, start, *refs):
    pieces, refs = refs[:count], refs[count:]
    total = sum(n for n, _, _ in choices)
    weights, (out, left, held, sems) = refs[:total], refs[total:]
    chunk = pieces[0].shape[1]
    left[...] = left_parts(jnp.concatenate([p[...] for p in pieces], axis=1))
    copies = []
    for j in range(held.shape[1] // step):
        lanes = pl.ds(j * step, step)
        blocks, at = [], 0
        for number, c, _ in choices:
            rows = pl.ds(c * chunk, chunk)
            block = weights[at][rows, lanes]
            for k in range(1, number):
                block = jnp.where(turn_ref[0] == k, weights[at + k][rows, lanes], block)
            blocks.append(block)
            at += number
        right = right_parts(jnp.concatenate(blocks, axis=0))
        made = start[:, lanes] + jnp.dot(left[...], right, preferred_element_type=jnp.float32)
        if last:
            held[:, lanes] = made
            copies += start_all([(held.at[:, lanes], out.at[:, lanes])], sems, j)
        else:
            out[:, lanes] = made
    wait_all(copies)


def add_product(turn, start, pieces, weights, last):
    rows, chunk = pieces[0].shape
    width = start.shape[1]
    step = min(2 * LANES, width)
    count = len(pieces)
    flat = [w for group in weights for w, _ in group]
    choices = [(len(group), group[0][1], 0) for group in weights]
    return pl.pallas_call(
        functools.partial(product_body, count, choices, step, last),
        out_shape=hbm(rows, width) if last else f32(rows, width),
        in_specs=[SMEM] + [VMEM] * (1 + count + len(flat)),
        out_specs=HBM if last else VMEM,
        scratch_shapes=[
            pltpu.VMEM((rows, 3 * count * chunk), jnp.bfloat16),
            scratch(rows, width),
            pltpu.SemaphoreType.DMA((width // step,)),
        ],
        compiler_params=PARAMS,
        cost_estimate=cost(6 * count * rows * chunk * width),
    )(turn, start, *pieces, *flat)


def solution(mesh):
    parts = mesh.shape["dom"]
    feats = mesh.shape["feat"]
    sides = 2 if feats % 2 == 0 else 1
    halves = feats // sides
    others = list(range(1, halves))

    def feat_target(f, dh, dl):
        return (f // sides + dh) % halves * sides + (f % sides + dl) % sides

    def feat_send(x, dh, dl):
        return lax.ppermute(x, "feat", [(f, feat_target(f, dh, dl)) for f in range(feats)])

    def dom_exchange(x):
        return lax.all_to_all(x, "dom", split_axis=0, concat_axis=0, tiled=True)

    def per_device(
        features,
        degree,
        diag_adj,
        remote_adj,
        read_block,
        tile_src,
        tile_row,
        w_first,
        b_first,
        w_second,
        b_second,
    ):
        part, cols = features.shape
        tile = diag_adj.shape[1]
        blocks = part // tile
        remote = remote_adj[0]
        chunk = LANES if cols % LANES == 0 else cols
        chunks = cols // chunk
        f = lax.axis_index("feat")
        want, source, row = read_block[0], tile_src[0], tile_row[0]
        shifts = [(dh, dl) for dh in range(halves) for dl in range(sides)]
        place = jnp.stack([jnp.asarray(feat_target(f, dh, dl), jnp.int32) for dh, dl in shifts])
        first = jnp.reshape(jnp.asarray(f * cols, jnp.int32), (1,))
        bias = b_first[None, :]

        x_all = [features] + [feat_send(features, 0, dl) for dl in range(1, sides)]
        w_all = [w_first] + [feat_send(w_first, 0, dl) for dl in range(1, sides)]

        shares = chunks if parts % chunks == 0 else 1
        share = jnp.reshape(jnp.asarray(lax.axis_index("dom") % shares, jnp.int32), (1,))
        share_rows = w_second.shape[0] // shares

        def share_send(x, k):
            pairs = [(s, s // shares * shares + (s % shares + k) % shares) for s in range(parts)]
            return lax.ppermute(x, "dom", pairs)

        w2_sent = row_block(share, w_second, share_rows)
        w2_got = [feat_send(w2_sent, dh, 0) for dh in others]

        scaling = lax.rsqrt(degree.astype(jnp.float32))
        spread = jnp.broadcast_to(scaling[:, None], (part, chunk))
        outgoing = outgoing_blocks(want, features, spread, tile)
        incoming = dom_exchange(outgoing)

        early = blocks * 5 // 12 * tile if chunks > 1 else part
        late = part - early
        marks = sorted({0, early // 2 // tile * tile, early, early + late // 2 // tile * tile, part})
        spans = list(zip(marks[:-1], marks[1:]))
        x_all[0], _ = lax.optimization_barrier((features, outgoing))
        send_steps = []
        for start, stop in spans:
            targets = [(0, 0, start)]
            for c in range(1, chunks):
                if stop <= early:
                    targets.append((c, 0, part + (c - 1) * early + start))
                else:
                    targets.append((c, 1, (c - 1) * late + start - early))
            send_steps.append((start, stop, targets))
        send_shapes = [(part + (chunks - 1) * early, chunk)]
        if late > 0:
            send_shapes.append(((chunks - 1) * late, chunk))
        sends = [partial_sums(place, [(dh * sides, send_steps)], x_all, w_all, send_shapes) for dh in others]
        sends, w2_got = lax.optimization_barrier((sends, w2_got))
        front = [feat_send(x[0], dh, 0) for dh, x in zip(others, sends)]

        own_steps = [(a, b, [(c, c, a) for c in range(chunks)]) for a, b in spans]
        own = list(partial_sums(place, [(0, own_steps)], x_all, w_all, [(part, chunk)] * chunks, HINT))

        w2_groups = [[got] + [share_send(got, k) for k in range(1, shares)] for got in w2_got]
        incoming, own = lax.optimization_barrier((incoming, list(own)))
        w2_core = [w_second] + [feat_send(w_second, 0, dl) for dl in range(1, sides)]
        chosen = chosen_blocks(source, incoming)
        chosen_all = [chosen] + [feat_send(chosen, 0, dl) for dl in range(1, sides)]
        height = chosen.shape[0]
        tail_rows = (chunks - 1) * late
        groups, remote_shapes, passing, carried = [], [], [], []
        for dh, x in zip(others, sends):
            at = len(remote_shapes)
            targets = [(0, at, 0)] + [(c, at + 1, tail_rows + (c - 1) * height) for c in range(1, chunks)]
            groups.append((dh * sides, [(0, height, targets)]))
            remote_shapes.append((height, chunk))
            if chunks > 1:
                remote_shapes.append((tail_rows + (chunks - 1) * height, chunk))
                passing += x[1:]
                carried += [(at + 1, 0)] * len(x[1:])
        at = len(remote_shapes)
        groups.append((0, [(0, height, [(c, at + c, 0) for c in range(chunks)])]))
        remote_shapes += [(height, chunk)] * chunks
        made = partial_sums(place, groups, chosen_all, w_all, remote_shapes, 0, passing, carried)
        each = at // max(len(others), 1)
        remote_front = [feat_send(made[i * each], dh, 0) for i, dh in enumerate(others)]
        rest = [feat_send(made[i * each + 1], dh, 0) for i, dh in enumerate(others)] if chunks > 1 else []
        remote_own = made[at:]

        reach = len(others)
        first_layout = [(h, h, 0, part, 0) for h in range(reach)]
        base = own_part(diag_adj, spread, own[0], front, first_layout, reach)
        collected = []
        outgoing = None
        for c in range(chunks):
            if c == 0:
                outgoing, base_next = hidden_blocks(
                    row, want, first, 0, bias, base, remote, spread, diag_adj, [remote_own[0]] + remote_front
                )
            else:
                begin, _ = lax.optimization_barrier((own[c], outgoing))
                layout = []
                for h in range(reach):
                    layout.append((h, h, part + (c - 1) * early, part + c * early, 0))
                    if late > 0:
                        layout.append((h, reach + h, (c - 1) * late, c * late, early))
                ends = tail_rows + c * height
                remote_sums = [remote_own[c]] + [r if ends == r.shape[0] else r[:ends] for r in rest]
                outgoing, base_next = later_blocks(
                    row,
                    want,
                    first,
                    c * chunk,
                    bias,
                    begin,
                    remote,
                    spread,
                    diag_adj,
                    remote_sums,
                    front + rest,
                    layout,
                    reach,
                )
            incoming = dom_exchange(outgoing)
            if c < chunks - 1:
                incoming = pinned(incoming)[0]
            pieces = feature_pieces(source, row, place, base_next, remote, spread, incoming)
            collected.append(
                [p if dh == 0 and dl == 0 else feat_send(p, dh, dl) for (dh, dl), p in zip(shifts, pieces)]
            )

        w2_groups, _ = lax.optimization_barrier((w2_groups, outgoing))
        w2_far = [[feat_send(w, 0, dl) if dl > 0 else w for w in g] for g in w2_groups for dl in range(sides)]
        out = b_second[None, :]
        for c in range(chunks):
            weights = [[(w, c)] for w in w2_core]
            if shares == 1:
                weights += [[(group[0], c)] for group in w2_far]
            else:
                weights += [[(w, 0) for w in group] for group in w2_far]
            out = add_product((share - c) % shares, out, collected[c], weights, c == chunks - 1)
        return out

    return jax.shard_map(
        per_device,
        mesh=mesh,
        in_specs=(
            P("dom", "feat"),
            P("dom"),
            P("dom", None),
            P("dom", None, None, None),
            P("dom", None),
            P("dom", None),
            P("dom", None),
            P("feat", None),
            P(),
            P("feat", None),
            P(),
        ),
        out_specs=P(("dom", "feat"), None),
        check_vma=False,
    )
```

```python
import functools

import jax
import jax.numpy as jnp
from jax import lax
from jax.experimental import pallas as pl
from jax.experimental.pallas import tpu as pltpu
from jax.sharding import PartitionSpec as P

LANES = 128
TOUCH = 2
HINT = 5 * 10**10
VMEM_LIMIT = 24 * 1024 * 1024
VMEM = pl.BlockSpec(memory_space=pltpu.VMEM)
SMEM = pl.BlockSpec(memory_space=pltpu.SMEM)
HBM = pl.BlockSpec(memory_space=pltpu.HBM)
PARAMS = pltpu.CompilerParams(vmem_limit_bytes=VMEM_LIMIT)


def dot3(a, b):
    return jnp.dot(a, b, precision=lax.Precision.HIGH, preferred_element_type=jnp.float32)


def two_parts(x):
    high = x.astype(jnp.bfloat16)
    return high, (x - high.astype(jnp.float32)).astype(jnp.bfloat16)


def left_parts(x):
    high, low = two_parts(x)
    return jnp.concatenate([high, low, high], axis=1)


def right_parts(w):
    high, low = two_parts(w)
    return jnp.concatenate([high, high, low], axis=0)


def f32(*dims):
    return jax.ShapeDtypeStruct(dims, jnp.float32)


def hbm(*dims):
    return pltpu.HBM(dims, jnp.float32)


def pinned(*arrays):
    return [pltpu.with_memory_space_constraint(a, pltpu.HBM) for a in arrays]


def rows_at(index, height):
    return pl.ds(pl.multiple_of(index * height, height), height)


def scratch(*dims):
    return pltpu.VMEM(dims, jnp.float32)


def start_all(pairs, sems, first):
    copies = [pltpu.make_async_copy(a, b, sems.at[first + i]) for i, (a, b) in enumerate(pairs)]
    for copy in copies:
        copy.start()
    return copies


def wait_all(copies):
    for copy in copies:
        copy.wait()


def cost(flops):
    return pl.CostEstimate(flops=flops, bytes_accessed=0, transcendentals=0)


def slice_body(index_ref, source, out, sems):
    wait_all(start_all([(source.at[rows_at(index_ref[0], out.shape[0])], out)], sems, 0))


def row_block(index, source, height):
    return pl.pallas_call(
        slice_body,
        out_shape=f32(height, source.shape[1]),
        in_specs=[SMEM, HBM],
        out_specs=VMEM,
        scratch_shapes=[pltpu.SemaphoreType.DMA((1,))],
        compiler_params=PARAMS,
        cost_estimate=cost(0),
    )(index, *pinned(source))


def outgoing_body(want_ref, features, spread, blocks, held, sems):
    count, tile, cols = held.shape
    chunk = spread.shape[1]
    last = features.shape[0] // tile - 1
    copies = []
    for d in range(count):
        rows = rows_at(jnp.minimum(want_ref[d], last), tile)
        for c in range(cols // chunk):
            lanes = pl.ds(c * chunk, chunk)
            held[d, :, lanes] = features[rows, lanes] * spread[rows, :]
        copies += start_all([(held.at[d], blocks.at[d])], sems, d)
    wait_all(copies)


def outgoing_blocks(want, features, spread, tile):
    cols = features.shape[1]
    count = want.shape[0]
    return pl.pallas_call(
        outgoing_body,
        out_shape=hbm(count, tile, cols),
        in_specs=[SMEM, VMEM, VMEM],
        out_specs=HBM,
        scratch_shapes=[scratch(count, tile, cols), pltpu.SemaphoreType.DMA((count,))],
        compiler_params=PARAMS,
        cost_estimate=cost(HINT),
    )(want, features, spread)


def partial_body(count, groups, carried, place_ref, *refs):
    lefts, rights, refs = refs[:count], refs[count : 2 * count], refs[2 * count :]
    passing, refs = refs[: len(carried)], refs[len(carried) :]
    held, refs = refs[len(refs) - len(carried) :], refs[: len(refs) - len(carried)]
    outs, (left, right, result, sems) = refs[:-4], refs[-4:]
    cols = lefts[0].shape[1]
    chunk = outs[0].shape[1]
    used = 0
    weights_in, loads, stores = [], [], []
    for n, (at, _) in enumerate(groups):
        lanes = pl.ds(pl.multiple_of(place_ref[at] * cols, cols), cols)
        weights_in.append(start_all([(w.at[:, lanes], right.at[n, j]) for j, w in enumerate(rights)], sems, used))
        used += count
    for start, stop, _ in groups[0][1]:
        rows = pl.ds(start, stop - start)
        pairs = [(x.at[rows], left.at[rows, pl.ds(j * cols, cols)]) for j, x in enumerate(lefts)]
        loads.append(start_all(pairs, sems, used))
        used += count
    passed = start_all(list(zip(passing, held)), sems, used)
    used += len(carried)
    for n, (_, steps) in enumerate(groups):
        wait_all(weights_in[n])
        weight = right_parts(jnp.concatenate([right[n, j] for j in range(count)], axis=0))
        for i, (start, stop, targets) in enumerate(steps):
            if n == 0:
                wait_all(loads[i])
            rows = pl.ds(start, stop - start)
            result[n, rows, :] = jnp.dot(left_parts(left[rows, :]), weight, preferred_element_type=jnp.float32)
            pairs = [
                (result.at[n, rows, pl.ds(c * chunk, chunk)], outs[o].at[pl.ds(offset, stop - start)])
                for c, o, offset in targets
            ]
            stores += start_all(pairs, sems, used)
            used += len(pairs)
    wait_all(passed)
    pairs = [(h, outs[o].at[pl.ds(offset, h.shape[0])]) for h, (o, offset) in zip(held, carried)]
    stores += start_all(pairs, sems, used)
    wait_all(stores)


def partial_sums(place, groups, lefts, weights, shapes, flops=0, passing=(), carried=()):
    rows, cols = lefts[0].shape
    depth = weights[0].shape[0]
    count = len(lefts)
    copies = count * (len(groups) + len(groups[0][1])) + 2 * len(carried)
    copies += sum(len(targets) for _, steps in groups for _, _, targets in steps)
    return pl.pallas_call(
        functools.partial(partial_body, count, groups, carried),
        out_shape=[hbm(*s) for s in shapes],
        in_specs=[SMEM] + [HBM] * (2 * count + len(passing)),
        out_specs=[HBM] * len(shapes),
        scratch_shapes=[
            scratch(rows, count * cols),
            scratch(len(groups), count, depth, cols),
            scratch(len(groups), rows, cols),
            pltpu.SemaphoreType.DMA((copies,)),
        ]
        + [scratch(*p.shape) for p in passing],
        compiler_params=PARAMS,
        cost_estimate=cost(flops),
    )(place, *pinned(lefts[0]), *lefts[1:], *pinned(weights[0]), *weights[1:], *pinned(*passing))


def chosen_body(source_ref, incoming, chosen):
    tile = incoming.shape[1]
    for g in range(chosen.shape[0] // tile):
        chosen[pl.ds(g * tile, tile), :] = incoming[source_ref[TOUCH * g]]


def chosen_blocks(source, incoming):
    tile, cols = incoming.shape[1:]
    groups = source.shape[0] // TOUCH
    return pl.pallas_call(
        chosen_body,
        out_shape=f32(groups * tile, cols),
        in_specs=[SMEM, VMEM],
        out_specs=VMEM,
        compiler_params=PARAMS,
        cost_estimate=cost(0),
    )(source, incoming)


def received_pairs(layout, received, recv_in):
    return [
        (received[r].at[pl.ds(start, stop - start)], recv_in.at[h, pl.ds(offset, stop - start)])
        for h, r, start, stop, offset in layout
    ]


def own_total(diag_in, spread_in, own_in, recv_in, total):
    tile = diag_in.shape[1]
    for i in range(diag_in.shape[0] // tile):
        rows = pl.ds(i * tile, tile)
        mixed = own_in[rows, :]
        for h in range(recv_in.shape[0]):
            mixed = mixed + recv_in[h, rows, :]
        total[rows, :] = dot3(diag_in[rows, :], mixed * spread_in[rows, :])


def own_body(layout, diag, spread, own, *refs):
    received, (base, diag_in, spread_in, own_in, recv_in, sems) = refs[:-6], refs[-6:]
    pairs = [(diag, diag_in), (spread, spread_in), (own, own_in)]
    wait_all(start_all(pairs + received_pairs(layout, received, recv_in), sems, 0))
    own_total(diag_in, spread_in, own_in, recv_in, base)


def own_part(diag, spread, own, received, layout, others):
    return pl.pallas_call(
        functools.partial(own_body, layout),
        out_shape=f32(*own.shape),
        in_specs=[HBM] * (3 + len(received)),
        out_specs=VMEM,
        scratch_shapes=[scratch(*a.shape) for a in (diag, spread, own)]
        + [scratch(others, *own.shape), pltpu.SemaphoreType.DMA((3 + len(layout),))],
        compiler_params=PARAMS,
        cost_estimate=cost(0),
    )(*pinned(diag, spread, own), *received)


def hidden_tail(
    lane_offset, row_ref, want_ref, first_ref, bias, remote, spread, diag, sums, blocks, base_out, total, scaled, sems, used
):
    tiles, tile = remote.shape[:2]
    parts = blocks.shape[0]
    chunk = total.shape[1]
    for g in range(tiles // TOUCH):
        block = sums[0][pl.ds(g * tile, tile), :]
        for x in sums[1:]:
            block = block + x[pl.ds(g * tile, tile), :]
        for k in range(TOUCH * g, TOUCH * g + TOUCH):
            total[rows_at(row_ref[k], tile), :] += dot3(remote[k], block)
    lanes = pl.ds(pl.multiple_of(first_ref[0] + lane_offset, chunk), chunk)
    scaled[...] = jnp.maximum(total[...] * spread[...] + bias[:, lanes], 0.0) * spread[...]
    last = scaled.shape[0] // tile - 1
    copies = start_all(
        [(scaled.at[rows_at(jnp.minimum(want_ref[d], last), tile)], blocks.at[d]) for d in range(parts)],
        sems,
        used,
    )
    for i in range(last + 1):
        rows = pl.ds(i * tile, tile)
        total[rows, :] = dot3(diag[rows, :], scaled[rows, :])
    copies += start_all([(total, base_out)], sems, used + parts)
    wait_all(copies)


def hidden_body(lane_offset, row_ref, want_ref, first_ref, bias, base, remote, spread, diag, *refs):
    sums, (blocks, base_out, total, scaled, sems) = refs[:-5], refs[-5:]
    total[...] = base[...]
    hidden_tail(
        lane_offset, row_ref, want_ref, first_ref, bias, remote, spread, diag, sums, blocks, base_out, total, scaled, sems, 0
    )


def hidden_blocks(row, want, first, lane_offset, bias, base, remote, spread, diag, remote_sums):
    rows, chunk = base.shape
    tile = diag.shape[1]
    parts = want.shape[0]
    return pl.pallas_call(
        functools.partial(hidden_body, lane_offset),
        out_shape=[hbm(parts, tile, chunk), hbm(rows, chunk)],
        in_specs=[SMEM] * 3 + [VMEM] * (5 + len(remote_sums)),
        out_specs=[HBM, HBM],
        scratch_shapes=[scratch(rows, chunk), scratch(rows, chunk), pltpu.SemaphoreType.DMA((parts + 1,))],
        compiler_params=PARAMS,
        cost_estimate=cost(HINT),
    )(row, want, first, bias, base, remote, spread, diag, *remote_sums)


def later_body(
    count, layout, lane_offset, row_ref, want_ref, first_ref, bias, own, remote, spread, diag, *refs
):
    remote_sums, refs = refs[:count], refs[count:]
    received, refs = refs[:-10], refs[-10:]
    blocks, base_out, total, remote_in, spread_in, diag_in, scaled, sums_in, recv_in, sems = refs
    height = sums_in.shape[1]
    pairs = [(own, scaled), (spread, spread_in), (diag, diag_in)]
    pairs += received_pairs(layout, received, recv_in)
    late = [(remote, remote_in)]
    late += [(s.at[pl.ds(s.shape[0] - height, height)], sums_in.at[j]) for j, s in enumerate(remote_sums)]
    first = start_all(pairs, sems, 0)
    tail = start_all(late, sems, len(pairs))
    wait_all(first)
    own_total(diag_in, spread_in, scaled, recv_in, total)
    wait_all(tail)
    sums = [sums_in.at[j] for j in range(count)]
    hidden_tail(
        lane_offset,
        row_ref,
        want_ref,
        first_ref,
        bias,
        remote_in,
        spread_in,
        diag_in,
        sums,
        blocks,
        base_out,
        total,
        scaled,
        sems,
        len(pairs) + len(late),
    )


def later_blocks(
    row, want, first, lane_offset, bias, own, remote, spread, diag, remote_sums, received, layout, others
):
    rows, chunk = own.shape
    tile = diag.shape[1]
    parts = want.shape[0]
    count = len(remote_sums)
    height = remote.shape[0] // TOUCH * tile
    return pl.pallas_call(
        functools.partial(later_body, count, layout, lane_offset),
        out_shape=[hbm(parts, tile, chunk), hbm(rows, chunk)],
        in_specs=[SMEM] * 3 + [VMEM] + [HBM] * (4 + count + len(received)),
        out_specs=[HBM, HBM],
        scratch_shapes=[scratch(*a.shape) for a in (own, remote, spread, diag, own)]
        + [scratch(count, height, chunk), scratch(others, *own.shape)]
        + [pltpu.SemaphoreType.DMA((5 + len(layout) + count + parts,))],
        compiler_params=PARAMS,
        cost_estimate=cost(HINT),
    )(row, want, first, bias, *pinned(own, remote, spread, diag, remote_sums[0]), *remote_sums[1:], *received)


def pieces_body(stored, source_ref, row_ref, place_ref, base, remote, spread, incoming, *refs):
    pieces, (total, remote_in, spread_in, incoming_in, sems) = refs[:-5], refs[-5:]
    tiles, tile = remote.shape[:2]
    early = start_all(
        [(incoming, incoming_in), (remote, remote_in), (base, total), (spread, spread_in)], sems, 0
    )
    wait_all(early[:3])
    for k in range(tiles):
        total[rows_at(row_ref[k], tile), :] += dot3(remote_in[k], incoming_in[source_ref[k]])
    wait_all(early[3:])
    height = pieces[0].shape[0]
    copies = []
    for j in reversed(range(len(pieces))):
        rows = rows_at(place_ref[j], height)
        made = total[rows, :] * spread_in[rows, :]
        if stored:
            total[rows, :] = made
            copies += start_all([(total.at[rows], pieces[j])], sems, 4 + j)
        else:
            pieces[j][...] = made
    wait_all(copies)


def feature_pieces(source, row, place, base, remote, spread, incoming, stored):
    rows, chunk = base.shape
    feats = place.shape[0]
    make = hbm if stored else f32
    return pl.pallas_call(
        functools.partial(pieces_body, stored),
        out_shape=[make(rows // feats, chunk)] * feats,
        in_specs=[SMEM] * 3 + [HBM] * 4,
        out_specs=[HBM if stored else VMEM] * feats,
        scratch_shapes=[scratch(*a.shape) for a in (base, remote, spread, incoming)]
        + [pltpu.SemaphoreType.DMA((4 + feats,))],
        compiler_params=PARAMS,
        cost_estimate=cost(0),
    )(source, row, place, *pinned(base, remote, spread), incoming)


def product_body(count, choices, step, last, turn_ref, start, *refs):
    pieces, refs = refs[:count], refs[count:]
    total = sum(n for n, _, _ in choices)
    weights, (out, left, held, sems) = refs[:total], refs[total:]
    chunk = pieces[0].shape[1]
    left[...] = left_parts(jnp.concatenate([p[...] for p in pieces], axis=1))
    copies = []
    for j in range(held.shape[1] // step):
        lanes = pl.ds(j * step, step)
        blocks, at = [], 0
        for number, c, _ in choices:
            rows = pl.ds(c * chunk, chunk)
            block = weights[at][rows, lanes]
            for k in range(1, number):
                block = jnp.where(turn_ref[0] == k, weights[at + k][rows, lanes], block)
            blocks.append(block)
            at += number
        right = right_parts(jnp.concatenate(blocks, axis=0))
        made = start[:, lanes] + jnp.dot(left[...], right, preferred_element_type=jnp.float32)
        if last:
            held[:, lanes] = made
            copies += start_all([(held.at[:, lanes], out.at[:, lanes])], sems, j)
        else:
            out[:, lanes] = made
    wait_all(copies)


def add_product(turn, start, pieces, weights, last):
    rows, chunk = pieces[0].shape
    width = start.shape[1]
    step = min(2 * LANES, width)
    count = len(pieces)
    flat = [w for group in weights for w, _ in group]
    choices = [(len(group), group[0][1], 0) for group in weights]
    return pl.pallas_call(
        functools.partial(product_body, count, choices, step, last),
        out_shape=hbm(rows, width) if last else f32(rows, width),
        in_specs=[SMEM] + [VMEM] * (1 + count + len(flat)),
        out_specs=HBM if last else VMEM,
        scratch_shapes=[
            pltpu.VMEM((rows, 3 * count * chunk), jnp.bfloat16),
            scratch(rows, width),
            pltpu.SemaphoreType.DMA((width // step,)),
        ],
        compiler_params=PARAMS,
        cost_estimate=cost(6 * count * rows * chunk * width),
    )(turn, start, *pieces, *flat)


def solution(mesh):
    parts = mesh.shape["dom"]
    feats = mesh.shape["feat"]
    sides = 2 if feats % 2 == 0 else 1
    halves = feats // sides
    others = list(range(1, halves))

    def feat_target(f, dh, dl):
        return (f // sides + dh) % halves * sides + (f % sides + dl) % sides

    def feat_send(x, dh, dl):
        return lax.ppermute(x, "feat", [(f, feat_target(f, dh, dl)) for f in range(feats)])

    def dom_exchange(x):
        return lax.all_to_all(x, "dom", split_axis=0, concat_axis=0, tiled=True)

    def per_device(
        features,
        degree,
        diag_adj,
        remote_adj,
        read_block,
        tile_src,
        tile_row,
        w_first,
        b_first,
        w_second,
        b_second,
    ):
        part, cols = features.shape
        tile = diag_adj.shape[1]
        blocks = part // tile
        remote = remote_adj[0]
        chunk = LANES if cols % LANES == 0 else cols
        chunks = cols // chunk
        f = lax.axis_index("feat")
        want, source, row = read_block[0], tile_src[0], tile_row[0]
        shifts = [(dh, dl) for dh in range(halves) for dl in range(sides)]
        place = jnp.stack([jnp.asarray(feat_target(f, dh, dl), jnp.int32) for dh, dl in shifts])
        first = jnp.reshape(jnp.asarray(f * cols, jnp.int32), (1,))
        bias = b_first[None, :]

        x_all = [features] + [feat_send(features, 0, dl) for dl in range(1, sides)]
        w_all = [w_first] + [feat_send(w_first, 0, dl) for dl in range(1, sides)]

        shares = chunks if parts % chunks == 0 else 1
        share = jnp.reshape(jnp.asarray(lax.axis_index("dom") % shares, jnp.int32), (1,))
        share_rows = w_second.shape[0] // shares

        def share_send(x, k):
            pairs = [(s, s // shares * shares + (s % shares + k) % shares) for s in range(parts)]
            return lax.ppermute(x, "dom", pairs)

        w2_sent = row_block(share, w_second, share_rows)
        w2_got = [feat_send(w2_sent, dh, 0) for dh in others]

        scaling = lax.rsqrt(degree.astype(jnp.float32))
        spread = jnp.broadcast_to(scaling[:, None], (part, chunk))
        outgoing = outgoing_blocks(want, features, spread, tile)
        incoming = dom_exchange(outgoing)

        early = blocks // 3 * tile if chunks > 1 else part
        late = part - early
        marks = sorted({0, early // 2 // tile * tile, early, early + late // 2 // tile * tile, part})
        spans = list(zip(marks[:-1], marks[1:]))
        x_all[0], _ = lax.optimization_barrier((features, outgoing))
        send_steps = []
        for start, stop in spans:
            targets = [(0, 0, start)]
            for c in range(1, chunks):
                if stop <= early:
                    targets.append((c, 0, part + (c - 1) * early + start))
                else:
                    targets.append((c, 1, (c - 1) * late + start - early))
            send_steps.append((start, stop, targets))
        send_shapes = [(part + (chunks - 1) * early, chunk)]
        if late > 0:
            send_shapes.append(((chunks - 1) * late, chunk))
        sends = [partial_sums(place, [(dh * sides, send_steps)], x_all, w_all, send_shapes) for dh in others]
        sends, w2_got = lax.optimization_barrier((sends, w2_got))
        front = [feat_send(x[0], dh, 0) for dh, x in zip(others, sends)]

        own_steps = [(a, b, [(c, c, a) for c in range(chunks)]) for a, b in spans]
        own = list(partial_sums(place, [(0, own_steps)], x_all, w_all, [(part, chunk)] * chunks, HINT))

        incoming, own = lax.optimization_barrier((incoming, list(own)))
        w2_core = [w_second] + [feat_send(w_second, 0, dl) for dl in range(1, sides)]
        chosen = chosen_blocks(source, incoming)
        chosen_all = [chosen] + [feat_send(chosen, 0, dl) for dl in range(1, sides)]
        height = chosen.shape[0]
        tail_rows = (chunks - 1) * late
        groups, remote_shapes, passing, carried = [], [], [], []
        for dh, x in zip(others, sends):
            at = len(remote_shapes)
            targets = [(0, at, 0)] + [(c, at + 1, tail_rows + (c - 1) * height) for c in range(1, chunks)]
            groups.append((dh * sides, [(0, height, targets)]))
            remote_shapes.append((height, chunk))
            if chunks > 1:
                remote_shapes.append((tail_rows + (chunks - 1) * height, chunk))
                passing += x[1:]
                carried += [(at + 1, 0)] * len(x[1:])
        at = len(remote_shapes)
        groups.append((0, [(0, height, [(c, at + c, 0) for c in range(chunks)])]))
        remote_shapes += [(height, chunk)] * chunks
        made = partial_sums(place, groups, chosen_all, w_all, remote_shapes, 0, passing, carried)
        each = at // max(len(others), 1)
        remote_front = [feat_send(made[i * each], dh, 0) for i, dh in enumerate(others)]
        rest = [feat_send(made[i * each + 1], dh, 0) for i, dh in enumerate(others)] if chunks > 1 else []
        remote_own = made[at:]

        reach = len(others)
        first_layout = [(h, h, 0, part, 0) for h in range(reach)]
        base = own_part(diag_adj, spread, own[0], front, first_layout, reach)
        collected = []
        outgoing = None
        for c in range(chunks):
            if c == 0:
                outgoing, base_next = hidden_blocks(
                    row, want, first, 0, bias, base, remote, spread, diag_adj, [remote_own[0]] + remote_front
                )
            else:
                begin, _ = lax.optimization_barrier((own[c], outgoing))
                layout = []
                for h in range(reach):
                    layout.append((h, h, part + (c - 1) * early, part + c * early, 0))
                    if late > 0:
                        layout.append((h, reach + h, (c - 1) * late, c * late, early))
                ends = tail_rows + c * height
                remote_sums = [remote_own[c]] + [r if ends == r.shape[0] else r[:ends] for r in rest]
                outgoing, base_next = later_blocks(
                    row,
                    want,
                    first,
                    c * chunk,
                    bias,
                    begin,
                    remote,
                    spread,
                    diag_adj,
                    remote_sums,
                    front + rest,
                    layout,
                    reach,
                )
            incoming = dom_exchange(outgoing)
            if c < chunks - 1:
                incoming = pinned(incoming)[0]
            pieces = feature_pieces(source, row, place, base_next, remote, spread, incoming, c < chunks - 1)
            if c == 0:
                w2_got, _ = lax.optimization_barrier((w2_got, pieces))
            collected.append(
                [p if dh == 0 and dl == 0 else feat_send(p, dh, dl) for (dh, dl), p in zip(shifts, pieces)]
            )

        w2_groups = [[got] + [share_send(got, k) for k in range(1, shares)] for got in w2_got]
        w2_far = [[feat_send(w, 0, dl) if dl > 0 else w for w in g] for g in w2_groups for dl in range(sides)]
        out = b_second[None, :]
        for c in range(chunks):
            weights = [[(w, c)] for w in w2_core]
            if shares == 1:
                weights += [[(group[0], c)] for group in w2_far]
            else:
                weights += [[(w, 0) for w in group] for group in w2_far]
            turn = (share - c) % shares
            if c < chunks - 1 or halves == 1:
                out = add_product(turn, out, collected[c], weights, c == chunks - 1)
            else:
                out = add_product(turn, out, collected[c][:sides], weights[:sides], False)
                out = add_product(turn, out, collected[c][sides:], weights[sides:], True)
        return out

    return jax.shard_map(
        per_device,
        mesh=mesh,
        in_specs=(
            P("dom", "feat"),
            P("dom"),
            P("dom", None),
            P("dom", None, None, None),
            P("dom", None),
            P("dom", None),
            P("dom", None),
            P("feat", None),
            P(),
            P("feat", None),
            P(),
        ),
        out_specs=P(("dom", "feat"), None),
        check_vma=False,
    )
```

```python
import functools

import jax
import jax.numpy as jnp
from jax import lax
from jax.experimental import pallas as pl
from jax.experimental.pallas import tpu as pltpu
from jax.sharding import PartitionSpec as P

LANES = 128
TOUCH = 2
HINT = 5 * 10**10
VMEM_LIMIT = 24 * 1024 * 1024
VMEM = pl.BlockSpec(memory_space=pltpu.VMEM)
SMEM = pl.BlockSpec(memory_space=pltpu.SMEM)
HBM = pl.BlockSpec(memory_space=pltpu.HBM)
PARAMS = pltpu.CompilerParams(vmem_limit_bytes=VMEM_LIMIT)


def dot3(a, b):
    return jnp.dot(a, b, precision=lax.Precision.HIGH, preferred_element_type=jnp.float32)


def two_parts(x):
    high = x.astype(jnp.bfloat16)
    return high, (x - high.astype(jnp.float32)).astype(jnp.bfloat16)


def left_parts(x):
    high, low = two_parts(x)
    return jnp.concatenate([high, low, high], axis=1)


def right_parts(w):
    high, low = two_parts(w)
    return jnp.concatenate([high, high, low], axis=0)


def f32(*dims):
    return jax.ShapeDtypeStruct(dims, jnp.float32)


def hbm(*dims):
    return pltpu.HBM(dims, jnp.float32)


def pinned(*arrays):
    return [pltpu.with_memory_space_constraint(a, pltpu.HBM) for a in arrays]


def rows_at(index, height):
    return pl.ds(pl.multiple_of(index * height, height), height)


def scratch(*dims):
    return pltpu.VMEM(dims, jnp.float32)


def start_all(pairs, sems, first):
    copies = [pltpu.make_async_copy(a, b, sems.at[first + i]) for i, (a, b) in enumerate(pairs)]
    for copy in copies:
        copy.start()
    return copies


def wait_all(copies):
    for copy in copies:
        copy.wait()


def cost(flops):
    return pl.CostEstimate(flops=flops, bytes_accessed=0, transcendentals=0)


def slice_body(index_ref, source, out, sems):
    wait_all(start_all([(source.at[rows_at(index_ref[0], out.shape[0])], out)], sems, 0))


def row_block(index, source, height):
    return pl.pallas_call(
        slice_body,
        out_shape=f32(height, source.shape[1]),
        in_specs=[SMEM, HBM],
        out_specs=VMEM,
        scratch_shapes=[pltpu.SemaphoreType.DMA((1,))],
        compiler_params=PARAMS,
        cost_estimate=cost(0),
    )(index, *pinned(source))


def outgoing_body(want_ref, features, spread, blocks, held, sems):
    count, tile, cols = held.shape
    chunk = spread.shape[1]
    last = features.shape[0] // tile - 1
    copies = []
    for d in range(count):
        rows = rows_at(jnp.minimum(want_ref[d], last), tile)
        for c in range(cols // chunk):
            lanes = pl.ds(c * chunk, chunk)
            held[d, :, lanes] = features[rows, lanes] * spread[rows, :]
        copies += start_all([(held.at[d], blocks.at[d])], sems, d)
    wait_all(copies)


def outgoing_blocks(want, features, spread, tile):
    cols = features.shape[1]
    count = want.shape[0]
    return pl.pallas_call(
        outgoing_body,
        out_shape=hbm(count, tile, cols),
        in_specs=[SMEM, VMEM, VMEM],
        out_specs=HBM,
        scratch_shapes=[scratch(count, tile, cols), pltpu.SemaphoreType.DMA((count,))],
        compiler_params=PARAMS,
        cost_estimate=cost(HINT),
    )(want, features, spread)


def partial_body(count, groups, carried, place_ref, *refs):
    lefts, rights, refs = refs[:count], refs[count : 2 * count], refs[2 * count :]
    passing, refs = refs[: len(carried)], refs[len(carried) :]
    held, refs = refs[len(refs) - len(carried) :], refs[: len(refs) - len(carried)]
    outs, (left, right, result, sems) = refs[:-4], refs[-4:]
    cols = lefts[0].shape[1]
    chunk = outs[0].shape[1]
    used = 0
    weights_in, loads, stores = [], [], []
    for n, (at, _) in enumerate(groups):
        lanes = pl.ds(pl.multiple_of(place_ref[at] * cols, cols), cols)
        weights_in.append(start_all([(w.at[:, lanes], right.at[n, j]) for j, w in enumerate(rights)], sems, used))
        used += count
    for start, stop, _ in groups[0][1]:
        rows = pl.ds(start, stop - start)
        pairs = [(x.at[rows], left.at[rows, pl.ds(j * cols, cols)]) for j, x in enumerate(lefts)]
        loads.append(start_all(pairs, sems, used))
        used += count
    passed = start_all(list(zip(passing, held)), sems, used)
    used += len(carried)
    for n, (_, steps) in enumerate(groups):
        wait_all(weights_in[n])
        weight = right_parts(jnp.concatenate([right[n, j] for j in range(count)], axis=0))
        for i, (start, stop, targets) in enumerate(steps):
            if n == 0:
                wait_all(loads[i])
            rows = pl.ds(start, stop - start)
            result[n, rows, :] = jnp.dot(left_parts(left[rows, :]), weight, preferred_element_type=jnp.float32)
            pairs = [
                (result.at[n, rows, pl.ds(c * chunk, chunk)], outs[o].at[pl.ds(offset, stop - start)])
                for c, o, offset in targets
            ]
            stores += start_all(pairs, sems, used)
            used += len(pairs)
    wait_all(passed)
    pairs = [(h, outs[o].at[pl.ds(offset, h.shape[0])]) for h, (o, offset) in zip(held, carried)]
    stores += start_all(pairs, sems, used)
    wait_all(stores)


def partial_sums(place, groups, lefts, weights, shapes, flops=0, passing=(), carried=()):
    rows, cols = lefts[0].shape
    depth = weights[0].shape[0]
    count = len(lefts)
    copies = count * (len(groups) + len(groups[0][1])) + 2 * len(carried)
    copies += sum(len(targets) for _, steps in groups for _, _, targets in steps)
    return pl.pallas_call(
        functools.partial(partial_body, count, groups, carried),
        out_shape=[hbm(*s) for s in shapes],
        in_specs=[SMEM] + [HBM] * (2 * count + len(passing)),
        out_specs=[HBM] * len(shapes),
        scratch_shapes=[
            scratch(rows, count * cols),
            scratch(len(groups), count, depth, cols),
            scratch(len(groups), rows, cols),
            pltpu.SemaphoreType.DMA((copies,)),
        ]
        + [scratch(*p.shape) for p in passing],
        compiler_params=PARAMS,
        cost_estimate=cost(flops),
    )(place, *pinned(lefts[0]), *lefts[1:], *pinned(weights[0]), *weights[1:], *pinned(*passing))


def chosen_body(source_ref, incoming, chosen):
    tile = incoming.shape[1]
    for g in range(chosen.shape[0] // tile):
        chosen[pl.ds(g * tile, tile), :] = incoming[source_ref[TOUCH * g]]


def chosen_blocks(source, incoming):
    tile, cols = incoming.shape[1:]
    groups = source.shape[0] // TOUCH
    return pl.pallas_call(
        chosen_body,
        out_shape=f32(groups * tile, cols),
        in_specs=[SMEM, VMEM],
        out_specs=VMEM,
        compiler_params=PARAMS,
        cost_estimate=cost(0),
    )(source, incoming)


def received_pairs(layout, received, recv_in):
    return [
        (received[r].at[pl.ds(start, stop - start)], recv_in.at[h, pl.ds(offset, stop - start)])
        for h, r, start, stop, offset in layout
    ]


def own_total(diag_in, spread_in, own_in, recv_in, total):
    tile = diag_in.shape[1]
    for i in range(diag_in.shape[0] // tile):
        rows = pl.ds(i * tile, tile)
        mixed = own_in[rows, :]
        for h in range(recv_in.shape[0]):
            mixed = mixed + recv_in[h, rows, :]
        total[rows, :] = dot3(diag_in[rows, :], mixed * spread_in[rows, :])


def own_body(layout, diag, spread, own, *refs):
    received, (base, diag_in, spread_in, own_in, recv_in, sems) = refs[:-6], refs[-6:]
    pairs = [(diag, diag_in), (spread, spread_in), (own, own_in)]
    wait_all(start_all(pairs + received_pairs(layout, received, recv_in), sems, 0))
    own_total(diag_in, spread_in, own_in, recv_in, base)


def own_part(diag, spread, own, received, layout, others):
    return pl.pallas_call(
        functools.partial(own_body, layout),
        out_shape=f32(*own.shape),
        in_specs=[HBM] * (3 + len(received)),
        out_specs=VMEM,
        scratch_shapes=[scratch(*a.shape) for a in (diag, spread, own)]
        + [scratch(others, *own.shape), pltpu.SemaphoreType.DMA((3 + len(layout),))],
        compiler_params=PARAMS,
        cost_estimate=cost(0),
    )(*pinned(diag, spread, own), *received)


def hidden_tail(
    lane_offset, row_ref, want_ref, first_ref, bias, remote, spread, diag, sums, blocks, base_out, total, scaled, sems, used
):
    tiles, tile = remote.shape[:2]
    parts = blocks.shape[0]
    chunk = total.shape[1]
    for g in range(tiles // TOUCH):
        block = sums[0][pl.ds(g * tile, tile), :]
        for x in sums[1:]:
            block = block + x[pl.ds(g * tile, tile), :]
        for k in range(TOUCH * g, TOUCH * g + TOUCH):
            total[rows_at(row_ref[k], tile), :] += dot3(remote[k], block)
    lanes = pl.ds(pl.multiple_of(first_ref[0] + lane_offset, chunk), chunk)
    scaled[...] = jnp.maximum(total[...] * spread[...] + bias[:, lanes], 0.0) * spread[...]
    last = scaled.shape[0] // tile - 1
    copies = start_all(
        [(scaled.at[rows_at(jnp.minimum(want_ref[d], last), tile)], blocks.at[d]) for d in range(parts)],
        sems,
        used,
    )
    for i in range(last + 1):
        rows = pl.ds(i * tile, tile)
        total[rows, :] = dot3(diag[rows, :], scaled[rows, :])
    copies += start_all([(total, base_out)], sems, used + parts)
    wait_all(copies)


def hidden_body(lane_offset, row_ref, want_ref, first_ref, bias, base, remote, spread, diag, *refs):
    sums, (blocks, base_out, total, scaled, sems) = refs[:-5], refs[-5:]
    total[...] = base[...]
    hidden_tail(
        lane_offset, row_ref, want_ref, first_ref, bias, remote, spread, diag, sums, blocks, base_out, total, scaled, sems, 0
    )


def hidden_blocks(row, want, first, lane_offset, bias, base, remote, spread, diag, remote_sums):
    rows, chunk = base.shape
    tile = diag.shape[1]
    parts = want.shape[0]
    return pl.pallas_call(
        functools.partial(hidden_body, lane_offset),
        out_shape=[hbm(parts, tile, chunk), hbm(rows, chunk)],
        in_specs=[SMEM] * 3 + [VMEM] * (5 + len(remote_sums)),
        out_specs=[HBM, HBM],
        scratch_shapes=[scratch(rows, chunk), scratch(rows, chunk), pltpu.SemaphoreType.DMA((parts + 1,))],
        compiler_params=PARAMS,
        cost_estimate=cost(HINT),
    )(row, want, first, bias, base, remote, spread, diag, *remote_sums)


def later_body(
    count, layout, lane_offset, row_ref, want_ref, first_ref, bias, own, remote, spread, diag, *refs
):
    remote_sums, refs = refs[:count], refs[count:]
    received, refs = refs[:-10], refs[-10:]
    blocks, base_out, total, remote_in, spread_in, diag_in, scaled, sums_in, recv_in, sems = refs
    height = sums_in.shape[1]
    pairs = [(own, scaled), (spread, spread_in), (diag, diag_in)]
    pairs += received_pairs(layout, received, recv_in)
    late = [(remote, remote_in)]
    late += [(s.at[pl.ds(s.shape[0] - height, height)], sums_in.at[j]) for j, s in enumerate(remote_sums)]
    first = start_all(pairs, sems, 0)
    tail = start_all(late, sems, len(pairs))
    wait_all(first)
    own_total(diag_in, spread_in, scaled, recv_in, total)
    wait_all(tail)
    sums = [sums_in.at[j] for j in range(count)]
    hidden_tail(
        lane_offset,
        row_ref,
        want_ref,
        first_ref,
        bias,
        remote_in,
        spread_in,
        diag_in,
        sums,
        blocks,
        base_out,
        total,
        scaled,
        sems,
        len(pairs) + len(late),
    )


def later_blocks(
    row, want, first, lane_offset, bias, own, remote, spread, diag, remote_sums, received, layout, others
):
    rows, chunk = own.shape
    tile = diag.shape[1]
    parts = want.shape[0]
    count = len(remote_sums)
    height = remote.shape[0] // TOUCH * tile
    return pl.pallas_call(
        functools.partial(later_body, count, layout, lane_offset),
        out_shape=[hbm(parts, tile, chunk), hbm(rows, chunk)],
        in_specs=[SMEM] * 3 + [VMEM] + [HBM] * (4 + count + len(received)),
        out_specs=[HBM, HBM],
        scratch_shapes=[scratch(*a.shape) for a in (own, remote, spread, diag, own)]
        + [scratch(count, height, chunk), scratch(others, *own.shape)]
        + [pltpu.SemaphoreType.DMA((5 + len(layout) + count + parts,))],
        compiler_params=PARAMS,
        cost_estimate=cost(HINT),
    )(row, want, first, bias, *pinned(own, remote, spread, diag, remote_sums[0]), *remote_sums[1:], *received)


def pieces_body(stored, source_ref, row_ref, place_ref, base, remote, spread, incoming, *refs):
    pieces, (total, remote_in, spread_in, incoming_in, sems) = refs[:-5], refs[-5:]
    tiles, tile = remote.shape[:2]
    early = start_all(
        [(incoming, incoming_in), (remote, remote_in), (base, total), (spread, spread_in)], sems, 0
    )
    wait_all(early[:3])
    for k in range(tiles):
        total[rows_at(row_ref[k], tile), :] += dot3(remote_in[k], incoming_in[source_ref[k]])
    wait_all(early[3:])
    height = pieces[0].shape[0]
    copies = []
    for j in reversed(range(len(pieces))):
        rows = rows_at(place_ref[j], height)
        made = total[rows, :] * spread_in[rows, :]
        if stored:
            total[rows, :] = made
            copies += start_all([(total.at[rows], pieces[j])], sems, 4 + j)
        else:
            pieces[j][...] = made
    wait_all(copies)


def feature_pieces(source, row, place, base, remote, spread, incoming, stored):
    rows, chunk = base.shape
    feats = place.shape[0]
    make = hbm if stored else f32
    return pl.pallas_call(
        functools.partial(pieces_body, stored),
        out_shape=[make(rows // feats, chunk)] * feats,
        in_specs=[SMEM] * 3 + [HBM] * 4,
        out_specs=[HBM if stored else VMEM] * feats,
        scratch_shapes=[scratch(*a.shape) for a in (base, remote, spread, incoming)]
        + [pltpu.SemaphoreType.DMA((4 + feats,))],
        compiler_params=PARAMS,
        cost_estimate=cost(0),
    )(source, row, place, *pinned(base, remote, spread), incoming)


def in_order_body(count, share_ref, *refs):
    parts, out = refs[:count], refs[count]
    for k, x in enumerate(parts):
        out[rows_at(lax.rem(share_ref[0] + count - k, count), x.shape[0]), :] = x[...]


def in_order(share, parts):
    count = len(parts)
    if count == 1:
        return parts[0]
    rows, cols = parts[0].shape
    return pl.pallas_call(
        functools.partial(in_order_body, count),
        out_shape=f32(count * rows, cols),
        in_specs=[SMEM] + [VMEM] * count,
        out_specs=VMEM,
        compiler_params=PARAMS,
        cost_estimate=cost(0),
    )(share, *parts)


def product_body(count, c, step, last, start, *refs):
    pieces, weights, (out, left, held, sems) = refs[:count], refs[count : 2 * count], refs[2 * count :]
    rows = pl.ds(c * pieces[0].shape[1], pieces[0].shape[1])
    left[...] = left_parts(jnp.concatenate([p[...] for p in pieces], axis=1))
    copies = []
    for j in range(held.shape[1] // step):
        lanes = pl.ds(j * step, step)
        right = right_parts(jnp.concatenate([w[rows, lanes] for w in weights], axis=0))
        made = start[:, lanes] + jnp.dot(left[...], right, preferred_element_type=jnp.float32)
        if last:
            held[:, lanes] = made
            copies += start_all([(held.at[:, lanes], out.at[:, lanes])], sems, j)
        else:
            out[:, lanes] = made
    wait_all(copies)


def add_product(start, pieces, weights, c, last):
    rows, chunk = pieces[0].shape
    width = start.shape[1]
    step = min(2 * LANES, width)
    count = len(pieces)
    return pl.pallas_call(
        functools.partial(product_body, count, c, step, last),
        out_shape=hbm(rows, width) if last else f32(rows, width),
        in_specs=[VMEM] * (1 + 2 * count),
        out_specs=HBM if last else VMEM,
        scratch_shapes=[
            pltpu.VMEM((rows, 3 * count * chunk), jnp.bfloat16),
            scratch(rows, width),
            pltpu.SemaphoreType.DMA((width // step,)),
        ],
        compiler_params=PARAMS,
        cost_estimate=cost(6 * count * rows * chunk * width),
    )(start, *pieces, *weights)


def solution(mesh):
    parts = mesh.shape["dom"]
    feats = mesh.shape["feat"]
    sides = 2 if feats % 2 == 0 else 1
    halves = feats // sides
    others = list(range(1, halves))

    def feat_target(f, dh, dl):
        return (f // sides + dh) % halves * sides + (f % sides + dl) % sides

    def feat_send(x, dh, dl):
        return lax.ppermute(x, "feat", [(f, feat_target(f, dh, dl)) for f in range(feats)])

    def dom_exchange(x):
        return lax.all_to_all(x, "dom", split_axis=0, concat_axis=0, tiled=True)

    def per_device(
        features,
        degree,
        diag_adj,
        remote_adj,
        read_block,
        tile_src,
        tile_row,
        w_first,
        b_first,
        w_second,
        b_second,
    ):
        part, cols = features.shape
        tile = diag_adj.shape[1]
        blocks = part // tile
        remote = remote_adj[0]
        chunk = LANES if cols % LANES == 0 else cols
        chunks = cols // chunk
        f = lax.axis_index("feat")
        want, source, row = read_block[0], tile_src[0], tile_row[0]
        shifts = [(dh, dl) for dh in range(halves) for dl in range(sides)]
        place = jnp.stack([jnp.asarray(feat_target(f, dh, dl), jnp.int32) for dh, dl in shifts])
        first = jnp.reshape(jnp.asarray(f * cols, jnp.int32), (1,))
        bias = b_first[None, :]

        x_all = [features] + [feat_send(features, 0, dl) for dl in range(1, sides)]
        w_all = [w_first] + [feat_send(w_first, 0, dl) for dl in range(1, sides)]

        shares = chunks if parts % chunks == 0 else 1
        share = jnp.reshape(jnp.asarray(lax.axis_index("dom") % shares, jnp.int32), (1,))
        share_rows = w_second.shape[0] // shares

        def share_send(x, k):
            pairs = [(s, s // shares * shares + (s % shares + k) % shares) for s in range(parts)]
            return lax.ppermute(x, "dom", pairs)

        w2_sent = row_block(share, w_second, share_rows)
        w2_got = [feat_send(w2_sent, dh, 0) for dh in others]

        scaling = lax.rsqrt(degree.astype(jnp.float32))
        spread = jnp.broadcast_to(scaling[:, None], (part, chunk))
        outgoing = outgoing_blocks(want, features, spread, tile)
        incoming = dom_exchange(outgoing)

        early = blocks * 5 // 12 * tile if chunks > 1 else part
        late = part - early
        marks = sorted({0, early // 2 // tile * tile, early, early + late // 2 // tile * tile, part})
        spans = list(zip(marks[:-1], marks[1:]))
        x_all[0], _ = lax.optimization_barrier((features, outgoing))
        send_steps = []
        for start, stop in spans:
            targets = [(0, 0, start)]
            for c in range(1, chunks):
                if stop <= early:
                    targets.append((c, 0, part + (c - 1) * early + start))
                else:
                    targets.append((c, 1, (c - 1) * late + start - early))
            send_steps.append((start, stop, targets))
        send_shapes = [(part + (chunks - 1) * early, chunk)]
        if late > 0:
            send_shapes.append(((chunks - 1) * late, chunk))
        sends = [partial_sums(place, [(dh * sides, send_steps)], x_all, w_all, send_shapes) for dh in others]
        sends, w2_got = lax.optimization_barrier((sends, w2_got))
        front = [feat_send(x[0], dh, 0) for dh, x in zip(others, sends)]

        own_steps = [(a, b, [(c, c, a) for c in range(chunks)]) for a, b in spans]
        own = list(partial_sums(place, [(0, own_steps)], x_all, w_all, [(part, chunk)] * chunks, HINT))

        incoming, own = lax.optimization_barrier((incoming, list(own)))
        w2_groups = [[got] + [share_send(got, k) for k in range(1, shares)] for got in w2_got]
        w2_core = [w_second] + [feat_send(w_second, 0, dl) for dl in range(1, sides)]
        chosen = chosen_blocks(source, incoming)
        chosen_all = [chosen] + [feat_send(chosen, 0, dl) for dl in range(1, sides)]
        height = chosen.shape[0]
        tail_rows = (chunks - 1) * late
        groups, remote_shapes, passing, carried = [], [], [], []
        for dh, x in zip(others, sends):
            at = len(remote_shapes)
            targets = [(0, at, 0)] + [(c, at + 1, tail_rows + (c - 1) * height) for c in range(1, chunks)]
            groups.append((dh * sides, [(0, height, targets)]))
            remote_shapes.append((height, chunk))
            if chunks > 1:
                remote_shapes.append((tail_rows + (chunks - 1) * height, chunk))
                passing += x[1:]
                carried += [(at + 1, 0)] * len(x[1:])
        at = len(remote_shapes)
        groups.append((0, [(0, height, [(c, at + c, 0) for c in range(chunks)])]))
        remote_shapes += [(height, chunk)] * chunks
        made = partial_sums(place, groups, chosen_all, w_all, remote_shapes, 0, passing, carried)
        each = at // max(len(others), 1)
        remote_front = [feat_send(made[i * each], dh, 0) for i, dh in enumerate(others)]
        rest = [feat_send(made[i * each + 1], dh, 0) for i, dh in enumerate(others)] if chunks > 1 else []
        remote_own = made[at:]

        reach = len(others)
        first_layout = [(h, h, 0, part, 0) for h in range(reach)]
        base = own_part(diag_adj, spread, own[0], front, first_layout, reach)
        collected = []
        outgoing = None
        for c in range(chunks):
            if c == 0:
                outgoing, base_next = hidden_blocks(
                    row, want, first, 0, bias, base, remote, spread, diag_adj, [remote_own[0]] + remote_front
                )
            else:
                begin, _ = lax.optimization_barrier((own[c], outgoing))
                layout = []
                for h in range(reach):
                    layout.append((h, h, part + (c - 1) * early, part + c * early, 0))
                    if late > 0:
                        layout.append((h, reach + h, (c - 1) * late, c * late, early))
                ends = tail_rows + c * height
                remote_sums = [remote_own[c]] + [r if ends == r.shape[0] else r[:ends] for r in rest]
                outgoing, base_next = later_blocks(
                    row,
                    want,
                    first,
                    c * chunk,
                    bias,
                    begin,
                    remote,
                    spread,
                    diag_adj,
                    remote_sums,
                    front + rest,
                    layout,
                    reach,
                )
            incoming = dom_exchange(outgoing)
            if c < chunks - 1:
                incoming = pinned(incoming)[0]
            pieces = feature_pieces(source, row, place, base_next, remote, spread, incoming, c < chunks - 1)
            collected.append(
                [p if dh == 0 and dl == 0 else feat_send(p, dh, dl) for (dh, dl), p in zip(shifts, pieces)]
            )

        w2_groups, _ = lax.optimization_barrier((w2_groups, outgoing))
        w2_far = []
        for group in w2_groups:
            ordered = in_order(share, group)
            w2_far += [ordered] + [feat_send(ordered, 0, dl) for dl in range(1, sides)]
        weights = w2_core + w2_far
        out = b_second[None, :]
        for c in range(chunks):
            if c < chunks - 1 or halves == 1:
                out = add_product(out, collected[c], weights, c, c == chunks - 1)
            else:
                out = add_product(out, collected[c][:sides], weights[:sides], c, False)
                out = add_product(out, collected[c][sides:], weights[sides:], c, True)
        return out

    return jax.shard_map(
        per_device,
        mesh=mesh,
        in_specs=(
            P("dom", "feat"),
            P("dom"),
            P("dom", None),
            P("dom", None, None, None),
            P("dom", None),
            P("dom", None),
            P("dom", None),
            P("feat", None),
            P(),
            P("feat", None),
            P(),
        ),
        out_specs=P(("dom", "feat"), None),
        check_vma=False,
    )
```

```python
import functools

import jax
import jax.numpy as jnp
from jax import lax
from jax.experimental import pallas as pl
from jax.experimental.pallas import tpu as pltpu
from jax.sharding import PartitionSpec as P

LANES = 128
TOUCH = 2
HINT = 5 * 10**10
VMEM_LIMIT = 24 * 1024 * 1024
VMEM = pl.BlockSpec(memory_space=pltpu.VMEM)
SMEM = pl.BlockSpec(memory_space=pltpu.SMEM)
HBM = pl.BlockSpec(memory_space=pltpu.HBM)
PARAMS = pltpu.CompilerParams(vmem_limit_bytes=VMEM_LIMIT)


def dot3(a, b):
    return jnp.dot(a, b, precision=lax.Precision.HIGH, preferred_element_type=jnp.float32)


def two_parts(x):
    high = x.astype(jnp.bfloat16)
    return high, (x - high.astype(jnp.float32)).astype(jnp.bfloat16)


def left_parts(x):
    high, low = two_parts(x)
    return jnp.concatenate([high, low, high], axis=1)


def right_parts(w):
    high, low = two_parts(w)
    return jnp.concatenate([high, high, low], axis=0)


def f32(*dims):
    return jax.ShapeDtypeStruct(dims, jnp.float32)


def hbm(*dims):
    return pltpu.HBM(dims, jnp.float32)


def pinned(*arrays):
    return [pltpu.with_memory_space_constraint(a, pltpu.HBM) for a in arrays]


def rows_at(index, height):
    return pl.ds(pl.multiple_of(index * height, height), height)


def scratch(*dims):
    return pltpu.VMEM(dims, jnp.float32)


def start_all(pairs, sems, first):
    copies = [pltpu.make_async_copy(a, b, sems.at[first + i]) for i, (a, b) in enumerate(pairs)]
    for copy in copies:
        copy.start()
    return copies


def wait_all(copies):
    for copy in copies:
        copy.wait()


def cost(flops):
    return pl.CostEstimate(flops=flops, bytes_accessed=0, transcendentals=0)


def outgoing_body(want_ref, features, spread, blocks, held, sems):
    count, tile, cols = held.shape
    chunk = spread.shape[1]
    last = features.shape[0] // tile - 1
    copies = []
    for d in range(count):
        rows = rows_at(jnp.minimum(want_ref[d], last), tile)
        for c in range(cols // chunk):
            lanes = pl.ds(c * chunk, chunk)
            held[d, :, lanes] = features[rows, lanes] * spread[rows, :]
        copies += start_all([(held.at[d], blocks.at[d])], sems, d)
    wait_all(copies)


def outgoing_blocks(want, features, spread, tile):
    cols = features.shape[1]
    count = want.shape[0]
    return pl.pallas_call(
        outgoing_body,
        out_shape=hbm(count, tile, cols),
        in_specs=[SMEM, VMEM, VMEM],
        out_specs=HBM,
        scratch_shapes=[scratch(count, tile, cols), pltpu.SemaphoreType.DMA((count,))],
        compiler_params=PARAMS,
        cost_estimate=cost(HINT),
    )(want, features, spread)


def partial_body(count, groups, place_ref, *refs):
    lefts, rights, refs = refs[:count], refs[count : 2 * count], refs[2 * count :]
    outs, (left, right, result, sems) = refs[:-4], refs[-4:]
    cols = lefts[0].shape[1]
    chunk = outs[0].shape[1]
    used = 0
    weights_in, loads, stores = [], [], []
    for n, (at, _) in enumerate(groups):
        lanes = pl.ds(pl.multiple_of(place_ref[at] * cols, cols), cols)
        weights_in.append(start_all([(w.at[:, lanes], right.at[n, j]) for j, w in enumerate(rights)], sems, used))
        used += count
    for start, stop, _ in groups[0][1]:
        rows = pl.ds(start, stop - start)
        pairs = [(x.at[rows], left.at[rows, pl.ds(j * cols, cols)]) for j, x in enumerate(lefts)]
        loads.append(start_all(pairs, sems, used))
        used += count
    for n, (_, steps) in enumerate(groups):
        wait_all(weights_in[n])
        weight = right_parts(jnp.concatenate([right[n, j] for j in range(count)], axis=0))
        for i, (start, stop, targets) in enumerate(steps):
            if n == 0:
                wait_all(loads[i])
            rows = pl.ds(start, stop - start)
            result[n, rows, :] = jnp.dot(left_parts(left[rows, :]), weight, preferred_element_type=jnp.float32)
            pairs = [
                (result.at[n, rows, pl.ds(c * chunk, chunk)], outs[o].at[pl.ds(offset, stop - start)])
                for c, o, offset in targets
            ]
            stores += start_all(pairs, sems, used)
            used += len(pairs)
    wait_all(stores)


def partial_sums(place, groups, lefts, weights, shapes, flops=0):
    rows, cols = lefts[0].shape
    depth = weights[0].shape[0]
    count = len(lefts)
    copies = count * (len(groups) + len(groups[0][1]))
    copies += sum(len(targets) for _, steps in groups for _, _, targets in steps)
    return pl.pallas_call(
        functools.partial(partial_body, count, groups),
        out_shape=[hbm(*s) for s in shapes],
        in_specs=[SMEM] + [HBM] * (2 * count),
        out_specs=[HBM] * len(shapes),
        scratch_shapes=[
            scratch(rows, count * cols),
            scratch(len(groups), count, depth, cols),
            scratch(len(groups), rows, cols),
            pltpu.SemaphoreType.DMA((copies,)),
        ],
        compiler_params=PARAMS,
        cost_estimate=cost(flops),
    )(place, *pinned(lefts[0]), *lefts[1:], *pinned(weights[0]), *weights[1:])


def loaded_body(ats, place_ref, *refs):
    sources, outs, sems = refs[: -1 - len(ats)], refs[-1 - len(ats) : -1], refs[-1]
    depth = sources[0].shape[0]
    pairs = []
    for at, out in zip(ats, outs):
        cols = out.shape[1]
        lanes = pl.ds(pl.multiple_of(place_ref[at] * cols, cols), cols)
        pairs += [(w.at[:, lanes], out.at[pl.ds(j * depth, depth)]) for j, w in enumerate(sources)]
    wait_all(start_all(pairs, sems, 0))


def loaded_weights(place, ats, weights, cols):
    depth = weights[0].shape[0]
    count = len(weights)
    return pl.pallas_call(
        functools.partial(loaded_body, ats),
        out_shape=[f32(count * depth, cols)] * len(ats),
        in_specs=[SMEM] + [HBM] * count,
        out_specs=[VMEM] * len(ats),
        scratch_shapes=[pltpu.SemaphoreType.DMA((count * len(ats),))],
        compiler_params=PARAMS,
        cost_estimate=cost(0),
    )(place, *pinned(weights[0]), *weights[1:])


def remote_body(count, *refs):
    lefts, refs = refs[:count], refs[count:]
    groups = len(refs) // (1 + lefts[0].shape[1] // refs[-1].shape[1])
    weights, outs = refs[:groups], refs[groups:]
    chunk = outs[0].shape[1]
    chunks = len(outs) // groups
    left = left_parts(jnp.concatenate([x[...] for x in lefts], axis=1))
    for n, weight in enumerate(weights):
        made = jnp.dot(left, right_parts(weight[...]), preferred_element_type=jnp.float32)
        for c in range(chunks):
            outs[n * chunks + c][...] = made[:, c * chunk : (c + 1) * chunk]


def remote_products(lefts, weights, chunks):
    rows, cols = lefts[0].shape
    outs = len(weights) * chunks
    return pl.pallas_call(
        functools.partial(remote_body, len(lefts)),
        out_shape=[f32(rows, cols // chunks)] * outs,
        in_specs=[VMEM] * (len(lefts) + len(weights)),
        out_specs=[VMEM] * outs,
        compiler_params=PARAMS,
        cost_estimate=cost(0),
    )(*lefts, *weights)


def joined_body(plan, count, *refs):
    stored, refs = refs[:count], refs[count:]
    fresh, refs = refs[: len(plan) - count], refs[len(plan) - count :]
    held, sems, outs = refs[-1 - count : -1], refs[-1], refs[: -1 - count]
    loads = start_all(list(zip(stored, held)), sems, 0)
    places = [outs[o].at[pl.ds(offset, x.shape[0])] for x, (o, offset) in zip([*stored, *fresh], plan)]
    stores = start_all(list(zip(fresh, places[count:])), sems, count)
    for j in range(count):
        loads[j].wait()
        stores += start_all([(held[j], places[j])], sems, len(plan) + j)
    wait_all(stores)


def joined(stored, fresh, plan, shapes):
    count = len(stored)
    return pl.pallas_call(
        functools.partial(joined_body, plan, count),
        out_shape=[hbm(*s) for s in shapes],
        in_specs=[HBM] * count + [VMEM] * len(fresh),
        out_specs=[HBM] * len(shapes),
        scratch_shapes=[scratch(*x.shape) for x in stored]
        + [pltpu.SemaphoreType.DMA((len(plan) + count,))],
        compiler_params=PARAMS,
        cost_estimate=cost(0),
    )(*pinned(*stored), *fresh)


def chosen_body(source_ref, incoming, chosen):
    tile = incoming.shape[1]
    for g in range(chosen.shape[0] // tile):
        chosen[pl.ds(g * tile, tile), :] = incoming[source_ref[TOUCH * g]]


def chosen_blocks(source, incoming):
    tile, cols = incoming.shape[1:]
    groups = source.shape[0] // TOUCH
    return pl.pallas_call(
        chosen_body,
        out_shape=f32(groups * tile, cols),
        in_specs=[SMEM, VMEM],
        out_specs=VMEM,
        compiler_params=PARAMS,
        cost_estimate=cost(0),
    )(source, incoming)


def received_pairs(layout, received, recv_in):
    return [
        (received[r].at[pl.ds(start, stop - start)], recv_in.at[h, pl.ds(offset, stop - start)])
        for h, r, start, stop, offset in layout
    ]


def own_total(diag_in, spread_in, own_in, recv_in, total):
    tile = diag_in.shape[1]
    for i in range(diag_in.shape[0] // tile):
        rows = pl.ds(i * tile, tile)
        mixed = own_in[rows, :]
        for h in range(recv_in.shape[0]):
            mixed = mixed + recv_in[h, rows, :]
        total[rows, :] = dot3(diag_in[rows, :], mixed * spread_in[rows, :])


def own_body(layout, diag, spread, own, *refs):
    received, (base, diag_in, spread_in, own_in, recv_in, sems) = refs[:-6], refs[-6:]
    pairs = [(diag, diag_in), (spread, spread_in), (own, own_in)]
    wait_all(start_all(pairs + received_pairs(layout, received, recv_in), sems, 0))
    own_total(diag_in, spread_in, own_in, recv_in, base)


def own_part(diag, spread, own, received, layout, others):
    return pl.pallas_call(
        functools.partial(own_body, layout),
        out_shape=f32(*own.shape),
        in_specs=[HBM] * (3 + len(received)),
        out_specs=VMEM,
        scratch_shapes=[scratch(*a.shape) for a in (diag, spread, own)]
        + [scratch(others, *own.shape), pltpu.SemaphoreType.DMA((3 + len(layout),))],
        compiler_params=PARAMS,
        cost_estimate=cost(0),
    )(*pinned(diag, spread, own), *received)


def hidden_tail(
    lane_offset, row_ref, want_ref, first_ref, bias, remote, spread, diag, sums, blocks, base_out, total, scaled, sems, used
):
    tiles, tile = remote.shape[:2]
    parts = blocks.shape[0]
    chunk = total.shape[1]
    for g in range(tiles // TOUCH):
        block = sums[0][pl.ds(g * tile, tile), :]
        for x in sums[1:]:
            block = block + x[pl.ds(g * tile, tile), :]
        for k in range(TOUCH * g, TOUCH * g + TOUCH):
            total[rows_at(row_ref[k], tile), :] += dot3(remote[k], block)
    lanes = pl.ds(pl.multiple_of(first_ref[0] + lane_offset, chunk), chunk)
    scaled[...] = jnp.maximum(total[...] * spread[...] + bias[:, lanes], 0.0) * spread[...]
    last = scaled.shape[0] // tile - 1
    copies = start_all(
        [(scaled.at[rows_at(jnp.minimum(want_ref[d], last), tile)], blocks.at[d]) for d in range(parts)],
        sems,
        used,
    )
    for i in range(last + 1):
        rows = pl.ds(i * tile, tile)
        total[rows, :] = dot3(diag[rows, :], scaled[rows, :])
    copies += start_all([(total, base_out)], sems, used + parts)
    wait_all(copies)


def hidden_body(lane_offset, row_ref, want_ref, first_ref, bias, base, remote, spread, diag, *refs):
    sums, (blocks, base_out, total, scaled, sems) = refs[:-5], refs[-5:]
    total[...] = base[...]
    hidden_tail(
        lane_offset, row_ref, want_ref, first_ref, bias, remote, spread, diag, sums, blocks, base_out, total, scaled, sems, 0
    )


def hidden_blocks(row, want, first, lane_offset, bias, base, remote, spread, diag, remote_sums):
    rows, chunk = base.shape
    tile = diag.shape[1]
    parts = want.shape[0]
    return pl.pallas_call(
        functools.partial(hidden_body, lane_offset),
        out_shape=[hbm(parts, tile, chunk), hbm(rows, chunk)],
        in_specs=[SMEM] * 3 + [VMEM] * (5 + len(remote_sums)),
        out_specs=[HBM, HBM],
        scratch_shapes=[scratch(rows, chunk), scratch(rows, chunk), pltpu.SemaphoreType.DMA((parts + 1,))],
        compiler_params=PARAMS,
        cost_estimate=cost(HINT),
    )(row, want, first, bias, base, remote, spread, diag, *remote_sums)


def later_body(
    count, layout, lane_offset, row_ref, want_ref, first_ref, bias, own, remote, spread, diag, *refs
):
    remote_sums, refs = refs[:count], refs[count:]
    received, refs = refs[:-10], refs[-10:]
    blocks, base_out, total, remote_in, spread_in, diag_in, scaled, sums_in, recv_in, sems = refs
    height = sums_in.shape[1]
    pairs = [(own, scaled), (spread, spread_in), (diag, diag_in)]
    pairs += received_pairs(layout, received, recv_in)
    late = [(remote, remote_in)]
    late += [(s.at[pl.ds(s.shape[0] - height, height)], sums_in.at[j]) for j, s in enumerate(remote_sums)]
    first = start_all(pairs, sems, 0)
    tail = start_all(late, sems, len(pairs))
    wait_all(first)
    own_total(diag_in, spread_in, scaled, recv_in, total)
    wait_all(tail)
    sums = [sums_in.at[j] for j in range(count)]
    hidden_tail(
        lane_offset,
        row_ref,
        want_ref,
        first_ref,
        bias,
        remote_in,
        spread_in,
        diag_in,
        sums,
        blocks,
        base_out,
        total,
        scaled,
        sems,
        len(pairs) + len(late),
    )


def later_blocks(
    row, want, first, lane_offset, bias, own, remote, spread, diag, remote_sums, received, layout, others
):
    rows, chunk = own.shape
    tile = diag.shape[1]
    parts = want.shape[0]
    count = len(remote_sums)
    height = remote.shape[0] // TOUCH * tile
    return pl.pallas_call(
        functools.partial(later_body, count, layout, lane_offset),
        out_shape=[hbm(parts, tile, chunk), hbm(rows, chunk)],
        in_specs=[SMEM] * 3 + [VMEM] + [HBM] * (4 + count + len(received)),
        out_specs=[HBM, HBM],
        scratch_shapes=[scratch(*a.shape) for a in (own, remote, spread, diag, own)]
        + [scratch(count, height, chunk), scratch(others, *own.shape)]
        + [pltpu.SemaphoreType.DMA((5 + len(layout) + count + parts,))],
        compiler_params=PARAMS,
        cost_estimate=cost(HINT),
    )(row, want, first, bias, *pinned(own, remote, spread, diag, remote_sums[0]), *remote_sums[1:], *received)


def pieces_body(stored, source_ref, row_ref, place_ref, base, remote, spread, incoming, *refs):
    pieces, (total, remote_in, spread_in, incoming_in, sems) = refs[:-5], refs[-5:]
    tiles, tile = remote.shape[:2]
    early = start_all(
        [(incoming, incoming_in), (remote, remote_in), (base, total), (spread, spread_in)], sems, 0
    )
    wait_all(early[:3])
    for k in range(tiles):
        total[rows_at(row_ref[k], tile), :] += dot3(remote_in[k], incoming_in[source_ref[k]])
    wait_all(early[3:])
    height = pieces[0].shape[0]
    copies = []
    for j in reversed(range(len(pieces))):
        rows = rows_at(place_ref[j], height)
        made = total[rows, :] * spread_in[rows, :]
        if stored:
            total[rows, :] = made
            copies += start_all([(total.at[rows], pieces[j])], sems, 4 + j)
        else:
            pieces[j][...] = made
    wait_all(copies)


def feature_pieces(source, row, place, base, remote, spread, incoming, stored):
    rows, chunk = base.shape
    feats = place.shape[0]
    make = hbm if stored else f32
    return pl.pallas_call(
        functools.partial(pieces_body, stored),
        out_shape=[make(rows // feats, chunk)] * feats,
        in_specs=[SMEM] * 3 + [HBM] * 4,
        out_specs=[HBM if stored else VMEM] * feats,
        scratch_shapes=[scratch(*a.shape) for a in (base, remote, spread, incoming)]
        + [pltpu.SemaphoreType.DMA((4 + feats,))],
        compiler_params=PARAMS,
        cost_estimate=cost(0),
    )(source, row, place, *pinned(base, remote, spread), incoming)


def in_order_body(count, share_ref, *refs):
    parts, out = refs[:count], refs[count]
    for k, x in enumerate(parts):
        out[rows_at(lax.rem(share_ref[0] + count - k, count), x.shape[0]), :] = x[...]


def in_order(share, parts):
    count = len(parts)
    if count == 1:
        return parts[0]
    rows, cols = parts[0].shape
    return pl.pallas_call(
        functools.partial(in_order_body, count),
        out_shape=f32(count * rows, cols),
        in_specs=[SMEM] + [VMEM] * count,
        out_specs=VMEM,
        compiler_params=PARAMS,
        cost_estimate=cost(0),
    )(share, *parts)


def product_body(count, c, step, last, start, *refs):
    pieces, weights, (out, left, held, sems) = refs[:count], refs[count : 2 * count], refs[2 * count :]
    rows = pl.ds(c * pieces[0].shape[1], pieces[0].shape[1])
    left[...] = left_parts(jnp.concatenate([p[...] for p in pieces], axis=1))
    copies = []
    for j in range(held.shape[1] // step):
        lanes = pl.ds(j * step, step)
        right = right_parts(jnp.concatenate([w[rows, lanes] for w in weights], axis=0))
        made = start[:, lanes] + jnp.dot(left[...], right, preferred_element_type=jnp.float32)
        if last:
            held[:, lanes] = made
            copies += start_all([(held.at[:, lanes], out.at[:, lanes])], sems, j)
        else:
            out[:, lanes] = made
    wait_all(copies)


def add_product(start, pieces, weights, c, last):
    rows, chunk = pieces[0].shape
    width = start.shape[1]
    step = min(2 * LANES, width)
    count = len(pieces)
    return pl.pallas_call(
        functools.partial(product_body, count, c, step, last),
        out_shape=hbm(rows, width) if last else f32(rows, width),
        in_specs=[VMEM] * (1 + 2 * count),
        out_specs=HBM if last else VMEM,
        scratch_shapes=[
            pltpu.VMEM((rows, 3 * count * chunk), jnp.bfloat16),
            scratch(rows, width),
            pltpu.SemaphoreType.DMA((width // step,)),
        ],
        compiler_params=PARAMS,
        cost_estimate=cost(6 * count * rows * chunk * width),
    )(start, *pieces, *weights)


def solution(mesh):
    parts = mesh.shape["dom"]
    feats = mesh.shape["feat"]
    sides = 2 if feats % 2 == 0 else 1
    halves = feats // sides
    others = list(range(1, halves))

    def feat_target(f, dh, dl):
        return (f // sides + dh) % halves * sides + (f % sides + dl) % sides

    def feat_send(x, dh, dl):
        return lax.ppermute(x, "feat", [(f, feat_target(f, dh, dl)) for f in range(feats)])

    def dom_exchange(x):
        return lax.all_to_all(x, "dom", split_axis=0, concat_axis=0, tiled=True)

    def per_device(
        features,
        degree,
        diag_adj,
        remote_adj,
        read_block,
        tile_src,
        tile_row,
        w_first,
        b_first,
        w_second,
        b_second,
    ):
        part, cols = features.shape
        tile = diag_adj.shape[1]
        blocks = part // tile
        remote = remote_adj[0]
        chunk = LANES if cols % LANES == 0 else cols
        chunks = cols // chunk
        f = lax.axis_index("feat")
        want, source, row = read_block[0], tile_src[0], tile_row[0]
        shifts = [(dh, dl) for dh in range(halves) for dl in range(sides)]
        place = jnp.stack([jnp.asarray(feat_target(f, dh, dl), jnp.int32) for dh, dl in shifts])
        first = jnp.reshape(jnp.asarray(f * cols, jnp.int32), (1,))
        bias = b_first[None, :]

        x_all = [features] + [feat_send(features, 0, dl) for dl in range(1, sides)]
        w_all = [w_first] + [feat_send(w_first, 0, dl) for dl in range(1, sides)]

        shares = chunks if parts % chunks == 0 else 1
        share = jnp.reshape(jnp.asarray(lax.axis_index("dom") % shares, jnp.int32), (1,))

        def share_send(x, k):
            pairs = [(s, s // shares * shares + (s % shares + k) % shares) for s in range(parts)]
            return lax.ppermute(x, "dom", pairs)

        w2_sent = lax.select_n(share[0], *jnp.split(w_second, shares)) if shares > 1 else w_second
        w2_got = [feat_send(w2_sent, dh, 0) for dh in others]

        scaling = lax.rsqrt(degree.astype(jnp.float32))
        spread = jnp.broadcast_to(scaling[:, None], (part, chunk))
        outgoing = outgoing_blocks(want, features, spread, tile)
        incoming = dom_exchange(outgoing)

        early = blocks // 4 * tile if chunks > 1 else part
        late = part - early
        marks = sorted({0, early // 2 // tile * tile, early, early + late // 2 // tile * tile, part})
        spans = list(zip(marks[:-1], marks[1:]))
        x_all[0], _ = lax.optimization_barrier((features, outgoing))
        send_steps = []
        for start, stop in spans:
            targets = [(0, 0, start)]
            for c in range(1, chunks):
                if stop <= early:
                    targets.append((c, 0, part + (c - 1) * early + start))
                else:
                    targets.append((c, 1, (c - 1) * late + start - early))
            send_steps.append((start, stop, targets))
        send_shapes = [(part + (chunks - 1) * early, chunk)]
        if late > 0:
            send_shapes.append(((chunks - 1) * late, chunk))
        sends = [partial_sums(place, [(dh * sides, send_steps)], x_all, w_all, send_shapes) for dh in others]
        sends, w2_got = lax.optimization_barrier((sends, w2_got))
        front = [feat_send(x[0], dh, 0) for dh, x in zip(others, sends)]

        own_steps = [(a, b, [(c, c, a) for c in range(chunks)]) for a, b in spans]
        own = list(partial_sums(place, [(0, own_steps)], x_all, w_all, [(part, chunk)] * chunks, HINT))

        incoming, own = lax.optimization_barrier((incoming, list(own)))
        w2_groups = [[got] + [share_send(got, k) for k in range(1, shares)] for got in w2_got]
        w2_core = [w_second] + [feat_send(w_second, 0, dl) for dl in range(1, sides)]
        chosen = chosen_blocks(source, incoming)
        chosen_all = [chosen] + [feat_send(chosen, 0, dl) for dl in range(1, sides)]
        height = chosen.shape[0]
        tail_rows = (chunks - 1) * late
        ats = [dh * sides for dh in others] + [0]
        turned, _ = lax.optimization_barrier((place, chosen))
        made = remote_products(chosen_all, loaded_weights(turned, ats, w_all, cols), chunks)
        remote_front = [feat_send(made[i * chunks], dh, 0) for i, dh in enumerate(others)]
        remote_own = list(made[len(others) * chunks :])
        rest = []
        if chunks > 1:
            stored, kept, fresh, turned_in, shapes = [], [], [], [], []
            for i, x in enumerate(sends):
                kept += [(i, 0)] * len(x[1:])
                stored += x[1:]
                for c in range(1, chunks):
                    fresh.append(made[i * chunks + c])
                    turned_in.append((i, tail_rows + (c - 1) * height))
                shapes.append((tail_rows + (chunks - 1) * height, chunk))
            for c in range(1, chunks):
                fresh.append(remote_own[c])
                turned_in.append((len(shapes), 0))
                shapes.append((height, chunk))
            written = joined(stored, fresh, kept + turned_in, shapes)
            rest = [feat_send(x, dh, 0) for dh, x in zip(others, written)]
            remote_own[1:] = written[len(others) :]

        reach = len(others)
        first_layout = [(h, h, 0, part, 0) for h in range(reach)]
        base = own_part(diag_adj, spread, own[0], front, first_layout, reach)
        collected = []
        outgoing = None
        for c in range(chunks):
            if c == 0:
                outgoing, base_next = hidden_blocks(
                    row, want, first, 0, bias, base, remote, spread, diag_adj, [remote_own[0]] + remote_front
                )
            else:
                begin, _ = lax.optimization_barrier((own[c], outgoing))
                layout = []
                for h in range(reach):
                    layout.append((h, h, part + (c - 1) * early, part + c * early, 0))
                    if late > 0:
                        layout.append((h, reach + h, (c - 1) * late, c * late, early))
                ends = tail_rows + c * height
                remote_sums = [remote_own[c]] + [r if ends == r.shape[0] else r[:ends] for r in rest]
                outgoing, base_next = later_blocks(
                    row,
                    want,
                    first,
                    c * chunk,
                    bias,
                    begin,
                    remote,
                    spread,
                    diag_adj,
                    remote_sums,
                    front + rest,
                    layout,
                    reach,
                )
            incoming = dom_exchange(outgoing)
            if c < chunks - 1:
                incoming = pinned(incoming)[0]
            pieces = feature_pieces(source, row, place, base_next, remote, spread, incoming, c < chunks - 1)
            collected.append(
                [p if dh == 0 and dl == 0 else feat_send(p, dh, dl) for (dh, dl), p in zip(shifts, pieces)]
            )

        w2_groups, _ = lax.optimization_barrier((w2_groups, outgoing))
        w2_far = []
        for group in w2_groups:
            ordered = in_order(share, group)
            w2_far += [ordered] + [feat_send(ordered, 0, dl) for dl in range(1, sides)]
        weights = w2_core + w2_far
        out = b_second[None, :]
        for c in range(chunks):
            if c < chunks - 1 or halves == 1:
                out = add_product(out, collected[c], weights, c, c == chunks - 1)
            else:
                out = add_product(out, collected[c][:sides], weights[:sides], c, False)
                out = add_product(out, collected[c][sides:], weights[sides:], c, True)
        return out

    return jax.shard_map(
        per_device,
        mesh=mesh,
        in_specs=(
            P("dom", "feat"),
            P("dom"),
            P("dom", None),
            P("dom", None, None, None),
            P("dom", None),
            P("dom", None),
            P("dom", None),
            P("feat", None),
            P(),
            P("feat", None),
            P(),
        ),
        out_specs=P(("dom", "feat"), None),
        check_vma=False,
    )
```

```python
import functools

import jax
import jax.numpy as jnp
from jax import lax
from jax.experimental import pallas as pl
from jax.experimental.pallas import tpu as pltpu
from jax.sharding import PartitionSpec as P

LANES = 128
TOUCH = 2
HINT = 5 * 10**10
VMEM_LIMIT = 24 * 1024 * 1024
VMEM = pl.BlockSpec(memory_space=pltpu.VMEM)
SMEM = pl.BlockSpec(memory_space=pltpu.SMEM)
HBM = pl.BlockSpec(memory_space=pltpu.HBM)
PARAMS = pltpu.CompilerParams(vmem_limit_bytes=VMEM_LIMIT)


def dot3(a, b):
    return jnp.dot(a, b, precision=lax.Precision.HIGH, preferred_element_type=jnp.float32)


def two_parts(x):
    high = x.astype(jnp.bfloat16)
    return high, (x - high.astype(jnp.float32)).astype(jnp.bfloat16)


def left_parts(x):
    high, low = two_parts(x)
    return jnp.concatenate([high, low, high], axis=1)


def right_parts(w):
    high, low = two_parts(w)
    return jnp.concatenate([high, high, low], axis=0)


def sum_of_products(lefts, parts):
    total = None
    for x, part in zip(lefts, parts):
        made = jnp.dot(left_parts(x), part, preferred_element_type=jnp.float32)
        total = made if total is None else total + made
    return total


def f32(*dims):
    return jax.ShapeDtypeStruct(dims, jnp.float32)


def hbm(*dims):
    return pltpu.HBM(dims, jnp.float32)


def pinned(*arrays):
    return [pltpu.with_memory_space_constraint(a, pltpu.HBM) for a in arrays]


def rows_at(index, height):
    return pl.ds(pl.multiple_of(index * height, height), height)


def scratch(*dims):
    return pltpu.VMEM(dims, jnp.float32)


def start_all(pairs, sems, first):
    copies = [pltpu.make_async_copy(a, b, sems.at[first + i]) for i, (a, b) in enumerate(pairs)]
    for copy in copies:
        copy.start()
    return copies


def wait_all(copies):
    for copy in copies:
        copy.wait()


def cost(flops):
    return pl.CostEstimate(flops=flops, bytes_accessed=0, transcendentals=0)


def outgoing_body(want_ref, features, spread, blocks, held, sems):
    count, tile, cols = held.shape
    chunk = spread.shape[1]
    last = features.shape[0] // tile - 1
    copies = []
    for d in range(count):
        rows = rows_at(jnp.minimum(want_ref[d], last), tile)
        for c in range(cols // chunk):
            lanes = pl.ds(c * chunk, chunk)
            held[d, :, lanes] = features[rows, lanes] * spread[rows, :]
        copies += start_all([(held.at[d], blocks.at[d])], sems, d)
    wait_all(copies)


def outgoing_blocks(want, features, spread, tile):
    cols = features.shape[1]
    count = want.shape[0]
    return pl.pallas_call(
        outgoing_body,
        out_shape=hbm(count, tile, cols),
        in_specs=[SMEM, VMEM, VMEM],
        out_specs=HBM,
        scratch_shapes=[scratch(count, tile, cols), pltpu.SemaphoreType.DMA((count,))],
        compiler_params=PARAMS,
        cost_estimate=cost(HINT),
    )(want, features, spread)


def partial_body(count, groups, place_ref, *refs):
    lefts, rights, refs = refs[:count], refs[count : 2 * count], refs[2 * count :]
    outs, (left, right, result, sems) = refs[:-4], refs[-4:]
    cols = lefts[0].shape[1]
    chunk = outs[0].shape[1]
    used = 0
    weights_in, loads, stores = [], [], []
    for n, (at, _) in enumerate(groups):
        lanes = pl.ds(pl.multiple_of(place_ref[at] * cols, cols), cols)
        weights_in.append(start_all([(w.at[:, lanes], right.at[n, j]) for j, w in enumerate(rights)], sems, used))
        used += count
    for start, stop, _ in groups[0][1]:
        rows = pl.ds(start, stop - start)
        pairs = [(x.at[rows], left.at[rows, pl.ds(j * cols, cols)]) for j, x in enumerate(lefts)]
        loads.append(start_all(pairs, sems, used))
        used += count
    for n, (_, steps) in enumerate(groups):
        wait_all(weights_in[n])
        parts = [right_parts(right[n, j]) for j in range(count)]
        for i, (start, stop, targets) in enumerate(steps):
            if n == 0:
                wait_all(loads[i])
            rows = pl.ds(start, stop - start)
            made = sum_of_products([left[rows, pl.ds(j * cols, cols)] for j in range(count)], parts)
            result[n, rows, :] = made
            pairs = [
                (result.at[n, rows, pl.ds(c * chunk, chunk)], outs[o].at[pl.ds(offset, stop - start)])
                for c, o, offset in targets
            ]
            stores += start_all(pairs, sems, used)
            used += len(pairs)
    wait_all(stores)


def partial_sums(place, groups, lefts, weights, shapes, flops=0):
    rows, cols = lefts[0].shape
    depth = weights[0].shape[0]
    count = len(lefts)
    copies = count * (len(groups) + len(groups[0][1]))
    copies += sum(len(targets) for _, steps in groups for _, _, targets in steps)
    return pl.pallas_call(
        functools.partial(partial_body, count, groups),
        out_shape=[hbm(*s) for s in shapes],
        in_specs=[SMEM] + [HBM] * (2 * count),
        out_specs=[HBM] * len(shapes),
        scratch_shapes=[
            scratch(rows, count * cols),
            scratch(len(groups), count, depth, cols),
            scratch(len(groups), rows, cols),
            pltpu.SemaphoreType.DMA((copies,)),
        ],
        compiler_params=PARAMS,
        cost_estimate=cost(flops),
    )(place, *pinned(lefts[0]), *lefts[1:], *pinned(weights[0]), *weights[1:])


def loaded_body(ats, place_ref, *refs):
    sources, outs, sems = refs[: -1 - len(ats)], refs[-1 - len(ats) : -1], refs[-1]
    depth = sources[0].shape[0]
    pairs = []
    for at, out in zip(ats, outs):
        cols = out.shape[1]
        lanes = pl.ds(pl.multiple_of(place_ref[at] * cols, cols), cols)
        pairs += [(w.at[:, lanes], out.at[pl.ds(j * depth, depth)]) for j, w in enumerate(sources)]
    wait_all(start_all(pairs, sems, 0))


def loaded_weights(place, ats, weights, cols):
    depth = weights[0].shape[0]
    count = len(weights)
    return pl.pallas_call(
        functools.partial(loaded_body, ats),
        out_shape=[f32(count * depth, cols)] * len(ats),
        in_specs=[SMEM] + [HBM] * count,
        out_specs=[VMEM] * len(ats),
        scratch_shapes=[pltpu.SemaphoreType.DMA((count * len(ats),))],
        compiler_params=PARAMS,
        cost_estimate=cost(0),
    )(place, *pinned(weights[0]), *weights[1:])


def remote_body(count, *refs):
    lefts, refs = refs[:count], refs[count:]
    groups = len(refs) // (1 + lefts[0].shape[1] // refs[-1].shape[1])
    weights, outs = refs[:groups], refs[groups:]
    chunk = outs[0].shape[1]
    chunks = len(outs) // groups
    depth = lefts[0].shape[1]
    for n, weight in enumerate(weights):
        parts = [right_parts(weight[pl.ds(j * depth, depth), :]) for j in range(count)]
        made = sum_of_products([x[...] for x in lefts], parts)
        for c in range(chunks):
            outs[n * chunks + c][...] = made[:, c * chunk : (c + 1) * chunk]


def remote_products(lefts, weights, chunks):
    rows, cols = lefts[0].shape
    outs = len(weights) * chunks
    return pl.pallas_call(
        functools.partial(remote_body, len(lefts)),
        out_shape=[f32(rows, cols // chunks)] * outs,
        in_specs=[VMEM] * (len(lefts) + len(weights)),
        out_specs=[VMEM] * outs,
        compiler_params=PARAMS,
        cost_estimate=cost(0),
    )(*lefts, *weights)


def joined_body(plan, count, *refs):
    stored, refs = refs[:count], refs[count:]
    fresh, refs = refs[: len(plan) - count], refs[len(plan) - count :]
    held, sems, outs = refs[-1 - count : -1], refs[-1], refs[: -1 - count]
    loads = start_all(list(zip(stored, held)), sems, 0)
    places = [outs[o].at[pl.ds(offset, x.shape[0])] for x, (o, offset) in zip([*stored, *fresh], plan)]
    stores = start_all(list(zip(fresh, places[count:])), sems, count)
    for j in range(count):
        loads[j].wait()
        stores += start_all([(held[j], places[j])], sems, len(plan) + j)
    wait_all(stores)


def joined(stored, fresh, plan, shapes):
    count = len(stored)
    return pl.pallas_call(
        functools.partial(joined_body, plan, count),
        out_shape=[hbm(*s) for s in shapes],
        in_specs=[HBM] * count + [VMEM] * len(fresh),
        out_specs=[HBM] * len(shapes),
        scratch_shapes=[scratch(*x.shape) for x in stored]
        + [pltpu.SemaphoreType.DMA((len(plan) + count,))],
        compiler_params=PARAMS,
        cost_estimate=cost(0),
    )(*pinned(*stored), *fresh)


def chosen_body(source_ref, incoming, chosen):
    tile = incoming.shape[1]
    for g in range(chosen.shape[0] // tile):
        chosen[pl.ds(g * tile, tile), :] = incoming[source_ref[TOUCH * g]]


def chosen_blocks(source, incoming):
    tile, cols = incoming.shape[1:]
    groups = source.shape[0] // TOUCH
    return pl.pallas_call(
        chosen_body,
        out_shape=f32(groups * tile, cols),
        in_specs=[SMEM, VMEM],
        out_specs=VMEM,
        compiler_params=PARAMS,
        cost_estimate=cost(0),
    )(source, incoming)


def received_pairs(layout, received, recv_in):
    return [
        (received[r].at[pl.ds(start, stop - start)], recv_in.at[h, pl.ds(offset, stop - start)])
        for h, r, start, stop, offset in layout
    ]


def own_total(diag_in, spread_in, own_in, recv_in, total):
    tile = diag_in.shape[1]
    for i in range(diag_in.shape[0] // tile):
        rows = pl.ds(i * tile, tile)
        mixed = own_in[rows, :]
        for h in range(recv_in.shape[0]):
            mixed = mixed + recv_in[h, rows, :]
        total[rows, :] = dot3(diag_in[rows, :], mixed * spread_in[rows, :])


def own_body(layout, diag, spread, own, *refs):
    received, (base, diag_in, spread_in, own_in, recv_in, sems) = refs[:-6], refs[-6:]
    pairs = [(diag, diag_in), (spread, spread_in), (own, own_in)]
    wait_all(start_all(pairs + received_pairs(layout, received, recv_in), sems, 0))
    own_total(diag_in, spread_in, own_in, recv_in, base)


def own_part(diag, spread, own, received, layout, others):
    return pl.pallas_call(
        functools.partial(own_body, layout),
        out_shape=f32(*own.shape),
        in_specs=[HBM] * (3 + len(received)),
        out_specs=VMEM,
        scratch_shapes=[scratch(*a.shape) for a in (diag, spread, own)]
        + [scratch(others, *own.shape), pltpu.SemaphoreType.DMA((3 + len(layout),))],
        compiler_params=PARAMS,
        cost_estimate=cost(0),
    )(*pinned(diag, spread, own), *received)


def hidden_tail(
    lane_offset, row_ref, want_ref, first_ref, bias, remote, spread, sums, blocks, scaled_out, total, scaled, sems, used
):
    tiles, tile = remote.shape[:2]
    parts = blocks.shape[0]
    chunk = total.shape[1]
    for g in range(tiles // TOUCH):
        block = sums[0][pl.ds(g * tile, tile), :]
        for x in sums[1:]:
            block = block + x[pl.ds(g * tile, tile), :]
        for k in range(TOUCH * g, TOUCH * g + TOUCH):
            total[rows_at(row_ref[k], tile), :] += dot3(remote[k], block)
    lanes = pl.ds(pl.multiple_of(first_ref[0] + lane_offset, chunk), chunk)
    scaled[...] = jnp.maximum(total[...] * spread[...] + bias[:, lanes], 0.0) * spread[...]
    last = scaled.shape[0] // tile - 1
    pairs = [(scaled.at[rows_at(jnp.minimum(want_ref[d], last), tile)], blocks.at[d]) for d in range(parts)]
    wait_all(start_all(pairs + [(scaled, scaled_out)], sems, used))


def hidden_body(lane_offset, row_ref, want_ref, first_ref, bias, base, remote, spread, *refs):
    sums, (blocks, scaled_out, total, scaled, sems) = refs[:-5], refs[-5:]
    total[...] = base[...]
    hidden_tail(
        lane_offset, row_ref, want_ref, first_ref, bias, remote, spread, sums, blocks, scaled_out, total, scaled, sems, 0
    )


def hidden_blocks(row, want, first, lane_offset, bias, base, remote, spread, remote_sums):
    rows, chunk = base.shape
    tile = remote.shape[1]
    parts = want.shape[0]
    return pl.pallas_call(
        functools.partial(hidden_body, lane_offset),
        out_shape=[hbm(parts, tile, chunk), hbm(rows, chunk)],
        in_specs=[SMEM] * 3 + [VMEM] * (4 + len(remote_sums)),
        out_specs=[HBM, HBM],
        scratch_shapes=[scratch(rows, chunk), scratch(rows, chunk), pltpu.SemaphoreType.DMA((parts + 1,))],
        compiler_params=PARAMS,
        cost_estimate=cost(HINT),
    )(row, want, first, bias, base, remote, spread, *remote_sums)


def later_body(
    count, layout, lane_offset, row_ref, want_ref, first_ref, bias, own, remote, spread, diag, *refs
):
    remote_sums, refs = refs[:count], refs[count:]
    received, refs = refs[:-10], refs[-10:]
    blocks, scaled_out, total, remote_in, spread_in, diag_in, scaled, sums_in, recv_in, sems = refs
    height = sums_in.shape[1]
    pairs = [(own, scaled), (spread, spread_in), (diag, diag_in)]
    pairs += received_pairs(layout, received, recv_in)
    late = [(remote, remote_in)]
    late += [(s.at[pl.ds(s.shape[0] - height, height)], sums_in.at[j]) for j, s in enumerate(remote_sums)]
    first = start_all(pairs, sems, 0)
    tail = start_all(late, sems, len(pairs))
    wait_all(first)
    own_total(diag_in, spread_in, scaled, recv_in, total)
    wait_all(tail)
    sums = [sums_in.at[j] for j in range(count)]
    hidden_tail(
        lane_offset,
        row_ref,
        want_ref,
        first_ref,
        bias,
        remote_in,
        spread_in,
        sums,
        blocks,
        scaled_out,
        total,
        scaled,
        sems,
        len(pairs) + len(late),
    )


def later_blocks(
    row, want, first, lane_offset, bias, own, remote, spread, diag, remote_sums, received, layout, others
):
    rows, chunk = own.shape
    tile = diag.shape[1]
    parts = want.shape[0]
    count = len(remote_sums)
    height = remote.shape[0] // TOUCH * tile
    return pl.pallas_call(
        functools.partial(later_body, count, layout, lane_offset),
        out_shape=[hbm(parts, tile, chunk), hbm(rows, chunk)],
        in_specs=[SMEM] * 3 + [VMEM] + [HBM] * (4 + count + len(received)),
        out_specs=[HBM, HBM],
        scratch_shapes=[scratch(*a.shape) for a in (own, remote, spread, diag, own)]
        + [scratch(count, height, chunk), scratch(others, *own.shape)]
        + [pltpu.SemaphoreType.DMA((5 + len(layout) + count + parts,))],
        compiler_params=PARAMS,
        cost_estimate=cost(HINT),
    )(row, want, first, bias, *pinned(own, remote, spread, diag, remote_sums[0]), *remote_sums[1:], *received)


def diagonal_body(diag, scaled, base, diag_in, scaled_in, total, sems):
    tile = diag.shape[1]
    wait_all(start_all([(diag, diag_in), (scaled, scaled_in)], sems, 0))
    for i in range(diag.shape[0] // tile):
        rows = pl.ds(i * tile, tile)
        total[rows, :] = dot3(diag_in[rows, :], scaled_in[rows, :])
    wait_all(start_all([(total, base)], sems, 2))


def diagonal_part(diag, scaled):
    return pl.pallas_call(
        diagonal_body,
        out_shape=hbm(*scaled.shape),
        in_specs=[HBM, HBM],
        out_specs=HBM,
        scratch_shapes=[scratch(*a.shape) for a in (diag, scaled, scaled)] + [pltpu.SemaphoreType.DMA((3,))],
        compiler_params=PARAMS,
        cost_estimate=cost(0),
    )(*pinned(diag, scaled))


def pieces_body(stored, source_ref, row_ref, place_ref, base, remote, spread, incoming, *refs):
    pieces, (total, remote_in, spread_in, incoming_in, sems) = refs[:-5], refs[-5:]
    tiles, tile = remote.shape[:2]
    early = start_all(
        [(incoming, incoming_in), (remote, remote_in), (base, total), (spread, spread_in)], sems, 0
    )
    wait_all(early[:3])
    for k in range(tiles):
        total[rows_at(row_ref[k], tile), :] += dot3(remote_in[k], incoming_in[source_ref[k]])
    wait_all(early[3:])
    height = pieces[0].shape[0]
    copies = []
    for j in reversed(range(len(pieces))):
        rows = rows_at(place_ref[j], height)
        made = total[rows, :] * spread_in[rows, :]
        if stored:
            total[rows, :] = made
            copies += start_all([(total.at[rows], pieces[j])], sems, 4 + j)
        else:
            pieces[j][...] = made
    wait_all(copies)


def feature_pieces(source, row, place, base, remote, spread, incoming, stored):
    rows, chunk = base.shape
    feats = place.shape[0]
    make = hbm if stored else f32
    return pl.pallas_call(
        functools.partial(pieces_body, stored),
        out_shape=[make(rows // feats, chunk)] * feats,
        in_specs=[SMEM] * 3 + [HBM] * 4,
        out_specs=[HBM if stored else VMEM] * feats,
        scratch_shapes=[scratch(*a.shape) for a in (base, remote, spread, incoming)]
        + [pltpu.SemaphoreType.DMA((4 + feats,))],
        compiler_params=PARAMS,
        cost_estimate=cost(0),
    )(source, row, place, *pinned(base, remote, spread), incoming)


def product_body(count, choices, c, step, last, turn_ref, start, *refs):
    pieces, refs = refs[:count], refs[count:]
    weights, (out, left, held, sems) = refs[: sum(choices)], refs[sum(choices) :]
    chunk = pieces[0].shape[1]
    pairs = [pieces[j : j + 2] for j in range(0, count, 2)]
    widths, at = [], 0
    for pair in pairs:
        lanes = pl.ds(at, 3 * chunk * len(pair))
        left[:, lanes] = left_parts(jnp.concatenate([p[...] for p in pair], axis=1))
        at += 3 * chunk * len(pair)
        widths.append(lanes)
    copies = []
    for j in range(held.shape[1] // step):
        lanes = pl.ds(j * step, step)
        blocks, at = [], 0
        for number in choices:
            rows = pl.ds(c * chunk if weights[at].shape[0] > chunk else 0, chunk)
            block = weights[at][rows, lanes]
            for k in range(1, number):
                block = jnp.where(turn_ref[0] == k, weights[at + k][rows, lanes], block)
            blocks.append(block)
            at += number
        made = start[:, lanes]
        for n, depth in enumerate(widths):
            right = right_parts(jnp.concatenate(blocks[2 * n : 2 * n + 2], axis=0))
            made = made + jnp.dot(left[:, depth], right, preferred_element_type=jnp.float32)
        if last:
            held[:, lanes] = made
            copies += start_all([(held.at[:, lanes], out.at[:, lanes])], sems, j)
        else:
            out[:, lanes] = made
    wait_all(copies)


def add_product(turn, start, pieces, weights, c, last):
    rows, chunk = pieces[0].shape
    width = start.shape[1]
    step = min(2 * LANES, width)
    count = len(pieces)
    flat = [w for group in weights for w in group]
    choices = [len(group) for group in weights]
    return pl.pallas_call(
        functools.partial(product_body, count, choices, c, step, last),
        out_shape=hbm(rows, width) if last else f32(rows, width),
        in_specs=[SMEM] + [VMEM] * (1 + count + len(flat)),
        out_specs=HBM if last else VMEM,
        scratch_shapes=[
            pltpu.VMEM((rows, 3 * count * chunk), jnp.bfloat16),
            scratch(rows, width),
            pltpu.SemaphoreType.DMA((width // step,)),
        ],
        compiler_params=PARAMS,
        cost_estimate=cost(6 * count * rows * chunk * width),
    )(turn, start, *pieces, *flat)


def solution(mesh):
    parts = mesh.shape["dom"]
    feats = mesh.shape["feat"]
    sides = 2 if feats % 2 == 0 else 1
    halves = feats // sides
    others = list(range(1, halves))

    def feat_target(f, dh, dl):
        return (f // sides + dh) % halves * sides + (f % sides + dl) % sides

    def feat_send(x, dh, dl):
        return lax.ppermute(x, "feat", [(f, feat_target(f, dh, dl)) for f in range(feats)])

    def dom_exchange(x):
        return lax.all_to_all(x, "dom", split_axis=0, concat_axis=0, tiled=True)

    def per_device(
        features,
        degree,
        diag_adj,
        remote_adj,
        read_block,
        tile_src,
        tile_row,
        w_first,
        b_first,
        w_second,
        b_second,
    ):
        part, cols = features.shape
        tile = diag_adj.shape[1]
        blocks = part // tile
        remote = remote_adj[0]
        chunk = LANES if cols % LANES == 0 else cols
        chunks = cols // chunk
        f = lax.axis_index("feat")
        want, source, row = read_block[0], tile_src[0], tile_row[0]
        shifts = [(dh, dl) for dh in range(halves) for dl in range(sides)]
        place = jnp.stack([jnp.asarray(feat_target(f, dh, dl), jnp.int32) for dh, dl in shifts])
        first = jnp.reshape(jnp.asarray(f * cols, jnp.int32), (1,))
        bias = b_first[None, :]

        x_all = [features] + [feat_send(features, 0, dl) for dl in range(1, sides)]
        w_all = [w_first] + [feat_send(w_first, 0, dl) for dl in range(1, sides)]

        shares = chunks if parts % chunks == 0 else 1
        share = jnp.reshape(jnp.asarray(lax.axis_index("dom") % shares, jnp.int32), (1,))

        def share_send(x, k):
            pairs = [(s, s // shares * shares + (s % shares + k) % shares) for s in range(parts)]
            return lax.ppermute(x, "dom", pairs)

        w2_sent = lax.select_n(share[0], *jnp.split(w_second, shares)) if shares > 1 else w_second
        w2_got = [feat_send(w2_sent, dh, 0) for dh in others]

        scaling = lax.rsqrt(degree.astype(jnp.float32))
        spread = jnp.broadcast_to(scaling[:, None], (part, chunk))
        outgoing = outgoing_blocks(want, features, spread, tile)
        incoming = dom_exchange(outgoing)

        early = blocks // 4 * tile if chunks > 1 else part
        late = part - early
        marks = sorted({0, early // 2 // tile * tile, early, early + late // 2 // tile * tile, part})
        spans = list(zip(marks[:-1], marks[1:]))
        x_all[0], _ = lax.optimization_barrier((features, outgoing))
        send_steps = []
        for start, stop in spans:
            targets = [(0, 0, start)]
            for c in range(1, chunks):
                if stop <= early:
                    targets.append((c, 0, part + (c - 1) * early + start))
                else:
                    targets.append((c, 1, (c - 1) * late + start - early))
            send_steps.append((start, stop, targets))
        send_shapes = [(part + (chunks - 1) * early, chunk)]
        if late > 0:
            send_shapes.append(((chunks - 1) * late, chunk))
        sends = [partial_sums(place, [(dh * sides, send_steps)], x_all, w_all, send_shapes) for dh in others]
        sends, w2_got = lax.optimization_barrier((sends, w2_got))
        front = [feat_send(x[0], dh, 0) for dh, x in zip(others, sends)]

        own_steps = [(a, b, [(c, c, a) for c in range(chunks)]) for a, b in spans]
        own = list(partial_sums(place, [(0, own_steps)], x_all, w_all, [(part, chunk)] * chunks, HINT))

        incoming, own = lax.optimization_barrier((incoming, list(own)))
        w2_groups = [[got] + [share_send(got, k) for k in range(1, shares)] for got in w2_got]
        w2_core = [w_second] + [feat_send(w_second, 0, dl) for dl in range(1, sides)]
        chosen = chosen_blocks(source, incoming)
        chosen_all = [chosen] + [feat_send(chosen, 0, dl) for dl in range(1, sides)]
        height = chosen.shape[0]
        tail_rows = (chunks - 1) * late
        ats = [dh * sides for dh in others] + [0]
        turned, _ = lax.optimization_barrier((place, chosen))
        made = remote_products(chosen_all, loaded_weights(turned, ats, w_all, cols), chunks)
        remote_front = [feat_send(made[i * chunks], dh, 0) for i, dh in enumerate(others)]
        remote_own = list(made[len(others) * chunks :])
        rest = []
        if chunks > 1:
            stored, kept, fresh, turned_in, shapes = [], [], [], [], []
            for i, x in enumerate(sends):
                kept += [(i, 0)] * len(x[1:])
                stored += x[1:]
                for c in range(1, chunks):
                    fresh.append(made[i * chunks + c])
                    turned_in.append((i, tail_rows + (c - 1) * height))
                shapes.append((tail_rows + (chunks - 1) * height, chunk))
            for c in range(1, chunks):
                fresh.append(remote_own[c])
                turned_in.append((len(shapes), 0))
                shapes.append((height, chunk))
            written = joined(stored, fresh, kept + turned_in, shapes)
            rest = [feat_send(x, dh, 0) for dh, x in zip(others, written)]
            remote_own[1:] = written[len(others) :]

        reach = len(others)
        first_layout = [(h, h, 0, part, 0) for h in range(reach)]
        base = own_part(diag_adj, spread, own[0], front, first_layout, reach)
        collected = []
        outgoing = None
        for c in range(chunks):
            if c == 0:
                outgoing, base_next = hidden_blocks(
                    row, want, first, 0, bias, base, remote, spread, [remote_own[0]] + remote_front
                )
            else:
                begin, _ = lax.optimization_barrier((own[c], outgoing))
                layout = []
                for h in range(reach):
                    layout.append((h, h, part + (c - 1) * early, part + c * early, 0))
                    if late > 0:
                        layout.append((h, reach + h, (c - 1) * late, c * late, early))
                ends = tail_rows + c * height
                remote_sums = [remote_own[c]] + [r if ends == r.shape[0] else r[:ends] for r in rest]
                outgoing, base_next = later_blocks(
                    row,
                    want,
                    first,
                    c * chunk,
                    bias,
                    begin,
                    remote,
                    spread,
                    diag_adj,
                    remote_sums,
                    front + rest,
                    layout,
                    reach,
                )
            incoming = dom_exchange(outgoing)
            if c < chunks - 1:
                incoming = pinned(incoming)[0]
            base_next = diagonal_part(diag_adj, base_next)
            pieces = feature_pieces(source, row, place, base_next, remote, spread, incoming, c < chunks - 1)
            collected.append(
                [p if dh == 0 and dl == 0 else feat_send(p, dh, dl) for (dh, dl), p in zip(shifts, pieces)]
            )

        w2_groups, _ = lax.optimization_barrier((w2_groups, outgoing))
        w2_far = [[feat_send(w, 0, dl) if dl > 0 else w for w in g] for g in w2_groups for dl in range(sides)]
        weights = [[w] for w in w2_core] + w2_far
        out = b_second[None, :]
        for c in range(chunks):
            turn = (share - c) % shares
            if c < chunks - 1 or halves == 1:
                out = add_product(turn, out, collected[c], weights, c, c == chunks - 1)
            else:
                out = add_product(turn, out, collected[c][:sides], weights[:sides], c, False)
                out = add_product(turn, out, collected[c][sides:], weights[sides:], c, True)
        return out

    return jax.shard_map(
        per_device,
        mesh=mesh,
        in_specs=(
            P("dom", "feat"),
            P("dom"),
            P("dom", None),
            P("dom", None, None, None),
            P("dom", None),
            P("dom", None),
            P("dom", None),
            P("feat", None),
            P(),
            P("feat", None),
            P(),
        ),
        out_specs=P(("dom", "feat"), None),
        check_vma=False,
    )
```

```python
import functools

import jax
import jax.numpy as jnp
from jax import lax
from jax.experimental import pallas as pl
from jax.experimental.pallas import tpu as pltpu
from jax.sharding import PartitionSpec as P

LANES = 128
TOUCH = 2
HINT = 5 * 10**10
VMEM_LIMIT = 24 * 1024 * 1024
VMEM = pl.BlockSpec(memory_space=pltpu.VMEM)
SMEM = pl.BlockSpec(memory_space=pltpu.SMEM)
HBM = pl.BlockSpec(memory_space=pltpu.HBM)
PARAMS = pltpu.CompilerParams(vmem_limit_bytes=VMEM_LIMIT)


def dot3(a, b):
    return jnp.dot(a, b, precision=lax.Precision.HIGH, preferred_element_type=jnp.float32)


def two_parts(x):
    high = x.astype(jnp.bfloat16)
    return high, (x - high.astype(jnp.float32)).astype(jnp.bfloat16)


def left_parts(x):
    high, low = two_parts(x)
    return jnp.concatenate([high, low, high], axis=1)


def right_parts(w):
    high, low = two_parts(w)
    return jnp.concatenate([high, high, low], axis=0)


def sum_of_products(lefts, parts):
    total = None
    for x, part in zip(lefts, parts):
        made = jnp.dot(left_parts(x), part, preferred_element_type=jnp.float32)
        total = made if total is None else total + made
    return total


def f32(*dims):
    return jax.ShapeDtypeStruct(dims, jnp.float32)


def hbm(*dims):
    return pltpu.HBM(dims, jnp.float32)


def pinned(*arrays):
    return [pltpu.with_memory_space_constraint(a, pltpu.HBM) for a in arrays]


def rows_at(index, height):
    return pl.ds(pl.multiple_of(index * height, height), height)


def scratch(*dims):
    return pltpu.VMEM(dims, jnp.float32)


def start_all(pairs, sems, first):
    copies = [pltpu.make_async_copy(a, b, sems.at[first + i]) for i, (a, b) in enumerate(pairs)]
    for copy in copies:
        copy.start()
    return copies


def wait_all(copies):
    for copy in copies:
        copy.wait()


def cost(flops):
    return pl.CostEstimate(flops=flops, bytes_accessed=0, transcendentals=0)


def outgoing_body(want_ref, features, spread, blocks, held, sems):
    count, tile, cols = held.shape
    chunk = spread.shape[1]
    last = features.shape[0] // tile - 1
    copies = []
    for d in range(count):
        rows = rows_at(jnp.minimum(want_ref[d], last), tile)
        for c in range(cols // chunk):
            lanes = pl.ds(c * chunk, chunk)
            held[d, :, lanes] = features[rows, lanes] * spread[rows, :]
        copies += start_all([(held.at[d], blocks.at[d])], sems, d)
    wait_all(copies)


def outgoing_blocks(want, features, spread, tile):
    cols = features.shape[1]
    count = want.shape[0]
    return pl.pallas_call(
        outgoing_body,
        out_shape=hbm(count, tile, cols),
        in_specs=[SMEM, VMEM, VMEM],
        out_specs=HBM,
        scratch_shapes=[scratch(count, tile, cols), pltpu.SemaphoreType.DMA((count,))],
        compiler_params=PARAMS,
        cost_estimate=cost(HINT),
    )(want, features, spread)


def partial_body(count, groups, place_ref, *refs):
    lefts, rights, refs = refs[:count], refs[count : 2 * count], refs[2 * count :]
    outs, (left, right, result, sems) = refs[:-4], refs[-4:]
    cols = lefts[0].shape[1]
    chunk = outs[0].shape[1]
    used = 0
    weights_in, loads, stores = [], [], []
    for n, (at, _) in enumerate(groups):
        lanes = pl.ds(pl.multiple_of(place_ref[at] * cols, cols), cols)
        weights_in.append(start_all([(w.at[:, lanes], right.at[n, j]) for j, w in enumerate(rights)], sems, used))
        used += count
    for start, stop, _ in groups[0][1]:
        rows = pl.ds(start, stop - start)
        pairs = [(x.at[rows], left.at[rows, pl.ds(j * cols, cols)]) for j, x in enumerate(lefts)]
        loads.append(start_all(pairs, sems, used))
        used += count
    for n, (_, steps) in enumerate(groups):
        wait_all(weights_in[n])
        parts = [right_parts(right[n, j]) for j in range(count)]
        for i, (start, stop, targets) in enumerate(steps):
            if n == 0:
                wait_all(loads[i])
            rows = pl.ds(start, stop - start)
            made = sum_of_products([left[rows, pl.ds(j * cols, cols)] for j in range(count)], parts)
            result[n, rows, :] = made
            pairs = [
                (result.at[n, rows, pl.ds(c * chunk, chunk)], outs[o].at[pl.ds(offset, stop - start)])
                for c, o, offset in targets
            ]
            stores += start_all(pairs, sems, used)
            used += len(pairs)
    wait_all(stores)


def partial_sums(place, groups, lefts, weights, shapes, flops=0):
    rows, cols = lefts[0].shape
    depth = weights[0].shape[0]
    count = len(lefts)
    copies = count * (len(groups) + len(groups[0][1]))
    copies += sum(len(targets) for _, steps in groups for _, _, targets in steps)
    return pl.pallas_call(
        functools.partial(partial_body, count, groups),
        out_shape=[hbm(*s) for s in shapes],
        in_specs=[SMEM] + [HBM] * (2 * count),
        out_specs=[HBM] * len(shapes),
        scratch_shapes=[
            scratch(rows, count * cols),
            scratch(len(groups), count, depth, cols),
            scratch(len(groups), rows, cols),
            pltpu.SemaphoreType.DMA((copies,)),
        ],
        compiler_params=PARAMS,
        cost_estimate=cost(flops),
    )(place, *pinned(lefts[0]), *lefts[1:], *pinned(weights[0]), *weights[1:])


def loaded_body(ats, place_ref, *refs):
    sources, outs, sems = refs[: -1 - len(ats)], refs[-1 - len(ats) : -1], refs[-1]
    depth = sources[0].shape[0]
    pairs = []
    for at, out in zip(ats, outs):
        cols = out.shape[1]
        lanes = pl.ds(pl.multiple_of(place_ref[at] * cols, cols), cols)
        pairs += [(w.at[:, lanes], out.at[pl.ds(j * depth, depth)]) for j, w in enumerate(sources)]
    wait_all(start_all(pairs, sems, 0))


def loaded_weights(place, ats, weights, cols):
    depth = weights[0].shape[0]
    count = len(weights)
    return pl.pallas_call(
        functools.partial(loaded_body, ats),
        out_shape=[f32(count * depth, cols)] * len(ats),
        in_specs=[SMEM] + [HBM] * count,
        out_specs=[VMEM] * len(ats),
        scratch_shapes=[pltpu.SemaphoreType.DMA((count * len(ats),))],
        compiler_params=PARAMS,
        cost_estimate=cost(0),
    )(place, *pinned(weights[0]), *weights[1:])


def remote_body(count, *refs):
    lefts, refs = refs[:count], refs[count:]
    groups = len(refs) // (1 + lefts[0].shape[1] // refs[-1].shape[1])
    weights, outs = refs[:groups], refs[groups:]
    chunk = outs[0].shape[1]
    chunks = len(outs) // groups
    depth = lefts[0].shape[1]
    for n, weight in enumerate(weights):
        parts = [right_parts(weight[pl.ds(j * depth, depth), :]) for j in range(count)]
        made = sum_of_products([x[...] for x in lefts], parts)
        for c in range(chunks):
            outs[n * chunks + c][...] = made[:, c * chunk : (c + 1) * chunk]


def remote_products(lefts, weights, chunks):
    rows, cols = lefts[0].shape
    outs = len(weights) * chunks
    return pl.pallas_call(
        functools.partial(remote_body, len(lefts)),
        out_shape=[f32(rows, cols // chunks)] * outs,
        in_specs=[VMEM] * (len(lefts) + len(weights)),
        out_specs=[VMEM] * outs,
        compiler_params=PARAMS,
        cost_estimate=cost(0),
    )(*lefts, *weights)


def joined_body(plan, count, *refs):
    stored, refs = refs[:count], refs[count:]
    fresh, refs = refs[: len(plan) - count], refs[len(plan) - count :]
    held, sems, outs = refs[-1 - count : -1], refs[-1], refs[: -1 - count]
    loads = start_all(list(zip(stored, held)), sems, 0)
    places = [outs[o].at[pl.ds(offset, x.shape[0])] for x, (o, offset) in zip([*stored, *fresh], plan)]
    stores = start_all(list(zip(fresh, places[count:])), sems, count)
    for j in range(count):
        loads[j].wait()
        stores += start_all([(held[j], places[j])], sems, len(plan) + j)
    wait_all(stores)


def joined(stored, fresh, plan, shapes):
    count = len(stored)
    return pl.pallas_call(
        functools.partial(joined_body, plan, count),
        out_shape=[hbm(*s) for s in shapes],
        in_specs=[HBM] * count + [VMEM] * len(fresh),
        out_specs=[HBM] * len(shapes),
        scratch_shapes=[scratch(*x.shape) for x in stored]
        + [pltpu.SemaphoreType.DMA((len(plan) + count,))],
        compiler_params=PARAMS,
        cost_estimate=cost(0),
    )(*pinned(*stored), *fresh)


def chosen_body(source_ref, incoming, chosen):
    tile = incoming.shape[1]
    for g in range(chosen.shape[0] // tile):
        chosen[pl.ds(g * tile, tile), :] = incoming[source_ref[TOUCH * g]]


def chosen_blocks(source, incoming):
    tile, cols = incoming.shape[1:]
    groups = source.shape[0] // TOUCH
    return pl.pallas_call(
        chosen_body,
        out_shape=f32(groups * tile, cols),
        in_specs=[SMEM, VMEM],
        out_specs=VMEM,
        compiler_params=PARAMS,
        cost_estimate=cost(0),
    )(source, incoming)


def received_pairs(layout, received, recv_in):
    return [
        (received[r].at[pl.ds(start, stop - start)], recv_in.at[h, pl.ds(offset, stop - start)])
        for h, r, start, stop, offset in layout
    ]


def own_total(diag_in, spread_in, own_in, recv_in, total):
    tile = diag_in.shape[1]
    for i in range(diag_in.shape[0] // tile):
        rows = pl.ds(i * tile, tile)
        mixed = own_in[rows, :]
        for h in range(recv_in.shape[0]):
            mixed = mixed + recv_in[h, rows, :]
        total[rows, :] = dot3(diag_in[rows, :], mixed * spread_in[rows, :])


def own_body(layout, diag, spread, own, *refs):
    received, (base, diag_in, spread_in, own_in, recv_in, sems) = refs[:-6], refs[-6:]
    pairs = [(diag, diag_in), (spread, spread_in), (own, own_in)]
    wait_all(start_all(pairs + received_pairs(layout, received, recv_in), sems, 0))
    own_total(diag_in, spread_in, own_in, recv_in, base)


def own_part(diag, spread, own, received, layout, others):
    return pl.pallas_call(
        functools.partial(own_body, layout),
        out_shape=f32(*own.shape),
        in_specs=[HBM] * (3 + len(received)),
        out_specs=VMEM,
        scratch_shapes=[scratch(*a.shape) for a in (diag, spread, own)]
        + [scratch(others, *own.shape), pltpu.SemaphoreType.DMA((3 + len(layout),))],
        compiler_params=PARAMS,
        cost_estimate=cost(0),
    )(*pinned(diag, spread, own), *received)


def hidden_tail(
    lane_offset, row_ref, want_ref, first_ref, bias, remote, spread, sums, blocks, scaled_out, total, scaled, sems, used
):
    tiles, tile = remote.shape[:2]
    parts = blocks.shape[0]
    chunk = total.shape[1]
    for g in range(tiles // TOUCH):
        block = sums[0][pl.ds(g * tile, tile), :]
        for x in sums[1:]:
            block = block + x[pl.ds(g * tile, tile), :]
        for k in range(TOUCH * g, TOUCH * g + TOUCH):
            total[rows_at(row_ref[k], tile), :] += dot3(remote[k], block)
    lanes = pl.ds(pl.multiple_of(first_ref[0] + lane_offset, chunk), chunk)
    scaled[...] = jnp.maximum(total[...] * spread[...] + bias[:, lanes], 0.0) * spread[...]
    last = scaled.shape[0] // tile - 1
    pairs = [(scaled.at[rows_at(jnp.minimum(want_ref[d], last), tile)], blocks.at[d]) for d in range(parts)]
    wait_all(start_all(pairs + [(scaled, scaled_out)], sems, used))


def hidden_body(lane_offset, row_ref, want_ref, first_ref, bias, base, remote, spread, *refs):
    sums, (blocks, scaled_out, total, scaled, sems) = refs[:-5], refs[-5:]
    total[...] = base[...]
    hidden_tail(
        lane_offset, row_ref, want_ref, first_ref, bias, remote, spread, sums, blocks, scaled_out, total, scaled, sems, 0
    )


def hidden_blocks(row, want, first, lane_offset, bias, base, remote, spread, remote_sums):
    rows, chunk = base.shape
    tile = remote.shape[1]
    parts = want.shape[0]
    return pl.pallas_call(
        functools.partial(hidden_body, lane_offset),
        out_shape=[hbm(parts, tile, chunk), hbm(rows, chunk)],
        in_specs=[SMEM] * 3 + [VMEM] * (4 + len(remote_sums)),
        out_specs=[HBM, HBM],
        scratch_shapes=[scratch(rows, chunk), scratch(rows, chunk), pltpu.SemaphoreType.DMA((parts + 1,))],
        compiler_params=PARAMS,
        cost_estimate=cost(HINT),
    )(row, want, first, bias, base, remote, spread, *remote_sums)


def resident_body(count, *refs):
    wait_all(start_all(list(zip(refs[:count], refs[count:-1])), refs[-1], 0))


def resident(*arrays):
    count = len(arrays)
    return pl.pallas_call(
        functools.partial(resident_body, count),
        out_shape=[f32(*a.shape) for a in arrays],
        in_specs=[HBM] * count,
        out_specs=[VMEM] * count,
        scratch_shapes=[pltpu.SemaphoreType.DMA((count,))],
        compiler_params=PARAMS,
        cost_estimate=cost(0),
    )(*pinned(*arrays))


def later_body(
    ends, layout, lane_offset, row_ref, want_ref, first_ref, bias, own, remote, spread, diag, own_sum, *refs
):
    received, refs = refs[:-7], refs[-7:]
    blocks, scaled_out, total, scaled, sums_in, recv_in, sems = refs
    others, height = sums_in.shape[:2]
    pairs = received_pairs(layout, received, recv_in)
    late = [(r.at[pl.ds(ends - height, height)], sums_in.at[j]) for j, r in enumerate(received[-others:])]
    first = start_all(pairs, sems, 0)
    tail = start_all(late, sems, len(pairs))
    wait_all(first)
    own_total(diag, spread, own, recv_in, total)
    wait_all(tail)
    sums = [own_sum] + [sums_in.at[j] for j in range(others)]
    hidden_tail(
        lane_offset,
        row_ref,
        want_ref,
        first_ref,
        bias,
        remote,
        spread,
        sums,
        blocks,
        scaled_out,
        total,
        scaled,
        sems,
        len(pairs) + len(late),
    )


def later_blocks(
    row, want, first, lane_offset, bias, own, remote, spread, diag, own_sum, received, layout, ends, others
):
    rows, chunk = own.shape
    tile = diag.shape[1]
    parts = want.shape[0]
    return pl.pallas_call(
        functools.partial(later_body, ends, layout, lane_offset),
        out_shape=[hbm(parts, tile, chunk), hbm(rows, chunk)],
        in_specs=[SMEM] * 3 + [VMEM] * 6 + [HBM] * len(received),
        out_specs=[HBM, HBM],
        scratch_shapes=[scratch(rows, chunk), scratch(rows, chunk)]
        + [scratch(others, *own_sum.shape), scratch(others, rows, chunk)]
        + [pltpu.SemaphoreType.DMA((len(layout) + others + parts + 1,))],
        compiler_params=PARAMS,
        cost_estimate=cost(HINT),
    )(row, want, first, bias, own, remote, spread, diag, own_sum, *received)


def diagonal_body(diag, scaled, base, diag_in, scaled_in, total, sems):
    tile = diag.shape[1]
    wait_all(start_all([(diag, diag_in), (scaled, scaled_in)], sems, 0))
    for i in range(diag.shape[0] // tile):
        rows = pl.ds(i * tile, tile)
        total[rows, :] = dot3(diag_in[rows, :], scaled_in[rows, :])
    wait_all(start_all([(total, base)], sems, 2))


def diagonal_part(diag, scaled):
    return pl.pallas_call(
        diagonal_body,
        out_shape=hbm(*scaled.shape),
        in_specs=[HBM, HBM],
        out_specs=HBM,
        scratch_shapes=[scratch(*a.shape) for a in (diag, scaled, scaled)] + [pltpu.SemaphoreType.DMA((3,))],
        compiler_params=PARAMS,
        cost_estimate=cost(0),
    )(*pinned(diag, scaled))


def pieces_body(stored, source_ref, row_ref, place_ref, base, remote, spread, incoming, *refs):
    pieces, (total, remote_in, spread_in, incoming_in, sems) = refs[:-5], refs[-5:]
    tiles, tile = remote.shape[:2]
    early = start_all(
        [(incoming, incoming_in), (remote, remote_in), (base, total), (spread, spread_in)], sems, 0
    )
    wait_all(early[:3])
    for k in range(tiles):
        total[rows_at(row_ref[k], tile), :] += dot3(remote_in[k], incoming_in[source_ref[k]])
    wait_all(early[3:])
    height = pieces[0].shape[0]
    copies = []
    for j in reversed(range(len(pieces))):
        rows = rows_at(place_ref[j], height)
        made = total[rows, :] * spread_in[rows, :]
        if stored:
            total[rows, :] = made
            copies += start_all([(total.at[rows], pieces[j])], sems, 4 + j)
        else:
            pieces[j][...] = made
    wait_all(copies)


def feature_pieces(source, row, place, base, remote, spread, incoming, stored):
    rows, chunk = base.shape
    feats = place.shape[0]
    make = hbm if stored else f32
    return pl.pallas_call(
        functools.partial(pieces_body, stored),
        out_shape=[make(rows // feats, chunk)] * feats,
        in_specs=[SMEM] * 3 + [HBM] * 4,
        out_specs=[HBM if stored else VMEM] * feats,
        scratch_shapes=[scratch(*a.shape) for a in (base, remote, spread, incoming)]
        + [pltpu.SemaphoreType.DMA((4 + feats,))],
        compiler_params=PARAMS,
        cost_estimate=cost(0),
    )(source, row, place, *pinned(base, remote, spread), incoming)


def chosen_block(weights, number, turn, c, chunk, lanes):
    rows = pl.ds(c * chunk if weights[0].shape[0] > chunk else 0, chunk)
    block = weights[0][rows, lanes]
    for k in range(1, number):
        block = jnp.where(turn == k, weights[k][rows, lanes], block)
    return block


def product_body(count, choices, later, c, step, last, turn_ref, start, *refs):
    pieces, refs = refs[:count], refs[count:]
    weights, refs = refs[: sum(choices)], refs[sum(choices) :]
    ahead, refs = refs[: sum(later)], refs[sum(later) :]
    kept, (out, left, held, sems) = refs[: len(later)], refs[len(later) :]
    chunk = pieces[0].shape[1]
    left[...] = left_parts(jnp.concatenate([p[...] for p in pieces], axis=1))
    copies = []
    for j in range(held.shape[1] // step):
        lanes = pl.ds(j * step, step)
        blocks, at = [], 0
        for number in choices:
            blocks.append(chosen_block(weights[at:], number, turn_ref[0], c, chunk, lanes))
            at += number
        right = right_parts(jnp.concatenate(blocks, axis=0))
        made = start[:, lanes] + jnp.dot(left[...], right, preferred_element_type=jnp.float32)
        if last:
            held[:, lanes] = made
            copies += start_all([(held.at[:, lanes], out.at[:, lanes])], sems, j)
        else:
            out[:, lanes] = made
    at = 0
    for number, block in zip(later, kept):
        block[...] = chosen_block(ahead[at:], number, turn_ref[0], c, chunk, pl.ds(0, held.shape[1]))
        at += number
    wait_all(copies)


def add_product(turn, start, pieces, weights, c, last, ahead=()):
    rows, chunk = pieces[0].shape
    width = start.shape[1]
    step = min(2 * LANES, width)
    count = len(pieces)
    flat = [w for group in [*weights, *ahead] for w in group]
    choices, later = [len(group) for group in weights], [len(group) for group in ahead]
    return pl.pallas_call(
        functools.partial(product_body, count, choices, later, c, step, last),
        out_shape=[f32(chunk, width)] * len(later) + [hbm(rows, width) if last else f32(rows, width)],
        in_specs=[SMEM] + [VMEM] * (1 + count + len(flat)),
        out_specs=[VMEM] * len(later) + [HBM if last else VMEM],
        scratch_shapes=[
            pltpu.VMEM((rows, 3 * count * chunk), jnp.bfloat16),
            scratch(rows, width),
            pltpu.SemaphoreType.DMA((width // step,)),
        ],
        compiler_params=PARAMS,
        cost_estimate=cost(6 * count * rows * chunk * width),
    )(turn, start, *pieces, *flat)


def solution(mesh):
    parts = mesh.shape["dom"]
    feats = mesh.shape["feat"]
    sides = 2 if feats % 2 == 0 else 1
    halves = feats // sides
    others = list(range(1, halves))

    def feat_target(f, dh, dl):
        return (f // sides + dh) % halves * sides + (f % sides + dl) % sides

    def feat_send(x, dh, dl):
        return lax.ppermute(x, "feat", [(f, feat_target(f, dh, dl)) for f in range(feats)])

    def dom_exchange(x):
        return lax.all_to_all(x, "dom", split_axis=0, concat_axis=0, tiled=True)

    def per_device(
        features,
        degree,
        diag_adj,
        remote_adj,
        read_block,
        tile_src,
        tile_row,
        w_first,
        b_first,
        w_second,
        b_second,
    ):
        part, cols = features.shape
        tile = diag_adj.shape[1]
        blocks = part // tile
        remote = remote_adj[0]
        chunk = LANES if cols % LANES == 0 else cols
        chunks = cols // chunk
        f = lax.axis_index("feat")
        want, source, row = read_block[0], tile_src[0], tile_row[0]
        shifts = [(dh, dl) for dh in range(halves) for dl in range(sides)]
        place = jnp.stack([jnp.asarray(feat_target(f, dh, dl), jnp.int32) for dh, dl in shifts])
        first = jnp.reshape(jnp.asarray(f * cols, jnp.int32), (1,))
        bias = b_first[None, :]

        x_all = [features] + [feat_send(features, 0, dl) for dl in range(1, sides)]
        w_all = [w_first] + [feat_send(w_first, 0, dl) for dl in range(1, sides)]

        shares = chunks if parts % chunks == 0 else 1
        share = jnp.reshape(jnp.asarray(lax.axis_index("dom") % shares, jnp.int32), (1,))

        def share_send(x, k):
            pairs = [(s, s // shares * shares + (s % shares + k) % shares) for s in range(parts)]
            return lax.ppermute(x, "dom", pairs)

        w2_sent = lax.select_n(share[0], *jnp.split(w_second, shares)) if shares > 1 else w_second
        w2_got = [feat_send(w2_sent, dh, 0) for dh in others]

        scaling = lax.rsqrt(degree.astype(jnp.float32))
        spread = jnp.broadcast_to(scaling[:, None], (part, chunk))
        outgoing = outgoing_blocks(want, features, spread, tile)
        incoming = dom_exchange(outgoing)

        early = blocks // 4 * tile if chunks > 1 else part
        late = part - early
        marks = sorted({0, early // 2 // tile * tile, early, early + late // 2 // tile * tile, part})
        spans = list(zip(marks[:-1], marks[1:]))
        x_all[0], _ = lax.optimization_barrier((features, outgoing))
        send_steps = []
        for start, stop in spans:
            targets = [(0, 0, start)]
            for c in range(1, chunks):
                if stop <= early:
                    targets.append((c, 0, part + (c - 1) * early + start))
                else:
                    targets.append((c, 1, (c - 1) * late + start - early))
            send_steps.append((start, stop, targets))
        send_shapes = [(part + (chunks - 1) * early, chunk)]
        if late > 0:
            send_shapes.append(((chunks - 1) * late, chunk))
        sends = [partial_sums(place, [(dh * sides, send_steps)], x_all, w_all, send_shapes) for dh in others]
        sends, w2_got = lax.optimization_barrier((sends, w2_got))
        front = [feat_send(x[0], dh, 0) for dh, x in zip(others, sends)]

        own_steps = [(a, b, [(c, c, a) for c in range(chunks)]) for a, b in spans]
        own = list(partial_sums(place, [(0, own_steps)], x_all, w_all, [(part, chunk)] * chunks, HINT))

        incoming, own = lax.optimization_barrier((incoming, list(own)))
        w2_core = [w_second] + [feat_send(w_second, 0, dl) for dl in range(1, sides)]
        chosen = chosen_blocks(source, incoming)
        chosen_all = [chosen] + [feat_send(chosen, 0, dl) for dl in range(1, sides)]
        height = chosen.shape[0]
        tail_rows = (chunks - 1) * late
        ats = [dh * sides for dh in others] + [0]
        turned, _ = lax.optimization_barrier((place, chosen))
        made = remote_products(chosen_all, loaded_weights(turned, ats, w_all, cols), chunks)
        remote_front = [feat_send(made[i * chunks], dh, 0) for i, dh in enumerate(others)]
        remote_own = list(made[len(others) * chunks :])
        rest = []
        if chunks > 1:
            stored, kept, fresh, turned_in, shapes = [], [], [], [], []
            for i, x in enumerate(sends):
                kept += [(i, 0)] * len(x[1:])
                stored += x[1:]
                for c in range(1, chunks):
                    fresh.append(made[i * chunks + c])
                    turned_in.append((i, tail_rows + (c - 1) * height))
                shapes.append((tail_rows + (chunks - 1) * height, chunk))
            for c in range(1, chunks):
                fresh.append(remote_own[c])
                turned_in.append((len(shapes), 0))
                shapes.append((height, chunk))
            written = joined(stored, fresh, kept + turned_in, shapes)
            rest = [feat_send(x, dh, 0) for dh, x in zip(others, written)]
            remote_own[1:] = written[len(others) :]

        reach = len(others)
        first_layout = [(h, h, 0, part, 0) for h in range(reach)]
        base = own_part(diag_adj, spread, own[0], front, first_layout, reach)
        collected = []
        outgoing = None
        for c in range(chunks):
            if c == 0:
                outgoing, scaled = hidden_blocks(
                    row, want, first, 0, bias, base, remote, spread, [remote_own[0]] + remote_front
                )
            else:
                begin, _ = lax.optimization_barrier((own[c], base_next))
                held = resident(begin, remote, spread, diag_adj, remote_own[c])
                layout = []
                for h in range(reach):
                    layout.append((h, h, part + (c - 1) * early, part + c * early, 0))
                    if late > 0:
                        layout.append((h, reach + h, (c - 1) * late, c * late, early))
                outgoing, scaled = later_blocks(
                    row, want, first, c * chunk, bias, *held, front + rest, layout, tail_rows + c * height, reach
                )
            incoming = dom_exchange(outgoing)
            if c < chunks - 1:
                incoming = pinned(incoming)[0]
            base_next = diagonal_part(diag_adj, scaled)
            if c == 0:
                w2_got, _ = lax.optimization_barrier((w2_got, base_next))
            pieces = feature_pieces(source, row, place, base_next, remote, spread, incoming, c < chunks - 1)
            collected.append(
                [p if dh == 0 and dl == 0 else feat_send(p, dh, dl) for (dh, dl), p in zip(shifts, pieces)]
            )

        w2_groups = [[got] + [share_send(got, k) for k in range(1, shares)] for got in w2_got]
        w2_groups, _ = lax.optimization_barrier((w2_groups, outgoing))
        w2_far = [[feat_send(w, 0, dl) if dl > 0 else w for w in g] for g in w2_groups for dl in range(sides)]
        weights = [[w] for w in w2_core] + w2_far
        out = b_second[None, :]
        for c in range(chunks):
            turn = (share - c) % shares
            if c < chunks - 1 or halves == 1:
                (out,) = add_product(turn, out, collected[c], weights, c, c == chunks - 1)
            else:
                near, far = collected[c][:sides], collected[c][sides:]
                *kept, out = add_product(turn, out, near, weights[:sides], c, False, weights[sides:])
                (out,) = add_product(turn, out, far, [[w] for w in kept], c, True)
        return out

    return jax.shard_map(
        per_device,
        mesh=mesh,
        in_specs=(
            P("dom", "feat"),
            P("dom"),
            P("dom", None),
            P("dom", None, None, None),
            P("dom", None),
            P("dom", None),
            P("dom", None),
            P("feat", None),
            P(),
            P("feat", None),
            P(),
        ),
        out_specs=P(("dom", "feat"), None),
        check_vma=False,
    )
```

```python
import functools

import jax
import jax.numpy as jnp
from jax import lax
from jax.experimental import pallas as pl
from jax.experimental.pallas import tpu as pltpu
from jax.sharding import PartitionSpec as P

LANES = 128
TOUCH = 2
HINT = 5 * 10**10
VMEM_LIMIT = 24 * 1024 * 1024
VMEM = pl.BlockSpec(memory_space=pltpu.VMEM)
SMEM = pl.BlockSpec(memory_space=pltpu.SMEM)
HBM = pl.BlockSpec(memory_space=pltpu.HBM)
PARAMS = pltpu.CompilerParams(vmem_limit_bytes=VMEM_LIMIT)


def dot3(a, b):
    return jnp.dot(a, b, precision=lax.Precision.HIGH, preferred_element_type=jnp.float32)


def two_parts(x):
    high = x.astype(jnp.bfloat16)
    return high, (x - high.astype(jnp.float32)).astype(jnp.bfloat16)


def left_parts(x):
    high, low = two_parts(x)
    return jnp.concatenate([high, low, high], axis=1)


def right_parts(w):
    high, low = two_parts(w)
    return jnp.concatenate([high, high, low], axis=0)


def sum_of_products(lefts, parts):
    total = None
    for x, part in zip(lefts, parts):
        made = jnp.dot(left_parts(x), part, preferred_element_type=jnp.float32)
        total = made if total is None else total + made
    return total


def f32(*dims):
    return jax.ShapeDtypeStruct(dims, jnp.float32)


def hbm(*dims):
    return pltpu.HBM(dims, jnp.float32)


def pinned(*arrays):
    return [pltpu.with_memory_space_constraint(a, pltpu.HBM) for a in arrays]


def rows_at(index, height):
    return pl.ds(pl.multiple_of(index * height, height), height)


def scratch(*dims):
    return pltpu.VMEM(dims, jnp.float32)


def start_all(pairs, sems, first):
    copies = [pltpu.make_async_copy(a, b, sems.at[first + i]) for i, (a, b) in enumerate(pairs)]
    for copy in copies:
        copy.start()
    return copies


def wait_all(copies):
    for copy in copies:
        copy.wait()


def cost(flops):
    return pl.CostEstimate(flops=flops, bytes_accessed=0, transcendentals=0)


def outgoing_body(want_ref, features, spread, blocks, held, sems):
    count, tile, cols = held.shape
    chunk = spread.shape[1]
    last = features.shape[0] // tile - 1
    copies = []
    for d in range(count):
        rows = rows_at(jnp.minimum(want_ref[d], last), tile)
        for c in range(cols // chunk):
            lanes = pl.ds(c * chunk, chunk)
            held[d, :, lanes] = features[rows, lanes] * spread[rows, :]
        copies += start_all([(held.at[d], blocks.at[d])], sems, d)
    wait_all(copies)


def outgoing_blocks(want, features, spread, tile):
    cols = features.shape[1]
    count = want.shape[0]
    return pl.pallas_call(
        outgoing_body,
        out_shape=hbm(count, tile, cols),
        in_specs=[SMEM, VMEM, VMEM],
        out_specs=HBM,
        scratch_shapes=[scratch(count, tile, cols), pltpu.SemaphoreType.DMA((count,))],
        compiler_params=PARAMS,
        cost_estimate=cost(HINT),
    )(want, features, spread)


def partial_body(count, groups, place_ref, *refs):
    lefts, rights, refs = refs[:count], refs[count : 2 * count], refs[2 * count :]
    outs, (left, right, result, sems) = refs[:-4], refs[-4:]
    cols = lefts[0].shape[1]
    chunk = outs[0].shape[1]
    used = 0
    weights_in, loads, stores = [], [], []
    for n, (at, _) in enumerate(groups):
        lanes = pl.ds(pl.multiple_of(place_ref[at] * cols, cols), cols)
        weights_in.append(start_all([(w.at[:, lanes], right.at[n, j]) for j, w in enumerate(rights)], sems, used))
        used += count
    for start, stop, _ in groups[0][1]:
        rows = pl.ds(start, stop - start)
        pairs = [(x.at[rows], left.at[rows, pl.ds(j * cols, cols)]) for j, x in enumerate(lefts)]
        loads.append(start_all(pairs, sems, used))
        used += count
    for n, (_, steps) in enumerate(groups):
        wait_all(weights_in[n])
        parts = [right_parts(right[n, j]) for j in range(count)]
        for i, (start, stop, targets) in enumerate(steps):
            if n == 0:
                wait_all(loads[i])
            rows = pl.ds(start, stop - start)
            made = sum_of_products([left[rows, pl.ds(j * cols, cols)] for j in range(count)], parts)
            result[n, rows, :] = made
            pairs = [
                (result.at[n, rows, pl.ds(c * chunk, chunk)], outs[o].at[pl.ds(offset, stop - start)])
                for c, o, offset in targets
            ]
            stores += start_all(pairs, sems, used)
            used += len(pairs)
    wait_all(stores)


def partial_sums(place, groups, lefts, weights, shapes, flops=0):
    rows, cols = lefts[0].shape
    depth = weights[0].shape[0]
    count = len(lefts)
    copies = count * (len(groups) + len(groups[0][1]))
    copies += sum(len(targets) for _, steps in groups for _, _, targets in steps)
    return pl.pallas_call(
        functools.partial(partial_body, count, groups),
        out_shape=[hbm(*s) for s in shapes],
        in_specs=[SMEM] + [HBM] * (2 * count),
        out_specs=[HBM] * len(shapes),
        scratch_shapes=[
            scratch(rows, count * cols),
            scratch(len(groups), count, depth, cols),
            scratch(len(groups), rows, cols),
            pltpu.SemaphoreType.DMA((copies,)),
        ],
        compiler_params=PARAMS,
        cost_estimate=cost(flops),
    )(place, *pinned(lefts[0]), *lefts[1:], *pinned(weights[0]), *weights[1:])


def loaded_body(ats, place_ref, *refs):
    sources, outs, sems = refs[: -1 - len(ats)], refs[-1 - len(ats) : -1], refs[-1]
    depth = sources[0].shape[0]
    pairs = []
    for at, out in zip(ats, outs):
        cols = out.shape[1]
        lanes = pl.ds(pl.multiple_of(place_ref[at] * cols, cols), cols)
        pairs += [(w.at[:, lanes], out.at[pl.ds(j * depth, depth)]) for j, w in enumerate(sources)]
    wait_all(start_all(pairs, sems, 0))


def loaded_weights(place, ats, weights, cols):
    depth = weights[0].shape[0]
    count = len(weights)
    return pl.pallas_call(
        functools.partial(loaded_body, ats),
        out_shape=[f32(count * depth, cols)] * len(ats),
        in_specs=[SMEM] + [HBM] * count,
        out_specs=[VMEM] * len(ats),
        scratch_shapes=[pltpu.SemaphoreType.DMA((count * len(ats),))],
        compiler_params=PARAMS,
        cost_estimate=cost(0),
    )(place, *pinned(weights[0]), *weights[1:])


def remote_body(count, *refs):
    lefts, refs = refs[:count], refs[count:]
    groups = len(refs) // (1 + lefts[0].shape[1] // refs[-1].shape[1])
    weights, outs = refs[:groups], refs[groups:]
    chunk = outs[0].shape[1]
    chunks = len(outs) // groups
    depth = lefts[0].shape[1]
    for n, weight in enumerate(weights):
        parts = [right_parts(weight[pl.ds(j * depth, depth), :]) for j in range(count)]
        made = sum_of_products([x[...] for x in lefts], parts)
        for c in range(chunks):
            outs[n * chunks + c][...] = made[:, c * chunk : (c + 1) * chunk]


def remote_products(lefts, weights, chunks):
    rows, cols = lefts[0].shape
    outs = len(weights) * chunks
    return pl.pallas_call(
        functools.partial(remote_body, len(lefts)),
        out_shape=[f32(rows, cols // chunks)] * outs,
        in_specs=[VMEM] * (len(lefts) + len(weights)),
        out_specs=[VMEM] * outs,
        compiler_params=PARAMS,
        cost_estimate=cost(0),
    )(*lefts, *weights)


def joined_body(plan, count, *refs):
    stored, refs = refs[:count], refs[count:]
    fresh, refs = refs[: len(plan) - count], refs[len(plan) - count :]
    held, sems, outs = refs[-1 - count : -1], refs[-1], refs[: -1 - count]
    loads = start_all(list(zip(stored, held)), sems, 0)
    places = [outs[o].at[pl.ds(offset, x.shape[0])] for x, (o, offset) in zip([*stored, *fresh], plan)]
    stores = start_all(list(zip(fresh, places[count:])), sems, count)
    for j in range(count):
        loads[j].wait()
        stores += start_all([(held[j], places[j])], sems, len(plan) + j)
    wait_all(stores)


def joined(stored, fresh, plan, shapes):
    count = len(stored)
    return pl.pallas_call(
        functools.partial(joined_body, plan, count),
        out_shape=[hbm(*s) for s in shapes],
        in_specs=[HBM] * count + [VMEM] * len(fresh),
        out_specs=[HBM] * len(shapes),
        scratch_shapes=[scratch(*x.shape) for x in stored]
        + [pltpu.SemaphoreType.DMA((len(plan) + count,))],
        compiler_params=PARAMS,
        cost_estimate=cost(0),
    )(*pinned(*stored), *fresh)


def chosen_body(source_ref, incoming, chosen):
    tile = incoming.shape[1]
    for g in range(chosen.shape[0] // tile):
        chosen[pl.ds(g * tile, tile), :] = incoming[source_ref[TOUCH * g]]


def chosen_blocks(source, incoming):
    tile, cols = incoming.shape[1:]
    groups = source.shape[0] // TOUCH
    return pl.pallas_call(
        chosen_body,
        out_shape=f32(groups * tile, cols),
        in_specs=[SMEM, VMEM],
        out_specs=VMEM,
        compiler_params=PARAMS,
        cost_estimate=cost(0),
    )(source, incoming)


def received_pairs(layout, received, recv_in):
    return [
        (received[r].at[pl.ds(start, stop - start)], recv_in.at[h, pl.ds(offset, stop - start)])
        for h, r, start, stop, offset in layout
    ]


def own_total(diag_in, spread_in, own_in, recv_in, total):
    tile = diag_in.shape[1]
    for i in range(diag_in.shape[0] // tile):
        rows = pl.ds(i * tile, tile)
        mixed = own_in[rows, :]
        for h in range(recv_in.shape[0]):
            mixed = mixed + recv_in[h, rows, :]
        total[rows, :] = dot3(diag_in[rows, :], mixed * spread_in[rows, :])


def own_body(layout, diag, spread, own, *refs):
    received, (base, diag_in, spread_in, own_in, recv_in, sems) = refs[:-6], refs[-6:]
    pairs = [(diag, diag_in), (spread, spread_in), (own, own_in)]
    wait_all(start_all(pairs + received_pairs(layout, received, recv_in), sems, 0))
    own_total(diag_in, spread_in, own_in, recv_in, base)


def own_part(diag, spread, own, received, layout, others):
    return pl.pallas_call(
        functools.partial(own_body, layout),
        out_shape=f32(*own.shape),
        in_specs=[HBM] * (3 + len(received)),
        out_specs=VMEM,
        scratch_shapes=[scratch(*a.shape) for a in (diag, spread, own)]
        + [scratch(others, *own.shape), pltpu.SemaphoreType.DMA((3 + len(layout),))],
        compiler_params=PARAMS,
        cost_estimate=cost(0),
    )(*pinned(diag, spread, own), *received)


def hidden_tail(
    lane_offset, row_ref, want_ref, first_ref, bias, remote, spread, sums, blocks, scaled_out, total, scaled, sems, used
):
    tiles, tile = remote.shape[:2]
    parts = blocks.shape[0]
    chunk = total.shape[1]
    for g in range(tiles // TOUCH):
        block = sums[0][pl.ds(g * tile, tile), :]
        for x in sums[1:]:
            block = block + x[pl.ds(g * tile, tile), :]
        for k in range(TOUCH * g, TOUCH * g + TOUCH):
            total[rows_at(row_ref[k], tile), :] += dot3(remote[k], block)
    lanes = pl.ds(pl.multiple_of(first_ref[0] + lane_offset, chunk), chunk)
    scaled[...] = jnp.maximum(total[...] * spread[...] + bias[:, lanes], 0.0) * spread[...]
    last = scaled.shape[0] // tile - 1
    pairs = [(scaled.at[rows_at(jnp.minimum(want_ref[d], last), tile)], blocks.at[d]) for d in range(parts)]
    wait_all(start_all(pairs + [(scaled, scaled_out)], sems, used))


def hidden_body(lane_offset, row_ref, want_ref, first_ref, bias, base, remote, spread, *refs):
    sums, (blocks, scaled_out, total, scaled, sems) = refs[:-5], refs[-5:]
    total[...] = base[...]
    hidden_tail(
        lane_offset, row_ref, want_ref, first_ref, bias, remote, spread, sums, blocks, scaled_out, total, scaled, sems, 0
    )


def hidden_blocks(row, want, first, lane_offset, bias, base, remote, spread, remote_sums):
    rows, chunk = base.shape
    tile = remote.shape[1]
    parts = want.shape[0]
    return pl.pallas_call(
        functools.partial(hidden_body, lane_offset),
        out_shape=[hbm(parts, tile, chunk), hbm(rows, chunk)],
        in_specs=[SMEM] * 3 + [VMEM] * (4 + len(remote_sums)),
        out_specs=[HBM, HBM],
        scratch_shapes=[scratch(rows, chunk), scratch(rows, chunk), pltpu.SemaphoreType.DMA((parts + 1,))],
        compiler_params=PARAMS,
        cost_estimate=cost(HINT),
    )(row, want, first, bias, base, remote, spread, *remote_sums)


def resident_body(count, *refs):
    wait_all(start_all(list(zip(refs[:count], refs[count:-1])), refs[-1], 0))


def resident(*arrays):
    count = len(arrays)
    return pl.pallas_call(
        functools.partial(resident_body, count),
        out_shape=[f32(*a.shape) for a in arrays],
        in_specs=[HBM] * count,
        out_specs=[VMEM] * count,
        scratch_shapes=[pltpu.SemaphoreType.DMA((count,))],
        compiler_params=PARAMS,
        cost_estimate=cost(0),
    )(*pinned(*arrays))


def later_body(
    ends, layout, lane_offset, row_ref, want_ref, first_ref, bias, own, remote, spread, diag, own_sum, *refs
):
    received, refs = refs[:-7], refs[-7:]
    blocks, scaled_out, total, scaled, sums_in, recv_in, sems = refs
    others, height = sums_in.shape[:2]
    pairs = received_pairs(layout, received, recv_in)
    late = [(r.at[pl.ds(ends - height, height)], sums_in.at[j]) for j, r in enumerate(received[-others:])]
    first = start_all(pairs, sems, 0)
    tail = start_all(late, sems, len(pairs))
    wait_all(first)
    own_total(diag, spread, own, recv_in, total)
    wait_all(tail)
    sums = [own_sum] + [sums_in.at[j] for j in range(others)]
    hidden_tail(
        lane_offset,
        row_ref,
        want_ref,
        first_ref,
        bias,
        remote,
        spread,
        sums,
        blocks,
        scaled_out,
        total,
        scaled,
        sems,
        len(pairs) + len(late),
    )


def later_blocks(
    row, want, first, lane_offset, bias, own, remote, spread, diag, own_sum, received, layout, ends, others
):
    rows, chunk = own.shape
    tile = diag.shape[1]
    parts = want.shape[0]
    return pl.pallas_call(
        functools.partial(later_body, ends, layout, lane_offset),
        out_shape=[hbm(parts, tile, chunk), hbm(rows, chunk)],
        in_specs=[SMEM] * 3 + [VMEM] * 6 + [HBM] * len(received),
        out_specs=[HBM, HBM],
        scratch_shapes=[scratch(rows, chunk), scratch(rows, chunk)]
        + [scratch(others, *own_sum.shape), scratch(others, rows, chunk)]
        + [pltpu.SemaphoreType.DMA((len(layout) + others + parts + 1,))],
        compiler_params=PARAMS,
        cost_estimate=cost(HINT),
    )(row, want, first, bias, own, remote, spread, diag, own_sum, *received)


def diagonal_body(diag, scaled, base, diag_in, scaled_in, total, sems):
    tile = diag.shape[1]
    wait_all(start_all([(diag, diag_in), (scaled, scaled_in)], sems, 0))
    for i in range(diag.shape[0] // tile):
        rows = pl.ds(i * tile, tile)
        total[rows, :] = dot3(diag_in[rows, :], scaled_in[rows, :])
    wait_all(start_all([(total, base)], sems, 2))


def diagonal_part(diag, scaled):
    return pl.pallas_call(
        diagonal_body,
        out_shape=hbm(*scaled.shape),
        in_specs=[HBM, HBM],
        out_specs=HBM,
        scratch_shapes=[scratch(*a.shape) for a in (diag, scaled, scaled)] + [pltpu.SemaphoreType.DMA((3,))],
        compiler_params=PARAMS,
        cost_estimate=cost(0),
    )(*pinned(diag, scaled))


def pieces_body(stored, source_ref, row_ref, place_ref, base, remote, spread, incoming, *refs):
    pieces, (total, remote_in, spread_in, incoming_in, sems) = refs[:-5], refs[-5:]
    tiles, tile = remote.shape[:2]
    early = start_all(
        [(incoming, incoming_in), (remote, remote_in), (base, total), (spread, spread_in)], sems, 0
    )
    wait_all(early[:3])
    for k in range(tiles):
        total[rows_at(row_ref[k], tile), :] += dot3(remote_in[k], incoming_in[source_ref[k]])
    wait_all(early[3:])
    height = pieces[0].shape[0]
    copies = []
    for j in reversed(range(len(pieces))):
        rows = rows_at(place_ref[j], height)
        made = total[rows, :] * spread_in[rows, :]
        if stored:
            total[rows, :] = made
            copies += start_all([(total.at[rows], pieces[j])], sems, 4 + j)
        else:
            pieces[j][...] = made
    wait_all(copies)


def feature_pieces(source, row, place, base, remote, spread, incoming, stored):
    rows, chunk = base.shape
    feats = place.shape[0]
    make = hbm if stored else f32
    return pl.pallas_call(
        functools.partial(pieces_body, stored),
        out_shape=[make(rows // feats, chunk)] * feats,
        in_specs=[SMEM] * 3 + [HBM] * 4,
        out_specs=[HBM if stored else VMEM] * feats,
        scratch_shapes=[scratch(*a.shape) for a in (base, remote, spread, incoming)]
        + [pltpu.SemaphoreType.DMA((4 + feats,))],
        compiler_params=PARAMS,
        cost_estimate=cost(0),
    )(source, row, place, *pinned(base, remote, spread), incoming)


def chosen_block(weights, number, turn, c, chunk, lanes):
    rows = pl.ds(c * chunk if weights[0].shape[0] > chunk else 0, chunk)
    block = weights[0][rows, lanes]
    for k in range(1, number):
        block = jnp.where(turn == k, weights[k][rows, lanes], block)
    return block


def product_body(count, choices, later, c, step, last, turn_ref, start, *refs):
    pieces, refs = refs[:count], refs[count:]
    weights, refs = refs[: sum(choices)], refs[sum(choices) :]
    ahead, refs = refs[: sum(later)], refs[sum(later) :]
    kept, (out, left, held, sems) = refs[: len(later)], refs[len(later) :]
    chunk = pieces[0].shape[1]
    left[...] = left_parts(jnp.concatenate([p[...] for p in pieces], axis=1))
    copies = []
    for j in range(held.shape[1] // step):
        lanes = pl.ds(j * step, step)
        blocks, at = [], 0
        for number in choices:
            blocks.append(chosen_block(weights[at:], number, turn_ref[0], c, chunk, lanes))
            at += number
        right = right_parts(jnp.concatenate(blocks, axis=0))
        made = start[:, lanes] + jnp.dot(left[...], right, preferred_element_type=jnp.float32)
        if last:
            held[:, lanes] = made
            copies += start_all([(held.at[:, lanes], out.at[:, lanes])], sems, j)
        else:
            out[:, lanes] = made
    at = 0
    for number, block in zip(later, kept):
        block[...] = chosen_block(ahead[at:], number, turn_ref[0], c, chunk, pl.ds(0, held.shape[1]))
        at += number
    wait_all(copies)


def add_product(turn, start, pieces, weights, c, last, ahead=()):
    rows, chunk = pieces[0].shape
    width = start.shape[1]
    step = min(2 * LANES, width)
    count = len(pieces)
    flat = [w for group in [*weights, *ahead] for w in group]
    choices, later = [len(group) for group in weights], [len(group) for group in ahead]
    return pl.pallas_call(
        functools.partial(product_body, count, choices, later, c, step, last),
        out_shape=[f32(chunk, width)] * len(later) + [hbm(rows, width) if last else f32(rows, width)],
        in_specs=[SMEM] + [VMEM] * (1 + count + len(flat)),
        out_specs=[VMEM] * len(later) + [HBM if last else VMEM],
        scratch_shapes=[
            pltpu.VMEM((rows, 3 * count * chunk), jnp.bfloat16),
            scratch(rows, width),
            pltpu.SemaphoreType.DMA((width // step,)),
        ],
        compiler_params=PARAMS,
        cost_estimate=cost(6 * count * rows * chunk * width),
    )(turn, start, *pieces, *flat)


def solution(mesh):
    parts = mesh.shape["dom"]
    feats = mesh.shape["feat"]
    sides = 2 if feats % 2 == 0 else 1
    halves = feats // sides
    others = list(range(1, halves))

    def feat_target(f, dh, dl):
        return (f // sides + dh) % halves * sides + (f % sides + dl) % sides

    def feat_send(x, dh, dl):
        return lax.ppermute(x, "feat", [(f, feat_target(f, dh, dl)) for f in range(feats)])

    def dom_exchange(x):
        return lax.all_to_all(x, "dom", split_axis=0, concat_axis=0, tiled=True)

    def per_device(
        features,
        degree,
        diag_adj,
        remote_adj,
        read_block,
        tile_src,
        tile_row,
        w_first,
        b_first,
        w_second,
        b_second,
    ):
        part, cols = features.shape
        tile = diag_adj.shape[1]
        blocks = part // tile
        remote = remote_adj[0]
        chunk = LANES if cols % LANES == 0 else cols
        chunks = cols // chunk
        f = lax.axis_index("feat")
        want, source, row = read_block[0], tile_src[0], tile_row[0]
        shifts = [(dh, dl) for dh in range(halves) for dl in range(sides)]
        place = jnp.stack([jnp.asarray(feat_target(f, dh, dl), jnp.int32) for dh, dl in shifts])
        first = jnp.reshape(jnp.asarray(f * cols, jnp.int32), (1,))
        bias = b_first[None, :]

        x_all = [features] + [feat_send(features, 0, dl) for dl in range(1, sides)]
        w_all = [w_first] + [feat_send(w_first, 0, dl) for dl in range(1, sides)]

        shares = chunks if parts % chunks == 0 else 1
        share = jnp.reshape(jnp.asarray(lax.axis_index("dom") % shares, jnp.int32), (1,))

        def share_send(x, k):
            pairs = [(s, s // shares * shares + (s % shares + k) % shares) for s in range(parts)]
            return lax.ppermute(x, "dom", pairs)

        w2_sent = lax.select_n(share[0], *jnp.split(w_second, shares)) if shares > 1 else w_second
        w2_got = [feat_send(w2_sent, dh, 0) for dh in others]

        scaling = lax.rsqrt(degree.astype(jnp.float32))
        spread = jnp.broadcast_to(scaling[:, None], (part, chunk))
        outgoing = outgoing_blocks(want, features, spread, tile)
        incoming = dom_exchange(outgoing)

        early = blocks // 4 * tile if chunks > 1 else part
        late = part - early
        marks = sorted({0, early // 2 // tile * tile, early, early + late // 2 // tile * tile, part})
        spans = list(zip(marks[:-1], marks[1:]))
        x_all[0], _ = lax.optimization_barrier((features, outgoing))
        send_steps = []
        for start, stop in spans:
            targets = [(0, 0, start)]
            for c in range(1, chunks):
                if stop <= early:
                    targets.append((c, 0, part + (c - 1) * early + start))
                else:
                    targets.append((c, 1, (c - 1) * late + start - early))
            send_steps.append((start, stop, targets))
        send_shapes = [(part + (chunks - 1) * early, chunk)]
        if late > 0:
            send_shapes.append(((chunks - 1) * late, chunk))
        sends = [partial_sums(place, [(dh * sides, send_steps)], x_all, w_all, send_shapes) for dh in others]
        sends, w2_got = lax.optimization_barrier((sends, w2_got))
        front = [feat_send(x[0], dh, 0) for dh, x in zip(others, sends)]

        own_steps = [(a, b, [(c, c, a) for c in range(chunks)]) for a, b in spans]
        own = list(partial_sums(place, [(0, own_steps)], x_all, w_all, [(part, chunk)] * chunks, HINT))

        incoming, own = lax.optimization_barrier((incoming, list(own)))
        w2_core = [w_second] + [feat_send(w_second, 0, dl) for dl in range(1, sides)]
        chosen = chosen_blocks(source, incoming)
        chosen_all = [chosen] + [feat_send(chosen, 0, dl) for dl in range(1, sides)]
        height = chosen.shape[0]
        tail_rows = (chunks - 1) * late
        ats = [dh * sides for dh in others] + [0]
        turned, _ = lax.optimization_barrier((place, chosen))
        made = remote_products(chosen_all, loaded_weights(turned, ats, w_all, cols), chunks)
        remote_front = [feat_send(made[i * chunks], dh, 0) for i, dh in enumerate(others)]
        remote_own = list(made[len(others) * chunks :])
        rest = []
        if chunks > 1:
            stored, kept, fresh, turned_in, shapes = [], [], [], [], []
            for i, x in enumerate(sends):
                kept += [(i, 0)] * len(x[1:])
                stored += x[1:]
                for c in range(1, chunks):
                    fresh.append(made[i * chunks + c])
                    turned_in.append((i, tail_rows + (c - 1) * height))
                shapes.append((tail_rows + (chunks - 1) * height, chunk))
            for c in range(1, chunks):
                fresh.append(remote_own[c])
                turned_in.append((len(shapes), 0))
                shapes.append((height, chunk))
            written = joined(stored, fresh, kept + turned_in, shapes)
            rest = [feat_send(x, dh, 0) for dh, x in zip(others, written)]
            remote_own[1:] = written[len(others) :]

        reach = len(others)
        first_layout = [(h, h, 0, part, 0) for h in range(reach)]
        base = own_part(diag_adj, spread, own[0], front, first_layout, reach)
        collected = []
        outgoing = None
        for c in range(chunks):
            if c == 0:
                outgoing, scaled = hidden_blocks(
                    row, want, first, 0, bias, base, remote, spread, [remote_own[0]] + remote_front
                )
            else:
                begin, _ = lax.optimization_barrier((own[c], outgoing))
                held = resident(begin, remote, spread, diag_adj, remote_own[c])
                layout = []
                for h in range(reach):
                    layout.append((h, h, part + (c - 1) * early, part + c * early, 0))
                    if late > 0:
                        layout.append((h, reach + h, (c - 1) * late, c * late, early))
                outgoing, scaled = later_blocks(
                    row, want, first, c * chunk, bias, *held, front + rest, layout, tail_rows + c * height, reach
                )
            incoming = dom_exchange(outgoing)
            if c < chunks - 1:
                incoming = pinned(incoming)[0]
            base_next = diagonal_part(diag_adj, scaled)
            pieces = feature_pieces(source, row, place, base_next, remote, spread, incoming, c < chunks - 1)
            collected.append(
                [p if dh == 0 and dl == 0 else feat_send(p, dh, dl) for (dh, dl), p in zip(shifts, pieces)]
            )

        w2_groups = [[got] + [share_send(got, k) for k in range(1, shares)] for got in w2_got]
        w2_groups, _ = lax.optimization_barrier((w2_groups, outgoing))
        w2_far = [[feat_send(w, 0, dl) if dl > 0 else w for w in g] for g in w2_groups for dl in range(sides)]
        weights = [[w] for w in w2_core] + w2_far
        out = b_second[None, :]
        for c in range(chunks):
            turn = (share - c) % shares
            if c < chunks - 1 or halves == 1:
                (out,) = add_product(turn, out, collected[c], weights, c, c == chunks - 1)
            else:
                near, far = collected[c][:sides], collected[c][sides:]
                *kept, out = add_product(turn, out, near, weights[:sides], c, False, weights[sides:])
                (out,) = add_product(turn, out, far, [[w] for w in kept], c, True)
        return out

    return jax.shard_map(
        per_device,
        mesh=mesh,
        in_specs=(
            P("dom", "feat"),
            P("dom"),
            P("dom", None),
            P("dom", None, None, None),
            P("dom", None),
            P("dom", None),
            P("dom", None),
            P("feat", None),
            P(),
            P("feat", None),
            P(),
        ),
        out_specs=P(("dom", "feat"), None),
        check_vma=False,
    )
```

```python
import functools

import jax
import jax.numpy as jnp
from jax import lax
from jax.experimental import pallas as pl
from jax.experimental.pallas import tpu as pltpu
from jax.sharding import PartitionSpec as P

LANES = 128
TOUCH = 2
HINT = 5 * 10**10
VMEM_LIMIT = 24 * 1024 * 1024
VMEM = pl.BlockSpec(memory_space=pltpu.VMEM)
SMEM = pl.BlockSpec(memory_space=pltpu.SMEM)
HBM = pl.BlockSpec(memory_space=pltpu.HBM)
PARAMS = pltpu.CompilerParams(vmem_limit_bytes=VMEM_LIMIT)


def dot3(a, b):
    return jnp.dot(a, b, precision=lax.Precision.HIGH, preferred_element_type=jnp.float32)


def two_parts(x):
    high = x.astype(jnp.bfloat16)
    return high, (x - high.astype(jnp.float32)).astype(jnp.bfloat16)


def left_parts(x):
    high, low = two_parts(x)
    return jnp.concatenate([high, low, high], axis=1)


def right_parts(w):
    high, low = two_parts(w)
    return jnp.concatenate([high, high, low], axis=0)


def sum_of_products(lefts, parts):
    total = None
    for x, part in zip(lefts, parts):
        made = jnp.dot(left_parts(x), part, preferred_element_type=jnp.float32)
        total = made if total is None else total + made
    return total


def f32(*dims):
    return jax.ShapeDtypeStruct(dims, jnp.float32)


def hbm(*dims):
    return pltpu.HBM(dims, jnp.float32)


def pinned(*arrays):
    return [pltpu.with_memory_space_constraint(a, pltpu.HBM) for a in arrays]


def rows_at(index, height):
    return pl.ds(pl.multiple_of(index * height, height), height)


def scratch(*dims):
    return pltpu.VMEM(dims, jnp.float32)


def start_all(pairs, sems, first):
    copies = [pltpu.make_async_copy(a, b, sems.at[first + i]) for i, (a, b) in enumerate(pairs)]
    for copy in copies:
        copy.start()
    return copies


def wait_all(copies):
    for copy in copies:
        copy.wait()


def cost(flops):
    return pl.CostEstimate(flops=flops, bytes_accessed=0, transcendentals=0)


def outgoing_body(want_ref, features, spread, blocks, held, sems):
    count, tile, cols = held.shape
    chunk = spread.shape[1]
    last = features.shape[0] // tile - 1
    copies = []
    for d in range(count):
        rows = rows_at(jnp.minimum(want_ref[d], last), tile)
        for c in range(cols // chunk):
            lanes = pl.ds(c * chunk, chunk)
            held[d, :, lanes] = features[rows, lanes] * spread[rows, :]
        copies += start_all([(held.at[d], blocks.at[d])], sems, d)
    wait_all(copies)


def outgoing_blocks(want, features, spread, tile):
    cols = features.shape[1]
    count = want.shape[0]
    return pl.pallas_call(
        outgoing_body,
        out_shape=hbm(count, tile, cols),
        in_specs=[SMEM, VMEM, VMEM],
        out_specs=HBM,
        scratch_shapes=[scratch(count, tile, cols), pltpu.SemaphoreType.DMA((count,))],
        compiler_params=PARAMS,
        cost_estimate=cost(HINT),
    )(want, features, spread)


def partial_body(count, groups, place_ref, *refs):
    lefts, rights, refs = refs[:count], refs[count : 2 * count], refs[2 * count :]
    outs, (left, right, result, sems) = refs[:-4], refs[-4:]
    cols = lefts[0].shape[1]
    chunk = outs[0].shape[1]
    used = 0
    weights_in, loads, stores = [], [], []
    for n, (at, _) in enumerate(groups):
        lanes = pl.ds(pl.multiple_of(place_ref[at] * cols, cols), cols)
        weights_in.append(start_all([(w.at[:, lanes], right.at[n, j]) for j, w in enumerate(rights)], sems, used))
        used += count
    for start, stop, _ in groups[0][1]:
        rows = pl.ds(start, stop - start)
        pairs = [(x.at[rows], left.at[rows, pl.ds(j * cols, cols)]) for j, x in enumerate(lefts)]
        loads.append(start_all(pairs, sems, used))
        used += count
    for n, (_, steps) in enumerate(groups):
        wait_all(weights_in[n])
        parts = [right_parts(right[n, j]) for j in range(count)]
        for i, (start, stop, targets) in enumerate(steps):
            if n == 0:
                wait_all(loads[i])
            rows = pl.ds(start, stop - start)
            made = sum_of_products([left[rows, pl.ds(j * cols, cols)] for j in range(count)], parts)
            result[n, rows, :] = made
            pairs = [
                (result.at[n, rows, pl.ds(c * chunk, chunk)], outs[o].at[pl.ds(offset, stop - start)])
                for c, o, offset in targets
            ]
            stores += start_all(pairs, sems, used)
            used += len(pairs)
    wait_all(stores)


def partial_sums(place, groups, lefts, weights, shapes, flops=0):
    rows, cols = lefts[0].shape
    depth = weights[0].shape[0]
    count = len(lefts)
    copies = count * (len(groups) + len(groups[0][1]))
    copies += sum(len(targets) for _, steps in groups for _, _, targets in steps)
    return pl.pallas_call(
        functools.partial(partial_body, count, groups),
        out_shape=[hbm(*s) for s in shapes],
        in_specs=[SMEM] + [HBM] * (2 * count),
        out_specs=[HBM] * len(shapes),
        scratch_shapes=[
            scratch(rows, count * cols),
            scratch(len(groups), count, depth, cols),
            scratch(len(groups), rows, cols),
            pltpu.SemaphoreType.DMA((copies,)),
        ],
        compiler_params=PARAMS,
        cost_estimate=cost(flops),
    )(place, *pinned(lefts[0]), *lefts[1:], *pinned(weights[0]), *weights[1:])


def loaded_body(ats, place_ref, *refs):
    sources, outs, sems = refs[: -1 - len(ats)], refs[-1 - len(ats) : -1], refs[-1]
    depth = sources[0].shape[0]
    pairs = []
    for at, out in zip(ats, outs):
        cols = out.shape[1]
        lanes = pl.ds(pl.multiple_of(place_ref[at] * cols, cols), cols)
        pairs += [(w.at[:, lanes], out.at[pl.ds(j * depth, depth)]) for j, w in enumerate(sources)]
    wait_all(start_all(pairs, sems, 0))


def loaded_weights(place, ats, weights, cols):
    depth = weights[0].shape[0]
    count = len(weights)
    return pl.pallas_call(
        functools.partial(loaded_body, ats),
        out_shape=[f32(count * depth, cols)] * len(ats),
        in_specs=[SMEM] + [HBM] * count,
        out_specs=[VMEM] * len(ats),
        scratch_shapes=[pltpu.SemaphoreType.DMA((count * len(ats),))],
        compiler_params=PARAMS,
        cost_estimate=cost(0),
    )(place, *pinned(weights[0]), *weights[1:])


def remote_body(count, *refs):
    lefts, refs = refs[:count], refs[count:]
    groups = len(refs) // (1 + lefts[0].shape[1] // refs[-1].shape[1])
    weights, outs = refs[:groups], refs[groups:]
    chunk = outs[0].shape[1]
    chunks = len(outs) // groups
    depth = lefts[0].shape[1]
    for n, weight in enumerate(weights):
        parts = [right_parts(weight[pl.ds(j * depth, depth), :]) for j in range(count)]
        made = sum_of_products([x[...] for x in lefts], parts)
        for c in range(chunks):
            outs[n * chunks + c][...] = made[:, c * chunk : (c + 1) * chunk]


def remote_products(lefts, weights, chunks):
    rows, cols = lefts[0].shape
    outs = len(weights) * chunks
    return pl.pallas_call(
        functools.partial(remote_body, len(lefts)),
        out_shape=[f32(rows, cols // chunks)] * outs,
        in_specs=[VMEM] * (len(lefts) + len(weights)),
        out_specs=[VMEM] * outs,
        compiler_params=PARAMS,
        cost_estimate=cost(0),
    )(*lefts, *weights)


def joined_body(plan, counts, *refs):
    count, new, kept = counts
    stored, refs = refs[:count], refs[count:]
    fresh, refs = refs[:new], refs[new:]
    extra, refs = refs[:kept], refs[kept:]
    held, sems, outs = refs[-1 - count : -1], refs[-1], refs[: -1 - count]
    residents = outs[len(outs) - kept :]
    loads = start_all(list(zip(stored, held)), sems, 0)
    places = [outs[o].at[pl.ds(offset, x.shape[0])] for x, (o, offset) in zip([*stored, *fresh], plan)]
    stores = start_all(list(zip(fresh, places[count:])), sems, count)
    stores += start_all(list(zip(extra, residents)), sems, count + new)
    for j in range(count):
        loads[j].wait()
        stores += start_all([(held[j], places[j])], sems, count + new + kept + j)
    wait_all(stores)


def joined(stored, fresh, plan, shapes, extra):
    counts = len(stored), len(fresh), len(extra)
    return pl.pallas_call(
        functools.partial(joined_body, plan, counts),
        out_shape=[hbm(*s) for s in shapes] + [f32(*x.shape) for x in extra],
        in_specs=[HBM] * len(stored) + [VMEM] * len(fresh) + [HBM] * len(extra),
        out_specs=[HBM] * len(shapes) + [VMEM] * len(extra),
        scratch_shapes=[scratch(*x.shape) for x in stored]
        + [pltpu.SemaphoreType.DMA((sum(counts) + len(stored),))],
        compiler_params=PARAMS,
        cost_estimate=cost(0),
    )(*pinned(*stored), *fresh, *pinned(*extra))


def chosen_body(source_ref, incoming, chosen):
    tile = incoming.shape[1]
    for g in range(chosen.shape[0] // tile):
        chosen[pl.ds(g * tile, tile), :] = incoming[source_ref[TOUCH * g]]


def chosen_blocks(source, incoming):
    tile, cols = incoming.shape[1:]
    groups = source.shape[0] // TOUCH
    return pl.pallas_call(
        chosen_body,
        out_shape=f32(groups * tile, cols),
        in_specs=[SMEM, VMEM],
        out_specs=VMEM,
        compiler_params=PARAMS,
        cost_estimate=cost(0),
    )(source, incoming)


def received_pairs(layout, received, recv_in):
    return [
        (received[r].at[pl.ds(start, stop - start)], recv_in.at[h, pl.ds(offset, stop - start)])
        for h, r, start, stop, offset in layout
    ]


def own_total(diag_in, spread_in, own_in, recv_in, total):
    tile = diag_in.shape[1]
    for i in range(diag_in.shape[0] // tile):
        rows = pl.ds(i * tile, tile)
        mixed = own_in[rows, :]
        for h in range(recv_in.shape[0]):
            mixed = mixed + recv_in[h, rows, :]
        total[rows, :] = dot3(diag_in[rows, :], mixed * spread_in[rows, :])


def own_body(layout, diag, spread, own, *refs):
    received, (base, recv_in, sems) = refs[:-3], refs[-3:]
    wait_all(start_all(received_pairs(layout, received, recv_in), sems, 0))
    own_total(diag, spread, own, recv_in, base)


def own_part(diag, spread, own, received, layout, others):
    return pl.pallas_call(
        functools.partial(own_body, layout),
        out_shape=f32(*own.shape),
        in_specs=[VMEM] * 3 + [HBM] * len(received),
        out_specs=VMEM,
        scratch_shapes=[scratch(others, *own.shape), pltpu.SemaphoreType.DMA((len(layout),))],
        compiler_params=PARAMS,
        cost_estimate=cost(0),
    )(diag, spread, own, *received)


def hidden_tail(
    lane_offset, row_ref, want_ref, first_ref, bias, remote, spread, sums, blocks, scaled_out, total, scaled, sems, used
):
    tiles, tile = remote.shape[:2]
    parts = blocks.shape[0]
    chunk = total.shape[1]
    for g in range(tiles // TOUCH):
        block = sums[0][pl.ds(g * tile, tile), :]
        for x in sums[1:]:
            block = block + x[pl.ds(g * tile, tile), :]
        for k in range(TOUCH * g, TOUCH * g + TOUCH):
            total[rows_at(row_ref[k], tile), :] += dot3(remote[k], block)
    lanes = pl.ds(pl.multiple_of(first_ref[0] + lane_offset, chunk), chunk)
    scaled[...] = jnp.maximum(total[...] * spread[...] + bias[:, lanes], 0.0) * spread[...]
    last = scaled.shape[0] // tile - 1
    pairs = [(scaled.at[rows_at(jnp.minimum(want_ref[d], last), tile)], blocks.at[d]) for d in range(parts)]
    wait_all(start_all(pairs + [(scaled, scaled_out)], sems, used))


def hidden_body(lane_offset, row_ref, want_ref, first_ref, bias, base, remote, spread, *refs):
    sums, (blocks, scaled_out, total, scaled, sems) = refs[:-5], refs[-5:]
    total[...] = base[...]
    hidden_tail(
        lane_offset, row_ref, want_ref, first_ref, bias, remote, spread, sums, blocks, scaled_out, total, scaled, sems, 0
    )


def hidden_blocks(row, want, first, lane_offset, bias, base, remote, spread, remote_sums):
    rows, chunk = base.shape
    tile = remote.shape[1]
    parts = want.shape[0]
    return pl.pallas_call(
        functools.partial(hidden_body, lane_offset),
        out_shape=[hbm(parts, tile, chunk), hbm(rows, chunk)],
        in_specs=[SMEM] * 3 + [VMEM] * (4 + len(remote_sums)),
        out_specs=[HBM, HBM],
        scratch_shapes=[scratch(rows, chunk), scratch(rows, chunk), pltpu.SemaphoreType.DMA((parts + 1,))],
        compiler_params=PARAMS,
        cost_estimate=cost(HINT),
    )(row, want, first, bias, base, remote, spread, *remote_sums)


def resident_body(count, *refs):
    wait_all(start_all(list(zip(refs[:count], refs[count:-1])), refs[-1], 0))


def resident(*arrays):
    count = len(arrays)
    return pl.pallas_call(
        functools.partial(resident_body, count),
        out_shape=[f32(*a.shape) for a in arrays],
        in_specs=[HBM] * count,
        out_specs=[VMEM] * count,
        scratch_shapes=[pltpu.SemaphoreType.DMA((count,))],
        compiler_params=PARAMS,
        cost_estimate=cost(0),
    )(*pinned(*arrays))


def later_body(
    ends, layout, lane_offset, row_ref, want_ref, first_ref, bias, own, remote, spread, diag, own_sum, *refs
):
    received, refs = refs[:-7], refs[-7:]
    blocks, scaled_out, total, scaled, sums_in, recv_in, sems = refs
    others, height = sums_in.shape[:2]
    pairs = received_pairs(layout, received, recv_in)
    late = [(r.at[pl.ds(ends - height, height)], sums_in.at[j]) for j, r in enumerate(received[-others:])]
    first = start_all(pairs, sems, 0)
    tail = start_all(late, sems, len(pairs))
    wait_all(first)
    own_total(diag, spread, own, recv_in, total)
    wait_all(tail)
    sums = [own_sum] + [sums_in.at[j] for j in range(others)]
    hidden_tail(
        lane_offset,
        row_ref,
        want_ref,
        first_ref,
        bias,
        remote,
        spread,
        sums,
        blocks,
        scaled_out,
        total,
        scaled,
        sems,
        len(pairs) + len(late),
    )


def later_blocks(
    row, want, first, lane_offset, bias, own, remote, spread, diag, own_sum, received, layout, ends, others
):
    rows, chunk = own.shape
    tile = diag.shape[1]
    parts = want.shape[0]
    return pl.pallas_call(
        functools.partial(later_body, ends, layout, lane_offset),
        out_shape=[hbm(parts, tile, chunk), hbm(rows, chunk)],
        in_specs=[SMEM] * 3 + [VMEM] * 6 + [HBM] * len(received),
        out_specs=[HBM, HBM],
        scratch_shapes=[scratch(rows, chunk), scratch(rows, chunk)]
        + [scratch(others, *own_sum.shape), scratch(others, rows, chunk)]
        + [pltpu.SemaphoreType.DMA((len(layout) + others + parts + 1,))],
        compiler_params=PARAMS,
        cost_estimate=cost(HINT),
    )(row, want, first, bias, own, remote, spread, diag, own_sum, *received)


def diagonal_body(row_ref, diag, scaled, spread, remote, base, tiles_out, *refs):
    diag_in, scaled_in, spread_in, remote_in, total, sems = refs
    tile = diag.shape[1]
    pairs = [(diag, diag_in), (scaled, scaled_in), (spread, spread_in), (remote, remote_in)]
    wait_all(start_all(pairs, sems, 0))
    for k in range(remote.shape[0]):
        remote_in[k] = remote_in[k] * spread_in[rows_at(row_ref[k], tile), :tile]
    stores = start_all([(remote_in, tiles_out)], sems, 4)
    for i in range(diag.shape[0] // tile):
        rows = pl.ds(i * tile, tile)
        total[rows, :] = dot3(diag_in[rows, :], scaled_in[rows, :]) * spread_in[rows, :]
    wait_all(stores + start_all([(total, base)], sems, 5))


def diagonal_part(row, diag, scaled, spread, remote):
    return pl.pallas_call(
        diagonal_body,
        out_shape=[hbm(*scaled.shape), hbm(*remote.shape)],
        in_specs=[SMEM] + [HBM] * 4,
        out_specs=[HBM, HBM],
        scratch_shapes=[scratch(*a.shape) for a in (diag, scaled, spread, remote, scaled)]
        + [pltpu.SemaphoreType.DMA((6,))],
        compiler_params=PARAMS,
        cost_estimate=cost(0),
    )(row, *pinned(diag, scaled, spread, remote))


def pieces_body(stored, source_ref, row_ref, place_ref, base, remote, incoming, *refs):
    pieces, (total, remote_in, incoming_in, sems) = refs[:-4], refs[-4:]
    tiles, tile = remote.shape[:2]
    wait_all(start_all([(incoming, incoming_in), (remote, remote_in), (base, total)], sems, 0))
    for k in range(tiles):
        total[rows_at(row_ref[k], tile), :] += dot3(remote_in[k], incoming_in[source_ref[k]])
    height = pieces[0].shape[0]
    places = [total.at[rows_at(place_ref[j], height)] for j in range(len(pieces))]
    if stored:
        wait_all(start_all(list(zip(places, pieces)), sems, 3))
    else:
        for place, piece in zip(places, pieces):
            piece[...] = place[...]


def feature_pieces(source, row, place, base, remote, incoming, stored):
    rows, chunk = base.shape
    feats = place.shape[0]
    make = hbm if stored else f32
    return pl.pallas_call(
        functools.partial(pieces_body, stored),
        out_shape=[make(rows // feats, chunk)] * feats,
        in_specs=[SMEM] * 3 + [HBM] * 3,
        out_specs=[HBM if stored else VMEM] * feats,
        scratch_shapes=[scratch(*a.shape) for a in (base, remote, incoming)]
        + [pltpu.SemaphoreType.DMA((3 + feats,))],
        compiler_params=PARAMS,
        cost_estimate=cost(0),
    )(source, row, place, *pinned(base, remote), incoming)


def product_body(count, ahead, c, step, last, start, *refs):
    pieces, weights, refs = refs[:count], refs[count : 2 * count], refs[2 * count :]
    coming, kept, (out, left, held, sems) = refs[:ahead], refs[ahead : 2 * ahead], refs[2 * ahead :]
    chunk = pieces[0].shape[1]
    brought = start_all(list(zip(coming, kept)), sems, 0)
    left[...] = left_parts(jnp.concatenate([p[...] for p in pieces], axis=1))
    copies = []
    for j in range(held.shape[1] // step):
        lanes = pl.ds(j * step, step)
        blocks = [w[pl.ds(c * chunk if w.shape[0] > chunk else 0, chunk), lanes] for w in weights]
        right = right_parts(jnp.concatenate(blocks, axis=0))
        made = start[:, lanes] + jnp.dot(left[...], right, preferred_element_type=jnp.float32)
        if last:
            held[:, lanes] = made
            copies += start_all([(held.at[:, lanes], out.at[:, lanes])], sems, ahead + j)
        else:
            out[:, lanes] = made
    wait_all(brought + copies)


def add_product(start, pieces, weights, c, last, ahead=()):
    rows, chunk = pieces[0].shape
    width = start.shape[1]
    step = min(2 * LANES, width)
    count, coming = len(pieces), len(ahead)
    return pl.pallas_call(
        functools.partial(product_body, count, coming, c, step, last),
        out_shape=[f32(*w.shape) for w in ahead] + [hbm(rows, width) if last else f32(rows, width)],
        in_specs=[VMEM] * (1 + 2 * count) + [HBM] * coming,
        out_specs=[VMEM] * coming + [HBM if last else VMEM],
        scratch_shapes=[
            pltpu.VMEM((rows, 3 * count * chunk), jnp.bfloat16),
            scratch(rows, width),
            pltpu.SemaphoreType.DMA((coming + width // step,)),
        ],
        compiler_params=PARAMS,
        cost_estimate=cost(6 * count * rows * chunk * width),
    )(start, *pieces, *weights, *ahead)


def solution(mesh):
    parts = mesh.shape["dom"]
    feats = mesh.shape["feat"]
    sides = 2 if feats % 2 == 0 else 1
    halves = feats // sides
    others = list(range(1, halves))

    def feat_target(f, dh, dl):
        return (f // sides + dh) % halves * sides + (f % sides + dl) % sides

    def feat_send(x, dh, dl):
        return lax.ppermute(x, "feat", [(f, feat_target(f, dh, dl)) for f in range(feats)])

    def dom_exchange(x):
        return lax.all_to_all(x, "dom", split_axis=0, concat_axis=0, tiled=True)

    def per_device(
        features,
        degree,
        diag_adj,
        remote_adj,
        read_block,
        tile_src,
        tile_row,
        w_first,
        b_first,
        w_second,
        b_second,
    ):
        part, cols = features.shape
        tile = diag_adj.shape[1]
        blocks = part // tile
        remote = remote_adj[0]
        chunk = LANES if cols % LANES == 0 else cols
        chunks = cols // chunk
        f = lax.axis_index("feat")
        want, source, row = read_block[0], tile_src[0], tile_row[0]
        shifts = [(dh, dl) for dh in range(halves) for dl in range(sides)]
        place = jnp.stack([jnp.asarray(feat_target(f, dh, dl), jnp.int32) for dh, dl in shifts])
        first = jnp.reshape(jnp.asarray(f * cols, jnp.int32), (1,))
        bias = b_first[None, :]

        x_all = [features] + [feat_send(features, 0, dl) for dl in range(1, sides)]
        w_all = [w_first] + [feat_send(w_first, 0, dl) for dl in range(1, sides)]

        w2_got = [feat_send(w_second[:chunk], dh, 0) for dh in others]

        scaling = lax.rsqrt(degree.astype(jnp.float32))
        spread = jnp.broadcast_to(scaling[:, None], (part, chunk))
        outgoing = outgoing_blocks(want, features, spread, tile)
        incoming = dom_exchange(outgoing)

        early = blocks // 3 * tile if chunks > 1 else part
        late = part - early
        marks = sorted({0, early // 2 // tile * tile, early, early + late // 2 // tile * tile, part})
        spans = list(zip(marks[:-1], marks[1:]))
        x_all[0], _ = lax.optimization_barrier((features, outgoing))
        send_steps = []
        for start, stop in spans:
            targets = [(0, 0, start)]
            for c in range(1, chunks):
                if stop <= early:
                    targets.append((c, 0, part + (c - 1) * early + start))
                else:
                    targets.append((c, 1, (c - 1) * late + start - early))
            send_steps.append((start, stop, targets))
        send_shapes = [(part + (chunks - 1) * early, chunk)]
        if late > 0:
            send_shapes.append(((chunks - 1) * late, chunk))
        sends = [partial_sums(place, [(dh * sides, send_steps)], x_all, w_all, send_shapes) for dh in others]
        sends, w2_got = lax.optimization_barrier((sends, w2_got))
        front = [feat_send(x[0], dh, 0) for dh, x in zip(others, sends)]

        own_steps = [(a, b, [(c, c, a) for c in range(chunks)]) for a, b in spans]
        own = list(partial_sums(place, [(0, own_steps)], x_all, w_all, [(part, chunk)] * chunks, HINT))

        incoming, own = lax.optimization_barrier((incoming, list(own)))
        w2_core = [w_second] + [feat_send(w_second, 0, dl) for dl in range(1, sides)]
        chosen = chosen_blocks(source, incoming)
        chosen_all = [chosen] + [feat_send(chosen, 0, dl) for dl in range(1, sides)]
        height = chosen.shape[0]
        tail_rows = (chunks - 1) * late
        ats = [dh * sides for dh in others] + [0]
        turned, _ = lax.optimization_barrier((place, chosen))
        made = remote_products(chosen_all, loaded_weights(turned, ats, w_all, cols), chunks)
        remote_front = [feat_send(made[i * chunks], dh, 0) for i, dh in enumerate(others)]
        remote_own = list(made[len(others) * chunks :])
        rest = []
        extra = [diag_adj, spread, own[0], remote]
        if chunks == 1:
            residents = resident(*extra)
        else:
            stored, kept, fresh, turned_in, shapes = [], [], [], [], []
            for i, x in enumerate(sends):
                kept += [(i, 0)] * len(x[1:])
                stored += x[1:]
                for c in range(1, chunks):
                    fresh.append(made[i * chunks + c])
                    turned_in.append((i, tail_rows + (c - 1) * height))
                shapes.append((tail_rows + (chunks - 1) * height, chunk))
            for c in range(1, chunks):
                fresh.append(remote_own[c])
                turned_in.append((len(shapes), 0))
                shapes.append((height, chunk))
            written = joined(stored, fresh, kept + turned_in, shapes, extra)
            residents, written = written[-len(extra) :], written[: -len(extra)]
            rest = [feat_send(x, dh, 0) for dh, x in zip(others, written)]
            remote_own[1:] = written[len(others) :]

        reach = len(others)
        first_layout = [(h, h, 0, part, 0) for h in range(reach)]
        base = own_part(*residents[:3], front, first_layout, reach)
        collected = []
        outgoing = None
        for c in range(chunks):
            if c == 0:
                outgoing, scaled = hidden_blocks(
                    row, want, first, 0, bias, base, residents[3], residents[1], [remote_own[0]] + remote_front
                )
            else:
                begin, _ = lax.optimization_barrier((own[c], outgoing))
                held = resident(begin, remote, spread, diag_adj, remote_own[c])
                layout = []
                for h in range(reach):
                    layout.append((h, h, part + (c - 1) * early, part + c * early, 0))
                    if late > 0:
                        layout.append((h, reach + h, (c - 1) * late, c * late, early))
                outgoing, scaled = later_blocks(
                    row, want, first, c * chunk, bias, *held, front + rest, layout, tail_rows + c * height, reach
                )
            incoming = dom_exchange(outgoing)
            if c < chunks - 1:
                incoming = pinned(incoming)[0]
            base_next, remote_next = diagonal_part(row, diag_adj, scaled, spread, remote)
            pieces = feature_pieces(source, row, place, base_next, remote_next, incoming, c < chunks - 1)
            collected.append(
                [p if dh == 0 and dl == 0 else feat_send(p, dh, dl) for (dh, dl), p in zip(shifts, pieces)]
            )

        w2_got, w2_late, _ = lax.optimization_barrier((w2_got, w_second, outgoing))
        out = b_second[None, :]
        for c in range(chunks):
            block = w2_late[c * chunk : (c + 1) * chunk]
            got = w2_got if c == 0 else [feat_send(block, dh, 0) for dh in others]
            far = [feat_send(w, 0, dl) if dl > 0 else w for w in got for dl in range(sides)]
            if c < chunks - 1 or halves == 1:
                (out,) = add_product(out, collected[c], w2_core + far, c, c == chunks - 1)
            else:
                pieces = collected[c]
                *kept, out = add_product(out, pieces[:sides], w2_core, c, False, far)
                (out,) = add_product(out, pieces[sides:], kept, c, True)
        return out

    return jax.shard_map(
        per_device,
        mesh=mesh,
        in_specs=(
            P("dom", "feat"),
            P("dom"),
            P("dom", None),
            P("dom", None, None, None),
            P("dom", None),
            P("dom", None),
            P("dom", None),
            P("feat", None),
            P(),
            P("feat", None),
            P(),
        ),
        out_specs=P(("dom", "feat"), None),
        check_vma=False,
    )
```

```python
import functools

import jax
import jax.numpy as jnp
from jax import lax
from jax.experimental import pallas as pl
from jax.experimental.pallas import tpu as pltpu
from jax.sharding import PartitionSpec as P

LANES = 128
TOUCH = 2
HINT = 5 * 10**10
VMEM_LIMIT = 24 * 1024 * 1024
VMEM = pl.BlockSpec(memory_space=pltpu.VMEM)
SMEM = pl.BlockSpec(memory_space=pltpu.SMEM)
HBM = pl.BlockSpec(memory_space=pltpu.HBM)
PARAMS = pltpu.CompilerParams(vmem_limit_bytes=VMEM_LIMIT)


def dot3(a, b):
    return jnp.dot(a, b, precision=lax.Precision.HIGH, preferred_element_type=jnp.float32)


def two_parts(x):
    high = x.astype(jnp.bfloat16)
    return high, (x - high.astype(jnp.float32)).astype(jnp.bfloat16)


def left_parts(x):
    high, low = two_parts(x)
    return jnp.concatenate([high, low, high], axis=1)


def right_parts(w):
    high, low = two_parts(w)
    return jnp.concatenate([high, high, low], axis=0)


def sum_of_products(lefts, parts):
    total = None
    for x, part in zip(lefts, parts):
        made = jnp.dot(left_parts(x), part, preferred_element_type=jnp.float32)
        total = made if total is None else total + made
    return total


def f32(*dims):
    return jax.ShapeDtypeStruct(dims, jnp.float32)


def hbm(*dims):
    return pltpu.HBM(dims, jnp.float32)


def pinned(*arrays):
    return [pltpu.with_memory_space_constraint(a, pltpu.HBM) for a in arrays]


def rows_at(index, height):
    return pl.ds(pl.multiple_of(index * height, height), height)


def scratch(*dims):
    return pltpu.VMEM(dims, jnp.float32)


def start_all(pairs, sems, first):
    copies = [pltpu.make_async_copy(a, b, sems.at[first + i]) for i, (a, b) in enumerate(pairs)]
    for copy in copies:
        copy.start()
    return copies


def wait_all(copies):
    for copy in copies:
        copy.wait()


def cost(flops):
    return pl.CostEstimate(flops=flops, bytes_accessed=0, transcendentals=0)


def outgoing_body(want_ref, features, spread, blocks, held, sems):
    count, tile, cols = held.shape
    chunk = spread.shape[1]
    last = features.shape[0] // tile - 1
    copies = []
    for d in range(count):
        rows = rows_at(jnp.minimum(want_ref[d], last), tile)
        for c in range(cols // chunk):
            lanes = pl.ds(c * chunk, chunk)
            held[d, :, lanes] = features[rows, lanes] * spread[rows, :]
        copies += start_all([(held.at[d], blocks.at[d])], sems, d)
    wait_all(copies)


def outgoing_blocks(want, features, spread, tile):
    cols = features.shape[1]
    count = want.shape[0]
    return pl.pallas_call(
        outgoing_body,
        out_shape=hbm(count, tile, cols),
        in_specs=[SMEM, VMEM, VMEM],
        out_specs=HBM,
        scratch_shapes=[scratch(count, tile, cols), pltpu.SemaphoreType.DMA((count,))],
        compiler_params=PARAMS,
        cost_estimate=cost(HINT),
    )(want, features, spread)


def partial_body(count, groups, place_ref, *refs):
    lefts, rights, refs = refs[:count], refs[count : 2 * count], refs[2 * count :]
    outs, (left, right, result, sems) = refs[:-4], refs[-4:]
    cols = lefts[0].shape[1]
    chunk = outs[0].shape[1]
    used = 0
    weights_in, loads, stores = [], [], []
    for n, (at, _) in enumerate(groups):
        lanes = pl.ds(pl.multiple_of(place_ref[at] * cols, cols), cols)
        weights_in.append(start_all([(w.at[:, lanes], right.at[n, j]) for j, w in enumerate(rights)], sems, used))
        used += count
    for start, stop, _ in groups[0][1]:
        rows = pl.ds(start, stop - start)
        pairs = [(x.at[rows], left.at[rows, pl.ds(j * cols, cols)]) for j, x in enumerate(lefts)]
        loads.append(start_all(pairs, sems, used))
        used += count
    for n, (_, steps) in enumerate(groups):
        wait_all(weights_in[n])
        parts = [right_parts(right[n, j]) for j in range(count)]
        for i, (start, stop, targets) in enumerate(steps):
            if n == 0:
                wait_all(loads[i])
            rows = pl.ds(start, stop - start)
            made = sum_of_products([left[rows, pl.ds(j * cols, cols)] for j in range(count)], parts)
            result[n, rows, :] = made
            pairs = [
                (result.at[n, rows, pl.ds(c * chunk, chunk)], outs[o].at[pl.ds(offset, stop - start)])
                for c, o, offset in targets
            ]
            stores += start_all(pairs, sems, used)
            used += len(pairs)
    wait_all(stores)


def partial_sums(place, groups, lefts, weights, shapes, flops=0):
    rows, cols = lefts[0].shape
    depth = weights[0].shape[0]
    count = len(lefts)
    copies = count * (len(groups) + len(groups[0][1]))
    copies += sum(len(targets) for _, steps in groups for _, _, targets in steps)
    return pl.pallas_call(
        functools.partial(partial_body, count, groups),
        out_shape=[hbm(*s) for s in shapes],
        in_specs=[SMEM] + [HBM] * (2 * count),
        out_specs=[HBM] * len(shapes),
        scratch_shapes=[
            scratch(rows, count * cols),
            scratch(len(groups), count, depth, cols),
            scratch(len(groups), rows, cols),
            pltpu.SemaphoreType.DMA((copies,)),
        ],
        compiler_params=PARAMS,
        cost_estimate=cost(flops),
    )(place, *pinned(lefts[0]), *lefts[1:], *pinned(weights[0]), *weights[1:])


def loaded_body(ats, place_ref, *refs):
    sources, outs, sems = refs[: -1 - len(ats)], refs[-1 - len(ats) : -1], refs[-1]
    depth = sources[0].shape[0]
    pairs = []
    for at, out in zip(ats, outs):
        cols = out.shape[1]
        lanes = pl.ds(pl.multiple_of(place_ref[at] * cols, cols), cols)
        pairs += [(w.at[:, lanes], out.at[pl.ds(j * depth, depth)]) for j, w in enumerate(sources)]
    wait_all(start_all(pairs, sems, 0))


def loaded_weights(place, ats, weights, cols):
    depth = weights[0].shape[0]
    count = len(weights)
    return pl.pallas_call(
        functools.partial(loaded_body, ats),
        out_shape=[f32(count * depth, cols)] * len(ats),
        in_specs=[SMEM] + [HBM] * count,
        out_specs=[VMEM] * len(ats),
        scratch_shapes=[pltpu.SemaphoreType.DMA((count * len(ats),))],
        compiler_params=PARAMS,
        cost_estimate=cost(0),
    )(place, *pinned(weights[0]), *weights[1:])


def remote_body(count, *refs):
    lefts, refs = refs[:count], refs[count:]
    groups = len(refs) // (1 + lefts[0].shape[1] // refs[-1].shape[1])
    weights, outs = refs[:groups], refs[groups:]
    chunk = outs[0].shape[1]
    chunks = len(outs) // groups
    depth = lefts[0].shape[1]
    for n, weight in enumerate(weights):
        parts = [right_parts(weight[pl.ds(j * depth, depth), :]) for j in range(count)]
        made = sum_of_products([x[...] for x in lefts], parts)
        for c in range(chunks):
            outs[n * chunks + c][...] = made[:, c * chunk : (c + 1) * chunk]


def remote_products(lefts, weights, chunks):
    rows, cols = lefts[0].shape
    outs = len(weights) * chunks
    return pl.pallas_call(
        functools.partial(remote_body, len(lefts)),
        out_shape=[f32(rows, cols // chunks)] * outs,
        in_specs=[VMEM] * (len(lefts) + len(weights)),
        out_specs=[VMEM] * outs,
        compiler_params=PARAMS,
        cost_estimate=cost(0),
    )(*lefts, *weights)


def joined_body(plan, counts, *refs):
    count, new, kept = counts
    stored, refs = refs[:count], refs[count:]
    fresh, refs = refs[:new], refs[new:]
    extra, refs = refs[:kept], refs[kept:]
    held, sems, outs = refs[-1 - count : -1], refs[-1], refs[: -1 - count]
    residents = outs[len(outs) - kept :]
    loads = start_all(list(zip(stored, held)), sems, 0)
    places = [outs[o].at[pl.ds(offset, x.shape[0])] for x, (o, offset) in zip([*stored, *fresh], plan)]
    stores = start_all(list(zip(fresh, places[count:])), sems, count)
    stores += start_all(list(zip(extra, residents)), sems, count + new)
    for j in range(count):
        loads[j].wait()
        stores += start_all([(held[j], places[j])], sems, count + new + kept + j)
    wait_all(stores)


def joined(stored, fresh, plan, shapes, extra):
    counts = len(stored), len(fresh), len(extra)
    return pl.pallas_call(
        functools.partial(joined_body, plan, counts),
        out_shape=[hbm(*s) for s in shapes] + [f32(*x.shape) for x in extra],
        in_specs=[HBM] * len(stored) + [VMEM] * len(fresh) + [HBM] * len(extra),
        out_specs=[HBM] * len(shapes) + [VMEM] * len(extra),
        scratch_shapes=[scratch(*x.shape) for x in stored]
        + [pltpu.SemaphoreType.DMA((sum(counts) + len(stored),))],
        compiler_params=PARAMS,
        cost_estimate=cost(0),
    )(*pinned(*stored), *fresh, *pinned(*extra))


def chosen_body(source_ref, incoming, chosen):
    tile = incoming.shape[1]
    for g in range(chosen.shape[0] // tile):
        chosen[pl.ds(g * tile, tile), :] = incoming[source_ref[TOUCH * g]]


def chosen_blocks(source, incoming):
    tile, cols = incoming.shape[1:]
    groups = source.shape[0] // TOUCH
    return pl.pallas_call(
        chosen_body,
        out_shape=f32(groups * tile, cols),
        in_specs=[SMEM, VMEM],
        out_specs=VMEM,
        compiler_params=PARAMS,
        cost_estimate=cost(0),
    )(source, incoming)


def received_pairs(layout, received, recv_in):
    return [
        (received[r].at[pl.ds(start, stop - start)], recv_in.at[h, pl.ds(offset, stop - start)])
        for h, r, start, stop, offset in layout
    ]


def own_total(diag_in, spread_in, own_in, recv_in, total):
    tile = diag_in.shape[1]
    for i in range(diag_in.shape[0] // tile):
        rows = pl.ds(i * tile, tile)
        mixed = own_in[rows, :]
        for h in range(recv_in.shape[0]):
            mixed = mixed + recv_in[h, rows, :]
        total[rows, :] = dot3(diag_in[rows, :], mixed * spread_in[rows, :])


def own_body(layout, diag, spread, own, *refs):
    received, (base, recv_in, sems) = refs[:-3], refs[-3:]
    wait_all(start_all(received_pairs(layout, received, recv_in), sems, 0))
    own_total(diag, spread, own, recv_in, base)


def own_part(diag, spread, own, received, layout, others):
    return pl.pallas_call(
        functools.partial(own_body, layout),
        out_shape=f32(*own.shape),
        in_specs=[VMEM] * 3 + [HBM] * len(received),
        out_specs=VMEM,
        scratch_shapes=[scratch(others, *own.shape), pltpu.SemaphoreType.DMA((len(layout),))],
        compiler_params=PARAMS,
        cost_estimate=cost(0),
    )(diag, spread, own, *received)


def hidden_tail(
    lane_offset, row_ref, want_ref, first_ref, bias, remote, spread, sums, blocks, scaled_out, total, scaled, sems, used
):
    tiles, tile = remote.shape[:2]
    parts = blocks.shape[0]
    chunk = total.shape[1]
    for g in range(tiles // TOUCH):
        block = sums[0][pl.ds(g * tile, tile), :]
        for x in sums[1:]:
            block = block + x[pl.ds(g * tile, tile), :]
        for k in range(TOUCH * g, TOUCH * g + TOUCH):
            total[rows_at(row_ref[k], tile), :] += dot3(remote[k], block)
    lanes = pl.ds(pl.multiple_of(first_ref[0] + lane_offset, chunk), chunk)
    scaled[...] = jnp.maximum(total[...] * spread[...] + bias[:, lanes], 0.0) * spread[...]
    last = scaled.shape[0] // tile - 1
    pairs = [(scaled.at[rows_at(jnp.minimum(want_ref[d], last), tile)], blocks.at[d]) for d in range(parts)]
    wait_all(start_all(pairs + [(scaled, scaled_out)], sems, used))


def hidden_body(lane_offset, row_ref, want_ref, first_ref, bias, base, remote, spread, *refs):
    sums, (blocks, scaled_out, total, scaled, sems) = refs[:-5], refs[-5:]
    total[...] = base[...]
    hidden_tail(
        lane_offset, row_ref, want_ref, first_ref, bias, remote, spread, sums, blocks, scaled_out, total, scaled, sems, 0
    )


def hidden_blocks(row, want, first, lane_offset, bias, base, remote, spread, remote_sums):
    rows, chunk = base.shape
    tile = remote.shape[1]
    parts = want.shape[0]
    return pl.pallas_call(
        functools.partial(hidden_body, lane_offset),
        out_shape=[hbm(parts, tile, chunk), hbm(rows, chunk)],
        in_specs=[SMEM] * 3 + [VMEM] * (4 + len(remote_sums)),
        out_specs=[HBM, HBM],
        scratch_shapes=[scratch(rows, chunk), scratch(rows, chunk), pltpu.SemaphoreType.DMA((parts + 1,))],
        compiler_params=PARAMS,
        cost_estimate=cost(HINT),
    )(row, want, first, bias, base, remote, spread, *remote_sums)


def resident_body(count, *refs):
    wait_all(start_all(list(zip(refs[:count], refs[count:-1])), refs[-1], 0))


def resident(*arrays):
    count = len(arrays)
    return pl.pallas_call(
        functools.partial(resident_body, count),
        out_shape=[f32(*a.shape) for a in arrays],
        in_specs=[HBM] * count,
        out_specs=[VMEM] * count,
        scratch_shapes=[pltpu.SemaphoreType.DMA((count,))],
        compiler_params=PARAMS,
        cost_estimate=cost(0),
    )(*pinned(*arrays))


def later_body(
    ends, layout, lane_offset, row_ref, want_ref, first_ref, bias, own, remote, spread, diag, own_sum, *refs
):
    received, refs = refs[:-7], refs[-7:]
    blocks, scaled_out, total, scaled, sums_in, recv_in, sems = refs
    others, height = sums_in.shape[:2]
    pairs = received_pairs(layout, received, recv_in)
    late = [(r.at[pl.ds(ends - height, height)], sums_in.at[j]) for j, r in enumerate(received[-others:])]
    first = start_all(pairs, sems, 0)
    tail = start_all(late, sems, len(pairs))
    wait_all(first)
    own_total(diag, spread, own, recv_in, total)
    wait_all(tail)
    sums = [own_sum] + [sums_in.at[j] for j in range(others)]
    hidden_tail(
        lane_offset,
        row_ref,
        want_ref,
        first_ref,
        bias,
        remote,
        spread,
        sums,
        blocks,
        scaled_out,
        total,
        scaled,
        sems,
        len(pairs) + len(late),
    )


def later_blocks(
    row, want, first, lane_offset, bias, own, remote, spread, diag, own_sum, received, layout, ends, others
):
    rows, chunk = own.shape
    tile = diag.shape[1]
    parts = want.shape[0]
    return pl.pallas_call(
        functools.partial(later_body, ends, layout, lane_offset),
        out_shape=[hbm(parts, tile, chunk), hbm(rows, chunk)],
        in_specs=[SMEM] * 3 + [VMEM] * 6 + [HBM] * len(received),
        out_specs=[HBM, HBM],
        scratch_shapes=[scratch(rows, chunk), scratch(rows, chunk)]
        + [scratch(others, *own_sum.shape), scratch(others, rows, chunk)]
        + [pltpu.SemaphoreType.DMA((len(layout) + others + parts + 1,))],
        compiler_params=PARAMS,
        cost_estimate=cost(HINT),
    )(row, want, first, bias, own, remote, spread, diag, own_sum, *received)


def diagonal_body(row_ref, diag, scaled, spread, remote, base, tiles_out, *refs):
    diag_in, scaled_in, spread_in, remote_in, total, sems = refs
    tile = diag.shape[1]
    pairs = [(diag, diag_in), (scaled, scaled_in), (spread, spread_in), (remote, remote_in)]
    wait_all(start_all(pairs, sems, 0))
    for k in range(remote.shape[0]):
        remote_in[k] = remote_in[k] * spread_in[rows_at(row_ref[k], tile), :tile]
    stores = start_all([(remote_in, tiles_out)], sems, 4)
    for i in range(diag.shape[0] // tile):
        rows = pl.ds(i * tile, tile)
        total[rows, :] = dot3(diag_in[rows, :], scaled_in[rows, :]) * spread_in[rows, :]
    wait_all(stores + start_all([(total, base)], sems, 5))


def diagonal_part(row, diag, scaled, spread, remote):
    return pl.pallas_call(
        diagonal_body,
        out_shape=[hbm(*scaled.shape), hbm(*remote.shape)],
        in_specs=[SMEM] + [HBM] * 4,
        out_specs=[HBM, HBM],
        scratch_shapes=[scratch(*a.shape) for a in (diag, scaled, spread, remote, scaled)]
        + [pltpu.SemaphoreType.DMA((6,))],
        compiler_params=PARAMS,
        cost_estimate=cost(0),
    )(row, *pinned(diag, scaled, spread, remote))


def pieces_body(stored, source_ref, row_ref, place_ref, base, remote, incoming, *refs):
    pieces, (total, remote_in, incoming_in, sems) = refs[:-4], refs[-4:]
    tiles, tile = remote.shape[:2]
    wait_all(start_all([(incoming, incoming_in), (remote, remote_in), (base, total)], sems, 0))
    for k in range(tiles):
        total[rows_at(row_ref[k], tile), :] += dot3(remote_in[k], incoming_in[source_ref[k]])
    height = pieces[0].shape[0]
    places = [total.at[rows_at(place_ref[j], height)] for j in range(len(pieces))]
    if stored:
        wait_all(start_all(list(zip(places, pieces)), sems, 3))
    else:
        for place, piece in zip(places, pieces):
            piece[...] = place[...]


def feature_pieces(source, row, place, base, remote, incoming, stored):
    rows, chunk = base.shape
    feats = place.shape[0]
    make = hbm if stored else f32
    return pl.pallas_call(
        functools.partial(pieces_body, stored),
        out_shape=[make(rows // feats, chunk)] * feats,
        in_specs=[SMEM] * 3 + [HBM] * 3,
        out_specs=[HBM if stored else VMEM] * feats,
        scratch_shapes=[scratch(*a.shape) for a in (base, remote, incoming)]
        + [pltpu.SemaphoreType.DMA((3 + feats,))],
        compiler_params=PARAMS,
        cost_estimate=cost(0),
    )(source, row, place, *pinned(base, remote), incoming)


def chosen_block(weights, number, turn, c, chunk, lanes):
    rows = pl.ds(c * chunk if weights[0].shape[0] > chunk else 0, chunk)
    block = weights[0][rows, lanes]
    for k in range(1, number):
        block = jnp.where(turn == k, weights[k][rows, lanes], block)
    return block


def product_body(count, choices, later, c, step, last, turn_ref, start, *refs):
    pieces, refs = refs[:count], refs[count:]
    weights, refs = refs[: sum(choices)], refs[sum(choices) :]
    ahead, refs = refs[: sum(later)], refs[sum(later) :]
    kept, (out, left, held, sems) = refs[: len(later)], refs[len(later) :]
    chunk = pieces[0].shape[1]
    left[...] = left_parts(jnp.concatenate([p[...] for p in pieces], axis=1))
    copies = []
    for j in range(held.shape[1] // step):
        lanes = pl.ds(j * step, step)
        blocks, at = [], 0
        for number in choices:
            blocks.append(chosen_block(weights[at:], number, turn_ref[0], c, chunk, lanes))
            at += number
        right = right_parts(jnp.concatenate(blocks, axis=0))
        made = start[:, lanes] + jnp.dot(left[...], right, preferred_element_type=jnp.float32)
        if last:
            held[:, lanes] = made
            copies += start_all([(held.at[:, lanes], out.at[:, lanes])], sems, j)
        else:
            out[:, lanes] = made
    at = 0
    for number, block in zip(later, kept):
        block[...] = chosen_block(ahead[at:], number, turn_ref[0], c, chunk, pl.ds(0, held.shape[1]))
        at += number
    wait_all(copies)


def add_product(turn, start, pieces, weights, c, last, ahead=()):
    rows, chunk = pieces[0].shape
    width = start.shape[1]
    step = min(2 * LANES, width)
    count = len(pieces)
    flat = [w for group in [*weights, *ahead] for w in group]
    choices, later = [len(group) for group in weights], [len(group) for group in ahead]
    return pl.pallas_call(
        functools.partial(product_body, count, choices, later, c, step, last),
        out_shape=[f32(chunk, width)] * len(later) + [hbm(rows, width) if last else f32(rows, width)],
        in_specs=[SMEM] + [VMEM] * (1 + count + len(flat)),
        out_specs=[VMEM] * len(later) + [HBM if last else VMEM],
        scratch_shapes=[
            pltpu.VMEM((rows, 3 * count * chunk), jnp.bfloat16),
            scratch(rows, width),
            pltpu.SemaphoreType.DMA((width // step,)),
        ],
        compiler_params=PARAMS,
        cost_estimate=cost(6 * count * rows * chunk * width),
    )(turn, start, *pieces, *flat)


def solution(mesh):
    parts = mesh.shape["dom"]
    feats = mesh.shape["feat"]
    sides = 2 if feats % 2 == 0 else 1
    halves = feats // sides
    others = list(range(1, halves))

    def feat_target(f, dh, dl):
        return (f // sides + dh) % halves * sides + (f % sides + dl) % sides

    def feat_send(x, dh, dl):
        return lax.ppermute(x, "feat", [(f, feat_target(f, dh, dl)) for f in range(feats)])

    def dom_exchange(x):
        return lax.all_to_all(x, "dom", split_axis=0, concat_axis=0, tiled=True)

    def per_device(
        features,
        degree,
        diag_adj,
        remote_adj,
        read_block,
        tile_src,
        tile_row,
        w_first,
        b_first,
        w_second,
        b_second,
    ):
        part, cols = features.shape
        tile = diag_adj.shape[1]
        blocks = part // tile
        remote = remote_adj[0]
        chunk = LANES if cols % LANES == 0 else cols
        chunks = cols // chunk
        f = lax.axis_index("feat")
        want, source, row = read_block[0], tile_src[0], tile_row[0]
        shifts = [(dh, dl) for dh in range(halves) for dl in range(sides)]
        place = jnp.stack([jnp.asarray(feat_target(f, dh, dl), jnp.int32) for dh, dl in shifts])
        first = jnp.reshape(jnp.asarray(f * cols, jnp.int32), (1,))
        bias = b_first[None, :]

        x_all = [features] + [feat_send(features, 0, dl) for dl in range(1, sides)]
        w_all = [w_first] + [feat_send(w_first, 0, dl) for dl in range(1, sides)]

        shares = chunks if parts % chunks == 0 else 1
        share = jnp.reshape(jnp.asarray(lax.axis_index("dom") % shares, jnp.int32), (1,))

        def share_send(x, k):
            pairs = [(s, s // shares * shares + (s % shares + k) % shares) for s in range(parts)]
            return lax.ppermute(x, "dom", pairs)

        w2_sent = lax.select_n(share[0], *jnp.split(w_second, shares)) if shares > 1 else w_second
        w2_got = [feat_send(w2_sent, dh, 0) for dh in others]

        scaling = lax.rsqrt(degree.astype(jnp.float32))
        spread = jnp.broadcast_to(scaling[:, None], (part, chunk))
        outgoing = outgoing_blocks(want, features, spread, tile)
        incoming = dom_exchange(outgoing)

        early = blocks // 3 * tile if chunks > 1 else part
        late = part - early
        marks = sorted({0, early // 2 // tile * tile, early, early + late // 2 // tile * tile, part})
        spans = list(zip(marks[:-1], marks[1:]))
        x_all[0], _ = lax.optimization_barrier((features, outgoing))
        send_steps = []
        for start, stop in spans:
            targets = [(0, 0, start)]
            for c in range(1, chunks):
                if stop <= early:
                    targets.append((c, 0, part + (c - 1) * early + start))
                else:
                    targets.append((c, 1, (c - 1) * late + start - early))
            send_steps.append((start, stop, targets))
        send_shapes = [(part + (chunks - 1) * early, chunk)]
        if late > 0:
            send_shapes.append(((chunks - 1) * late, chunk))
        sends = [partial_sums(place, [(dh * sides, send_steps)], x_all, w_all, send_shapes) for dh in others]
        sends, w2_got = lax.optimization_barrier((sends, w2_got))
        front = [feat_send(x[0], dh, 0) for dh, x in zip(others, sends)]

        own_steps = [(a, b, [(c, c, a) for c in range(chunks)]) for a, b in spans]
        own = list(partial_sums(place, [(0, own_steps)], x_all, w_all, [(part, chunk)] * chunks, HINT))

        incoming, own = lax.optimization_barrier((incoming, list(own)))
        w2_core = [w_second] + [feat_send(w_second, 0, dl) for dl in range(1, sides)]
        chosen = chosen_blocks(source, incoming)
        chosen_all = [chosen] + [feat_send(chosen, 0, dl) for dl in range(1, sides)]
        height = chosen.shape[0]
        tail_rows = (chunks - 1) * late
        ats = [dh * sides for dh in others] + [0]
        turned, _ = lax.optimization_barrier((place, chosen))
        made = remote_products(chosen_all, loaded_weights(turned, ats, w_all, cols), chunks)
        remote_front = [feat_send(made[i * chunks], dh, 0) for i, dh in enumerate(others)]
        remote_own = list(made[len(others) * chunks :])
        rest = []
        extra = [diag_adj, spread, own[0], remote]
        if chunks == 1:
            residents = resident(*extra)
        else:
            stored, kept, fresh, turned_in, shapes = [], [], [], [], []
            for i, x in enumerate(sends):
                kept += [(i, 0)] * len(x[1:])
                stored += x[1:]
                for c in range(1, chunks):
                    fresh.append(made[i * chunks + c])
                    turned_in.append((i, tail_rows + (c - 1) * height))
                shapes.append((tail_rows + (chunks - 1) * height, chunk))
            for c in range(1, chunks):
                fresh.append(remote_own[c])
                turned_in.append((len(shapes), 0))
                shapes.append((height, chunk))
            written = joined(stored, fresh, kept + turned_in, shapes, extra)
            residents, written = written[-len(extra) :], written[: -len(extra)]
            rest = [feat_send(x, dh, 0) for dh, x in zip(others, written)]
            remote_own[1:] = written[len(others) :]

        reach = len(others)
        first_layout = [(h, h, 0, part, 0) for h in range(reach)]
        base = own_part(*residents[:3], front, first_layout, reach)
        collected = []
        outgoing = None
        for c in range(chunks):
            if c == 0:
                outgoing, scaled = hidden_blocks(
                    row, want, first, 0, bias, base, residents[3], residents[1], [remote_own[0]] + remote_front
                )
            else:
                begin, _ = lax.optimization_barrier((own[c], outgoing))
                held = resident(begin, remote, spread, diag_adj, remote_own[c])
                layout = []
                for h in range(reach):
                    layout.append((h, h, part + (c - 1) * early, part + c * early, 0))
                    if late > 0:
                        layout.append((h, reach + h, (c - 1) * late, c * late, early))
                outgoing, scaled = later_blocks(
                    row, want, first, c * chunk, bias, *held, front + rest, layout, tail_rows + c * height, reach
                )
            incoming = dom_exchange(outgoing)
            if c < chunks - 1:
                incoming = pinned(incoming)[0]
            base_next, remote_next = diagonal_part(row, diag_adj, scaled, spread, remote)
            pieces = feature_pieces(source, row, place, base_next, remote_next, incoming, c < chunks - 1)
            collected.append(
                [p if dh == 0 and dl == 0 else feat_send(p, dh, dl) for (dh, dl), p in zip(shifts, pieces)]
            )

        w2_groups = [[got] + [share_send(got, k) for k in range(1, shares)] for got in w2_got]
        w2_groups, _ = lax.optimization_barrier((w2_groups, outgoing))
        w2_far = [[feat_send(w, 0, dl) if dl > 0 else w for w in g] for g in w2_groups for dl in range(sides)]
        weights = [[w] for w in w2_core] + w2_far
        out = b_second[None, :]
        for c in range(chunks):
            turn = (share - c) % shares
            if c < chunks - 1 or halves == 1:
                (out,) = add_product(turn, out, collected[c], weights, c, c == chunks - 1)
            else:
                near, far = collected[c][:sides], collected[c][sides:]
                *kept, out = add_product(turn, out, near, weights[:sides], c, False, weights[sides:])
                (out,) = add_product(turn, out, far, [[w] for w in kept], c, True)
        return out

    return jax.shard_map(
        per_device,
        mesh=mesh,
        in_specs=(
            P("dom", "feat"),
            P("dom"),
            P("dom", None),
            P("dom", None, None, None),
            P("dom", None),
            P("dom", None),
            P("dom", None),
            P("feat", None),
            P(),
            P("feat", None),
            P(),
        ),
        out_specs=P(("dom", "feat"), None),
        check_vma=False,
    )
```

```python
import functools

import jax
import jax.numpy as jnp
from jax import lax
from jax.experimental import pallas as pl
from jax.experimental.pallas import tpu as pltpu
from jax.sharding import PartitionSpec as P

LANES = 128
TOUCH = 2
HINT = 5 * 10**10
VMEM_LIMIT = 24 * 1024 * 1024
VMEM = pl.BlockSpec(memory_space=pltpu.VMEM)
SMEM = pl.BlockSpec(memory_space=pltpu.SMEM)
HBM = pl.BlockSpec(memory_space=pltpu.HBM)
PARAMS = pltpu.CompilerParams(vmem_limit_bytes=VMEM_LIMIT)


def dot3(a, b):
    return jnp.dot(a, b, precision=lax.Precision.HIGH, preferred_element_type=jnp.float32)


def two_parts(x):
    high = x.astype(jnp.bfloat16)
    return high, (x - high.astype(jnp.float32)).astype(jnp.bfloat16)


def left_parts(x):
    high, low = two_parts(x)
    return jnp.concatenate([high, low, high], axis=1)


def right_parts(w):
    high, low = two_parts(w)
    return jnp.concatenate([high, high, low], axis=0)


def sum_of_products(lefts, parts):
    total = None
    for x, part in zip(lefts, parts):
        made = jnp.dot(left_parts(x), part, preferred_element_type=jnp.float32)
        total = made if total is None else total + made
    return total


def f32(*dims):
    return jax.ShapeDtypeStruct(dims, jnp.float32)


def hbm(*dims):
    return pltpu.HBM(dims, jnp.float32)


def pinned(*arrays):
    return [pltpu.with_memory_space_constraint(a, pltpu.HBM) for a in arrays]


def rows_at(index, height):
    return pl.ds(pl.multiple_of(index * height, height), height)


def scratch(*dims):
    return pltpu.VMEM(dims, jnp.float32)


def start_all(pairs, sems, first):
    copies = [pltpu.make_async_copy(a, b, sems.at[first + i]) for i, (a, b) in enumerate(pairs)]
    for copy in copies:
        copy.start()
    return copies


def wait_all(copies):
    for copy in copies:
        copy.wait()


def cost(flops):
    return pl.CostEstimate(flops=flops, bytes_accessed=0, transcendentals=0)


def outgoing_body(want_ref, features, spread, blocks, held, sems):
    count, tile, cols = held.shape
    chunk = spread.shape[1]
    last = features.shape[0] // tile - 1
    copies = []
    for d in range(count):
        rows = rows_at(jnp.minimum(want_ref[d], last), tile)
        for c in range(cols // chunk):
            lanes = pl.ds(c * chunk, chunk)
            held[d, :, lanes] = features[rows, lanes] * spread[rows, :]
        copies += start_all([(held.at[d], blocks.at[d])], sems, d)
    wait_all(copies)


def outgoing_blocks(want, features, spread, tile):
    cols = features.shape[1]
    count = want.shape[0]
    return pl.pallas_call(
        outgoing_body,
        out_shape=hbm(count, tile, cols),
        in_specs=[SMEM, VMEM, VMEM],
        out_specs=HBM,
        scratch_shapes=[scratch(count, tile, cols), pltpu.SemaphoreType.DMA((count,))],
        compiler_params=PARAMS,
        cost_estimate=cost(HINT),
    )(want, features, spread)


def partial_body(count, groups, place_ref, *refs):
    lefts, rights, refs = refs[:count], refs[count : 2 * count], refs[2 * count :]
    outs, (left, right, result, sems) = refs[:-4], refs[-4:]
    cols = lefts[0].shape[1]
    chunk = outs[0].shape[1]
    used = 0
    weights_in, loads, stores = [], [], []
    for n, (at, _) in enumerate(groups):
        lanes = pl.ds(pl.multiple_of(place_ref[at] * cols, cols), cols)
        weights_in.append(start_all([(w.at[:, lanes], right.at[n, j]) for j, w in enumerate(rights)], sems, used))
        used += count
    for start, stop, _ in groups[0][1]:
        rows = pl.ds(start, stop - start)
        pairs = [(x.at[rows], left.at[rows, pl.ds(j * cols, cols)]) for j, x in enumerate(lefts)]
        loads.append(start_all(pairs, sems, used))
        used += count
    for n, (_, steps) in enumerate(groups):
        wait_all(weights_in[n])
        parts = [right_parts(right[n, j]) for j in range(count)]
        for i, (start, stop, targets) in enumerate(steps):
            if n == 0:
                wait_all(loads[i])
            rows = pl.ds(start, stop - start)
            made = sum_of_products([left[rows, pl.ds(j * cols, cols)] for j in range(count)], parts)
            result[n, rows, :] = made
            pairs = [
                (result.at[n, rows, pl.ds(c * chunk, chunk)], outs[o].at[pl.ds(offset, stop - start)])
                for c, o, offset in targets
            ]
            stores += start_all(pairs, sems, used)
            used += len(pairs)
    wait_all(stores)


def partial_sums(place, groups, lefts, weights, shapes, flops=0):
    rows, cols = lefts[0].shape
    depth = weights[0].shape[0]
    count = len(lefts)
    copies = count * (len(groups) + len(groups[0][1]))
    copies += sum(len(targets) for _, steps in groups for _, _, targets in steps)
    return pl.pallas_call(
        functools.partial(partial_body, count, groups),
        out_shape=[hbm(*s) for s in shapes],
        in_specs=[SMEM] + [HBM] * (2 * count),
        out_specs=[HBM] * len(shapes),
        scratch_shapes=[
            scratch(rows, count * cols),
            scratch(len(groups), count, depth, cols),
            scratch(len(groups), rows, cols),
            pltpu.SemaphoreType.DMA((copies,)),
        ],
        compiler_params=PARAMS,
        cost_estimate=cost(flops),
    )(place, *pinned(lefts[0]), *lefts[1:], *pinned(weights[0]), *weights[1:])


def loaded_body(ats, place_ref, *refs):
    sources, outs, sems = refs[: -1 - len(ats)], refs[-1 - len(ats) : -1], refs[-1]
    depth = sources[0].shape[0]
    pairs = []
    for at, out in zip(ats, outs):
        cols = out.shape[1]
        lanes = pl.ds(pl.multiple_of(place_ref[at] * cols, cols), cols)
        pairs += [(w.at[:, lanes], out.at[pl.ds(j * depth, depth)]) for j, w in enumerate(sources)]
    wait_all(start_all(pairs, sems, 0))


def loaded_weights(place, ats, weights, cols):
    depth = weights[0].shape[0]
    count = len(weights)
    return pl.pallas_call(
        functools.partial(loaded_body, ats),
        out_shape=[f32(count * depth, cols)] * len(ats),
        in_specs=[SMEM] + [HBM] * count,
        out_specs=[VMEM] * len(ats),
        scratch_shapes=[pltpu.SemaphoreType.DMA((count * len(ats),))],
        compiler_params=PARAMS,
        cost_estimate=cost(0),
    )(place, *pinned(weights[0]), *weights[1:])


def remote_body(count, *refs):
    lefts, refs = refs[:count], refs[count:]
    groups = len(refs) // (1 + lefts[0].shape[1] // refs[-1].shape[1])
    weights, outs = refs[:groups], refs[groups:]
    chunk = outs[0].shape[1]
    chunks = len(outs) // groups
    depth = lefts[0].shape[1]
    for n, weight in enumerate(weights):
        parts = [right_parts(weight[pl.ds(j * depth, depth), :]) for j in range(count)]
        made = sum_of_products([x[...] for x in lefts], parts)
        for c in range(chunks):
            outs[n * chunks + c][...] = made[:, c * chunk : (c + 1) * chunk]


def remote_products(lefts, weights, chunks):
    rows, cols = lefts[0].shape
    outs = len(weights) * chunks
    return pl.pallas_call(
        functools.partial(remote_body, len(lefts)),
        out_shape=[f32(rows, cols // chunks)] * outs,
        in_specs=[VMEM] * (len(lefts) + len(weights)),
        out_specs=[VMEM] * outs,
        compiler_params=PARAMS,
        cost_estimate=cost(0),
    )(*lefts, *weights)


def joined_body(plan, count, *refs):
    stored, refs = refs[:count], refs[count:]
    fresh, refs = refs[: len(plan) - count], refs[len(plan) - count :]
    held, sems, outs = refs[-1 - count : -1], refs[-1], refs[: -1 - count]
    loads = start_all(list(zip(stored, held)), sems, 0)
    places = [outs[o].at[pl.ds(offset, x.shape[0])] for x, (o, offset) in zip([*stored, *fresh], plan)]
    stores = start_all(list(zip(fresh, places[count:])), sems, count)
    for j in range(count):
        loads[j].wait()
        stores += start_all([(held[j], places[j])], sems, len(plan) + j)
    wait_all(stores)


def joined(stored, fresh, plan, shapes):
    count = len(stored)
    return pl.pallas_call(
        functools.partial(joined_body, plan, count),
        out_shape=[hbm(*s) for s in shapes],
        in_specs=[HBM] * count + [VMEM] * len(fresh),
        out_specs=[HBM] * len(shapes),
        scratch_shapes=[scratch(*x.shape) for x in stored]
        + [pltpu.SemaphoreType.DMA((len(plan) + count,))],
        compiler_params=PARAMS,
        cost_estimate=cost(0),
    )(*pinned(*stored), *fresh)


def chosen_body(source_ref, incoming, chosen):
    tile = incoming.shape[1]
    for g in range(chosen.shape[0] // tile):
        chosen[pl.ds(g * tile, tile), :] = incoming[source_ref[TOUCH * g]]


def chosen_blocks(source, incoming):
    tile, cols = incoming.shape[1:]
    groups = source.shape[0] // TOUCH
    return pl.pallas_call(
        chosen_body,
        out_shape=f32(groups * tile, cols),
        in_specs=[SMEM, VMEM],
        out_specs=VMEM,
        compiler_params=PARAMS,
        cost_estimate=cost(0),
    )(source, incoming)


def received_pairs(layout, received, recv_in):
    return [
        (received[r].at[pl.ds(start, stop - start)], recv_in.at[h, pl.ds(offset, stop - start)])
        for h, r, start, stop, offset in layout
    ]


def own_total(diag_in, spread_in, own_in, recv_in, total):
    tile = diag_in.shape[1]
    for i in range(diag_in.shape[0] // tile):
        rows = pl.ds(i * tile, tile)
        mixed = own_in[rows, :]
        for h in range(recv_in.shape[0]):
            mixed = mixed + recv_in[h, rows, :]
        total[rows, :] = dot3(diag_in[rows, :], mixed * spread_in[rows, :])


def own_body(layout, diag, spread, own, *refs):
    received, (base, diag_in, spread_in, own_in, recv_in, sems) = refs[:-6], refs[-6:]
    pairs = [(diag, diag_in), (spread, spread_in), (own, own_in)]
    wait_all(start_all(pairs + received_pairs(layout, received, recv_in), sems, 0))
    own_total(diag_in, spread_in, own_in, recv_in, base)


def own_part(diag, spread, own, received, layout, others):
    return pl.pallas_call(
        functools.partial(own_body, layout),
        out_shape=f32(*own.shape),
        in_specs=[HBM] * (3 + len(received)),
        out_specs=VMEM,
        scratch_shapes=[scratch(*a.shape) for a in (diag, spread, own)]
        + [scratch(others, *own.shape), pltpu.SemaphoreType.DMA((3 + len(layout),))],
        compiler_params=PARAMS,
        cost_estimate=cost(0),
    )(*pinned(diag, spread, own), *received)


def hidden_tail(
    lane_offset, row_ref, want_ref, first_ref, bias, remote, spread, sums, blocks, scaled_out, total, scaled, sems, used
):
    tiles, tile = remote.shape[:2]
    parts = blocks.shape[0]
    chunk = total.shape[1]
    for g in range(tiles // TOUCH):
        block = sums[0][pl.ds(g * tile, tile), :]
        for x in sums[1:]:
            block = block + x[pl.ds(g * tile, tile), :]
        for k in range(TOUCH * g, TOUCH * g + TOUCH):
            total[rows_at(row_ref[k], tile), :] += dot3(remote[k], block)
    lanes = pl.ds(pl.multiple_of(first_ref[0] + lane_offset, chunk), chunk)
    scaled[...] = jnp.maximum(total[...] * spread[...] + bias[:, lanes], 0.0) * spread[...]
    last = scaled.shape[0] // tile - 1
    pairs = [(scaled.at[rows_at(jnp.minimum(want_ref[d], last), tile)], blocks.at[d]) for d in range(parts)]
    wait_all(start_all(pairs + [(scaled, scaled_out)], sems, used))


def hidden_body(lane_offset, row_ref, want_ref, first_ref, bias, base, remote, spread, *refs):
    sums, (blocks, scaled_out, total, scaled, sems) = refs[:-5], refs[-5:]
    total[...] = base[...]
    hidden_tail(
        lane_offset, row_ref, want_ref, first_ref, bias, remote, spread, sums, blocks, scaled_out, total, scaled, sems, 0
    )


def hidden_blocks(row, want, first, lane_offset, bias, base, remote, spread, remote_sums):
    rows, chunk = base.shape
    tile = remote.shape[1]
    parts = want.shape[0]
    return pl.pallas_call(
        functools.partial(hidden_body, lane_offset),
        out_shape=[hbm(parts, tile, chunk), hbm(rows, chunk)],
        in_specs=[SMEM] * 3 + [VMEM] * (4 + len(remote_sums)),
        out_specs=[HBM, HBM],
        scratch_shapes=[scratch(rows, chunk), scratch(rows, chunk), pltpu.SemaphoreType.DMA((parts + 1,))],
        compiler_params=PARAMS,
        cost_estimate=cost(HINT),
    )(row, want, first, bias, base, remote, spread, *remote_sums)


def resident_body(diag, scaled, others, *refs):
    sources, refs = refs[:others], refs[others:]
    diag_out, outs, refs = refs[0], refs[1 : 1 + others], refs[1 + others :]
    base, scaled_in, total, sems = refs
    tile = diag.shape[1]
    first = start_all([(diag, diag_out), (scaled, scaled_in)], sems, 0)
    copies = start_all(list(zip(sources, outs)), sems, 2)
    wait_all(first)
    for i in range(diag.shape[0] // tile):
        rows = pl.ds(i * tile, tile)
        total[rows, :] = dot3(diag_out[rows, :], scaled_in[rows, :])
    wait_all(copies + start_all([(total, base)], sems, 2 + others))


def resident_and_diagonal(diag, scaled, *arrays):
    count = len(arrays)

    def body(diag, scaled, *refs):
        resident_body(diag, scaled, count, *refs)

    *held, base = pl.pallas_call(
        body,
        out_shape=[f32(*a.shape) for a in (diag, *arrays)] + [hbm(*scaled.shape)],
        in_specs=[HBM] * (2 + count),
        out_specs=[VMEM] * (1 + count) + [HBM],
        scratch_shapes=[scratch(*scaled.shape)] * 2 + [pltpu.SemaphoreType.DMA((3 + count,))],
        compiler_params=PARAMS,
        cost_estimate=cost(0),
    )(*pinned(diag, scaled, *arrays))
    return held, base


def later_body(
    ends, layout, lane_offset, row_ref, want_ref, first_ref, bias, own, remote, spread, diag, own_sum, *refs
):
    received, refs = refs[:-7], refs[-7:]
    blocks, scaled_out, total, scaled, sums_in, recv_in, sems = refs
    others, height = sums_in.shape[:2]
    pairs = received_pairs(layout, received, recv_in)
    late = [(r.at[pl.ds(ends - height, height)], sums_in.at[j]) for j, r in enumerate(received[-others:])]
    first = start_all(pairs, sems, 0)
    tail = start_all(late, sems, len(pairs))
    wait_all(first)
    own_total(diag, spread, own, recv_in, total)
    wait_all(tail)
    sums = [own_sum] + [sums_in.at[j] for j in range(others)]
    hidden_tail(
        lane_offset,
        row_ref,
        want_ref,
        first_ref,
        bias,
        remote,
        spread,
        sums,
        blocks,
        scaled_out,
        total,
        scaled,
        sems,
        len(pairs) + len(late),
    )


def later_blocks(
    row, want, first, lane_offset, bias, own, remote, spread, diag, own_sum, received, layout, ends, others
):
    rows, chunk = own.shape
    tile = diag.shape[1]
    parts = want.shape[0]
    return pl.pallas_call(
        functools.partial(later_body, ends, layout, lane_offset),
        out_shape=[hbm(parts, tile, chunk), hbm(rows, chunk)],
        in_specs=[SMEM] * 3 + [VMEM] * 6 + [HBM] * len(received),
        out_specs=[HBM, HBM],
        scratch_shapes=[scratch(rows, chunk), scratch(rows, chunk)]
        + [scratch(others, *own_sum.shape), scratch(others, rows, chunk)]
        + [pltpu.SemaphoreType.DMA((len(layout) + others + parts + 1,))],
        compiler_params=PARAMS,
        cost_estimate=cost(HINT),
    )(row, want, first, bias, own, remote, spread, diag, own_sum, *received)


def diagonal_body(diag, scaled, base, diag_in, scaled_in, total, sems):
    tile = diag.shape[1]
    wait_all(start_all([(diag, diag_in), (scaled, scaled_in)], sems, 0))
    for i in range(diag.shape[0] // tile):
        rows = pl.ds(i * tile, tile)
        total[rows, :] = dot3(diag_in[rows, :], scaled_in[rows, :])
    wait_all(start_all([(total, base)], sems, 2))


def diagonal_part(diag, scaled):
    return pl.pallas_call(
        diagonal_body,
        out_shape=hbm(*scaled.shape),
        in_specs=[HBM, HBM],
        out_specs=HBM,
        scratch_shapes=[scratch(*a.shape) for a in (diag, scaled, scaled)] + [pltpu.SemaphoreType.DMA((3,))],
        compiler_params=PARAMS,
        cost_estimate=cost(0),
    )(*pinned(diag, scaled))


def pieces_body(stored, source_ref, row_ref, place_ref, base, remote, spread, incoming, *refs):
    pieces, (total, remote_in, spread_in, incoming_in, sems) = refs[:-5], refs[-5:]
    tiles, tile = remote.shape[:2]
    early = start_all(
        [(incoming, incoming_in), (remote, remote_in), (base, total), (spread, spread_in)], sems, 0
    )
    wait_all(early[:3])
    for k in range(tiles):
        total[rows_at(row_ref[k], tile), :] += dot3(remote_in[k], incoming_in[source_ref[k]])
    wait_all(early[3:])
    height = pieces[0].shape[0]
    copies = []
    for j in reversed(range(len(pieces))):
        rows = rows_at(place_ref[j], height)
        made = total[rows, :] * spread_in[rows, :]
        if stored:
            total[rows, :] = made
            copies += start_all([(total.at[rows], pieces[j])], sems, 4 + j)
        else:
            pieces[j][...] = made
    wait_all(copies)


def feature_pieces(source, row, place, base, remote, spread, incoming, stored):
    rows, chunk = base.shape
    feats = place.shape[0]
    make = hbm if stored else f32
    return pl.pallas_call(
        functools.partial(pieces_body, stored),
        out_shape=[make(rows // feats, chunk)] * feats,
        in_specs=[SMEM] * 3 + [HBM] * 4,
        out_specs=[HBM if stored else VMEM] * feats,
        scratch_shapes=[scratch(*a.shape) for a in (base, remote, spread, incoming)]
        + [pltpu.SemaphoreType.DMA((4 + feats,))],
        compiler_params=PARAMS,
        cost_estimate=cost(0),
    )(source, row, place, *pinned(base, remote, spread), incoming)


def chosen_block(weights, number, turn, c, chunk, lanes):
    rows = pl.ds(c * chunk if weights[0].shape[0] > chunk else 0, chunk)
    block = weights[0][rows, lanes]
    for k in range(1, number):
        block = jnp.where(turn == k, weights[k][rows, lanes], block)
    return block


def product_body(count, choices, later, c, step, last, turn_ref, start, *refs):
    pieces, refs = refs[:count], refs[count:]
    weights, refs = refs[: sum(choices)], refs[sum(choices) :]
    ahead, refs = refs[: sum(later)], refs[sum(later) :]
    kept, (out, left, held, sems) = refs[: len(later)], refs[len(later) :]
    chunk = pieces[0].shape[1]
    left[...] = left_parts(jnp.concatenate([p[...] for p in pieces], axis=1))
    copies = []
    for j in range(held.shape[1] // step):
        lanes = pl.ds(j * step, step)
        blocks, at = [], 0
        for number in choices:
            blocks.append(chosen_block(weights[at:], number, turn_ref[0], c, chunk, lanes))
            at += number
        right = right_parts(jnp.concatenate(blocks, axis=0))
        made = start[:, lanes] + jnp.dot(left[...], right, preferred_element_type=jnp.float32)
        if last:
            held[:, lanes] = made
            copies += start_all([(held.at[:, lanes], out.at[:, lanes])], sems, j)
        else:
            out[:, lanes] = made
    at = 0
    for number, block in zip(later, kept):
        block[...] = chosen_block(ahead[at:], number, turn_ref[0], c, chunk, pl.ds(0, held.shape[1]))
        at += number
    wait_all(copies)


def add_product(turn, start, pieces, weights, c, last, ahead=()):
    rows, chunk = pieces[0].shape
    width = start.shape[1]
    step = min(2 * LANES, width)
    count = len(pieces)
    flat = [w for group in [*weights, *ahead] for w in group]
    choices, later = [len(group) for group in weights], [len(group) for group in ahead]
    return pl.pallas_call(
        functools.partial(product_body, count, choices, later, c, step, last),
        out_shape=[f32(chunk, width)] * len(later) + [hbm(rows, width) if last else f32(rows, width)],
        in_specs=[SMEM] + [VMEM] * (1 + count + len(flat)),
        out_specs=[VMEM] * len(later) + [HBM if last else VMEM],
        scratch_shapes=[
            pltpu.VMEM((rows, 3 * count * chunk), jnp.bfloat16),
            scratch(rows, width),
            pltpu.SemaphoreType.DMA((width // step,)),
        ],
        compiler_params=PARAMS,
        cost_estimate=cost(6 * count * rows * chunk * width),
    )(turn, start, *pieces, *flat)


def solution(mesh):
    parts = mesh.shape["dom"]
    feats = mesh.shape["feat"]
    sides = 2 if feats % 2 == 0 else 1
    halves = feats // sides
    others = list(range(1, halves))

    def feat_target(f, dh, dl):
        return (f // sides + dh) % halves * sides + (f % sides + dl) % sides

    def feat_send(x, dh, dl):
        return lax.ppermute(x, "feat", [(f, feat_target(f, dh, dl)) for f in range(feats)])

    def dom_exchange(x):
        return lax.all_to_all(x, "dom", split_axis=0, concat_axis=0, tiled=True)

    def per_device(
        features,
        degree,
        diag_adj,
        remote_adj,
        read_block,
        tile_src,
        tile_row,
        w_first,
        b_first,
        w_second,
        b_second,
    ):
        part, cols = features.shape
        tile = diag_adj.shape[1]
        blocks = part // tile
        remote = remote_adj[0]
        chunk = LANES if cols % LANES == 0 else cols
        chunks = cols // chunk
        f = lax.axis_index("feat")
        want, source, row = read_block[0], tile_src[0], tile_row[0]
        shifts = [(dh, dl) for dh in range(halves) for dl in range(sides)]
        place = jnp.stack([jnp.asarray(feat_target(f, dh, dl), jnp.int32) for dh, dl in shifts])
        first = jnp.reshape(jnp.asarray(f * cols, jnp.int32), (1,))
        bias = b_first[None, :]

        x_all = [features] + [feat_send(features, 0, dl) for dl in range(1, sides)]
        w_all = [w_first] + [feat_send(w_first, 0, dl) for dl in range(1, sides)]

        shares = chunks if parts % chunks == 0 else 1
        share = jnp.reshape(jnp.asarray(lax.axis_index("dom") % shares, jnp.int32), (1,))

        def share_send(x, k):
            pairs = [(s, s // shares * shares + (s % shares + k) % shares) for s in range(parts)]
            return lax.ppermute(x, "dom", pairs)

        w2_sent = lax.select_n(share[0], *jnp.split(w_second, shares)) if shares > 1 else w_second
        w2_got = [feat_send(w2_sent, dh, 0) for dh in others]

        scaling = lax.rsqrt(degree.astype(jnp.float32))
        spread = jnp.broadcast_to(scaling[:, None], (part, chunk))
        outgoing = outgoing_blocks(want, features, spread, tile)
        incoming = dom_exchange(outgoing)

        early = blocks // 4 * tile if chunks > 1 else part
        late = part - early
        marks = sorted({0, early // 2 // tile * tile, early, early + late // 2 // tile * tile, part})
        spans = list(zip(marks[:-1], marks[1:]))
        x_all[0], _ = lax.optimization_barrier((features, outgoing))
        send_steps = []
        for start, stop in spans:
            targets = [(0, 0, start)]
            for c in range(1, chunks):
                if stop <= early:
                    targets.append((c, 0, part + (c - 1) * early + start))
                else:
                    targets.append((c, 1, (c - 1) * late + start - early))
            send_steps.append((start, stop, targets))
        send_shapes = [(part + (chunks - 1) * early, chunk)]
        if late > 0:
            send_shapes.append(((chunks - 1) * late, chunk))
        sends = [partial_sums(place, [(dh * sides, send_steps)], x_all, w_all, send_shapes) for dh in others]
        sends, w2_got = lax.optimization_barrier((sends, w2_got))
        front = [feat_send(x[0], dh, 0) for dh, x in zip(others, sends)]

        own_steps = [(a, b, [(c, c, a) for c in range(chunks)]) for a, b in spans]
        own = list(partial_sums(place, [(0, own_steps)], x_all, w_all, [(part, chunk)] * chunks, HINT))

        incoming, own = lax.optimization_barrier((incoming, list(own)))
        w2_core = [w_second] + [feat_send(w_second, 0, dl) for dl in range(1, sides)]
        chosen = chosen_blocks(source, incoming)
        chosen_all = [chosen] + [feat_send(chosen, 0, dl) for dl in range(1, sides)]
        height = chosen.shape[0]
        tail_rows = (chunks - 1) * late
        ats = [dh * sides for dh in others] + [0]
        turned, _ = lax.optimization_barrier((place, chosen))
        made = remote_products(chosen_all, loaded_weights(turned, ats, w_all, cols), chunks)
        remote_front = [feat_send(made[i * chunks], dh, 0) for i, dh in enumerate(others)]
        remote_own = list(made[len(others) * chunks :])
        rest = []
        if chunks > 1:
            stored, kept, fresh, turned_in, shapes = [], [], [], [], []
            for i, x in enumerate(sends):
                kept += [(i, 0)] * len(x[1:])
                stored += x[1:]
                for c in range(1, chunks):
                    fresh.append(made[i * chunks + c])
                    turned_in.append((i, tail_rows + (c - 1) * height))
                shapes.append((tail_rows + (chunks - 1) * height, chunk))
            for c in range(1, chunks):
                fresh.append(remote_own[c])
                turned_in.append((len(shapes), 0))
                shapes.append((height, chunk))
            written = joined(stored, fresh, kept + turned_in, shapes)
            rest = [feat_send(x, dh, 0) for dh, x in zip(others, written)]
            remote_own[1:] = written[len(others) :]

        reach = len(others)
        first_layout = [(h, h, 0, part, 0) for h in range(reach)]
        base = own_part(diag_adj, spread, own[0], front, first_layout, reach)
        incoming, bases = [], []
        for c in range(chunks):
            if c == 0:
                outgoing, scaled = hidden_blocks(
                    row, want, first, 0, bias, base, remote, spread, [remote_own[0]] + remote_front
                )
            else:
                begin, _ = lax.optimization_barrier((own[c], outgoing))
                (held_diag, *held), base = resident_and_diagonal(
                    diag_adj, scaled, begin, remote, spread, remote_own[c]
                )
                bases.append(base)
                layout = []
                for h in range(reach):
                    layout.append((h, h, part + (c - 1) * early, part + c * early, 0))
                    if late > 0:
                        layout.append((h, reach + h, (c - 1) * late, c * late, early))
                outgoing, scaled = later_blocks(
                    row,
                    want,
                    first,
                    c * chunk,
                    bias,
                    *held[:3],
                    held_diag,
                    held[3],
                    front + rest,
                    layout,
                    tail_rows + c * height,
                    reach,
                )
            arrived = dom_exchange(outgoing)
            incoming.append(pinned(arrived)[0] if c < chunks - 1 else arrived)
        bases.append(diagonal_part(diag_adj, scaled))

        collected = []
        for c in range(chunks):
            pieces = feature_pieces(source, row, place, bases[c], remote, spread, incoming[c], c < chunks - 1)
            collected.append(
                [p if dh == 0 and dl == 0 else feat_send(p, dh, dl) for (dh, dl), p in zip(shifts, pieces)]
            )

        w2_groups = [[got] + [share_send(got, k) for k in range(1, shares)] for got in w2_got]
        w2_groups, _ = lax.optimization_barrier((w2_groups, outgoing))
        w2_far = [[feat_send(w, 0, dl) if dl > 0 else w for w in g] for g in w2_groups for dl in range(sides)]
        weights = [[w] for w in w2_core] + w2_far
        out = b_second[None, :]
        for c in range(chunks):
            turn = (share - c) % shares
            if c < chunks - 1 or halves == 1:
                (out,) = add_product(turn, out, collected[c], weights, c, c == chunks - 1)
            else:
                near, far = collected[c][:sides], collected[c][sides:]
                *kept, out = add_product(turn, out, near, weights[:sides], c, False, weights[sides:])
                (out,) = add_product(turn, out, far, [[w] for w in kept], c, True)
        return out

    return jax.shard_map(
        per_device,
        mesh=mesh,
        in_specs=(
            P("dom", "feat"),
            P("dom"),
            P("dom", None),
            P("dom", None, None, None),
            P("dom", None),
            P("dom", None),
            P("dom", None),
            P("feat", None),
            P(),
            P("feat", None),
            P(),
        ),
        out_specs=P(("dom", "feat"), None),
        check_vma=False,
    )
```

```python
import functools

import jax
import jax.numpy as jnp
from jax import lax
from jax.experimental import pallas as pl
from jax.experimental.pallas import tpu as pltpu
from jax.sharding import PartitionSpec as P

LANES = 128
TOUCH = 2
HINT = 5 * 10**10
VMEM_LIMIT = 24 * 1024 * 1024
VMEM = pl.BlockSpec(memory_space=pltpu.VMEM)
SMEM = pl.BlockSpec(memory_space=pltpu.SMEM)
HBM = pl.BlockSpec(memory_space=pltpu.HBM)
PARAMS = pltpu.CompilerParams(vmem_limit_bytes=VMEM_LIMIT)


def dot3(a, b):
    return jnp.dot(a, b, precision=lax.Precision.HIGH, preferred_element_type=jnp.float32)


def two_parts(x):
    high = x.astype(jnp.bfloat16)
    return high, (x - high.astype(jnp.float32)).astype(jnp.bfloat16)


def left_parts(x):
    high, low = two_parts(x)
    return jnp.concatenate([high, low, high], axis=1)


def right_parts(w):
    high, low = two_parts(w)
    return jnp.concatenate([high, high, low], axis=0)


def sum_of_products(lefts, parts):
    total = None
    for x, part in zip(lefts, parts):
        made = jnp.dot(left_parts(x), part, preferred_element_type=jnp.float32)
        total = made if total is None else total + made
    return total


def f32(*dims):
    return jax.ShapeDtypeStruct(dims, jnp.float32)


def hbm(*dims):
    return pltpu.HBM(dims, jnp.float32)


def pinned(*arrays):
    return [pltpu.with_memory_space_constraint(a, pltpu.HBM) for a in arrays]


def rows_at(index, height):
    return pl.ds(pl.multiple_of(index * height, height), height)


def scratch(*dims):
    return pltpu.VMEM(dims, jnp.float32)


def start_all(pairs, sems, first):
    copies = [pltpu.make_async_copy(a, b, sems.at[first + i]) for i, (a, b) in enumerate(pairs)]
    for copy in copies:
        copy.start()
    return copies


def wait_all(copies):
    for copy in copies:
        copy.wait()


def cost(flops):
    return pl.CostEstimate(flops=flops, bytes_accessed=0, transcendentals=0)


def slice_body(index_ref, source, out, sems):
    wait_all(start_all([(source.at[rows_at(index_ref[0], out.shape[0])], out)], sems, 0))


def row_block(index, source, height):
    return pl.pallas_call(
        slice_body,
        out_shape=f32(height, source.shape[1]),
        in_specs=[SMEM, HBM],
        out_specs=VMEM,
        scratch_shapes=[pltpu.SemaphoreType.DMA((1,))],
        compiler_params=PARAMS,
        cost_estimate=cost(0),
    )(index, *pinned(source))


def outgoing_body(want_ref, features, spread, blocks, held, sems):
    count, tile, cols = held.shape
    chunk = spread.shape[1]
    last = features.shape[0] // tile - 1
    copies = []
    for d in range(count):
        rows = rows_at(jnp.minimum(want_ref[d], last), tile)
        for c in range(cols // chunk):
            lanes = pl.ds(c * chunk, chunk)
            held[d, :, lanes] = features[rows, lanes] * spread[rows, :]
        copies += start_all([(held.at[d], blocks.at[d])], sems, d)
    wait_all(copies)


def outgoing_blocks(want, features, spread, tile):
    cols = features.shape[1]
    count = want.shape[0]
    return pl.pallas_call(
        outgoing_body,
        out_shape=hbm(count, tile, cols),
        in_specs=[SMEM, VMEM, VMEM],
        out_specs=HBM,
        scratch_shapes=[scratch(count, tile, cols), pltpu.SemaphoreType.DMA((count,))],
        compiler_params=PARAMS,
        cost_estimate=cost(HINT),
    )(want, features, spread)


def partial_body(count, groups, place_ref, *refs):
    lefts, rights, refs = refs[:count], refs[count : 2 * count], refs[2 * count :]
    outs, (left, right, result, sems) = refs[:-4], refs[-4:]
    cols = lefts[0].shape[1]
    chunk = outs[0].shape[1]
    used = 0
    weights_in, loads, stores = [], [], []
    for n, (at, _) in enumerate(groups):
        lanes = pl.ds(pl.multiple_of(place_ref[at] * cols, cols), cols)
        weights_in.append(start_all([(w.at[:, lanes], right.at[n, j]) for j, w in enumerate(rights)], sems, used))
        used += count
    for start, stop, _ in groups[0][1]:
        rows = pl.ds(start, stop - start)
        pairs = [(x.at[rows], left.at[rows, pl.ds(j * cols, cols)]) for j, x in enumerate(lefts)]
        loads.append(start_all(pairs, sems, used))
        used += count
    for n, (_, steps) in enumerate(groups):
        wait_all(weights_in[n])
        parts = [right_parts(right[n, j]) for j in range(count)]
        for i, (start, stop, targets) in enumerate(steps):
            if n == 0:
                wait_all(loads[i])
            rows = pl.ds(start, stop - start)
            made = sum_of_products([left[rows, pl.ds(j * cols, cols)] for j in range(count)], parts)
            result[n, rows, :] = made
            pairs = [
                (result.at[n, rows, pl.ds(c * chunk, chunk)], outs[o].at[pl.ds(offset, stop - start)])
                for c, o, offset in targets
            ]
            stores += start_all(pairs, sems, used)
            used += len(pairs)
    wait_all(stores)


def partial_sums(place, groups, lefts, weights, shapes, flops=0):
    rows, cols = lefts[0].shape
    depth = weights[0].shape[0]
    count = len(lefts)
    copies = count * (len(groups) + len(groups[0][1]))
    copies += sum(len(targets) for _, steps in groups for _, _, targets in steps)
    return pl.pallas_call(
        functools.partial(partial_body, count, groups),
        out_shape=[hbm(*s) for s in shapes],
        in_specs=[SMEM] + [HBM] * (2 * count),
        out_specs=[HBM] * len(shapes),
        scratch_shapes=[
            scratch(rows, count * cols),
            scratch(len(groups), count, depth, cols),
            scratch(len(groups), rows, cols),
            pltpu.SemaphoreType.DMA((copies,)),
        ],
        compiler_params=PARAMS,
        cost_estimate=cost(flops),
    )(place, *pinned(lefts[0]), *lefts[1:], *pinned(weights[0]), *weights[1:])


def loaded_body(ats, place_ref, *refs):
    sources, outs, sems = refs[: -1 - len(ats)], refs[-1 - len(ats) : -1], refs[-1]
    depth = sources[0].shape[0]
    pairs = []
    for at, out in zip(ats, outs):
        cols = out.shape[1]
        lanes = pl.ds(pl.multiple_of(place_ref[at] * cols, cols), cols)
        pairs += [(w.at[:, lanes], out.at[pl.ds(j * depth, depth)]) for j, w in enumerate(sources)]
    wait_all(start_all(pairs, sems, 0))


def loaded_weights(place, ats, weights, cols):
    depth = weights[0].shape[0]
    count = len(weights)
    return pl.pallas_call(
        functools.partial(loaded_body, ats),
        out_shape=[f32(count * depth, cols)] * len(ats),
        in_specs=[SMEM] + [HBM] * count,
        out_specs=[VMEM] * len(ats),
        scratch_shapes=[pltpu.SemaphoreType.DMA((count * len(ats),))],
        compiler_params=PARAMS,
        cost_estimate=cost(0),
    )(place, *pinned(weights[0]), *weights[1:])


def remote_body(count, *refs):
    lefts, refs = refs[:count], refs[count:]
    groups = len(refs) // (1 + lefts[0].shape[1] // refs[-1].shape[1])
    weights, outs = refs[:groups], refs[groups:]
    chunk = outs[0].shape[1]
    chunks = len(outs) // groups
    depth = lefts[0].shape[1]
    for n, weight in enumerate(weights):
        parts = [right_parts(weight[pl.ds(j * depth, depth), :]) for j in range(count)]
        made = sum_of_products([x[...] for x in lefts], parts)
        for c in range(chunks):
            outs[n * chunks + c][...] = made[:, c * chunk : (c + 1) * chunk]


def remote_products(lefts, weights, chunks):
    rows, cols = lefts[0].shape
    outs = len(weights) * chunks
    return pl.pallas_call(
        functools.partial(remote_body, len(lefts)),
        out_shape=[f32(rows, cols // chunks)] * outs,
        in_specs=[VMEM] * (len(lefts) + len(weights)),
        out_specs=[VMEM] * outs,
        compiler_params=PARAMS,
        cost_estimate=cost(0),
    )(*lefts, *weights)


def joined_body(plan, count, *refs):
    fresh, outs, sems = refs[count : count + len(plan)], refs[count + len(plan) : -1], refs[-1]
    places = [outs[o].at[pl.ds(offset, x.shape[0])] for x, (o, offset) in zip(fresh, plan)]
    wait_all(start_all(list(zip(fresh, places)), sems, 0))


def joined(buffers, fresh, plan, shapes):
    count = len(buffers)
    return pl.pallas_call(
        functools.partial(joined_body, plan, count),
        out_shape=[hbm(*s) for s in shapes],
        in_specs=[HBM] * count + [VMEM] * len(fresh),
        out_specs=[HBM] * len(shapes),
        scratch_shapes=[pltpu.SemaphoreType.DMA((len(plan),))],
        input_output_aliases={i: i for i in range(count)},
        compiler_params=PARAMS,
        cost_estimate=cost(0),
    )(*pinned(*buffers), *fresh)


def chosen_body(source_ref, incoming, chosen):
    tile = incoming.shape[1]
    for g in range(chosen.shape[0] // tile):
        chosen[pl.ds(g * tile, tile), :] = incoming[source_ref[TOUCH * g]]


def chosen_blocks(source, incoming):
    tile, cols = incoming.shape[1:]
    groups = source.shape[0] // TOUCH
    return pl.pallas_call(
        chosen_body,
        out_shape=f32(groups * tile, cols),
        in_specs=[SMEM, VMEM],
        out_specs=VMEM,
        compiler_params=PARAMS,
        cost_estimate=cost(0),
    )(source, incoming)


def received_pairs(layout, received, recv_in):
    return [
        (received[r].at[pl.ds(start, stop - start)], recv_in.at[h, pl.ds(offset, stop - start)])
        for h, r, start, stop, offset in layout
    ]


def own_total(diag_in, spread_in, own_in, recv_in, total):
    tile = diag_in.shape[1]
    for i in range(diag_in.shape[0] // tile):
        rows = pl.ds(i * tile, tile)
        mixed = own_in[rows, :]
        for h in range(recv_in.shape[0]):
            mixed = mixed + recv_in[h, rows, :]
        total[rows, :] = dot3(diag_in[rows, :], mixed * spread_in[rows, :])


def own_body(layout, diag, spread, own, *refs):
    received, (base, diag_in, spread_in, own_in, recv_in, sems) = refs[:-6], refs[-6:]
    pairs = [(diag, diag_in), (spread, spread_in), (own, own_in)]
    wait_all(start_all(pairs + received_pairs(layout, received, recv_in), sems, 0))
    own_total(diag_in, spread_in, own_in, recv_in, base)


def own_part(diag, spread, own, received, layout, others):
    return pl.pallas_call(
        functools.partial(own_body, layout),
        out_shape=f32(*own.shape),
        in_specs=[HBM] * (3 + len(received)),
        out_specs=VMEM,
        scratch_shapes=[scratch(*a.shape) for a in (diag, spread, own)]
        + [scratch(others, *own.shape), pltpu.SemaphoreType.DMA((3 + len(layout),))],
        compiler_params=PARAMS,
        cost_estimate=cost(0),
    )(*pinned(diag, spread, own), *received)


def hidden_tail(
    lane_offset, row_ref, want_ref, first_ref, bias, remote, spread, sums, blocks, scaled_out, total, scaled, sems, used
):
    tiles, tile = remote.shape[:2]
    parts = blocks.shape[0]
    chunk = total.shape[1]
    for g in range(tiles // TOUCH):
        block = sums[0][pl.ds(g * tile, tile), :]
        for x in sums[1:]:
            block = block + x[pl.ds(g * tile, tile), :]
        for k in range(TOUCH * g, TOUCH * g + TOUCH):
            total[rows_at(row_ref[k], tile), :] += dot3(remote[k], block)
    lanes = pl.ds(pl.multiple_of(first_ref[0] + lane_offset, chunk), chunk)
    last = scaled.shape[0] // tile - 1
    copies = []
    for i in range(last + 1):
        rows = pl.ds(i * tile, tile)
        scaled[rows, :] = jnp.maximum(total[rows, :] * spread[rows, :] + bias[:, lanes], 0.0) * spread[rows, :]
        copies += start_all([(scaled.at[rows], scaled_out.at[rows])], sems, used + parts + i)
    pairs = [(scaled.at[rows_at(jnp.minimum(want_ref[d], last), tile)], blocks.at[d]) for d in range(parts)]
    wait_all(copies + start_all(pairs, sems, used))


def hidden_body(lane_offset, row_ref, want_ref, first_ref, bias, base, remote, spread, *refs):
    sums, (blocks, scaled_out, total, scaled, sems) = refs[:-5], refs[-5:]
    total[...] = base[...]
    hidden_tail(
        lane_offset, row_ref, want_ref, first_ref, bias, remote, spread, sums, blocks, scaled_out, total, scaled, sems, 0
    )


def hidden_blocks(row, want, first, lane_offset, bias, base, remote, spread, remote_sums):
    rows, chunk = base.shape
    tile = remote.shape[1]
    parts = want.shape[0]
    return pl.pallas_call(
        functools.partial(hidden_body, lane_offset),
        out_shape=[hbm(parts, tile, chunk), hbm(rows, chunk)],
        in_specs=[SMEM] * 3 + [VMEM] * (4 + len(remote_sums)),
        out_specs=[HBM, HBM],
        scratch_shapes=[scratch(rows, chunk), scratch(rows, chunk), pltpu.SemaphoreType.DMA((parts + rows // tile,))],
        compiler_params=PARAMS,
        cost_estimate=cost(HINT),
    )(row, want, first, bias, base, remote, spread, *remote_sums)


def resident_body(diag, scaled, others, *refs):
    sources, refs = refs[:others], refs[others:]
    diag_out, outs, refs = refs[0], refs[1 : 1 + others], refs[1 + others :]
    base, scaled_in, total, sems = refs
    tile = diag.shape[1]
    first = start_all([(diag, diag_out), (scaled, scaled_in)], sems, 0)
    copies = start_all(list(zip(sources, outs)), sems, 2)
    wait_all(first)
    for i in range(diag.shape[0] // tile):
        rows = pl.ds(i * tile, tile)
        total[rows, :] = dot3(diag_out[rows, :], scaled_in[rows, :])
    wait_all(copies + start_all([(total, base)], sems, 2 + others))


def resident_and_diagonal(diag, scaled, *arrays):
    count = len(arrays)

    def body(diag, scaled, *refs):
        resident_body(diag, scaled, count, *refs)

    *held, base = pl.pallas_call(
        body,
        out_shape=[f32(*a.shape) for a in (diag, *arrays)] + [hbm(*scaled.shape)],
        in_specs=[HBM] * (2 + count),
        out_specs=[VMEM] * (1 + count) + [HBM],
        scratch_shapes=[scratch(*scaled.shape)] * 2 + [pltpu.SemaphoreType.DMA((3 + count,))],
        compiler_params=PARAMS,
        cost_estimate=cost(0),
    )(*pinned(diag, scaled, *arrays))
    return held, base


def later_body(
    ends, layout, lane_offset, row_ref, want_ref, first_ref, bias, own, remote, spread, diag, own_sum, *refs
):
    received, refs = refs[:-7], refs[-7:]
    blocks, scaled_out, total, scaled, sums_in, recv_in, sems = refs
    others, height = sums_in.shape[:2]
    pairs = received_pairs(layout, received, recv_in)
    late = [(r.at[pl.ds(ends - height, height)], sums_in.at[j]) for j, r in enumerate(received[-others:])]
    first = start_all(pairs, sems, 0)
    tail = start_all(late, sems, len(pairs))
    wait_all(first)
    own_total(diag, spread, own, recv_in, total)
    wait_all(tail)
    sums = [own_sum] + [sums_in.at[j] for j in range(others)]
    hidden_tail(
        lane_offset,
        row_ref,
        want_ref,
        first_ref,
        bias,
        remote,
        spread,
        sums,
        blocks,
        scaled_out,
        total,
        scaled,
        sems,
        len(pairs) + len(late),
    )


def later_blocks(
    row, want, first, lane_offset, bias, own, remote, spread, diag, own_sum, received, layout, ends, others
):
    rows, chunk = own.shape
    tile = diag.shape[1]
    parts = want.shape[0]
    return pl.pallas_call(
        functools.partial(later_body, ends, layout, lane_offset),
        out_shape=[hbm(parts, tile, chunk), hbm(rows, chunk)],
        in_specs=[SMEM] * 3 + [VMEM] * 6 + [HBM] * len(received),
        out_specs=[HBM, HBM],
        scratch_shapes=[scratch(rows, chunk), scratch(rows, chunk)]
        + [scratch(others, *own_sum.shape), scratch(others, rows, chunk)]
        + [pltpu.SemaphoreType.DMA((len(layout) + others + parts + rows // tile,))],
        compiler_params=PARAMS,
        cost_estimate=cost(HINT),
    )(row, want, first, bias, own, remote, spread, diag, own_sum, *received)


def diagonal_body(diag, scaled, base, diag_in, scaled_in, total, sems):
    tile = diag.shape[1]
    wait_all(start_all([(diag, diag_in), (scaled, scaled_in)], sems, 0))
    for i in range(diag.shape[0] // tile):
        rows = pl.ds(i * tile, tile)
        total[rows, :] = dot3(diag_in[rows, :], scaled_in[rows, :])
    wait_all(start_all([(total, base)], sems, 2))


def diagonal_part(diag, scaled):
    return pl.pallas_call(
        diagonal_body,
        out_shape=hbm(*scaled.shape),
        in_specs=[HBM, HBM],
        out_specs=HBM,
        scratch_shapes=[scratch(*a.shape) for a in (diag, scaled, scaled)] + [pltpu.SemaphoreType.DMA((3,))],
        compiler_params=PARAMS,
        cost_estimate=cost(0),
    )(*pinned(diag, scaled))


def pieces_body(stored, source_ref, row_ref, place_ref, base, remote, spread, incoming, *refs):
    pieces, (total, remote_in, spread_in, incoming_in, sems) = refs[:-5], refs[-5:]
    tiles, tile = remote.shape[:2]
    early = start_all(
        [(incoming, incoming_in), (remote, remote_in), (base, total), (spread, spread_in)], sems, 0
    )
    wait_all(early[:3])
    for k in range(tiles):
        total[rows_at(row_ref[k], tile), :] += dot3(remote_in[k], incoming_in[source_ref[k]])
    wait_all(early[3:])
    height = pieces[0].shape[0]
    copies = []
    for j in reversed(range(len(pieces))):
        rows = rows_at(place_ref[j], height)
        made = total[rows, :] * spread_in[rows, :]
        if stored:
            total[rows, :] = made
            copies += start_all([(total.at[rows], pieces[j])], sems, 4 + j)
        else:
            pieces[j][...] = made
    wait_all(copies)


def feature_pieces(source, row, place, base, remote, spread, incoming, stored):
    rows, chunk = base.shape
    feats = place.shape[0]
    make = hbm if stored else f32
    return pl.pallas_call(
        functools.partial(pieces_body, stored),
        out_shape=[make(rows // feats, chunk)] * feats,
        in_specs=[SMEM] * 3 + [HBM] * 4,
        out_specs=[HBM if stored else VMEM] * feats,
        scratch_shapes=[scratch(*a.shape) for a in (base, remote, spread, incoming)]
        + [pltpu.SemaphoreType.DMA((4 + feats,))],
        compiler_params=PARAMS,
        cost_estimate=cost(0),
    )(source, row, place, *pinned(base, remote, spread), incoming)


def chosen_block(weights, number, turn, c, chunk, lanes):
    rows = pl.ds(c * chunk if weights[0].shape[0] > chunk else 0, chunk)
    block = weights[0][rows, lanes]
    for k in range(1, number):
        block = jnp.where(turn == k, weights[k][rows, lanes], block)
    return block


def product_body(count, choices, later, c, step, last, turn_ref, start, *refs):
    pieces, refs = refs[:count], refs[count:]
    weights, refs = refs[: sum(choices)], refs[sum(choices) :]
    ahead, refs = refs[: sum(later)], refs[sum(later) :]
    kept, (out, left, held, sems) = refs[: len(later)], refs[len(later) :]
    chunk = pieces[0].shape[1]
    left[...] = left_parts(jnp.concatenate([p[...] for p in pieces], axis=1))
    copies = []
    for j in range(held.shape[1] // step):
        lanes = pl.ds(j * step, step)
        blocks, at = [], 0
        for number in choices:
            blocks.append(chosen_block(weights[at:], number, turn_ref[0], c, chunk, lanes))
            at += number
        right = right_parts(jnp.concatenate(blocks, axis=0))
        made = start[:, lanes] + jnp.dot(left[...], right, preferred_element_type=jnp.float32)
        if last:
            held[:, lanes] = made
            copies += start_all([(held.at[:, lanes], out.at[:, lanes])], sems, j)
        else:
            out[:, lanes] = made
    at = 0
    for number, block in zip(later, kept):
        block[...] = chosen_block(ahead[at:], number, turn_ref[0], c, chunk, pl.ds(0, held.shape[1]))
        at += number
    wait_all(copies)


def add_product(turn, start, pieces, weights, c, last, ahead=()):
    rows, chunk = pieces[0].shape
    width = start.shape[1]
    step = min(2 * LANES, width)
    count = len(pieces)
    flat = [w for group in [*weights, *ahead] for w in group]
    choices, later = [len(group) for group in weights], [len(group) for group in ahead]
    return pl.pallas_call(
        functools.partial(product_body, count, choices, later, c, step, last),
        out_shape=[f32(chunk, width)] * len(later) + [hbm(rows, width) if last else f32(rows, width)],
        in_specs=[SMEM] + [VMEM] * (1 + count + len(flat)),
        out_specs=[VMEM] * len(later) + [HBM if last else VMEM],
        scratch_shapes=[
            pltpu.VMEM((rows, 3 * count * chunk), jnp.bfloat16),
            scratch(rows, width),
            pltpu.SemaphoreType.DMA((width // step,)),
        ],
        compiler_params=PARAMS,
        cost_estimate=cost(6 * count * rows * chunk * width),
    )(turn, start, *pieces, *flat)


def solution(mesh):
    parts = mesh.shape["dom"]
    feats = mesh.shape["feat"]
    sides = 2 if feats % 2 == 0 else 1
    halves = feats // sides
    others = list(range(1, halves))

    def feat_target(f, dh, dl):
        return (f // sides + dh) % halves * sides + (f % sides + dl) % sides

    def feat_send(x, dh, dl):
        return lax.ppermute(x, "feat", [(f, feat_target(f, dh, dl)) for f in range(feats)])

    def dom_exchange(x):
        return lax.all_to_all(x, "dom", split_axis=0, concat_axis=0, tiled=True)

    def per_device(
        features,
        degree,
        diag_adj,
        remote_adj,
        read_block,
        tile_src,
        tile_row,
        w_first,
        b_first,
        w_second,
        b_second,
    ):
        part, cols = features.shape
        tile = diag_adj.shape[1]
        blocks = part // tile
        remote = remote_adj[0]
        chunk = LANES if cols % LANES == 0 else cols
        chunks = cols // chunk
        f = lax.axis_index("feat")
        want, source, row = read_block[0], tile_src[0], tile_row[0]
        shifts = [(dh, dl) for dh in range(halves) for dl in range(sides)]
        place = jnp.stack([jnp.asarray(feat_target(f, dh, dl), jnp.int32) for dh, dl in shifts])
        first = jnp.reshape(jnp.asarray(f * cols, jnp.int32), (1,))
        bias = b_first[None, :]

        x_all = [features] + [feat_send(features, 0, dl) for dl in range(1, sides)]
        w_all = [w_first] + [feat_send(w_first, 0, dl) for dl in range(1, sides)]

        shares = chunks if parts % chunks == 0 else 1
        share = jnp.reshape(jnp.asarray(lax.axis_index("dom") % shares, jnp.int32), (1,))

        def share_send(x, k):
            pairs = [(s, s // shares * shares + (s % shares + k) % shares) for s in range(parts)]
            return lax.ppermute(x, "dom", pairs)

        w2_sent = row_block(share, w_second, w_second.shape[0] // shares)
        w2_got = [feat_send(w2_sent, dh, 0) for dh in others]

        scaling = lax.rsqrt(degree.astype(jnp.float32))
        spread = jnp.broadcast_to(scaling[:, None], (part, chunk))
        outgoing = outgoing_blocks(want, features, spread, tile)
        incoming = dom_exchange(outgoing)

        early = blocks // 4 * tile if chunks > 1 else part
        late = part - early
        marks = sorted({0, early // 2 // tile * tile, early, early + late // 2 // tile * tile, part})
        spans = list(zip(marks[:-1], marks[1:]))
        x_all[0], _ = lax.optimization_barrier((features, outgoing))
        send_steps = []
        for start, stop in spans:
            targets = [(0, 0, start)]
            for c in range(1, chunks):
                if stop <= early:
                    targets.append((c, 0, part + (c - 1) * early + start))
                else:
                    targets.append((c, 1, (c - 1) * late + start - early))
            send_steps.append((start, stop, targets))
        send_shapes = [(part + (chunks - 1) * early, chunk)]
        if chunks > 1:
            send_shapes.append(((chunks - 1) * (late + remote.shape[0] // TOUCH * tile), chunk))
        sends = [partial_sums(place, [(dh * sides, send_steps)], x_all, w_all, send_shapes) for dh in others]
        sends, w2_got = lax.optimization_barrier((sends, w2_got))
        front = [feat_send(x[0], dh, 0) for dh, x in zip(others, sends)]

        own_steps = [(a, b, [(c, c, a) for c in range(chunks)]) for a, b in spans]
        own = list(partial_sums(place, [(0, own_steps)], x_all, w_all, [(part, chunk)] * chunks, HINT))

        incoming, own = lax.optimization_barrier((incoming, list(own)))
        w2_core = [w_second] + [feat_send(w_second, 0, dl) for dl in range(1, sides)]
        chosen = chosen_blocks(source, incoming)
        chosen_all = [chosen] + [feat_send(chosen, 0, dl) for dl in range(1, sides)]
        height = chosen.shape[0]
        tail_rows = (chunks - 1) * late
        ats = [dh * sides for dh in others] + [0]
        turned, _ = lax.optimization_barrier((place, chosen))
        made = remote_products(chosen_all, loaded_weights(turned, ats, w_all, cols), chunks)
        remote_front = [feat_send(made[i * chunks], dh, 0) for i, dh in enumerate(others)]
        remote_own = list(made[len(others) * chunks :])
        rest = []
        if chunks > 1:
            buffers, fresh, plan, shapes = [x[1] for x in sends], [], [], []
            for i, x in enumerate(sends):
                for c in range(1, chunks):
                    fresh.append(made[i * chunks + c])
                    plan.append((i, tail_rows + (c - 1) * height))
                shapes.append(x[1].shape)
            for c in range(1, chunks):
                fresh.append(remote_own[c])
                plan.append((len(shapes), 0))
                shapes.append((height, chunk))
            written = joined(buffers, fresh, plan, shapes)
            rest = [feat_send(x, dh, 0) for dh, x in zip(others, written)]
            remote_own[1:] = written[len(others) :]

        reach = len(others)
        first_layout = [(h, h, 0, part, 0) for h in range(reach)]
        base = own_part(diag_adj, spread, own[0], front, first_layout, reach)
        incoming, bases = [], []
        for c in range(chunks):
            if c == 0:
                outgoing, scaled = hidden_blocks(
                    row, want, first, 0, bias, base, remote, spread, [remote_own[0]] + remote_front
                )
            else:
                begin, _ = lax.optimization_barrier((own[c], outgoing))
                (held_diag, *held), base = resident_and_diagonal(
                    diag_adj, scaled, begin, remote, spread, remote_own[c]
                )
                bases.append(base)
                layout = []
                for h in range(reach):
                    layout.append((h, h, part + (c - 1) * early, part + c * early, 0))
                    if late > 0:
                        layout.append((h, reach + h, (c - 1) * late, c * late, early))
                outgoing, scaled = later_blocks(
                    row,
                    want,
                    first,
                    c * chunk,
                    bias,
                    *held[:3],
                    held_diag,
                    held[3],
                    front + rest,
                    layout,
                    tail_rows + c * height,
                    reach,
                )
            arrived = dom_exchange(outgoing)
            incoming.append(pinned(arrived)[0] if c < chunks - 1 else arrived)
        bases.append(diagonal_part(diag_adj, scaled))

        collected = []
        for c in range(chunks):
            pieces = feature_pieces(source, row, place, bases[c], remote, spread, incoming[c], c < chunks - 1)
            collected.append(
                [p if dh == 0 and dl == 0 else feat_send(p, dh, dl) for (dh, dl), p in zip(shifts, pieces)]
            )

        w2_groups = [[got] + [share_send(got, k) for k in range(1, shares)] for got in w2_got]
        w2_groups, _ = lax.optimization_barrier((w2_groups, outgoing))
        w2_far = [[feat_send(w, 0, dl) if dl > 0 else w for w in g] for g in w2_groups for dl in range(sides)]
        weights = [[w] for w in w2_core] + w2_far
        out = b_second[None, :]
        for c in range(chunks):
            turn = (share - c) % shares
            if c < chunks - 1 or halves == 1:
                (out,) = add_product(turn, out, collected[c], weights, c, c == chunks - 1)
            else:
                near, far = collected[c][:sides], collected[c][sides:]
                *kept, out = add_product(turn, out, near, weights[:sides], c, False, weights[sides:])
                (out,) = add_product(turn, out, far, [[w] for w in kept], c, True)
        return out

    return jax.shard_map(
        per_device,
        mesh=mesh,
        in_specs=(
            P("dom", "feat"),
            P("dom"),
            P("dom", None),
            P("dom", None, None, None),
            P("dom", None),
            P("dom", None),
            P("dom", None),
            P("feat", None),
            P(),
            P("feat", None),
            P(),
        ),
        out_specs=P(("dom", "feat"), None),
        check_vma=False,
    )
```

```python
import functools

import jax
import jax.numpy as jnp
from jax import lax
from jax.experimental import pallas as pl
from jax.experimental.pallas import tpu as pltpu
from jax.sharding import PartitionSpec as P

LANES = 128
TOUCH = 2
HINT = 5 * 10**10
VMEM_LIMIT = 24 * 1024 * 1024
VMEM = pl.BlockSpec(memory_space=pltpu.VMEM)
SMEM = pl.BlockSpec(memory_space=pltpu.SMEM)
HBM = pl.BlockSpec(memory_space=pltpu.HBM)
PARAMS = pltpu.CompilerParams(vmem_limit_bytes=VMEM_LIMIT)


def dot3(a, b):
    return jnp.dot(a, b, precision=lax.Precision.HIGH, preferred_element_type=jnp.float32)


def two_parts(x):
    high = x.astype(jnp.bfloat16)
    return high, (x - high.astype(jnp.float32)).astype(jnp.bfloat16)


def left_parts(x):
    high, low = two_parts(x)
    return jnp.concatenate([high, low, high], axis=1)


def right_parts(w):
    high, low = two_parts(w)
    return jnp.concatenate([high, high, low], axis=0)


def sum_of_products(lefts, parts):
    total = None
    for x, part in zip(lefts, parts):
        made = jnp.dot(left_parts(x), part, preferred_element_type=jnp.float32)
        total = made if total is None else total + made
    return total


def f32(*dims):
    return jax.ShapeDtypeStruct(dims, jnp.float32)


def hbm(*dims):
    return pltpu.HBM(dims, jnp.float32)


def pinned(*arrays):
    return [pltpu.with_memory_space_constraint(a, pltpu.HBM) for a in arrays]


def rows_at(index, height):
    return pl.ds(pl.multiple_of(index * height, height), height)


def scratch(*dims):
    return pltpu.VMEM(dims, jnp.float32)


def start_all(pairs, sems, first):
    copies = [pltpu.make_async_copy(a, b, sems.at[first + i]) for i, (a, b) in enumerate(pairs)]
    for copy in copies:
        copy.start()
    return copies


def wait_all(copies):
    for copy in copies:
        copy.wait()


def cost(flops):
    return pl.CostEstimate(flops=flops, bytes_accessed=0, transcendentals=0)


def slice_body(index_ref, source, out, sems):
    wait_all(start_all([(source.at[rows_at(index_ref[0], out.shape[0])], out)], sems, 0))


def row_block(index, source, height):
    return pl.pallas_call(
        slice_body,
        out_shape=f32(height, source.shape[1]),
        in_specs=[SMEM, HBM],
        out_specs=VMEM,
        scratch_shapes=[pltpu.SemaphoreType.DMA((1,))],
        compiler_params=PARAMS,
        cost_estimate=cost(0),
    )(index, *pinned(source))


def outgoing_body(want_ref, features, spread, blocks, held, sems):
    count, tile, cols = held.shape
    chunk = spread.shape[1]
    last = features.shape[0] // tile - 1
    copies = []
    for d in range(count):
        rows = rows_at(jnp.minimum(want_ref[d], last), tile)
        for c in range(cols // chunk):
            lanes = pl.ds(c * chunk, chunk)
            held[d, :, lanes] = features[rows, lanes] * spread[rows, :]
        copies += start_all([(held.at[d], blocks.at[d])], sems, d)
    wait_all(copies)


def outgoing_blocks(want, features, spread, tile):
    cols = features.shape[1]
    count = want.shape[0]
    return pl.pallas_call(
        outgoing_body,
        out_shape=hbm(count, tile, cols),
        in_specs=[SMEM, VMEM, VMEM],
        out_specs=HBM,
        scratch_shapes=[scratch(count, tile, cols), pltpu.SemaphoreType.DMA((count,))],
        compiler_params=PARAMS,
        cost_estimate=cost(HINT),
    )(want, features, spread)


def partial_body(count, groups, place_ref, *refs):
    lefts, rights, refs = refs[:count], refs[count : 2 * count], refs[2 * count :]
    outs, (left, right, result, sems) = refs[:-4], refs[-4:]
    cols = lefts[0].shape[1]
    chunk = outs[0].shape[1]
    used = 0
    weights_in, loads, stores = [], [], []
    for n, (at, _) in enumerate(groups):
        lanes = pl.ds(pl.multiple_of(place_ref[at] * cols, cols), cols)
        weights_in.append(start_all([(w.at[:, lanes], right.at[n, j]) for j, w in enumerate(rights)], sems, used))
        used += count
    for start, stop, _ in groups[0][1]:
        rows = pl.ds(start, stop - start)
        pairs = [(x.at[rows], left.at[rows, pl.ds(j * cols, cols)]) for j, x in enumerate(lefts)]
        loads.append(start_all(pairs, sems, used))
        used += count
    for n, (_, steps) in enumerate(groups):
        wait_all(weights_in[n])
        parts = [right_parts(right[n, j]) for j in range(count)]
        for i, (start, stop, targets) in enumerate(steps):
            if n == 0:
                wait_all(loads[i])
            rows = pl.ds(start, stop - start)
            made = sum_of_products([left[rows, pl.ds(j * cols, cols)] for j in range(count)], parts)
            result[n, rows, :] = made
            pairs = [
                (result.at[n, rows, pl.ds(c * chunk, chunk)], outs[o].at[pl.ds(offset, stop - start)])
                for c, o, offset in targets
            ]
            stores += start_all(pairs, sems, used)
            used += len(pairs)
    wait_all(stores)


def partial_sums(place, groups, lefts, weights, shapes, flops=0):
    rows, cols = lefts[0].shape
    depth = weights[0].shape[0]
    count = len(lefts)
    copies = count * (len(groups) + len(groups[0][1]))
    copies += sum(len(targets) for _, steps in groups for _, _, targets in steps)
    return pl.pallas_call(
        functools.partial(partial_body, count, groups),
        out_shape=[hbm(*s) for s in shapes],
        in_specs=[SMEM] + [HBM] * (2 * count),
        out_specs=[HBM] * len(shapes),
        scratch_shapes=[
            scratch(rows, count * cols),
            scratch(len(groups), count, depth, cols),
            scratch(len(groups), rows, cols),
            pltpu.SemaphoreType.DMA((copies,)),
        ],
        compiler_params=PARAMS,
        cost_estimate=cost(flops),
    )(place, *pinned(lefts[0]), *lefts[1:], *pinned(weights[0]), *weights[1:])


def loaded_body(ats, place_ref, *refs):
    sources, outs, sems = refs[: -1 - len(ats)], refs[-1 - len(ats) : -1], refs[-1]
    depth = sources[0].shape[0]
    pairs = []
    for at, out in zip(ats, outs):
        cols = out.shape[1]
        lanes = pl.ds(pl.multiple_of(place_ref[at] * cols, cols), cols)
        pairs += [(w.at[:, lanes], out.at[pl.ds(j * depth, depth)]) for j, w in enumerate(sources)]
    wait_all(start_all(pairs, sems, 0))


def loaded_weights(place, ats, weights, cols):
    depth = weights[0].shape[0]
    count = len(weights)
    return pl.pallas_call(
        functools.partial(loaded_body, ats),
        out_shape=[f32(count * depth, cols)] * len(ats),
        in_specs=[SMEM] + [HBM] * count,
        out_specs=[VMEM] * len(ats),
        scratch_shapes=[pltpu.SemaphoreType.DMA((count * len(ats),))],
        compiler_params=PARAMS,
        cost_estimate=cost(0),
    )(place, *pinned(weights[0]), *weights[1:])


def remote_body(count, *refs):
    lefts, refs = refs[:count], refs[count:]
    groups = len(refs) // (1 + lefts[0].shape[1] // refs[-1].shape[1])
    weights, outs = refs[:groups], refs[groups:]
    chunk = outs[0].shape[1]
    chunks = len(outs) // groups
    depth = lefts[0].shape[1]
    for n, weight in enumerate(weights):
        parts = [right_parts(weight[pl.ds(j * depth, depth), :]) for j in range(count)]
        made = sum_of_products([x[...] for x in lefts], parts)
        for c in range(chunks):
            outs[n * chunks + c][...] = made[:, c * chunk : (c + 1) * chunk]


def remote_products(lefts, weights, chunks):
    rows, cols = lefts[0].shape
    outs = len(weights) * chunks
    return pl.pallas_call(
        functools.partial(remote_body, len(lefts)),
        out_shape=[f32(rows, cols // chunks)] * outs,
        in_specs=[VMEM] * (len(lefts) + len(weights)),
        out_specs=[VMEM] * outs,
        compiler_params=PARAMS,
        cost_estimate=cost(0),
    )(*lefts, *weights)


def joined_body(plan, count, *refs):
    fresh, outs, sems = refs[count : count + len(plan)], refs[count + len(plan) : -1], refs[-1]
    places = [outs[o].at[pl.ds(offset, x.shape[0])] for x, (o, offset) in zip(fresh, plan)]
    wait_all(start_all(list(zip(fresh, places)), sems, 0))


def joined(buffers, fresh, plan, shapes):
    count = len(buffers)
    return pl.pallas_call(
        functools.partial(joined_body, plan, count),
        out_shape=[hbm(*s) for s in shapes],
        in_specs=[HBM] * count + [VMEM] * len(fresh),
        out_specs=[HBM] * len(shapes),
        scratch_shapes=[pltpu.SemaphoreType.DMA((len(plan),))],
        input_output_aliases={i: i for i in range(count)},
        compiler_params=PARAMS,
        cost_estimate=cost(0),
    )(*pinned(*buffers), *fresh)


def chosen_body(source_ref, incoming, chosen):
    tile = incoming.shape[1]
    for g in range(chosen.shape[0] // tile):
        chosen[pl.ds(g * tile, tile), :] = incoming[source_ref[TOUCH * g]]


def chosen_blocks(source, incoming):
    tile, cols = incoming.shape[1:]
    groups = source.shape[0] // TOUCH
    return pl.pallas_call(
        chosen_body,
        out_shape=f32(groups * tile, cols),
        in_specs=[SMEM, VMEM],
        out_specs=VMEM,
        compiler_params=PARAMS,
        cost_estimate=cost(0),
    )(source, incoming)


def received_pairs(layout, received, recv_in):
    return [
        (received[r].at[pl.ds(start, stop - start)], recv_in.at[h, pl.ds(offset, stop - start)])
        for h, r, start, stop, offset in layout
    ]


def own_total(diag_in, spread_in, own_in, recv_in, total, arriving=()):
    tile = diag_in.shape[1]
    for i in range(diag_in.shape[0] // tile):
        wait_all([copy for offset, copy in arriving if i * tile <= offset < (i + 1) * tile])
        rows = pl.ds(i * tile, tile)
        mixed = own_in[rows, :]
        for h in range(recv_in.shape[0]):
            mixed = mixed + recv_in[h, rows, :]
        total[rows, :] = dot3(diag_in[rows, :], mixed * spread_in[rows, :])


def own_body(layout, diag, spread, own, *refs):
    received, (base, diag_in, spread_in, own_in, recv_in, sems) = refs[:-6], refs[-6:]
    pairs = [(diag, diag_in), (spread, spread_in), (own, own_in)]
    wait_all(start_all(pairs + received_pairs(layout, received, recv_in), sems, 0))
    own_total(diag_in, spread_in, own_in, recv_in, base)


def own_part(diag, spread, own, received, layout, others):
    return pl.pallas_call(
        functools.partial(own_body, layout),
        out_shape=f32(*own.shape),
        in_specs=[HBM] * (3 + len(received)),
        out_specs=VMEM,
        scratch_shapes=[scratch(*a.shape) for a in (diag, spread, own)]
        + [scratch(others, *own.shape), pltpu.SemaphoreType.DMA((3 + len(layout),))],
        compiler_params=PARAMS,
        cost_estimate=cost(0),
    )(*pinned(diag, spread, own), *received)


def hidden_tail(
    lane_offset, row_ref, want_ref, first_ref, bias, remote, spread, sums, blocks, scaled_out, total, scaled, sems, used
):
    tiles, tile = remote.shape[:2]
    parts = blocks.shape[0]
    chunk = total.shape[1]
    for g in range(tiles // TOUCH):
        block = sums[0][pl.ds(g * tile, tile), :]
        for x in sums[1:]:
            block = block + x[pl.ds(g * tile, tile), :]
        for k in range(TOUCH * g, TOUCH * g + TOUCH):
            total[rows_at(row_ref[k], tile), :] += dot3(remote[k], block)
    lanes = pl.ds(pl.multiple_of(first_ref[0] + lane_offset, chunk), chunk)
    last = scaled.shape[0] // tile - 1
    copies = []
    for i in range(last + 1):
        rows = pl.ds(i * tile, tile)
        scaled[rows, :] = jnp.maximum(total[rows, :] * spread[rows, :] + bias[:, lanes], 0.0) * spread[rows, :]
        copies += start_all([(scaled.at[rows], scaled_out.at[rows])], sems, used + parts + i)
    pairs = [(scaled.at[rows_at(jnp.minimum(want_ref[d], last), tile)], blocks.at[d]) for d in range(parts)]
    wait_all(copies + start_all(pairs, sems, used))


def hidden_body(lane_offset, row_ref, want_ref, first_ref, bias, base, remote, spread, *refs):
    sums, (blocks, scaled_out, total, scaled, sems) = refs[:-5], refs[-5:]
    total[...] = base[...]
    hidden_tail(
        lane_offset, row_ref, want_ref, first_ref, bias, remote, spread, sums, blocks, scaled_out, total, scaled, sems, 0
    )


def hidden_blocks(row, want, first, lane_offset, bias, base, remote, spread, remote_sums):
    rows, chunk = base.shape
    tile = remote.shape[1]
    parts = want.shape[0]
    return pl.pallas_call(
        functools.partial(hidden_body, lane_offset),
        out_shape=[hbm(parts, tile, chunk), hbm(rows, chunk)],
        in_specs=[SMEM] * 3 + [VMEM] * (4 + len(remote_sums)),
        out_specs=[HBM, HBM],
        scratch_shapes=[scratch(rows, chunk), scratch(rows, chunk), pltpu.SemaphoreType.DMA((parts + rows // tile,))],
        compiler_params=PARAMS,
        cost_estimate=cost(HINT),
    )(row, want, first, bias, base, remote, spread, *remote_sums)


def resident_body(diag, scaled, others, *refs):
    sources, refs = refs[:others], refs[others:]
    diag_out, outs, refs = refs[0], refs[1 : 1 + others], refs[1 + others :]
    base, scaled_in, total, sems = refs
    tile = diag.shape[1]
    first = start_all([(diag, diag_out), (scaled, scaled_in)], sems, 0)
    copies = start_all(list(zip(sources, outs)), sems, 2)
    wait_all(first)
    for i in range(diag.shape[0] // tile):
        rows = pl.ds(i * tile, tile)
        total[rows, :] = dot3(diag_out[rows, :], scaled_in[rows, :])
    wait_all(copies + start_all([(total, base)], sems, 2 + others))


def resident_and_diagonal(diag, scaled, *arrays):
    count = len(arrays)

    def body(diag, scaled, *refs):
        resident_body(diag, scaled, count, *refs)

    *held, base = pl.pallas_call(
        body,
        out_shape=[f32(*a.shape) for a in (diag, *arrays)] + [hbm(*scaled.shape)],
        in_specs=[HBM] * (2 + count),
        out_specs=[VMEM] * (1 + count) + [HBM],
        scratch_shapes=[scratch(*scaled.shape)] * 2 + [pltpu.SemaphoreType.DMA((3 + count,))],
        compiler_params=PARAMS,
        cost_estimate=cost(0),
    )(*pinned(diag, scaled, *arrays))
    return held, base


def later_body(
    ends, layout, lane_offset, row_ref, want_ref, first_ref, bias, own, remote, spread, diag, own_sum, *refs
):
    received, refs = refs[:-7], refs[-7:]
    blocks, scaled_out, total, scaled, sums_in, recv_in, sems = refs
    others, height = sums_in.shape[:2]
    pairs = received_pairs(layout, received, recv_in)
    late = [(r.at[pl.ds(ends - height, height)], sums_in.at[j]) for j, r in enumerate(received[-others:])]
    first = start_all(pairs, sems, 0)
    tail = start_all(late, sems, len(pairs))
    own_total(diag, spread, own, recv_in, total, [(entry[-1], copy) for entry, copy in zip(layout, first)])
    wait_all(tail)
    sums = [own_sum] + [sums_in.at[j] for j in range(others)]
    hidden_tail(
        lane_offset,
        row_ref,
        want_ref,
        first_ref,
        bias,
        remote,
        spread,
        sums,
        blocks,
        scaled_out,
        total,
        scaled,
        sems,
        len(pairs) + len(late),
    )


def later_blocks(
    row, want, first, lane_offset, bias, own, remote, spread, diag, own_sum, received, layout, ends, others
):
    rows, chunk = own.shape
    tile = diag.shape[1]
    parts = want.shape[0]
    return pl.pallas_call(
        functools.partial(later_body, ends, layout, lane_offset),
        out_shape=[hbm(parts, tile, chunk), hbm(rows, chunk)],
        in_specs=[SMEM] * 3 + [VMEM] * 6 + [HBM] * len(received),
        out_specs=[HBM, HBM],
        scratch_shapes=[scratch(rows, chunk), scratch(rows, chunk)]
        + [scratch(others, *own_sum.shape), scratch(others, rows, chunk)]
        + [pltpu.SemaphoreType.DMA((len(layout) + others + parts + rows // tile,))],
        compiler_params=PARAMS,
        cost_estimate=cost(HINT),
    )(row, want, first, bias, own, remote, spread, diag, own_sum, *received)


def diagonal_body(diag, scaled, base, diag_in, scaled_in, total, sems):
    tile = diag.shape[1]
    wait_all(start_all([(diag, diag_in), (scaled, scaled_in)], sems, 0))
    for i in range(diag.shape[0] // tile):
        rows = pl.ds(i * tile, tile)
        total[rows, :] = dot3(diag_in[rows, :], scaled_in[rows, :])
    wait_all(start_all([(total, base)], sems, 2))


def diagonal_part(diag, scaled):
    return pl.pallas_call(
        diagonal_body,
        out_shape=hbm(*scaled.shape),
        in_specs=[HBM, HBM],
        out_specs=HBM,
        scratch_shapes=[scratch(*a.shape) for a in (diag, scaled, scaled)] + [pltpu.SemaphoreType.DMA((3,))],
        compiler_params=PARAMS,
        cost_estimate=cost(0),
    )(*pinned(diag, scaled))


def pieces_body(stored, source_ref, row_ref, place_ref, base, remote, spread, incoming, *refs):
    pieces, (total, remote_in, spread_in, incoming_in, sems) = refs[:-5], refs[-5:]
    tiles, tile = remote.shape[:2]
    early = start_all(
        [(incoming, incoming_in), (remote, remote_in), (base, total), (spread, spread_in)], sems, 0
    )
    wait_all(early[:3])
    for k in range(tiles):
        total[rows_at(row_ref[k], tile), :] += dot3(remote_in[k], incoming_in[source_ref[k]])
    wait_all(early[3:])
    height = pieces[0].shape[0]
    copies = []
    for j in reversed(range(len(pieces))):
        rows = rows_at(place_ref[j], height)
        made = total[rows, :] * spread_in[rows, :]
        if stored:
            total[rows, :] = made
            copies += start_all([(total.at[rows], pieces[j])], sems, 4 + j)
        else:
            pieces[j][...] = made
    wait_all(copies)


def feature_pieces(source, row, place, base, remote, spread, incoming, stored):
    rows, chunk = base.shape
    feats = place.shape[0]
    make = hbm if stored else f32
    return pl.pallas_call(
        functools.partial(pieces_body, stored),
        out_shape=[make(rows // feats, chunk)] * feats,
        in_specs=[SMEM] * 3 + [HBM] * 4,
        out_specs=[HBM if stored else VMEM] * feats,
        scratch_shapes=[scratch(*a.shape) for a in (base, remote, spread, incoming)]
        + [pltpu.SemaphoreType.DMA((4 + feats,))],
        compiler_params=PARAMS,
        cost_estimate=cost(0),
    )(source, row, place, *pinned(base, remote, spread), incoming)


def chosen_block(weights, number, turn, c, chunk, lanes):
    rows = pl.ds(c * chunk if weights[0].shape[0] > chunk else 0, chunk)
    block = weights[0][rows, lanes]
    for k in range(1, number):
        block = jnp.where(turn == k, weights[k][rows, lanes], block)
    return block


def product_body(count, choices, later, c, step, last, turn_ref, start, *refs):
    pieces, refs = refs[:count], refs[count:]
    weights, refs = refs[: sum(choices)], refs[sum(choices) :]
    ahead, refs = refs[: sum(later)], refs[sum(later) :]
    kept, (out, left, held, sems) = refs[: len(later)], refs[len(later) :]
    chunk = pieces[0].shape[1]
    left[...] = left_parts(jnp.concatenate([p[...] for p in pieces], axis=1))
    copies = []
    for j in range(held.shape[1] // step):
        lanes = pl.ds(j * step, step)
        blocks, at = [], 0
        for number in choices:
            blocks.append(chosen_block(weights[at:], number, turn_ref[0], c, chunk, lanes))
            at += number
        right = right_parts(jnp.concatenate(blocks, axis=0))
        made = start[:, lanes] + jnp.dot(left[...], right, preferred_element_type=jnp.float32)
        if last:
            held[:, lanes] = made
            copies += start_all([(held.at[:, lanes], out.at[:, lanes])], sems, j)
        else:
            out[:, lanes] = made
    at = 0
    for number, block in zip(later, kept):
        block[...] = chosen_block(ahead[at:], number, turn_ref[0], c, chunk, pl.ds(0, held.shape[1]))
        at += number
    wait_all(copies)


def add_product(turn, start, pieces, weights, c, last, ahead=()):
    rows, chunk = pieces[0].shape
    width = start.shape[1]
    step = min(2 * LANES, width)
    count = len(pieces)
    flat = [w for group in [*weights, *ahead] for w in group]
    choices, later = [len(group) for group in weights], [len(group) for group in ahead]
    return pl.pallas_call(
        functools.partial(product_body, count, choices, later, c, step, last),
        out_shape=[f32(chunk, width)] * len(later) + [hbm(rows, width) if last else f32(rows, width)],
        in_specs=[SMEM] + [VMEM] * (1 + count + len(flat)),
        out_specs=[VMEM] * len(later) + [HBM if last else VMEM],
        scratch_shapes=[
            pltpu.VMEM((rows, 3 * count * chunk), jnp.bfloat16),
            scratch(rows, width),
            pltpu.SemaphoreType.DMA((width // step,)),
        ],
        compiler_params=PARAMS,
        cost_estimate=cost(6 * count * rows * chunk * width),
    )(turn, start, *pieces, *flat)


def solution(mesh):
    parts = mesh.shape["dom"]
    feats = mesh.shape["feat"]
    sides = 2 if feats % 2 == 0 else 1
    halves = feats // sides
    others = list(range(1, halves))

    def feat_target(f, dh, dl):
        return (f // sides + dh) % halves * sides + (f % sides + dl) % sides

    def feat_send(x, dh, dl):
        return lax.ppermute(x, "feat", [(f, feat_target(f, dh, dl)) for f in range(feats)])

    def dom_exchange(x):
        return lax.all_to_all(x, "dom", split_axis=0, concat_axis=0, tiled=True)

    def per_device(
        features,
        degree,
        diag_adj,
        remote_adj,
        read_block,
        tile_src,
        tile_row,
        w_first,
        b_first,
        w_second,
        b_second,
    ):
        part, cols = features.shape
        tile = diag_adj.shape[1]
        blocks = part // tile
        remote = remote_adj[0]
        chunk = LANES if cols % LANES == 0 else cols
        chunks = cols // chunk
        f = lax.axis_index("feat")
        want, source, row = read_block[0], tile_src[0], tile_row[0]
        shifts = [(dh, dl) for dh in range(halves) for dl in range(sides)]
        place = jnp.stack([jnp.asarray(feat_target(f, dh, dl), jnp.int32) for dh, dl in shifts])
        first = jnp.reshape(jnp.asarray(f * cols, jnp.int32), (1,))
        bias = b_first[None, :]

        x_all = [features] + [feat_send(features, 0, dl) for dl in range(1, sides)]
        w_all = [w_first] + [feat_send(w_first, 0, dl) for dl in range(1, sides)]

        shares = chunks if parts % chunks == 0 else 1
        share = jnp.reshape(jnp.asarray(lax.axis_index("dom") % shares, jnp.int32), (1,))

        def share_send(x, k):
            pairs = [(s, s // shares * shares + (s % shares + k) % shares) for s in range(parts)]
            return lax.ppermute(x, "dom", pairs)

        w2_sent = row_block(share, w_second, w_second.shape[0] // shares)
        w2_got = [feat_send(w2_sent, dh, 0) for dh in others]

        scaling = lax.rsqrt(degree.astype(jnp.float32))
        spread = jnp.broadcast_to(scaling[:, None], (part, chunk))
        outgoing = outgoing_blocks(want, features, spread, tile)
        incoming = dom_exchange(outgoing)

        early = blocks // 4 * tile if chunks > 1 else part
        late = part - early
        left_tiles = late // tile
        marks = sorted({0, early, early + left_tiles * 4 // 9 * tile, early + left_tiles * 7 // 9 * tile, part})
        spans = list(zip(marks[:-1], marks[1:]))
        x_all[0], _ = lax.optimization_barrier((features, outgoing))
        send_steps = []
        for start, stop in spans:
            targets = [(0, 0, start)]
            for c in range(1, chunks):
                if stop <= early:
                    targets.append((c, 0, part + (c - 1) * early + start))
                else:
                    targets.append((c, 1, (c - 1) * late + start - early))
            send_steps.append((start, stop, targets))
        send_shapes = [(part + (chunks - 1) * early, chunk)]
        if chunks > 1:
            send_shapes.append(((chunks - 1) * (late + remote.shape[0] // TOUCH * tile), chunk))
        sends = [partial_sums(place, [(dh * sides, send_steps)], x_all, w_all, send_shapes) for dh in others]
        sends, w2_got = lax.optimization_barrier((sends, w2_got))
        front = [feat_send(x[0], dh, 0) for dh, x in zip(others, sends)]

        own_steps = [(a, b, [(c, c, a) for c in range(chunks)]) for a, b in spans]
        own = list(partial_sums(place, [(0, own_steps)], x_all, w_all, [(part, chunk)] * chunks, HINT))

        incoming, own = lax.optimization_barrier((incoming, list(own)))
        w2_core = [w_second] + [feat_send(w_second, 0, dl) for dl in range(1, sides)]
        chosen = chosen_blocks(source, incoming)
        chosen_all = [chosen] + [feat_send(chosen, 0, dl) for dl in range(1, sides)]
        height = chosen.shape[0]
        tail_rows = (chunks - 1) * late
        ats = [dh * sides for dh in others] + [0]
        turned, _ = lax.optimization_barrier((place, chosen))
        made = remote_products(chosen_all, loaded_weights(turned, ats, w_all, cols), chunks)
        remote_front = [feat_send(made[i * chunks], dh, 0) for i, dh in enumerate(others)]
        remote_own = list(made[len(others) * chunks :])
        rest = []
        if chunks > 1:
            buffers, fresh, plan, shapes = [x[1] for x in sends], [], [], []
            for i, x in enumerate(sends):
                for c in range(1, chunks):
                    fresh.append(made[i * chunks + c])
                    plan.append((i, tail_rows + (c - 1) * height))
                shapes.append(x[1].shape)
            for c in range(1, chunks):
                fresh.append(remote_own[c])
                plan.append((len(shapes), 0))
                shapes.append((height, chunk))
            written = joined(buffers, fresh, plan, shapes)
            rest = [feat_send(x, dh, 0) for dh, x in zip(others, written)]
            remote_own[1:] = written[len(others) :]

        reach = len(others)
        first_layout = [(h, h, 0, part, 0) for h in range(reach)]
        base = own_part(diag_adj, spread, own[0], front, first_layout, reach)
        incoming, bases = [], []
        for c in range(chunks):
            if c == 0:
                outgoing, scaled = hidden_blocks(
                    row, want, first, 0, bias, base, remote, spread, [remote_own[0]] + remote_front
                )
            else:
                begin, _ = lax.optimization_barrier((own[c], outgoing))
                (held_diag, *held), base = resident_and_diagonal(
                    diag_adj, scaled, begin, remote, spread, remote_own[c]
                )
                bases.append(base)
                layout = []
                for h in range(reach):
                    layout.append((h, h, part + (c - 1) * early, part + c * early, 0))
                    for at in range(0, late, early):
                        begins = (c - 1) * late + at
                        layout.append((h, reach + h, begins, min(begins + early, c * late), early + at))
                outgoing, scaled = later_blocks(
                    row,
                    want,
                    first,
                    c * chunk,
                    bias,
                    *held[:3],
                    held_diag,
                    held[3],
                    front + rest,
                    layout,
                    tail_rows + c * height,
                    reach,
                )
            arrived = dom_exchange(outgoing)
            incoming.append(pinned(arrived)[0] if c < chunks - 1 else arrived)
        bases.append(diagonal_part(diag_adj, scaled))

        collected = []
        for c in range(chunks):
            pieces = feature_pieces(source, row, place, bases[c], remote, spread, incoming[c], c < chunks - 1)
            collected.append(
                [p if dh == 0 and dl == 0 else feat_send(p, dh, dl) for (dh, dl), p in zip(shifts, pieces)]
            )

        w2_groups = [[got] + [share_send(got, k) for k in range(1, shares)] for got in w2_got]
        w2_groups, _ = lax.optimization_barrier((w2_groups, outgoing))
        w2_far = [[feat_send(w, 0, dl) if dl > 0 else w for w in g] for g in w2_groups for dl in range(sides)]
        weights = [[w] for w in w2_core] + w2_far
        out = b_second[None, :]
        for c in range(chunks):
            turn = (share - c) % shares
            if c < chunks - 1 or halves == 1:
                (out,) = add_product(turn, out, collected[c], weights, c, c == chunks - 1)
            else:
                near, far = collected[c][:sides], collected[c][sides:]
                *kept, out = add_product(turn, out, near, weights[:sides], c, False, weights[sides:])
                (out,) = add_product(turn, out, far, [[w] for w in kept], c, True)
        return out

    return jax.shard_map(
        per_device,
        mesh=mesh,
        in_specs=(
            P("dom", "feat"),
            P("dom"),
            P("dom", None),
            P("dom", None, None, None),
            P("dom", None),
            P("dom", None),
            P("dom", None),
            P("feat", None),
            P(),
            P("feat", None),
            P(),
        ),
        out_specs=P(("dom", "feat"), None),
        check_vma=False,
    )
```

```python
import functools

import jax
import jax.numpy as jnp
from jax import lax
from jax.experimental import pallas as pl
from jax.experimental.pallas import tpu as pltpu
from jax.sharding import PartitionSpec as P

LANES = 128
TOUCH = 2
HINT = 5 * 10**10
VMEM_LIMIT = 24 * 1024 * 1024
VMEM = pl.BlockSpec(memory_space=pltpu.VMEM)
SMEM = pl.BlockSpec(memory_space=pltpu.SMEM)
HBM = pl.BlockSpec(memory_space=pltpu.HBM)
PARAMS = pltpu.CompilerParams(vmem_limit_bytes=VMEM_LIMIT)


def dot3(a, b):
    return jnp.dot(a, b, precision=lax.Precision.HIGH, preferred_element_type=jnp.float32)


def two_parts(x):
    high = x.astype(jnp.bfloat16)
    return high, (x - high.astype(jnp.float32)).astype(jnp.bfloat16)


def left_parts(x):
    high, low = two_parts(x)
    return jnp.concatenate([high, low, high], axis=1)


def right_parts(w):
    high, low = two_parts(w)
    return jnp.concatenate([high, high, low], axis=0)


def sum_of_products(lefts, parts):
    total = None
    for x, part in zip(lefts, parts):
        made = jnp.dot(left_parts(x), part, preferred_element_type=jnp.float32)
        total = made if total is None else total + made
    return total


def f32(*dims):
    return jax.ShapeDtypeStruct(dims, jnp.float32)


def hbm(*dims):
    return pltpu.HBM(dims, jnp.float32)


def pinned(*arrays):
    return [pltpu.with_memory_space_constraint(a, pltpu.HBM) for a in arrays]


def rows_at(index, height):
    return pl.ds(pl.multiple_of(index * height, height), height)


def scratch(*dims):
    return pltpu.VMEM(dims, jnp.float32)


def start_all(pairs, sems, first):
    copies = [pltpu.make_async_copy(a, b, sems.at[first + i]) for i, (a, b) in enumerate(pairs)]
    for copy in copies:
        copy.start()
    return copies


def wait_all(copies):
    for copy in copies:
        copy.wait()


def cost(flops):
    return pl.CostEstimate(flops=flops, bytes_accessed=0, transcendentals=0)


def slice_body(index_ref, source, out, sems):
    wait_all(start_all([(source.at[rows_at(index_ref[0], out.shape[0])], out)], sems, 0))


def row_block(index, source, height):
    return pl.pallas_call(
        slice_body,
        out_shape=f32(height, source.shape[1]),
        in_specs=[SMEM, HBM],
        out_specs=VMEM,
        scratch_shapes=[pltpu.SemaphoreType.DMA((1,))],
        compiler_params=PARAMS,
        cost_estimate=cost(0),
    )(index, *pinned(source))


def outgoing_body(want_ref, features, spread, blocks, held, sems):
    count, tile, cols = held.shape
    chunk = spread.shape[1]
    last = features.shape[0] // tile - 1
    copies = []
    for d in range(count):
        rows = rows_at(jnp.minimum(want_ref[d], last), tile)
        for c in range(cols // chunk):
            lanes = pl.ds(c * chunk, chunk)
            held[d, :, lanes] = features[rows, lanes] * spread[rows, :]
        copies += start_all([(held.at[d], blocks.at[d])], sems, d)
    wait_all(copies)


def outgoing_blocks(want, features, spread, tile):
    cols = features.shape[1]
    count = want.shape[0]
    return pl.pallas_call(
        outgoing_body,
        out_shape=hbm(count, tile, cols),
        in_specs=[SMEM, VMEM, VMEM],
        out_specs=HBM,
        scratch_shapes=[scratch(count, tile, cols), pltpu.SemaphoreType.DMA((count,))],
        compiler_params=PARAMS,
        cost_estimate=cost(HINT),
    )(want, features, spread)


def partial_body(count, groups, place_ref, *refs):
    lefts, rights, refs = refs[:count], refs[count : 2 * count], refs[2 * count :]
    outs, (left, right, result, sems) = refs[:-4], refs[-4:]
    cols = lefts[0].shape[1]
    chunk = outs[0].shape[1]
    used = 0
    weights_in, loads, stores = [], [], []
    for n, (at, _) in enumerate(groups):
        lanes = pl.ds(pl.multiple_of(place_ref[at] * cols, cols), cols)
        weights_in.append(start_all([(w.at[:, lanes], right.at[n, j]) for j, w in enumerate(rights)], sems, used))
        used += count
    for start, stop, _ in groups[0][1]:
        rows = pl.ds(start, stop - start)
        pairs = [(x.at[rows], left.at[rows, pl.ds(j * cols, cols)]) for j, x in enumerate(lefts)]
        loads.append(start_all(pairs, sems, used))
        used += count
    for n, (_, steps) in enumerate(groups):
        wait_all(weights_in[n])
        parts = [right_parts(right[n, j]) for j in range(count)]
        for i, (start, stop, targets) in enumerate(steps):
            if n == 0:
                wait_all(loads[i])
            rows = pl.ds(start, stop - start)
            made = sum_of_products([left[rows, pl.ds(j * cols, cols)] for j in range(count)], parts)
            result[n, rows, :] = made
            pairs = [
                (result.at[n, rows, pl.ds(c * chunk, chunk)], outs[o].at[pl.ds(offset, stop - start)])
                for c, o, offset in targets
            ]
            stores += start_all(pairs, sems, used)
            used += len(pairs)
    wait_all(stores)


def partial_sums(place, groups, lefts, weights, shapes, flops=0):
    rows, cols = lefts[0].shape
    depth = weights[0].shape[0]
    count = len(lefts)
    copies = count * (len(groups) + len(groups[0][1]))
    copies += sum(len(targets) for _, steps in groups for _, _, targets in steps)
    return pl.pallas_call(
        functools.partial(partial_body, count, groups),
        out_shape=[hbm(*s) for s in shapes],
        in_specs=[SMEM] + [HBM] * (2 * count),
        out_specs=[HBM] * len(shapes),
        scratch_shapes=[
            scratch(rows, count * cols),
            scratch(len(groups), count, depth, cols),
            scratch(len(groups), rows, cols),
            pltpu.SemaphoreType.DMA((copies,)),
        ],
        compiler_params=PARAMS,
        cost_estimate=cost(flops),
    )(place, *pinned(lefts[0]), *lefts[1:], *pinned(weights[0]), *weights[1:])


def loaded_body(ats, place_ref, *refs):
    sources, outs, sems = refs[: -1 - len(ats)], refs[-1 - len(ats) : -1], refs[-1]
    depth = sources[0].shape[0]
    pairs = []
    for at, out in zip(ats, outs):
        cols = out.shape[1]
        lanes = pl.ds(pl.multiple_of(place_ref[at] * cols, cols), cols)
        pairs += [(w.at[:, lanes], out.at[pl.ds(j * depth, depth)]) for j, w in enumerate(sources)]
    wait_all(start_all(pairs, sems, 0))


def loaded_weights(place, ats, weights, cols):
    depth = weights[0].shape[0]
    count = len(weights)
    return pl.pallas_call(
        functools.partial(loaded_body, ats),
        out_shape=[f32(count * depth, cols)] * len(ats),
        in_specs=[SMEM] + [HBM] * count,
        out_specs=[VMEM] * len(ats),
        scratch_shapes=[pltpu.SemaphoreType.DMA((count * len(ats),))],
        compiler_params=PARAMS,
        cost_estimate=cost(0),
    )(place, *pinned(weights[0]), *weights[1:])


def remote_body(count, *refs):
    lefts, refs = refs[:count], refs[count:]
    groups = len(refs) // (1 + lefts[0].shape[1] // refs[-1].shape[1])
    weights, outs = refs[:groups], refs[groups:]
    chunk = outs[0].shape[1]
    chunks = len(outs) // groups
    depth = lefts[0].shape[1]
    for n, weight in enumerate(weights):
        parts = [right_parts(weight[pl.ds(j * depth, depth), :]) for j in range(count)]
        made = sum_of_products([x[...] for x in lefts], parts)
        for c in range(chunks):
            outs[n * chunks + c][...] = made[:, c * chunk : (c + 1) * chunk]


def remote_products(lefts, weights, chunks):
    rows, cols = lefts[0].shape
    outs = len(weights) * chunks
    return pl.pallas_call(
        functools.partial(remote_body, len(lefts)),
        out_shape=[f32(rows, cols // chunks)] * outs,
        in_specs=[VMEM] * (len(lefts) + len(weights)),
        out_specs=[VMEM] * outs,
        compiler_params=PARAMS,
        cost_estimate=cost(0),
    )(*lefts, *weights)


def joined_body(plan, count, *refs):
    fresh, outs, sems = refs[count : count + len(plan)], refs[count + len(plan) : -1], refs[-1]
    places = [outs[o].at[pl.ds(offset, x.shape[0])] for x, (o, offset) in zip(fresh, plan)]
    wait_all(start_all(list(zip(fresh, places)), sems, 0))


def joined(buffers, fresh, plan, shapes):
    count = len(buffers)
    return pl.pallas_call(
        functools.partial(joined_body, plan, count),
        out_shape=[hbm(*s) for s in shapes],
        in_specs=[HBM] * count + [VMEM] * len(fresh),
        out_specs=[HBM] * len(shapes),
        scratch_shapes=[pltpu.SemaphoreType.DMA((len(plan),))],
        input_output_aliases={i: i for i in range(count)},
        compiler_params=PARAMS,
        cost_estimate=cost(0),
    )(*pinned(*buffers), *fresh)


def chosen_body(source_ref, incoming, chosen):
    tile = incoming.shape[1]
    for g in range(chosen.shape[0] // tile):
        chosen[pl.ds(g * tile, tile), :] = incoming[source_ref[TOUCH * g]]


def chosen_blocks(source, incoming):
    tile, cols = incoming.shape[1:]
    groups = source.shape[0] // TOUCH
    return pl.pallas_call(
        chosen_body,
        out_shape=f32(groups * tile, cols),
        in_specs=[SMEM, VMEM],
        out_specs=VMEM,
        compiler_params=PARAMS,
        cost_estimate=cost(0),
    )(source, incoming)


def received_pairs(layout, received, recv_in):
    return [
        (received[r].at[pl.ds(start, stop - start)], recv_in.at[h, pl.ds(offset, stop - start)])
        for h, r, start, stop, offset in layout
    ]


def own_total(diag_in, spread_in, own_in, recv_in, total):
    tile = diag_in.shape[1]
    for i in range(diag_in.shape[0] // tile):
        rows = pl.ds(i * tile, tile)
        mixed = own_in[rows, :]
        for h in range(recv_in.shape[0]):
            mixed = mixed + recv_in[h, rows, :]
        total[rows, :] = dot3(diag_in[rows, :], mixed * spread_in[rows, :])


def own_body(layout, diag, spread, own, *refs):
    received, (base, diag_in, spread_in, own_in, recv_in, sems) = refs[:-6], refs[-6:]
    pairs = [(diag, diag_in), (spread, spread_in), (own, own_in)]
    wait_all(start_all(pairs + received_pairs(layout, received, recv_in), sems, 0))
    own_total(diag_in, spread_in, own_in, recv_in, base)


def own_part(diag, spread, own, received, layout, others):
    return pl.pallas_call(
        functools.partial(own_body, layout),
        out_shape=f32(*own.shape),
        in_specs=[HBM] * (3 + len(received)),
        out_specs=VMEM,
        scratch_shapes=[scratch(*a.shape) for a in (diag, spread, own)]
        + [scratch(others, *own.shape), pltpu.SemaphoreType.DMA((3 + len(layout),))],
        compiler_params=PARAMS,
        cost_estimate=cost(0),
    )(*pinned(diag, spread, own), *received)


def hidden_tail(
    lane_offset, row_ref, want_ref, first_ref, bias, remote, spread, sums, blocks, scaled_out, total, scaled, sems, used
):
    tiles, tile = remote.shape[:2]
    parts = blocks.shape[0]
    chunk = total.shape[1]
    for g in range(tiles // TOUCH):
        block = sums[0][pl.ds(g * tile, tile), :]
        for x in sums[1:]:
            block = block + x[pl.ds(g * tile, tile), :]
        for k in range(TOUCH * g, TOUCH * g + TOUCH):
            total[rows_at(row_ref[k], tile), :] += dot3(remote[k], block)
    lanes = pl.ds(pl.multiple_of(first_ref[0] + lane_offset, chunk), chunk)
    last = scaled.shape[0] // tile - 1
    copies = []
    for i in range(last + 1):
        rows = pl.ds(i * tile, tile)
        scaled[rows, :] = jnp.maximum(total[rows, :] * spread[rows, :] + bias[:, lanes], 0.0) * spread[rows, :]
        copies += start_all([(scaled.at[rows], scaled_out.at[rows])], sems, used + parts + i)
    pairs = [(scaled.at[rows_at(jnp.minimum(want_ref[d], last), tile)], blocks.at[d]) for d in range(parts)]
    wait_all(copies + start_all(pairs, sems, used))


def hidden_body(lane_offset, row_ref, want_ref, first_ref, bias, base, remote, spread, *refs):
    sums, (blocks, scaled_out, total, scaled, sems) = refs[:-5], refs[-5:]
    total[...] = base[...]
    hidden_tail(
        lane_offset, row_ref, want_ref, first_ref, bias, remote, spread, sums, blocks, scaled_out, total, scaled, sems, 0
    )


def hidden_blocks(row, want, first, lane_offset, bias, base, remote, spread, remote_sums):
    rows, chunk = base.shape
    tile = remote.shape[1]
    parts = want.shape[0]
    return pl.pallas_call(
        functools.partial(hidden_body, lane_offset),
        out_shape=[hbm(parts, tile, chunk), hbm(rows, chunk)],
        in_specs=[SMEM] * 3 + [VMEM] * (4 + len(remote_sums)),
        out_specs=[HBM, HBM],
        scratch_shapes=[scratch(rows, chunk), scratch(rows, chunk), pltpu.SemaphoreType.DMA((parts + rows // tile,))],
        compiler_params=PARAMS,
        cost_estimate=cost(HINT),
    )(row, want, first, bias, base, remote, spread, *remote_sums)


def resident_body(diag, scaled, others, *refs):
    sources, refs = refs[:others], refs[others:]
    diag_out, outs, refs = refs[0], refs[1 : 1 + others], refs[1 + others :]
    base, scaled_in, total, sems = refs
    tile = diag.shape[1]
    first = start_all([(diag, diag_out), (scaled, scaled_in)], sems, 0)
    copies = start_all(list(zip(sources, outs)), sems, 2)
    wait_all(first)
    for i in range(diag.shape[0] // tile):
        rows = pl.ds(i * tile, tile)
        total[rows, :] = dot3(diag_out[rows, :], scaled_in[rows, :])
    wait_all(copies + start_all([(total, base)], sems, 2 + others))


def resident_and_diagonal(diag, scaled, *arrays):
    count = len(arrays)

    def body(diag, scaled, *refs):
        resident_body(diag, scaled, count, *refs)

    *held, base = pl.pallas_call(
        body,
        out_shape=[f32(*a.shape) for a in (diag, *arrays)] + [hbm(*scaled.shape)],
        in_specs=[HBM] * (2 + count),
        out_specs=[VMEM] * (1 + count) + [HBM],
        scratch_shapes=[scratch(*scaled.shape)] * 2 + [pltpu.SemaphoreType.DMA((3 + count,))],
        compiler_params=PARAMS,
        cost_estimate=cost(0),
    )(*pinned(diag, scaled, *arrays))
    return held, base


def later_body(layout, diag, spread, own, *refs):
    received, (base, recv_in, sems) = refs[:-3], refs[-3:]
    wait_all(start_all(received_pairs(layout, received, recv_in), sems, 0))
    own_total(diag, spread, own, recv_in, base)


def later_part(diag, spread, own, received, layout, others):
    return pl.pallas_call(
        functools.partial(later_body, layout),
        out_shape=f32(*own.shape),
        in_specs=[VMEM] * 3 + [HBM] * len(received),
        out_specs=VMEM,
        scratch_shapes=[scratch(others, *own.shape), pltpu.SemaphoreType.DMA((len(layout),))],
        compiler_params=PARAMS,
        cost_estimate=cost(0),
    )(diag, spread, own, *received)


def diagonal_body(diag, scaled, base, diag_in, scaled_in, total, sems):
    tile = diag.shape[1]
    wait_all(start_all([(diag, diag_in), (scaled, scaled_in)], sems, 0))
    for i in range(diag.shape[0] // tile):
        rows = pl.ds(i * tile, tile)
        total[rows, :] = dot3(diag_in[rows, :], scaled_in[rows, :])
    wait_all(start_all([(total, base)], sems, 2))


def diagonal_part(diag, scaled):
    return pl.pallas_call(
        diagonal_body,
        out_shape=hbm(*scaled.shape),
        in_specs=[HBM, HBM],
        out_specs=HBM,
        scratch_shapes=[scratch(*a.shape) for a in (diag, scaled, scaled)] + [pltpu.SemaphoreType.DMA((3,))],
        compiler_params=PARAMS,
        cost_estimate=cost(0),
    )(*pinned(diag, scaled))


def pieces_body(stored, source_ref, row_ref, place_ref, base, remote, spread, incoming, *refs):
    pieces, (total, remote_in, spread_in, incoming_in, sems) = refs[:-5], refs[-5:]
    tiles, tile = remote.shape[:2]
    early = start_all(
        [(incoming, incoming_in), (remote, remote_in), (base, total), (spread, spread_in)], sems, 0
    )
    wait_all(early[:3])
    for k in range(tiles):
        total[rows_at(row_ref[k], tile), :] += dot3(remote_in[k], incoming_in[source_ref[k]])
    wait_all(early[3:])
    height = pieces[0].shape[0]
    copies = []
    for j in reversed(range(len(pieces))):
        rows = rows_at(place_ref[j], height)
        made = total[rows, :] * spread_in[rows, :]
        if stored:
            total[rows, :] = made
            copies += start_all([(total.at[rows], pieces[j])], sems, 4 + j)
        else:
            pieces[j][...] = made
    wait_all(copies)


def feature_pieces(source, row, place, base, remote, spread, incoming, stored):
    rows, chunk = base.shape
    feats = place.shape[0]
    make = hbm if stored else f32
    return pl.pallas_call(
        functools.partial(pieces_body, stored),
        out_shape=[make(rows // feats, chunk)] * feats,
        in_specs=[SMEM] * 3 + [HBM] * 4,
        out_specs=[HBM if stored else VMEM] * feats,
        scratch_shapes=[scratch(*a.shape) for a in (base, remote, spread, incoming)]
        + [pltpu.SemaphoreType.DMA((4 + feats,))],
        compiler_params=PARAMS,
        cost_estimate=cost(0),
    )(source, row, place, *pinned(base, remote, spread), incoming)


def chosen_block(weights, number, turn, c, chunk, lanes):
    rows = pl.ds(c * chunk if weights[0].shape[0] > chunk else 0, chunk)
    block = weights[0][rows, lanes]
    for k in range(1, number):
        block = jnp.where(turn == k, weights[k][rows, lanes], block)
    return block


def product_body(count, choices, later, c, step, last, turn_ref, start, *refs):
    pieces, refs = refs[:count], refs[count:]
    weights, refs = refs[: sum(choices)], refs[sum(choices) :]
    ahead, refs = refs[: sum(later)], refs[sum(later) :]
    kept, (out, left, held, sems) = refs[: len(later)], refs[len(later) :]
    chunk = pieces[0].shape[1]
    left[...] = left_parts(jnp.concatenate([p[...] for p in pieces], axis=1))
    copies = []
    for j in range(held.shape[1] // step):
        lanes = pl.ds(j * step, step)
        blocks, at = [], 0
        for number in choices:
            blocks.append(chosen_block(weights[at:], number, turn_ref[0], c, chunk, lanes))
            at += number
        right = right_parts(jnp.concatenate(blocks, axis=0))
        made = start[:, lanes] + jnp.dot(left[...], right, preferred_element_type=jnp.float32)
        if last:
            held[:, lanes] = made
            copies += start_all([(held.at[:, lanes], out.at[:, lanes])], sems, j)
        else:
            out[:, lanes] = made
    at = 0
    for number, block in zip(later, kept):
        block[...] = chosen_block(ahead[at:], number, turn_ref[0], c, chunk, pl.ds(0, held.shape[1]))
        at += number
    wait_all(copies)


def add_product(turn, start, pieces, weights, c, last, ahead=()):
    rows, chunk = pieces[0].shape
    width = start.shape[1]
    step = min(2 * LANES, width)
    count = len(pieces)
    flat = [w for group in [*weights, *ahead] for w in group]
    choices, later = [len(group) for group in weights], [len(group) for group in ahead]
    return pl.pallas_call(
        functools.partial(product_body, count, choices, later, c, step, last),
        out_shape=[f32(chunk, width)] * len(later) + [hbm(rows, width) if last else f32(rows, width)],
        in_specs=[SMEM] + [VMEM] * (1 + count + len(flat)),
        out_specs=[VMEM] * len(later) + [HBM if last else VMEM],
        scratch_shapes=[
            pltpu.VMEM((rows, 3 * count * chunk), jnp.bfloat16),
            scratch(rows, width),
            pltpu.SemaphoreType.DMA((width // step,)),
        ],
        compiler_params=PARAMS,
        cost_estimate=cost(6 * count * rows * chunk * width),
    )(turn, start, *pieces, *flat)


def solution(mesh):
    parts = mesh.shape["dom"]
    feats = mesh.shape["feat"]
    sides = 2 if feats % 2 == 0 else 1
    halves = feats // sides
    others = list(range(1, halves))

    def feat_target(f, dh, dl):
        return (f // sides + dh) % halves * sides + (f % sides + dl) % sides

    def feat_send(x, dh, dl):
        return lax.ppermute(x, "feat", [(f, feat_target(f, dh, dl)) for f in range(feats)])

    def dom_exchange(x):
        return lax.all_to_all(x, "dom", split_axis=0, concat_axis=0, tiled=True)

    def per_device(
        features,
        degree,
        diag_adj,
        remote_adj,
        read_block,
        tile_src,
        tile_row,
        w_first,
        b_first,
        w_second,
        b_second,
    ):
        part, cols = features.shape
        tile = diag_adj.shape[1]
        blocks = part // tile
        remote = remote_adj[0]
        chunk = LANES if cols % LANES == 0 else cols
        chunks = cols // chunk
        f = lax.axis_index("feat")
        want, source, row = read_block[0], tile_src[0], tile_row[0]
        shifts = [(dh, dl) for dh in range(halves) for dl in range(sides)]
        place = jnp.stack([jnp.asarray(feat_target(f, dh, dl), jnp.int32) for dh, dl in shifts])
        first = jnp.reshape(jnp.asarray(f * cols, jnp.int32), (1,))
        bias = b_first[None, :]

        x_all = [features] + [feat_send(features, 0, dl) for dl in range(1, sides)]
        w_all = [w_first] + [feat_send(w_first, 0, dl) for dl in range(1, sides)]

        shares = chunks if parts % chunks == 0 else 1
        share = jnp.reshape(jnp.asarray(lax.axis_index("dom") % shares, jnp.int32), (1,))

        def share_send(x, k):
            pairs = [(s, s // shares * shares + (s % shares + k) % shares) for s in range(parts)]
            return lax.ppermute(x, "dom", pairs)

        w2_sent = row_block(share, w_second, w_second.shape[0] // shares)
        w2_got = [feat_send(w2_sent, dh, 0) for dh in others]

        scaling = lax.rsqrt(degree.astype(jnp.float32))
        spread = jnp.broadcast_to(scaling[:, None], (part, chunk))
        outgoing = outgoing_blocks(want, features, spread, tile)
        incoming = dom_exchange(outgoing)

        early = blocks // 4 * tile if chunks > 1 else part
        late = part - early
        marks = sorted({0, early // 2 // tile * tile, early, early + late // 2 // tile * tile, part})
        spans = list(zip(marks[:-1], marks[1:]))
        x_all[0], _ = lax.optimization_barrier((features, outgoing))
        send_steps = []
        for start, stop in spans:
            targets = [(0, 0, start)]
            for c in range(1, chunks):
                if stop <= early:
                    targets.append((c, 0, part + (c - 1) * early + start))
                else:
                    targets.append((c, 1, (c - 1) * late + start - early))
            send_steps.append((start, stop, targets))
        send_shapes = [(part + (chunks - 1) * early, chunk)]
        if chunks > 1:
            send_shapes.append(((chunks - 1) * late, chunk))
        sends = [partial_sums(place, [(dh * sides, send_steps)], x_all, w_all, send_shapes) for dh in others]
        sends, w2_got = lax.optimization_barrier((sends, w2_got))
        front = [feat_send(x[0], dh, 0) for dh, x in zip(others, sends)]

        own_steps = [(a, b, [(c, c, a) for c in range(chunks)]) for a, b in spans]
        own = list(partial_sums(place, [(0, own_steps)], x_all, w_all, [(part, chunk)] * chunks, HINT))

        incoming, own = lax.optimization_barrier((incoming, list(own)))
        w2_core = [w_second] + [feat_send(w_second, 0, dl) for dl in range(1, sides)]
        chosen = chosen_blocks(source, incoming)
        chosen_all = [chosen] + [feat_send(chosen, 0, dl) for dl in range(1, sides)]
        height = chosen.shape[0]
        tail_rows = (chunks - 1) * late
        ats = [dh * sides for dh in others] + [0]
        turned, _ = lax.optimization_barrier((place, chosen))
        made = remote_products(chosen_all, loaded_weights(turned, ats, w_all, cols), chunks)
        remote_front = [feat_send(made[i * chunks], dh, 0) for i, dh in enumerate(others)]
        remote_own = list(made[len(others) * chunks :])
        rest = []
        if chunks > 1:
            fresh, shapes = [], []
            for i in range(len(others)):
                fresh += made[i * chunks + 1 : (i + 1) * chunks]
            fresh += remote_own[1:]
            shapes = [x.shape for x in fresh]
            written = joined([], fresh, [(i, 0) for i in range(len(fresh))], shapes)
            lates, _ = lax.optimization_barrier(([x[1] for x in sends], written))
            rest = [feat_send(x, dh, 0) for dh, x in zip(others, lates)]
            remote_own[1:] = written[len(others) * (chunks - 1) :]

        reach = len(others)
        first_layout = [(h, h, 0, part, 0) for h in range(reach)]
        base = own_part(diag_adj, spread, own[0], front, first_layout, reach)
        if chunks > 1:
            written, _ = lax.optimization_barrier((written, base))
            late_sums = [
                [feat_send(written[i * (chunks - 1) + c], dh, 0) for i, dh in enumerate(others)]
                for c in range(chunks - 1)
            ]
        incoming, bases = [], []
        for c in range(chunks):
            if c == 0:
                outgoing, scaled = hidden_blocks(
                    row, want, first, 0, bias, base, remote, spread, [remote_own[0]] + remote_front
                )
            else:
                begin, _ = lax.optimization_barrier((own[c], outgoing))
                (held_diag, *held), base = resident_and_diagonal(
                    diag_adj, scaled, begin, remote, spread, remote_own[c]
                )
                bases.append(base)
                layout = []
                for h in range(reach):
                    layout.append((h, h, part + (c - 1) * early, part + c * early, 0))
                    if late > 0:
                        layout.append((h, reach + h, (c - 1) * late, c * late, early))
                begin = later_part(held_diag, held[2], held[0], front + rest, layout, reach)
                outgoing, scaled = hidden_blocks(
                    row, want, first, c * chunk, bias, begin, held[1], held[2], [held[3]] + late_sums[c - 1]
                )
            arrived = dom_exchange(outgoing)
            incoming.append(pinned(arrived)[0] if c < chunks - 1 else arrived)
        bases.append(diagonal_part(diag_adj, scaled))

        collected = []
        for c in range(chunks):
            pieces = feature_pieces(source, row, place, bases[c], remote, spread, incoming[c], c < chunks - 1)
            collected.append(
                [p if dh == 0 and dl == 0 else feat_send(p, dh, dl) for (dh, dl), p in zip(shifts, pieces)]
            )

        w2_groups = [[got] + [share_send(got, k) for k in range(1, shares)] for got in w2_got]
        w2_groups, _ = lax.optimization_barrier((w2_groups, outgoing))
        w2_far = [[feat_send(w, 0, dl) if dl > 0 else w for w in g] for g in w2_groups for dl in range(sides)]
        weights = [[w] for w in w2_core] + w2_far
        out = b_second[None, :]
        for c in range(chunks):
            turn = (share - c) % shares
            if c < chunks - 1 or halves == 1:
                (out,) = add_product(turn, out, collected[c], weights, c, c == chunks - 1)
            else:
                near, far = collected[c][:sides], collected[c][sides:]
                *kept, out = add_product(turn, out, near, weights[:sides], c, False, weights[sides:])
                (out,) = add_product(turn, out, far, [[w] for w in kept], c, True)
        return out

    return jax.shard_map(
        per_device,
        mesh=mesh,
        in_specs=(
            P("dom", "feat"),
            P("dom"),
            P("dom", None),
            P("dom", None, None, None),
            P("dom", None),
            P("dom", None),
            P("dom", None),
            P("feat", None),
            P(),
            P("feat", None),
            P(),
        ),
        out_specs=P(("dom", "feat"), None),
        check_vma=False,
    )
```

```python
import functools

import jax
import jax.numpy as jnp
from jax import lax
from jax.experimental import pallas as pl
from jax.experimental.pallas import tpu as pltpu
from jax.sharding import PartitionSpec as P

LANES = 128
TOUCH = 2
HINT = 5 * 10**10
VMEM_LIMIT = 24 * 1024 * 1024
VMEM = pl.BlockSpec(memory_space=pltpu.VMEM)
SMEM = pl.BlockSpec(memory_space=pltpu.SMEM)
HBM = pl.BlockSpec(memory_space=pltpu.HBM)
PARAMS = pltpu.CompilerParams(vmem_limit_bytes=VMEM_LIMIT)


def dot3(a, b):
    return jnp.dot(a, b, precision=lax.Precision.HIGH, preferred_element_type=jnp.float32)


def two_parts(x):
    high = x.astype(jnp.bfloat16)
    return high, (x - high.astype(jnp.float32)).astype(jnp.bfloat16)


def left_parts(x):
    high, low = two_parts(x)
    return jnp.concatenate([high, low, high], axis=1)


def right_parts(w):
    high, low = two_parts(w)
    return jnp.concatenate([high, high, low], axis=0)


def sum_of_products(lefts, parts):
    total = None
    for x, part in zip(lefts, parts):
        made = jnp.dot(left_parts(x), part, preferred_element_type=jnp.float32)
        total = made if total is None else total + made
    return total


def f32(*dims):
    return jax.ShapeDtypeStruct(dims, jnp.float32)


def hbm(*dims):
    return pltpu.HBM(dims, jnp.float32)


def pinned(*arrays):
    return [pltpu.with_memory_space_constraint(a, pltpu.HBM) for a in arrays]


def rows_at(index, height):
    return pl.ds(pl.multiple_of(index * height, height), height)


def scratch(*dims):
    return pltpu.VMEM(dims, jnp.float32)


def start_all(pairs, sems, first):
    copies = [pltpu.make_async_copy(a, b, sems.at[first + i]) for i, (a, b) in enumerate(pairs)]
    for copy in copies:
        copy.start()
    return copies


def wait_all(copies):
    for copy in copies:
        copy.wait()


def cost(flops):
    return pl.CostEstimate(flops=flops, bytes_accessed=0, transcendentals=0)


def slice_body(index_ref, source, out, sems):
    wait_all(start_all([(source.at[rows_at(index_ref[0], out.shape[0])], out)], sems, 0))


def row_block(index, source, height):
    return pl.pallas_call(
        slice_body,
        out_shape=f32(height, source.shape[1]),
        in_specs=[SMEM, HBM],
        out_specs=VMEM,
        scratch_shapes=[pltpu.SemaphoreType.DMA((1,))],
        compiler_params=PARAMS,
        cost_estimate=cost(0),
    )(index, *pinned(source))


def outgoing_body(want_ref, features, spread, blocks, held, sems):
    count, tile, cols = held.shape
    chunk = spread.shape[1]
    last = features.shape[0] // tile - 1
    copies = []
    for d in range(count):
        rows = rows_at(jnp.minimum(want_ref[d], last), tile)
        for c in range(cols // chunk):
            lanes = pl.ds(c * chunk, chunk)
            held[d, :, lanes] = features[rows, lanes] * spread[rows, :]
        copies += start_all([(held.at[d], blocks.at[d])], sems, d)
    wait_all(copies)


def outgoing_blocks(want, features, spread, tile):
    cols = features.shape[1]
    count = want.shape[0]
    return pl.pallas_call(
        outgoing_body,
        out_shape=hbm(count, tile, cols),
        in_specs=[SMEM, VMEM, VMEM],
        out_specs=HBM,
        scratch_shapes=[scratch(count, tile, cols), pltpu.SemaphoreType.DMA((count,))],
        compiler_params=PARAMS,
        cost_estimate=cost(HINT),
    )(want, features, spread)


def partial_body(count, groups, place_ref, *refs):
    lefts, rights, refs = refs[:count], refs[count : 2 * count], refs[2 * count :]
    outs, (left, right, result, sems) = refs[:-4], refs[-4:]
    cols = lefts[0].shape[1]
    chunk = outs[0].shape[1]
    used = 0
    weights_in, loads, stores = [], [], []
    for n, (at, _) in enumerate(groups):
        lanes = pl.ds(pl.multiple_of(place_ref[at] * cols, cols), cols)
        weights_in.append(start_all([(w.at[:, lanes], right.at[n, j]) for j, w in enumerate(rights)], sems, used))
        used += count
    for start, stop, _ in groups[0][1]:
        rows = pl.ds(start, stop - start)
        pairs = [(x.at[rows], left.at[rows, pl.ds(j * cols, cols)]) for j, x in enumerate(lefts)]
        loads.append(start_all(pairs, sems, used))
        used += count
    for n, (_, steps) in enumerate(groups):
        wait_all(weights_in[n])
        parts = [right_parts(right[n, j]) for j in range(count)]
        for i, (start, stop, targets) in enumerate(steps):
            if n == 0:
                wait_all(loads[i])
            rows = pl.ds(start, stop - start)
            made = sum_of_products([left[rows, pl.ds(j * cols, cols)] for j in range(count)], parts)
            result[n, rows, :] = made
            pairs = [
                (result.at[n, rows, pl.ds(c * chunk, chunk)], outs[o].at[pl.ds(offset, stop - start)])
                for c, o, offset in targets
            ]
            stores += start_all(pairs, sems, used)
            used += len(pairs)
    wait_all(stores)


def partial_sums(place, groups, lefts, weights, shapes, flops=0):
    rows, cols = lefts[0].shape
    depth = weights[0].shape[0]
    count = len(lefts)
    copies = count * (len(groups) + len(groups[0][1]))
    copies += sum(len(targets) for _, steps in groups for _, _, targets in steps)
    return pl.pallas_call(
        functools.partial(partial_body, count, groups),
        out_shape=[hbm(*s) for s in shapes],
        in_specs=[SMEM] + [HBM] * (2 * count),
        out_specs=[HBM] * len(shapes),
        scratch_shapes=[
            scratch(rows, count * cols),
            scratch(len(groups), count, depth, cols),
            scratch(len(groups), rows, cols),
            pltpu.SemaphoreType.DMA((copies,)),
        ],
        compiler_params=PARAMS,
        cost_estimate=cost(flops),
    )(place, *pinned(lefts[0]), *lefts[1:], *pinned(weights[0]), *weights[1:])


def loaded_body(ats, place_ref, *refs):
    sources, outs, sems = refs[: -1 - len(ats)], refs[-1 - len(ats) : -1], refs[-1]
    depth = sources[0].shape[0]
    pairs = []
    for at, out in zip(ats, outs):
        cols = out.shape[1]
        lanes = pl.ds(pl.multiple_of(place_ref[at] * cols, cols), cols)
        pairs += [(w.at[:, lanes], out.at[pl.ds(j * depth, depth)]) for j, w in enumerate(sources)]
    wait_all(start_all(pairs, sems, 0))


def loaded_weights(place, ats, weights, cols):
    depth = weights[0].shape[0]
    count = len(weights)
    return pl.pallas_call(
        functools.partial(loaded_body, ats),
        out_shape=[f32(count * depth, cols)] * len(ats),
        in_specs=[SMEM] + [HBM] * count,
        out_specs=[VMEM] * len(ats),
        scratch_shapes=[pltpu.SemaphoreType.DMA((count * len(ats),))],
        compiler_params=PARAMS,
        cost_estimate=cost(0),
    )(place, *pinned(weights[0]), *weights[1:])


def remote_body(count, *refs):
    lefts, refs = refs[:count], refs[count:]
    groups = len(refs) // (1 + lefts[0].shape[1] // refs[-1].shape[1])
    weights, outs = refs[:groups], refs[groups:]
    chunk = outs[0].shape[1]
    chunks = len(outs) // groups
    depth = lefts[0].shape[1]
    for n, weight in enumerate(weights):
        parts = [right_parts(weight[pl.ds(j * depth, depth), :]) for j in range(count)]
        made = sum_of_products([x[...] for x in lefts], parts)
        for c in range(chunks):
            outs[n * chunks + c][...] = made[:, c * chunk : (c + 1) * chunk]


def remote_products(lefts, weights, chunks):
    rows, cols = lefts[0].shape
    outs = len(weights) * chunks
    return pl.pallas_call(
        functools.partial(remote_body, len(lefts)),
        out_shape=[f32(rows, cols // chunks)] * outs,
        in_specs=[VMEM] * (len(lefts) + len(weights)),
        out_specs=[VMEM] * outs,
        compiler_params=PARAMS,
        cost_estimate=cost(0),
    )(*lefts, *weights)


def joined_body(plan, count, *refs):
    fresh, outs, sems = refs[count : count + len(plan)], refs[count + len(plan) : -1], refs[-1]
    places = [outs[o].at[pl.ds(offset, x.shape[0])] for x, (o, offset) in zip(fresh, plan)]
    wait_all(start_all(list(zip(fresh, places)), sems, 0))


def joined(buffers, fresh, plan, shapes):
    count = len(buffers)
    return pl.pallas_call(
        functools.partial(joined_body, plan, count),
        out_shape=[hbm(*s) for s in shapes],
        in_specs=[HBM] * count + [VMEM] * len(fresh),
        out_specs=[HBM] * len(shapes),
        scratch_shapes=[pltpu.SemaphoreType.DMA((len(plan),))],
        input_output_aliases={i: i for i in range(count)},
        compiler_params=PARAMS,
        cost_estimate=cost(0),
    )(*pinned(*buffers), *fresh)


def chosen_body(source_ref, incoming, chosen):
    tile = incoming.shape[1]
    for g in range(chosen.shape[0] // tile):
        chosen[pl.ds(g * tile, tile), :] = incoming[source_ref[TOUCH * g]]


def chosen_blocks(source, incoming):
    tile, cols = incoming.shape[1:]
    groups = source.shape[0] // TOUCH
    return pl.pallas_call(
        chosen_body,
        out_shape=f32(groups * tile, cols),
        in_specs=[SMEM, VMEM],
        out_specs=VMEM,
        compiler_params=PARAMS,
        cost_estimate=cost(0),
    )(source, incoming)


def received_pairs(layout, received, recv_in):
    return [
        (received[r].at[pl.ds(start, stop - start)], recv_in.at[h, pl.ds(offset, stop - start)])
        for h, r, start, stop, offset in layout
    ]


def own_total(diag_in, spread_in, own_in, recv_in, total):
    tile = diag_in.shape[1]
    for i in range(diag_in.shape[0] // tile):
        rows = pl.ds(i * tile, tile)
        mixed = own_in[rows, :]
        for h in range(recv_in.shape[0]):
            mixed = mixed + recv_in[h, rows, :]
        total[rows, :] = dot3(diag_in[rows, :], mixed * spread_in[rows, :])


def own_body(layout, diag, spread, own, *refs):
    received, (base, diag_in, spread_in, own_in, recv_in, sems) = refs[:-6], refs[-6:]
    pairs = [(diag, diag_in), (spread, spread_in), (own, own_in)]
    wait_all(start_all(pairs + received_pairs(layout, received, recv_in), sems, 0))
    own_total(diag_in, spread_in, own_in, recv_in, base)


def own_part(diag, spread, own, received, layout, others):
    return pl.pallas_call(
        functools.partial(own_body, layout),
        out_shape=f32(*own.shape),
        in_specs=[HBM] * (3 + len(received)),
        out_specs=VMEM,
        scratch_shapes=[scratch(*a.shape) for a in (diag, spread, own)]
        + [scratch(others, *own.shape), pltpu.SemaphoreType.DMA((3 + len(layout),))],
        compiler_params=PARAMS,
        cost_estimate=cost(0),
    )(*pinned(diag, spread, own), *received)


def hidden_tail(
    lane_offset, row_ref, want_ref, first_ref, bias, remote, spread, sums, blocks, scaled_out, total, scaled, sems, used
):
    tiles, tile = remote.shape[:2]
    parts = blocks.shape[0]
    chunk = total.shape[1]
    for g in range(tiles // TOUCH):
        block = sums[0][pl.ds(g * tile, tile), :]
        for x in sums[1:]:
            block = block + x[pl.ds(g * tile, tile), :]
        for k in range(TOUCH * g, TOUCH * g + TOUCH):
            total[rows_at(row_ref[k], tile), :] += dot3(remote[k], block)
    lanes = pl.ds(pl.multiple_of(first_ref[0] + lane_offset, chunk), chunk)
    last = scaled.shape[0] // tile - 1
    copies = []
    for i in range(last + 1):
        rows = pl.ds(i * tile, tile)
        scaled[rows, :] = jnp.maximum(total[rows, :] * spread[rows, :] + bias[:, lanes], 0.0) * spread[rows, :]
        copies += start_all([(scaled.at[rows], scaled_out.at[rows])], sems, used + parts + i)
    pairs = [(scaled.at[rows_at(jnp.minimum(want_ref[d], last), tile)], blocks.at[d]) for d in range(parts)]
    wait_all(copies + start_all(pairs, sems, used))


def hidden_body(lane_offset, row_ref, want_ref, first_ref, bias, base, remote, spread, *refs):
    sums, (blocks, scaled_out, total, scaled, sems) = refs[:-5], refs[-5:]
    total[...] = base[...]
    hidden_tail(
        lane_offset, row_ref, want_ref, first_ref, bias, remote, spread, sums, blocks, scaled_out, total, scaled, sems, 0
    )


def hidden_blocks(row, want, first, lane_offset, bias, base, remote, spread, remote_sums):
    rows, chunk = base.shape
    tile = remote.shape[1]
    parts = want.shape[0]
    return pl.pallas_call(
        functools.partial(hidden_body, lane_offset),
        out_shape=[hbm(parts, tile, chunk), hbm(rows, chunk)],
        in_specs=[SMEM] * 3 + [VMEM] * (4 + len(remote_sums)),
        out_specs=[HBM, HBM],
        scratch_shapes=[scratch(rows, chunk), scratch(rows, chunk), pltpu.SemaphoreType.DMA((parts + rows // tile,))],
        compiler_params=PARAMS,
        cost_estimate=cost(HINT),
    )(row, want, first, bias, base, remote, spread, *remote_sums)


def resident_body(diag, scaled, others, *refs):
    sources, refs = refs[:others], refs[others:]
    diag_out, outs, refs = refs[0], refs[1 : 1 + others], refs[1 + others :]
    base, scaled_in, total, sems = refs
    tile = diag.shape[1]
    first = start_all([(diag, diag_out), (scaled, scaled_in)], sems, 0)
    copies = start_all(list(zip(sources, outs)), sems, 2)
    wait_all(first)
    for i in range(diag.shape[0] // tile):
        rows = pl.ds(i * tile, tile)
        total[rows, :] = dot3(diag_out[rows, :], scaled_in[rows, :])
    wait_all(copies + start_all([(total, base)], sems, 2 + others))


def resident_and_diagonal(diag, scaled, *arrays):
    count = len(arrays)

    def body(diag, scaled, *refs):
        resident_body(diag, scaled, count, *refs)

    *held, base = pl.pallas_call(
        body,
        out_shape=[f32(*a.shape) for a in (diag, *arrays)] + [hbm(*scaled.shape)],
        in_specs=[HBM] * (2 + count),
        out_specs=[VMEM] * (1 + count) + [HBM],
        scratch_shapes=[scratch(*scaled.shape)] * 2 + [pltpu.SemaphoreType.DMA((3 + count,))],
        compiler_params=PARAMS,
        cost_estimate=cost(0),
    )(*pinned(diag, scaled, *arrays))
    return held, base


def later_body(layout, diag, spread, own, *refs):
    received, (base, recv_in, sems) = refs[:-3], refs[-3:]
    wait_all(start_all(received_pairs(layout, received, recv_in), sems, 0))
    own_total(diag, spread, own, recv_in, base)


def later_part(diag, spread, own, received, layout, others):
    return pl.pallas_call(
        functools.partial(later_body, layout),
        out_shape=f32(*own.shape),
        in_specs=[VMEM] * 3 + [HBM] * len(received),
        out_specs=VMEM,
        scratch_shapes=[scratch(others, *own.shape), pltpu.SemaphoreType.DMA((len(layout),))],
        compiler_params=PARAMS,
        cost_estimate=cost(0),
    )(diag, spread, own, *received)


def diagonal_body(diag, scaled, base, diag_in, scaled_in, total, sems):
    tile = diag.shape[1]
    wait_all(start_all([(diag, diag_in), (scaled, scaled_in)], sems, 0))
    for i in range(diag.shape[0] // tile):
        rows = pl.ds(i * tile, tile)
        total[rows, :] = dot3(diag_in[rows, :], scaled_in[rows, :])
    wait_all(start_all([(total, base)], sems, 2))


def diagonal_part(diag, scaled):
    return pl.pallas_call(
        diagonal_body,
        out_shape=hbm(*scaled.shape),
        in_specs=[HBM, HBM],
        out_specs=HBM,
        scratch_shapes=[scratch(*a.shape) for a in (diag, scaled, scaled)] + [pltpu.SemaphoreType.DMA((3,))],
        compiler_params=PARAMS,
        cost_estimate=cost(0),
    )(*pinned(diag, scaled))


def pieces_body(stored, source_ref, row_ref, place_ref, base, remote, spread, incoming, *refs):
    pieces, (total, remote_in, spread_in, incoming_in, sems) = refs[:-5], refs[-5:]
    tiles, tile = remote.shape[:2]
    early = start_all(
        [(incoming, incoming_in), (remote, remote_in), (base, total), (spread, spread_in)], sems, 0
    )
    wait_all(early[:3])
    for k in range(tiles):
        total[rows_at(row_ref[k], tile), :] += dot3(remote_in[k], incoming_in[source_ref[k]])
    wait_all(early[3:])
    height = pieces[0].shape[0]
    copies = []
    for j in reversed(range(len(pieces))):
        rows = rows_at(place_ref[j], height)
        made = total[rows, :] * spread_in[rows, :]
        if stored:
            total[rows, :] = made
            copies += start_all([(total.at[rows], pieces[j])], sems, 4 + j)
        else:
            pieces[j][...] = made
    wait_all(copies)


def feature_pieces(source, row, place, base, remote, spread, incoming, stored):
    rows, chunk = base.shape
    feats = place.shape[0]
    make = hbm if stored else f32
    return pl.pallas_call(
        functools.partial(pieces_body, stored),
        out_shape=[make(rows // feats, chunk)] * feats,
        in_specs=[SMEM] * 3 + [HBM] * 4,
        out_specs=[HBM if stored else VMEM] * feats,
        scratch_shapes=[scratch(*a.shape) for a in (base, remote, spread, incoming)]
        + [pltpu.SemaphoreType.DMA((4 + feats,))],
        compiler_params=PARAMS,
        cost_estimate=cost(0),
    )(source, row, place, *pinned(base, remote, spread), incoming)


def chosen_block(weights, number, turn, c, chunk, lanes):
    rows = pl.ds(c * chunk if weights[0].shape[0] > chunk else 0, chunk)
    block = weights[0][rows, lanes]
    for k in range(1, number):
        block = jnp.where(turn == k, weights[k][rows, lanes], block)
    return block


def product_body(count, choices, later, c, step, last, turn_ref, start, *refs):
    pieces, refs = refs[:count], refs[count:]
    weights, refs = refs[: sum(choices)], refs[sum(choices) :]
    ahead, refs = refs[: sum(later)], refs[sum(later) :]
    kept, (out, left, held, sems) = refs[: len(later)], refs[len(later) :]
    chunk = pieces[0].shape[1]
    left[...] = left_parts(jnp.concatenate([p[...] for p in pieces], axis=1))
    copies = []
    for j in range(held.shape[1] // step):
        lanes = pl.ds(j * step, step)
        blocks, at = [], 0
        for number in choices:
            blocks.append(chosen_block(weights[at:], number, turn_ref[0], c, chunk, lanes))
            at += number
        right = right_parts(jnp.concatenate(blocks, axis=0))
        made = start[:, lanes] + jnp.dot(left[...], right, preferred_element_type=jnp.float32)
        if last:
            held[:, lanes] = made
            copies += start_all([(held.at[:, lanes], out.at[:, lanes])], sems, j)
        else:
            out[:, lanes] = made
    at = 0
    for number, block in zip(later, kept):
        block[...] = chosen_block(ahead[at:], number, turn_ref[0], c, chunk, pl.ds(0, held.shape[1]))
        at += number
    wait_all(copies)


def add_product(turn, start, pieces, weights, c, last, ahead=()):
    rows, chunk = pieces[0].shape
    width = start.shape[1]
    step = min(2 * LANES, width)
    count = len(pieces)
    flat = [w for group in [*weights, *ahead] for w in group]
    choices, later = [len(group) for group in weights], [len(group) for group in ahead]
    return pl.pallas_call(
        functools.partial(product_body, count, choices, later, c, step, last),
        out_shape=[f32(chunk, width)] * len(later) + [hbm(rows, width) if last else f32(rows, width)],
        in_specs=[SMEM] + [VMEM] * (1 + count + len(flat)),
        out_specs=[VMEM] * len(later) + [HBM if last else VMEM],
        scratch_shapes=[
            pltpu.VMEM((rows, 3 * count * chunk), jnp.bfloat16),
            scratch(rows, width),
            pltpu.SemaphoreType.DMA((width // step,)),
        ],
        compiler_params=PARAMS,
        cost_estimate=cost(6 * count * rows * chunk * width),
    )(turn, start, *pieces, *flat)


def solution(mesh):
    parts = mesh.shape["dom"]
    feats = mesh.shape["feat"]
    sides = 2 if feats % 2 == 0 else 1
    halves = feats // sides
    others = list(range(1, halves))

    def feat_target(f, dh, dl):
        return (f // sides + dh) % halves * sides + (f % sides + dl) % sides

    def feat_send(x, dh, dl):
        return lax.ppermute(x, "feat", [(f, feat_target(f, dh, dl)) for f in range(feats)])

    def dom_exchange(x):
        return lax.all_to_all(x, "dom", split_axis=0, concat_axis=0, tiled=True)

    def per_device(
        features,
        degree,
        diag_adj,
        remote_adj,
        read_block,
        tile_src,
        tile_row,
        w_first,
        b_first,
        w_second,
        b_second,
    ):
        part, cols = features.shape
        tile = diag_adj.shape[1]
        blocks = part // tile
        remote = remote_adj[0]
        chunk = LANES if cols % LANES == 0 else cols
        chunks = cols // chunk
        f = lax.axis_index("feat")
        want, source, row = read_block[0], tile_src[0], tile_row[0]
        shifts = [(dh, dl) for dh in range(halves) for dl in range(sides)]
        place = jnp.stack([jnp.asarray(feat_target(f, dh, dl), jnp.int32) for dh, dl in shifts])
        first = jnp.reshape(jnp.asarray(f * cols, jnp.int32), (1,))
        bias = b_first[None, :]

        x_all = [features] + [feat_send(features, 0, dl) for dl in range(1, sides)]
        w_all = [w_first] + [feat_send(w_first, 0, dl) for dl in range(1, sides)]

        shares = chunks if parts % chunks == 0 else 1
        share = jnp.reshape(jnp.asarray(lax.axis_index("dom") % shares, jnp.int32), (1,))

        def share_send(x, k):
            pairs = [(s, s // shares * shares + (s % shares + k) % shares) for s in range(parts)]
            return lax.ppermute(x, "dom", pairs)

        w2_sent = row_block(share, w_second, w_second.shape[0] // shares)
        w2_got = [feat_send(w2_sent, dh, 0) for dh in others]

        scaling = lax.rsqrt(degree.astype(jnp.float32))
        spread = jnp.broadcast_to(scaling[:, None], (part, chunk))
        outgoing = outgoing_blocks(want, features, spread, tile)
        incoming = dom_exchange(outgoing)

        early = blocks // 6 * tile if chunks > 1 else part
        late = part - early
        marks = sorted({0, early // 2 // tile * tile, early, early + late // 2 // tile * tile, part})
        spans = list(zip(marks[:-1], marks[1:]))
        x_all[0], _ = lax.optimization_barrier((features, outgoing))
        send_steps = []
        for start, stop in spans:
            targets = [(0, 0, start)]
            for c in range(1, chunks):
                if stop <= early:
                    targets.append((c, 0, part + (c - 1) * early + start))
                else:
                    targets.append((c, 1, (c - 1) * late + start - early))
            send_steps.append((start, stop, targets))
        send_shapes = [(part + (chunks - 1) * early, chunk)]
        if chunks > 1:
            send_shapes.append(((chunks - 1) * late, chunk))
        sends = [partial_sums(place, [(dh * sides, send_steps)], x_all, w_all, send_shapes) for dh in others]
        sends, w2_got = lax.optimization_barrier((sends, w2_got))
        front = [feat_send(x[0], dh, 0) for dh, x in zip(others, sends)]

        own_steps = [(a, b, [(c, c, a) for c in range(chunks)]) for a, b in spans]
        own = list(partial_sums(place, [(0, own_steps)], x_all, w_all, [(part, chunk)] * chunks, HINT))

        incoming, own = lax.optimization_barrier((incoming, list(own)))
        w2_core = [w_second] + [feat_send(w_second, 0, dl) for dl in range(1, sides)]
        chosen = chosen_blocks(source, incoming)
        chosen_all = [chosen] + [feat_send(chosen, 0, dl) for dl in range(1, sides)]
        height = chosen.shape[0]
        tail_rows = (chunks - 1) * late
        ats = [dh * sides for dh in others] + [0]
        turned, _ = lax.optimization_barrier((place, chosen))
        made = remote_products(chosen_all, loaded_weights(turned, ats, w_all, cols), chunks)
        remote_front = [feat_send(made[i * chunks], dh, 0) for i, dh in enumerate(others)]
        remote_own = list(made[len(others) * chunks :])
        rest = []
        if chunks > 1:
            fresh, shapes = [], []
            for i in range(len(others)):
                fresh += made[i * chunks + 1 : (i + 1) * chunks]
            fresh += remote_own[1:]
            shapes = [x.shape for x in fresh]
            written = joined([], fresh, [(i, 0) for i in range(len(fresh))], shapes)
            lates, _ = lax.optimization_barrier(([x[1] for x in sends], written))
            rest = [feat_send(x, dh, 0) for dh, x in zip(others, lates)]
            remote_own[1:] = written[len(others) * (chunks - 1) :]

        reach = len(others)
        first_layout = [(h, h, 0, part, 0) for h in range(reach)]
        base = own_part(diag_adj, spread, own[0], front, first_layout, reach)
        if chunks > 1:
            written, _ = lax.optimization_barrier((written, base))
            late_sums = [
                [feat_send(written[i * (chunks - 1) + c], dh, 0) for i, dh in enumerate(others)]
                for c in range(chunks - 1)
            ]
        incoming, bases = [], []
        for c in range(chunks):
            if c == 0:
                outgoing, scaled = hidden_blocks(
                    row, want, first, 0, bias, base, remote, spread, [remote_own[0]] + remote_front
                )
            else:
                begin, _ = lax.optimization_barrier((own[c], outgoing))
                (held_diag, *held), base = resident_and_diagonal(
                    diag_adj, scaled, begin, remote, spread, remote_own[c]
                )
                bases.append(base)
                layout = []
                for h in range(reach):
                    layout.append((h, h, part + (c - 1) * early, part + c * early, 0))
                    if late > 0:
                        layout.append((h, reach + h, (c - 1) * late, c * late, early))
                begin = later_part(held_diag, held[2], held[0], front + rest, layout, reach)
                outgoing, scaled = hidden_blocks(
                    row, want, first, c * chunk, bias, begin, held[1], held[2], [held[3]] + late_sums[c - 1]
                )
            arrived = dom_exchange(outgoing)
            incoming.append(pinned(arrived)[0] if c < chunks - 1 else arrived)
        bases.append(diagonal_part(diag_adj, scaled))

        collected = []
        for c in range(chunks):
            pieces = feature_pieces(source, row, place, bases[c], remote, spread, incoming[c], c < chunks - 1)
            collected.append(
                [p if dh == 0 and dl == 0 else feat_send(p, dh, dl) for (dh, dl), p in zip(shifts, pieces)]
            )

        w2_groups = [[got] + [share_send(got, k) for k in range(1, shares)] for got in w2_got]
        w2_groups, _ = lax.optimization_barrier((w2_groups, outgoing))
        w2_far = [[feat_send(w, 0, dl) if dl > 0 else w for w in g] for g in w2_groups for dl in range(sides)]
        weights = [[w] for w in w2_core] + w2_far
        out = b_second[None, :]
        for c in range(chunks):
            turn = (share - c) % shares
            if c < chunks - 1 or halves == 1:
                (out,) = add_product(turn, out, collected[c], weights, c, c == chunks - 1)
            else:
                near, far = collected[c][:sides], collected[c][sides:]
                *kept, out = add_product(turn, out, near, weights[:sides], c, False, weights[sides:])
                (out,) = add_product(turn, out, far, [[w] for w in kept], c, True)
        return out

    return jax.shard_map(
        per_device,
        mesh=mesh,
        in_specs=(
            P("dom", "feat"),
            P("dom"),
            P("dom", None),
            P("dom", None, None, None),
            P("dom", None),
            P("dom", None),
            P("dom", None),
            P("feat", None),
            P(),
            P("feat", None),
            P(),
        ),
        out_specs=P(("dom", "feat"), None),
        check_vma=False,
    )
```
